32 devices in a mesh: dp: 4 (over z), seq: 8 (over y, x, core).
Axes of the slice: x: 2, y: 2, z: 4, core: 2. Of those that a mesh axis runs over, the one named last changes fastest.
Arguments:
- tokens: bfloat16 [4096, 2048], P(('dp', 'seq')), may hold values from -7 to 7
- doc_starts: int32 [4, 16], P('dp', 'seq'), may hold values from 0 to 960, as said below
- pad_mask: int32 [4, 1024], P('dp', 'seq'), may hold values from 0 to 1, as said below
- norm1_gain: bfloat16 [2048], P(('dp', 'seq')), may hold values from 0.5 to 1.5
- query_weight: bfloat16 [2048, 2048], P(('dp', 'seq')), may hold values from -0.125 to 0.125
- key_weight: bfloat16 [2048, 2048], P(('dp', 'seq')), may hold values from -0.125 to 0.125
- value_weight: bfloat16 [2048, 2048], P(('dp', 'seq')), may hold values from -0.125 to 0.125
- conv_weight: bfloat16 [3, 4, 2048], P(None, None, ('dp', 'seq')), may hold values from -3 to 3
- beta_weight: bfloat16 [2048, 16], replicated, may hold values from -1 to 1
- out_norm_gain: bfloat16 [128], replicated, may hold values from 0.5 to 1.5
- out_weight: bfloat16 [2048, 2048], P(('dp', 'seq')), may hold values from -0.125 to 0.125
- norm2_gain: bfloat16 [2048], P(('dp', 'seq')), may hold values from 0.5 to 1.5
- gate_weight: bfloat16 [2048, 5632], P(('dp', 'seq')), may hold values from -0.125 to 0.125
- up_weight: bfloat16 [2048, 5632], P(('dp', 'seq')), may hold values from -0.125 to 0.125
- down_weight: bfloat16 [5632, 2048], P(None, ('dp', 'seq')), may hold values from -0.078125 to 0.078125
- cotangent: bfloat16 [4096, 2048], P(('dp', 'seq')), may hold values from -6 to 6
Outputs:
- output: bfloat16 [4096, 2048], P(('dp', 'seq'))
- tokens_grad: float32 [4096, 2048], P(('dp', 'seq'))
- norm1_gain_grad: float32 [2048], P(('dp', 'seq'))
- query_grad: float32 [2048, 2048], P(('dp', 'seq'))
- key_grad: float32 [2048, 2048], P(('dp', 'seq'))
- value_grad: float32 [2048, 2048], P(('dp', 'seq'))
- conv_grad: float32 [3, 4, 2048], P(None, None, ('dp', 'seq'))
- beta_grad: float32 [2048, 16], replicated
- out_norm_grad: float32 [128], replicated
- out_grad: float32 [2048, 2048], P(('dp', 'seq'))
- norm2_gain_grad: float32 [2048], P(('dp', 'seq'))
- gate_grad: float32 [2048, 5632], P(('dp', 'seq'))
- up_grad: float32 [2048, 5632], P(('dp', 'seq'))
- down_grad: float32 [5632, 2048], P(None, ('dp', 'seq'))
The draws below stay inside these ranges and needn't reach their ends.
Inputs may be any that keep to these rules, and one draw needn't show every extreme that they name: `doc_starts`: in each group, entries never fall along the row; an entry equals its own block's offset (64 times the block's index) where a document begins and the previous entry elsewhere; a document begins at block 0 and at the last block; one document begins within the first 128 tokens and runs into the last 128 tokens of the group. `pad_mask`: 0 marks padding, which stands only at the end of a document's last block of 64 tokens and covers 0 to 47 of its tokens.
All inputs are finite; a program needn't handle non-finite values.
Results may differ from the reference program's by a relative error of at most 0.012.
The reference program's roundings to bfloat16 on the way count: a program that leaves them out, or rounds other values in their place, can miss the bound.
Values may be sent and summed in bfloat16 or wider, within the bound.
A program may use at most 448 MiB of HBM per device.

```python
import jax
import jax.numpy as jnp
from jax import lax

D = 2048
HEADS = 16
HEAD = 128
FF = 5632
CONV = 4
BLOCK = 64
TOK_DEV = 128
GROUPS = 4
GROUP_TOK = 1024
BLOCKS = 16
TOKENS = 4096


common_level = 0.5


def layout(key):
    per_device = TOK_DEV // BLOCK
    indices = jnp.arange(BLOCKS, dtype=jnp.int32)[None, :]
    beginnings = jax.random.randint(jax.random.fold_in(key, 11), (GROUPS, BLOCKS), 0, 2)
    span_first = jax.random.randint(jax.random.fold_in(key, 12), (GROUPS, 1), 0, per_device)
    span_last = BLOCKS - 1 - jax.random.randint(jax.random.fold_in(key, 13), (GROUPS, 1), 0, per_device - 1)
    beginnings = jnp.where((indices > span_first) & (indices < span_last), 0, beginnings)
    marked = (indices == 0) | (indices == span_first) | (indices == span_last) | (indices == BLOCKS - 1)
    beginnings = jnp.where(marked, 1, beginnings).astype(jnp.int32)
    padding = jax.random.randint(jax.random.fold_in(key, 14), (GROUPS, BLOCKS), 0, 48)
    return (beginnings, padding)


def draw_doc_starts(key, part):
    beginnings, padding = layout(key)
    indices = jnp.arange(BLOCKS, dtype=jnp.int32)[None, :]
    opened = lax.cummax(jnp.where(beginnings == 1, indices, 0), axis=1)
    return (opened * BLOCK).astype(jnp.int32)


def draw_pad_mask(key, part):
    beginnings, padding = layout(key)
    closing = jnp.concatenate([beginnings[:, 1:], jnp.ones((GROUPS, 1), jnp.int32)], axis=1)
    within = jnp.arange(BLOCK, dtype=jnp.int32)[None, None, :]
    padded = (closing[:, :, None] == 1) & (within >= BLOCK - padding[:, :, None])
    return (1 - padded.astype(jnp.int32)).reshape(GROUPS, GROUP_TOK)


def shared_signs(key):
    picks = jax.random.randint(jax.random.fold_in(key, 21), (D,), 0, 2)
    return (2 * picks - 1).astype(jnp.float32)


def draw_tokens(key, part):
    signs = shared_signs(key)
    key = jax.random.fold_in(key, 31)
    noise = jax.random.truncated_normal(key, -6.0, 6.0, (TOKENS, D), jnp.float32)
    return (noise + common_level * signs[None, :]).astype(jnp.bfloat16)


def draw_beta_weight(key, part):
    signs = shared_signs(key)
    key = jax.random.fold_in(key, 32)
    base = jax.random.truncated_normal(jax.random.fold_in(key, 1), -6.0, 6.0, (D, HEADS), jnp.float32) * D ** (-0.5)
    count = max(1, HEADS // 4) + jax.random.randint(jax.random.fold_in(key, 2), (), 0, HEADS // 4 + 1)
    order = jax.random.permutation(jax.random.fold_in(key, 3), HEADS)
    slow = (order < count).astype(jnp.float32)
    depth = jax.random.uniform(jax.random.fold_in(key, 4), (HEADS,), jnp.float32, 5.0, 7.0)
    shift = slow * depth * (1.0 + common_level * common_level) ** 0.5 / (common_level * D)
    return (base - signs[:, None] * shift[None, :]).astype(jnp.bfloat16)


def block_scale(rng, shape, cuts, low, top_value):
    level = 1.0
    for axis_at, parts in cuts:
        steps = jax.random.uniform(jax.random.fold_in(jax.random.fold_in(rng, 6), axis_at), (parts,), jnp.float32, low / len(cuts), top_value / len(cuts))
        level = level * jnp.repeat(jnp.exp(steps), shape[axis_at] // parts).reshape((-1,) + (1,) * (len(shape) - 1 - axis_at))
    return level


def scatter_about(key, dims, width, bound, shards=(), held_as=jnp.bfloat16):
    factor_of = block_scale(key, dims, shards, -0.22, 0.18) if shards else 1.0
    drawn = jax.random.normal(key, dims, jnp.float32) * width * factor_of
    return jnp.minimum(jnp.maximum(drawn, -bound), bound).astype(held_as)


def setup_inputs(seed: int = 0) -> dict:
    keys = jax.random.split(jax.random.key(seed), 17)
    return {
        "tokens": draw_tokens(jax.random.fold_in(keys[16], 71), 0),
        "doc_starts": draw_doc_starts(jax.random.fold_in(keys[16], 71), 0),
        "pad_mask": draw_pad_mask(jax.random.fold_in(keys[16], 71), 0),
        "norm1_gain": jnp.clip(1.0 + 0.1 * jax.random.normal(keys[3], (D,), jnp.float32), 0.5, 1.5).astype(jnp.bfloat16),
        "query_weight": scatter_about(keys[4], (D, D), D ** -0.5, 0.125, ((0, 32),)),
        "key_weight": scatter_about(keys[5], (D, D), D ** -0.5, 0.125, ((0, 32),)),
        "value_weight": scatter_about(keys[6], (D, D), D ** -0.5, 0.125, ((0, 32),)),
        "conv_weight": scatter_about(keys[7], (3, CONV, D), CONV ** -0.5, 3.0, ((2, 32),)),
        "beta_weight": draw_beta_weight(jax.random.fold_in(keys[16], 71), 0),
        "out_norm_gain": jnp.clip(1.0 + 0.1 * jax.random.normal(keys[9], (HEAD,), jnp.float32), 0.5, 1.5).astype(jnp.bfloat16),
        "out_weight": scatter_about(keys[10], (D, D), D ** -0.5, 0.125, ((0, 32),)),
        "norm2_gain": jnp.clip(1.0 + 0.1 * jax.random.normal(keys[11], (D,), jnp.float32), 0.5, 1.5).astype(jnp.bfloat16),
        "gate_weight": scatter_about(keys[12], (D, FF), D ** -0.5, 0.125, ((0, 32),)),
        "up_weight": scatter_about(keys[13], (D, FF), D ** -0.5, 0.125, ((0, 32),)),
        "down_weight": scatter_about(keys[14], (FF, D), FF ** -0.5, 0.078125, ((1, 32),)),
        "cotangent": scatter_about(keys[15], (TOKENS, D), 1.0, 6.0, ((0, 32),)),
    }


EPSILON = 1e-06
PRECISE = lax.Precision.HIGHEST

@jax.custom_vjp
def low(v):
    return lax.optimization_barrier(v.astype(jnp.bfloat16)).astype(jnp.float32)

@jax.custom_vjp
def low_back(v):
    return v

def low_keep(v):
    return (low(v), None)

def low_pass(kept, grad):
    return (grad,)

def back_keep(v):
    return (v, None)

def back_low(kept, grad):
    return (low(grad),)
low.defvjp(low_keep, low_pass)
low_back.defvjp(back_keep, back_low)

def product(left, right):
    return jnp.dot(left.astype(jnp.float32), right.astype(jnp.float32), precision=PRECISE, preferred_element_type=jnp.float32)

def rms_norm(value, gain):
    return value * lax.rsqrt(lax.optimization_barrier(jnp.mean(value * value, axis=-1, keepdims=True)) + EPSILON) * gain

def block_parts(queries, key_rows, values, strength):
    keyed = key_rows * strength[..., None]
    block_len = key_rows.shape[1]
    lower_part = jnp.tril(jnp.einsum('hcd,hed->hce', keyed, key_rows, precision=PRECISE), -1)
    system = lower_part + jnp.eye(block_len, dtype=jnp.float32)
    weights = jax.scipy.linalg.solve_triangular(system, keyed, lower=True, unit_diagonal=True)
    updates = jax.scipy.linalg.solve_triangular(system, values * strength[..., None], lower=True, unit_diagonal=True)
    scores = jnp.tril(jnp.einsum('hcd,hed->hce', queries, key_rows, precision=PRECISE))
    return (weights, updates, scores)

def delta_step(state_now, inputs):
    queries, key_rows, values, strength, persist = inputs
    state_now = state_now * persist
    weights, updates, scores = block_parts(queries, key_rows, values, strength)
    corrected = updates - jnp.einsum('hcd,hde->hce', weights, state_now, precision=PRECISE)
    outputs = jnp.einsum('hcd,hde->hce', queries, state_now, precision=PRECISE) + jnp.einsum('hce,hef->hcf', scores, corrected, precision=PRECISE)
    state_now = state_now + jnp.einsum('hcd,hce->hde', key_rows, corrected, precision=PRECISE)
    return (state_now, outputs)

def delta_rule(queries, key_rows, values, strength, persist):
    length = queries.shape[0]
    block_total = length // BLOCK

    def blocks_of(array):
        return array.reshape(block_total, BLOCK, HEADS, HEAD).transpose(0, 2, 1, 3)
    strength_blocks = strength.reshape(block_total, BLOCK, HEADS).transpose(0, 2, 1)
    state_zero = jnp.zeros((HEADS, HEAD, HEAD), jnp.float32)
    ending, outputs = lax.scan(jax.checkpoint(delta_step), state_zero, (blocks_of(queries), blocks_of(key_rows), blocks_of(values), strength_blocks, persist))
    return outputs.transpose(0, 2, 1, 3).reshape(length, HEADS, HEAD)

def mixer_input(projected, conv_full, offsets):
    length = projected.shape[0]
    features = projected.shape[1] // 3
    positions = jnp.arange(length, dtype=jnp.int32)
    padded = jnp.concatenate([jnp.zeros((CONV - 1, projected.shape[1]), jnp.float32), projected], axis=0)
    results = []
    for member in range(3):
        columns = padded[:, member * features:(member + 1) * features]
        summed = jnp.zeros((length, features), jnp.float32)
        for lagged in range(CONV):
            inside = (positions - lagged >= offsets).astype(jnp.float32)[:, None]
            summed = summed + conv_full[member, lagged] * inside * columns[CONV - 1 - lagged:CONV - 1 - lagged + length]
        activated = jax.nn.silu(summed).reshape(length, HEADS, HEAD)
        if member < 2:
            activated = activated * lax.rsqrt(lax.optimization_barrier(jnp.sum(activated * activated, axis=-1, keepdims=True)) + EPSILON)
        if member == 0:
            activated = activated * HEAD ** (-0.5)
        results.append(activated)
    return results

def group_forward(residual_in, starts, pad_rows, weights):
    gain_first, w_query, w_key, w_value, conv_full, w_beta, out_gain, w_out, gain_second, w_gate, w_up, w_down = weights
    normed = low(rms_norm(residual_in, gain_first))
    projected = jnp.concatenate([low_back(low(product(normed, w_query))), low_back(low(product(normed, w_key))), low_back(low(product(normed, w_value)))], axis=1)
    logits = low_back(product(normed, w_beta))
    strength = jax.nn.sigmoid(logits) * pad_rows[:, None]
    offsets = jnp.repeat(starts, BLOCK)
    queries, key_rows, values = mixer_input(projected, conv_full, offsets)
    persist = (starts != BLOCK * jnp.arange(BLOCKS, dtype=jnp.int32)).astype(jnp.float32)
    mixed = delta_rule(low(queries), low(key_rows), low(values), strength, persist)
    out_normed = low(rms_norm(mixed, out_gain).reshape(GROUP_TOK, D))
    residual_mid = residual_in + low_back(product(out_normed, w_out))
    normed_two = low(rms_norm(residual_mid, gain_second))
    hidden = low(jax.nn.silu(low_back(product(normed_two, w_gate))) * low_back(product(normed_two, w_up)))
    return residual_mid + low_back(product(hidden, w_down))

def reference(tokens, doc_starts, pad_mask, norm1_gain, query_weight, key_weight, value_weight, conv_weight, beta_weight, out_norm_gain, out_weight, norm2_gain, gate_weight, up_weight, down_weight, cotangent):
    weights = tuple((array.astype(jnp.float32) for array in (norm1_gain, query_weight, key_weight, value_weight, conv_weight, beta_weight, out_norm_gain, out_weight, norm2_gain, gate_weight, up_weight, down_weight)))
    inputs = tokens.astype(jnp.float32).reshape(GROUPS, GROUP_TOK, D)
    masks = pad_mask.astype(jnp.float32)

    def forward(residuals, weight_set):

        def one_group(group_item):
            return group_forward(group_item[0], group_item[1], group_item[2], weight_set)
        return lax.map(jax.checkpoint(one_group), (residuals, doc_starts, masks))
    result, pull = jax.vjp(forward, inputs, weights)
    input_grad, grads = pull(cotangent.astype(jnp.float32).reshape(GROUPS, GROUP_TOK, D))
    return (result.reshape(TOKENS, D).astype(jnp.bfloat16), input_grad.reshape(TOKENS, D), grads[0], grads[1], grads[2], grads[3], grads[4], grads[5], grads[6], grads[7], grads[8], grads[9], grads[10], grads[11])
```

```python
import functools

import jax
import jax.numpy as jnp
from jax import lax
from jax.experimental import pallas as pl
from jax.experimental.pallas import tpu as pltpu
from jax.sharding import PartitionSpec as P

CONV = 4
BLOCK = 64


EPSILON = 1e-06
PRECISE = lax.Precision.HIGHEST


def from_behind(array, axis, by):
    length = lax.axis_size(axis)
    pairs = [(i, i + by) for i in range(length) if 0 <= i + by < length]
    return lax.ppermute(array, axis, pairs)


def product(left, right):
    return jnp.dot(left, right, preferred_element_type=jnp.float32)


def product_left(left, right):
    return lax.dot_general(
        left, right, (((0,), (0,)), ((), ())), preferred_element_type=jnp.float32
    )


def product_right(left, right):
    return lax.dot_general(
        left, right, (((1,), (1,)), ((), ())), preferred_element_type=jnp.float32
    )


def rounded(value):
    return lax.optimization_barrier(value.astype(jnp.bfloat16)).astype(jnp.float32)


def rms_norm(value, gain):
    return value * lax.rsqrt(jnp.mean(value * value, axis=-1, keepdims=True) + EPSILON) * gain


def block_parts(queries, key_rows, values, strength):
    keyed = key_rows * strength[..., None]
    block_len = key_rows.shape[1]
    lower_part = jnp.tril(jnp.einsum("hcd,hed->hce", keyed, key_rows, precision=PRECISE), -1)
    system = lower_part + jnp.eye(block_len, dtype=jnp.float32)
    weights = jax.scipy.linalg.solve_triangular(system, keyed, lower=True, unit_diagonal=True)
    updates = jax.scipy.linalg.solve_triangular(
        system, values * strength[..., None], lower=True, unit_diagonal=True
    )
    scores = jnp.tril(jnp.einsum("hcd,hed->hce", queries, key_rows, precision=PRECISE))
    return (weights, updates, scores)


def delta_step(state_now, inputs):
    queries, key_rows, values, strength, persist = inputs
    state_now = state_now * persist
    weights, updates, scores = block_parts(queries, key_rows, values, strength)
    corrected = updates - jnp.einsum("hcd,hde->hce", weights, state_now, precision=PRECISE)
    outputs = jnp.einsum("hcd,hde->hce", queries, state_now, precision=PRECISE) + jnp.einsum(
        "hce,hef->hcf", scores, corrected, precision=PRECISE
    )
    state_now = state_now + jnp.einsum("hcd,hce->hde", key_rows, corrected, precision=PRECISE)
    return (state_now, outputs)


def track_step(holding, inputs):
    state_now, transit = holding
    queries, key_rows, values, strength, persist = inputs
    state_now = state_now * persist
    transit = transit * persist
    weights, updates, scores = block_parts(queries, key_rows, values, strength)
    corrected = updates - jnp.einsum("hcd,hde->hce", weights, state_now, precision=PRECISE)
    outputs = jnp.einsum("hcd,hde->hce", queries, state_now, precision=PRECISE) + jnp.einsum(
        "hce,hef->hcf", scores, corrected, precision=PRECISE
    )
    leading = queries - jnp.einsum("hce,hed->hcd", scores, weights, precision=PRECISE)
    state_now = state_now + jnp.einsum("hcd,hce->hde", key_rows, corrected, precision=PRECISE)
    eraser = jnp.eye(key_rows.shape[2], dtype=jnp.float32) - jnp.einsum(
        "hcd,hce->hde", key_rows, weights, precision=PRECISE
    )
    return (
        (state_now, jnp.einsum("hde,hef->hdf", eraser, transit, precision=PRECISE)),
        (outputs, leading, transit),
    )


def advance(linear, offset_part, incoming):
    return jnp.einsum("hde,hef->hdf", linear, incoming, precision=PRECISE) + offset_part


def into_blocks(array):
    row_count, head_count, head_dim = array.shape
    return array.reshape(row_count // BLOCK, BLOCK, head_count, head_dim).transpose(0, 2, 1, 3)


def from_blocks(array):
    block_count, head_count, block_len, head_dim = array.shape
    return array.transpose(0, 2, 1, 3).reshape(block_count * block_len, head_count, head_dim)


def local_sequence(
    tokens,
    doc_starts,
    pad_mask,
    norm1_gain,
    query_weight,
    key_weight,
    value_weight,
    conv_weight,
    beta_weight,
    out_norm_gain,
    out_weight,
    norm2_gain,
    gate_weight,
    up_weight,
    down_weight,
    cotangent,
):
    row_count, features = tokens.shape
    head_count = beta_weight.shape[1]
    head_dim = out_norm_gain.shape[0]
    block_count = row_count // BLOCK
    w_query, w_key, w_value, w_out, conv_full, gain_first = (
        lax.all_gather(query_weight, ("dp", "seq"), axis=0, tiled=True),
        lax.all_gather(key_weight, ("dp", "seq"), axis=0, tiled=True),
        lax.all_gather(value_weight, ("dp", "seq"), axis=0, tiled=True),
        lax.all_gather(out_weight, ("dp", "seq"), axis=0, tiled=True),
        lax.all_gather(conv_weight, ("dp", "seq"), axis=2, tiled=True),
        lax.all_gather(norm1_gain, ("dp", "seq"), axis=0, tiled=True),
    )
    w_gate, w_up, w_down, gain_second = (
        lax.all_gather(gate_weight, ("dp", "seq"), axis=0, tiled=True),
        lax.all_gather(up_weight, ("dp", "seq"), axis=0, tiled=True),
        lax.all_gather(down_weight, ("dp", "seq"), axis=1, tiled=True),
        lax.all_gather(norm2_gain, ("dp", "seq"), axis=0, tiled=True),
    )
    seq_place = lax.axis_index("seq")
    positions = seq_place * row_count + jnp.arange(row_count, dtype=jnp.int32)
    starts = doc_starts[0]
    offsets = jnp.repeat(starts, BLOCK)
    persist = (
        starts != seq_place * row_count + BLOCK * jnp.arange(block_count, dtype=jnp.int32)
    ).astype(jnp.float32)
    pad_rows = pad_mask[0].astype(jnp.float32)[:, None]

    def mixer_in(extended, conv_taps):
        results = []
        for member in range(3):
            columns = extended[:, member * features : (member + 1) * features]
            summed = jnp.zeros((row_count, features), jnp.float32)
            for lagged in range(CONV):
                inside = (positions - lagged >= offsets).astype(jnp.float32)[:, None]
                summed = (
                    summed
                    + conv_taps[member, lagged]
                    * inside
                    * columns[CONV - 1 - lagged : CONV - 1 - lagged + row_count]
                )
            activated = jax.nn.silu(summed).reshape(row_count, head_count, head_dim)
            if member < 2:
                activated = activated * lax.rsqrt(
                    jnp.sum(activated * activated, axis=-1, keepdims=True) + EPSILON
                )
            if member == 0:
                activated = activated * head_dim ** (-0.5)
            results.append(activated)
        return tuple(results)

    residual_in = tokens.astype(jnp.float32)
    normed, norm_first_pull = jax.vjp(rms_norm, residual_in, gain_first.astype(jnp.float32))
    normed_low = normed.astype(jnp.bfloat16)
    projected = jnp.concatenate(
        [product(normed_low, w_query), product(normed_low, w_key), product(normed_low, w_value)],
        axis=1,
    ).astype(jnp.bfloat16)
    logits = product(normed_low, beta_weight)
    sigma_vals = jax.nn.sigmoid(logits)
    strength = sigma_vals * pad_rows
    rims = from_behind(projected[row_count - CONV + 1 :], "seq", 1)
    extended_in = jnp.concatenate([rims, projected], axis=0).astype(jnp.float32)
    (queries, key_rows, values), mixer_pull = jax.vjp(
        mixer_in, extended_in, conv_full.astype(jnp.float32)
    )
    query_blocks = into_blocks(rounded(queries))
    key_blocks = into_blocks(rounded(key_rows))
    value_blocks = into_blocks(rounded(values))
    strength_blocks = strength.reshape(block_count, BLOCK, head_count).transpose(0, 2, 1)
    zero_state = jnp.zeros((head_count, head_dim, head_dim), jnp.float32)
    identity = jnp.broadcast_to(
        jnp.eye(head_dim, dtype=jnp.float32), (head_count, head_dim, head_dim)
    )
    block_inputs = (query_blocks, key_blocks, value_blocks, strength_blocks, persist)
    (final_state, final_transit), (local_out, leading, transit) = lax.scan(
        track_step, (zero_state, identity), block_inputs
    )

    def forward_turn(turn_index, incoming):
        return from_behind(advance(final_transit, final_state, incoming), "seq", 1)

    start_state = lax.fori_loop(0, lax.axis_size("seq") - 1, forward_turn, zero_state)
    carried = jnp.einsum("nhde,hef->nhdf", transit, start_state, precision=PRECISE)
    mixed = from_blocks(
        local_out + jnp.einsum("nhcd,nhdf->nhcf", leading, carried, precision=PRECISE)
    )
    out_normed, out_norm_pull = jax.vjp(rms_norm, mixed, out_norm_gain.astype(jnp.float32))
    out_low = out_normed.reshape(row_count, features).astype(jnp.bfloat16)
    residual_mid = residual_in + product(out_low, w_out)
    normed_two, norm_second_pull = jax.vjp(rms_norm, residual_mid, gain_second.astype(jnp.float32))
    normed_two_low = normed_two.astype(jnp.bfloat16)
    gate_out = product(normed_two_low, w_gate)
    up_out = product(normed_two_low, w_up)
    hidden = (jax.nn.silu(gate_out) * up_out).astype(jnp.bfloat16)
    output = (residual_mid + product(hidden, w_down)).astype(jnp.bfloat16)
    grad_out = cotangent.astype(jnp.float32)
    down_grad = product_left(hidden, cotangent)
    hidden_grad = product_right(cotangent, w_down)
    gate_sigma = jax.nn.sigmoid(gate_out)
    gate_grad_low = (
        hidden_grad * up_out * gate_sigma * (1.0 + gate_out * (1.0 - gate_sigma))
    ).astype(jnp.bfloat16)
    up_grad_low = (hidden_grad * jax.nn.silu(gate_out)).astype(jnp.bfloat16)
    gate_grad = product_left(normed_two_low, gate_grad_low)
    up_grad = product_left(normed_two_low, up_grad_low)
    normed_two_grad = product_right(gate_grad_low, w_gate) + product_right(up_grad_low, w_up)
    mid_from_norm, gain_second_grad = norm_second_pull(normed_two_grad)
    residual_mid_grad = grad_out + mid_from_norm
    mid_low = residual_mid_grad.astype(jnp.bfloat16)
    out_grad = product_left(out_low, mid_low)
    out_normed_grad = product_right(mid_low, w_out).reshape(row_count, head_count, head_dim)
    mixed_grad, out_gain_grad = out_norm_pull(out_normed_grad)
    mixed_blocks = into_blocks(mixed_grad)
    pulled = jnp.einsum("nhcd,nhcf->nhdf", leading, mixed_blocks, precision=PRECISE)
    local_back = jnp.einsum("nhed,nhef->hdf", transit, pulled, precision=PRECISE)
    transit_turned = jnp.swapaxes(final_transit, 1, 2)

    def backward_turn(turn_index, incoming):
        return from_behind(advance(transit_turned, local_back, incoming), "seq", -1)

    end_grad = lax.fori_loop(0, lax.axis_size("seq") - 1, backward_turn, zero_state)

    def delta_local(query_in, key_in, value_in, strength_in):
        ending, outputs = lax.scan(
            jax.checkpoint(delta_step),
            start_state,
            (query_in, key_in, value_in, strength_in, persist),
        )
        return (outputs, ending)

    unused_out, delta_pull = jax.vjp(
        delta_local, query_blocks, key_blocks, value_blocks, strength_blocks
    )
    query_grad_blocks, key_grad_blocks, value_grad_blocks, strength_grad_blocks = delta_pull(
        (mixed_blocks, end_grad)
    )
    extended_grad, conv_grad = mixer_pull(
        (
            from_blocks(query_grad_blocks),
            from_blocks(key_grad_blocks),
            from_blocks(value_grad_blocks),
        )
    )
    rim_grad = from_behind(extended_grad[: CONV - 1], "seq", -1)
    projected_grad = jnp.concatenate(
        [extended_grad[CONV - 1 : row_count], extended_grad[row_count:] + rim_grad], axis=0
    ).astype(jnp.bfloat16)
    strength_grad = strength_grad_blocks.transpose(0, 2, 1).reshape(row_count, head_count)
    logits_grad = (strength_grad * pad_rows * sigma_vals * (1.0 - sigma_vals)).astype(jnp.bfloat16)
    part_query = projected_grad[:, :features]
    part_key = projected_grad[:, features : 2 * features]
    part_value = projected_grad[:, 2 * features :]
    query_grad = product_left(normed_low, part_query)
    key_grad = product_left(normed_low, part_key)
    value_grad = product_left(normed_low, part_value)
    beta_grad = product_left(normed_low, logits_grad)
    normed_grad = (
        product_right(part_query, w_query)
        + product_right(part_key, w_key)
        + product_right(part_value, w_value)
        + product_right(logits_grad, beta_weight)
    )
    input_from_norm, gain_first_grad = norm_first_pull(normed_grad)
    tokens_grad = residual_mid_grad + input_from_norm
    (
        shard_q,
        shard_k,
        shard_v,
        shard_o,
        shard_conv,
        shard_gain_one,
        shard_gate,
        shard_up,
        shard_down,
        shard_gain_two,
    ) = (
        lax.psum_scatter(query_grad, ("dp", "seq"), scatter_dimension=0, tiled=True),
        lax.psum_scatter(key_grad, ("dp", "seq"), scatter_dimension=0, tiled=True),
        lax.psum_scatter(value_grad, ("dp", "seq"), scatter_dimension=0, tiled=True),
        lax.psum_scatter(out_grad, ("dp", "seq"), scatter_dimension=0, tiled=True),
        lax.psum_scatter(conv_grad, ("dp", "seq"), scatter_dimension=2, tiled=True),
        lax.psum_scatter(gain_first_grad, ("dp", "seq"), scatter_dimension=0, tiled=True),
        lax.psum_scatter(gate_grad, ("dp", "seq"), scatter_dimension=0, tiled=True),
        lax.psum_scatter(up_grad, ("dp", "seq"), scatter_dimension=0, tiled=True),
        lax.psum_scatter(down_grad, ("dp", "seq"), scatter_dimension=1, tiled=True),
        lax.psum_scatter(gain_second_grad, ("dp", "seq"), scatter_dimension=0, tiled=True),
    )
    beta_total, out_gain_total = lax.psum((beta_grad, out_gain_grad), ("dp", "seq"))
    return (
        output,
        tokens_grad,
        shard_gain_one,
        shard_q,
        shard_k,
        shard_v,
        shard_conv,
        beta_total,
        out_gain_total,
        shard_o,
        shard_gain_two,
        shard_gate,
        shard_up,
        shard_down,
    )


F32 = jnp.float32
BF = jnp.bfloat16
NN=(((1,),(0,)),((),())); NT=(((1,),(1,)),((),())); TN=(((0,),(0,)),((),()))

def mm(a,b,dims=NN):
    return lax.dot_general(a,b,dims,preferred_element_type=F32)

def halves(a):
    high=a.astype(BF)
    return high,(a-high.astype(F32)).astype(BF)

def mm_lw(a,b,dims=NN):
    high,low=halves(b)
    return mm(a,high,dims)+mm(a,low,dims)

def mm_wl(a,b,dims=NN):
    high,low=halves(a)
    return mm(high,b,dims)+mm(low,b,dims)

def mm_ww(a,b,dims=NN):
    ah,al=halves(a); bh,bl=halves(b)
    return mm(ah,bh,dims)+(mm(al,bh,dims)+mm(ah,bl,dims))

def tile_masks(tile):
    row=lax.broadcasted_iota(jnp.int32,(tile,tile),0)
    col=lax.broadcasted_iota(jnp.int32,(tile,tile),1)
    return row,col

def delta_forward(heads,blocks,persist_ref,q_ref,k_ref,v_ref,brow_ref,o_ref,t_ref,w_ref,s_ref,f_ref,a_ref,u_buf,c_buf):
    hd=q_ref.shape[1]//heads
    tile=min(2*BLOCK,blocks*BLOCK); per=tile//BLOCK; tiles=blocks//per
    def first(index,carry):
        row,col=tile_masks(tile)
        same=(row//BLOCK)==(col//BLOCK)
        rows=pl.ds(pl.multiple_of(index*tile,tile),tile)
        eye=(row==col).astype(F32)
        ts=[];ls=[];ks=[];vs=[];bs=[]
        for h in range(heads):
            lanes=slice(h*hd,(h+1)*hd)
            k=k_ref[rows,lanes]; v=v_ref[rows,lanes]
            b=brow_ref[index,h:h+1,:]
            gram=mm(k,k,NT)
            bcol=jnp.sum(eye*b,axis=1,keepdims=True)
            low=jnp.where(same&(row>col),gram*bcol,0.0)
            ls.append(low); ks.append(k); vs.append(v); bs.append(b)
            ts.append(eye-jnp.where((row//2)==(col//2),low,0.0))
        size=2
        while size<BLOCK:
            cut=((row//(2*size))==(col//(2*size)))&((row//size)!=(col//size))
            mids=[mm_ww(jnp.where(cut,l,0.0),t) for l,t in zip(ls,ts)]
            ts=[t-mm_ww(t,m) for t,m in zip(ts,mids)]
            size*=2
        for h in range(heads):
            lanes=slice(h*hd,(h+1)*hd)
            t_ref[h,rows,:]=ts[h]
            tb=ts[h]*bs[h]
            wu=mm_wl(tb,jnp.concatenate([ks[h],vs[h]],axis=1))
            w_ref[rows,lanes]=wu[:,:hd]
            u_buf[rows,lanes]=wu[:,hd:]
            eyed=(lax.broadcasted_iota(jnp.int32,(hd,hd),0)==lax.broadcasted_iota(jnp.int32,(hd,hd),1)).astype(F32)
            for part in range(per):
                sub=slice(part*BLOCK,(part+1)*BLOCK)
                ab=mm_lw(ks[h][sub],wu[sub],TN)
                a_ref[h,index*per+part]=eyed-ab[:,:hd]
                c_buf[h,index*per+part]=ab[:,hd:]
        return carry
    lax.fori_loop(0,tiles,first,0)
    def chain(index,states):
        keep=persist_ref[index]
        new=[]
        for h in range(heads):
            s=states[h]*keep
            s_ref[h,index]=s
            new.append(mm_ww(a_ref[h,index],s)+c_buf[h,index])
        return tuple(new)
    lax.fori_loop(0,blocks,chain,tuple(jnp.zeros((hd,hd),F32) for _ in range(heads)))
    def last(index,carry):
        row,col=tile_masks(BLOCK)
        rows=pl.ds(pl.multiple_of(index*BLOCK,BLOCK),BLOCK)
        for h in range(heads):
            lanes=slice(h*hd,(h+1)*hd)
            q=q_ref[rows,lanes]; k=k_ref[rows,lanes]; s=s_ref[h,index]
            f=u_buf[rows,lanes]-mm_ww(w_ref[rows,lanes],s)
            p=jnp.where(row>=col,mm(q,k,NT),0.0)
            f_ref[rows,lanes]=f
            o_ref[rows,lanes]=mm_lw(q,s)+mm_ww(p,f)
        return carry
    lax.fori_loop(0,blocks,last,0)

def delta_backward(heads,blocks,persist_ref,q_ref,k_ref,v_ref,brow_ref,do_ref,t_ref,w_ref,s_ref,f_ref,a_ref,dq_ref,dk_ref,dv_ref,db_ref,y_buf,c_buf,g_buf):
    hd=q_ref.shape[1]//heads
    tile=min(2*BLOCK,blocks*BLOCK); per=tile//BLOCK
    def first(index,carry):
        row,col=tile_masks(BLOCK)
        rows=pl.ds(pl.multiple_of(index*BLOCK,BLOCK),BLOCK)
        for h in range(heads):
            lanes=slice(h*hd,(h+1)*hd)
            q=q_ref[rows,lanes]; k=k_ref[rows,lanes]; do=do_ref[rows,lanes]
            p=jnp.where(row>=col,mm(q,k,NT),0.0)
            y=mm_ww(p,do,TN)
            y_buf[rows,lanes]=y
            c_buf[h,index]=mm_lw(q,do,TN)-mm_ww(w_ref[rows,lanes],y,TN)
        return carry
    lax.fori_loop(0,blocks,first,0)
    def chain(step,grads):
        index=blocks-1-step
        keep=persist_ref[index]
        new=[]
        for h in range(heads):
            g=grads[h]
            g_buf[h,index]=g
            new.append((mm_ww(a_ref[h,index],g,TN)+c_buf[h,index])*keep)
        return tuple(new)
    lax.fori_loop(0,blocks,chain,tuple(jnp.zeros((hd,hd),F32) for _ in range(heads)))
    def last(index,carry):
        row,col=tile_masks(BLOCK)
        rows=pl.ds(pl.multiple_of(index*BLOCK,BLOCK),BLOCK)
        for h in range(heads):
            lanes=slice(h*hd,(h+1)*hd)
            q=q_ref[rows,lanes]; k=k_ref[rows,lanes]; v=v_ref[rows,lanes]; do=do_ref[rows,lanes]
            s=s_ref[h,index]; f=f_ref[rows,lanes]; g=g_buf[h,index]
            whole=brow_ref[index//per,h:h+1,:]
            part=index%per
            b=whole[:,:BLOCK]
            if per==2:
                b=jnp.where(part==0,whole[:,:BLOCK],whole[:,BLOCK:])
            bcol=jnp.sum(jnp.where(row==col,b,0.0),axis=1,keepdims=True)
            ttile=t_ref[h,rows,:]
            t=ttile[:,:BLOCK]
            if per==2:
                t=jnp.where(part==0,ttile[:,:BLOCK],ttile[:,BLOCK:])
            df=y_buf[rows,lanes]+mm_lw(k,g)
            dr=mm_ww(t,df,TN)
            dp=jnp.where(row>=col,mm_ww(do,f,NT),0.0)
            dl=jnp.where(row>col,-mm_ww(dr,f,NT),0.0)
            dq_ref[rows,lanes]=mm_ww(do,s,NT)+mm_wl(dp,k)
            dkb=mm_wl(dl,k)-mm_ww(dr,s,NT)
            dk=mm_wl(dp,q,TN)+mm_ww(f,g,NT)+mm_wl(dl*bcol,k,TN)+bcol*dkb
            dk_ref[rows,lanes]=dk
            dv_ref[rows,lanes]=bcol*dr
            kf=k.astype(F32); vf=v.astype(F32)
            db_ref[h,rows,:]=jnp.sum(dr*vf+dkb*kf,axis=1,keepdims=True)
        return carry
    lax.fori_loop(0,blocks,last,0)

def run_forward(q,k,v,strength,persist):
    rows,width=q.shape; heads=strength.shape[1]; hd=width//heads; blocks=rows//BLOCK
    tile=min(2*BLOCK,rows)
    brow=strength.reshape(rows//tile,tile,heads).transpose(0,2,1)
    shapes=lambda *s: jax.ShapeDtypeStruct(s,F32)
    vm=pl.BlockSpec(memory_space=pltpu.VMEM)
    outs=pl.pallas_call(functools.partial(delta_forward,heads,blocks),
        out_shape=(shapes(rows,width),shapes(heads,rows,tile),shapes(rows,width),shapes(heads,blocks,hd,hd),shapes(rows,width),shapes(heads,blocks,hd,hd)),
        in_specs=[pl.BlockSpec(memory_space=pltpu.SMEM)]+[vm]*4, out_specs=(vm,)*6,
        scratch_shapes=[pltpu.VMEM((rows,width),F32),pltpu.VMEM((heads,blocks,hd,hd),F32)],
        compiler_params=pltpu.CompilerParams(vmem_limit_bytes=40*2**20),
        )(persist,q,k,v,brow)
    return outs, brow

def run_backward(q,k,v,brow,persist,do,saved):
    t,w,s,f,a=saved
    rows,width=q.shape; heads=brow.shape[1]; hd=width//heads; blocks=rows//BLOCK
    shapes=lambda *s: jax.ShapeDtypeStruct(s,F32)
    vm=pl.BlockSpec(memory_space=pltpu.VMEM)
    return pl.pallas_call(functools.partial(delta_backward,heads,blocks),
        out_shape=(shapes(rows,width),)*3+(shapes(heads,rows,1),),
        in_specs=[pl.BlockSpec(memory_space=pltpu.SMEM)]+[vm]*10, out_specs=(vm,)*4,
        scratch_shapes=[pltpu.VMEM((rows,width),F32),pltpu.VMEM((heads,blocks,hd,hd),F32),pltpu.VMEM((heads,blocks,hd,hd),F32)],
        compiler_params=pltpu.CompilerParams(vmem_limit_bytes=40*2**20),
        )(persist,q,k,v,brow,do,t,w,s,f,a)


def gather_seq(array):
    return lax.all_gather(array, "seq", axis=0, tiled=True)


def scatter_seq(array):
    return lax.psum_scatter(array, "seq", scatter_dimension=0, tiled=True)


def exchange_seq(array):
    return lax.all_to_all(array, "seq", split_axis=0, concat_axis=0, tiled=True)


def columns_of(weights, count):
    rows = weights[0].shape[0]
    cut = jnp.stack([w.reshape(rows, count, -1) for w in weights], axis=1)
    cut = cut.transpose(2, 0, 1, 3).reshape(count * rows, -1)
    return lax.all_gather(exchange_seq(cut), "dp", axis=0, tiled=True)


def rows_of(grads, count, members):
    part = lax.psum_scatter(grads, "dp", scatter_dimension=0, tiled=True)
    back = exchange_seq(part)
    rows = back.shape[0] // count
    back = back.reshape(count, rows, members, -1).transpose(2, 1, 0, 3).astype(F32)
    return [back[m].reshape(rows, -1) for m in range(members)]


def local_heads(
    tokens,
    doc_starts,
    pad_mask,
    norm1_gain,
    query_weight,
    key_weight,
    value_weight,
    conv_weight,
    beta_weight,
    out_norm_gain,
    out_weight,
    norm2_gain,
    gate_weight,
    up_weight,
    down_weight,
    cotangent,
):
    row_count, features = tokens.shape
    width = lax.axis_size("seq")
    place = lax.axis_index("seq")
    head_dim = out_norm_gain.shape[0]
    heads = beta_weight.shape[1] // width
    mine = heads * head_dim
    total = row_count * width
    block_total = total // BLOCK
    hidden_mine = gate_weight.shape[1] // width

    small = jnp.concatenate(
        [
            norm1_gain[None],
            norm2_gain[None],
            conv_weight.reshape(3 * CONV, -1),
        ],
        axis=0,
    )
    small = lax.all_gather(small, ("dp", "seq"), axis=1, tiled=True).astype(F32)
    gain_first, gain_second = small[0], small[1]
    conv_full = small[2:].reshape(3, CONV, features)
    taps = lax.dynamic_slice_in_dim(conv_full, place * mine, mine, axis=2)
    marks = lax.all_gather(
        jnp.concatenate([doc_starts[0], pad_mask[0]]), "seq", axis=0
    )
    starts = marks[:, : doc_starts.shape[1]].reshape(-1)
    pad_rows = marks[:, doc_starts.shape[1] :].reshape(-1).astype(F32)[:, None]
    positions = jnp.arange(total, dtype=jnp.int32)
    offsets = jnp.repeat(starts, BLOCK)
    persist = (starts != BLOCK * jnp.arange(block_total, dtype=jnp.int32)).astype(F32)

    w_mixer = columns_of([query_weight, key_weight, value_weight, out_weight], width)
    w_qkv, w_out = w_mixer[:, : 3 * mine], w_mixer[:, 3 * mine :]
    w_hidden = columns_of([gate_weight, up_weight, down_weight.T], width)
    w_pair, w_down = w_hidden[:, : 2 * hidden_mine], w_hidden[:, 2 * hidden_mine :]
    w_beta = lax.dynamic_slice_in_dim(beta_weight, place * heads, heads, axis=1)
    w_out_rows = exchange_seq(w_out)

    def mixer_in(projected, taps_in):
        padded = jnp.concatenate([jnp.zeros((CONV - 1, 3 * mine), F32), projected], axis=0)
        results = []
        for member in range(3):
            columns = padded[:, member * mine : (member + 1) * mine]
            summed = jnp.zeros((total, mine), F32)
            for lagged in range(CONV):
                inside = (positions - lagged >= offsets).astype(F32)[:, None]
                summed = (
                    summed
                    + taps_in[member, lagged]
                    * inside
                    * columns[CONV - 1 - lagged : CONV - 1 - lagged + total]
                )
            activated = jax.nn.silu(summed).reshape(total, heads, head_dim)
            if member < 2:
                activated = activated * lax.rsqrt(
                    jnp.sum(activated * activated, axis=-1, keepdims=True) + EPSILON
                )
            if member == 0:
                activated = activated * head_dim ** (-0.5)
            results.append(activated.reshape(total, mine))
        return tuple(results)

    residual_in = tokens.astype(F32)
    normed, norm_first_pull = jax.vjp(rms_norm, residual_in, gain_first)
    normed_full = gather_seq(normed.astype(BF))
    cotangent_full = gather_seq(cotangent)
    projected = product(normed_full, w_qkv).astype(BF)
    logits = product(normed_full, w_beta)
    sigma_vals = jax.nn.sigmoid(logits)
    strength = sigma_vals * pad_rows
    (queries, key_rows, values), mixer_pull = jax.vjp(mixer_in, projected.astype(F32), taps)
    queries, key_rows, values = (a.astype(BF) for a in (queries, key_rows, values))
    (mixed, *saved), strength_rows = run_forward(queries, key_rows, values, strength, persist)
    out_normed, out_norm_pull = jax.vjp(
        rms_norm, mixed.reshape(total, heads, head_dim), out_norm_gain.astype(F32)
    )
    out_low = out_normed.reshape(total, mine).astype(BF)
    out_full = gather_seq(out_low).reshape(width, total, mine)
    out_full = out_full.transpose(1, 0, 2).reshape(total, features)
    attended = exchange_seq(product(out_full, w_out))
    attended = attended.reshape(width, row_count, mine).transpose(1, 0, 2)
    residual_mid = residual_in + attended.reshape(row_count, features)
    normed_two, norm_second_pull = jax.vjp(rms_norm, residual_mid, gain_second)
    normed_two_full = gather_seq(normed_two.astype(BF))
    pair = product(normed_two_full, w_pair)
    gate_out, up_out = pair[:, :hidden_mine], pair[:, hidden_mine:]
    gate_sigma = jax.nn.sigmoid(gate_out)
    gate_silu = gate_out * gate_sigma
    hidden = (gate_silu * up_out).astype(BF)
    added = scatter_seq(product_right(hidden, w_down).astype(BF))
    output = (residual_mid + added.astype(F32)).astype(BF)
    hidden_grad = product(cotangent_full, w_down)
    gate_grad_low = (
        hidden_grad * up_out * gate_sigma * (1.0 + gate_out * (1.0 - gate_sigma))
    ).astype(BF)
    up_grad_low = (hidden_grad * gate_silu).astype(BF)
    pair_grad_low = jnp.concatenate([gate_grad_low, up_grad_low], axis=1)
    normed_two_grad = scatter_seq(product_right(pair_grad_low, w_pair).astype(BF))
    hidden_grads = jnp.concatenate(
        [
            product_left(normed_two_full, pair_grad_low).astype(BF),
            product_left(cotangent_full, hidden).astype(BF),
        ],
        axis=1,
    )
    shard_gate, shard_up, shard_down = rows_of(hidden_grads, width, 3)
    mid_from_norm, gain_second_grad = norm_second_pull(normed_two_grad.astype(F32))
    residual_mid_grad = cotangent.astype(F32) + mid_from_norm
    mid_full = gather_seq(residual_mid_grad.astype(BF))
    mid_blocks = mid_full.reshape(total, width, mine)
    out_normed_grad = sum(
        product_right(mid_blocks[:, i], w_out_rows[i * mine : (i + 1) * mine]) for i in range(width)
    )
    mixed_grad, out_gain_grad = out_norm_pull(out_normed_grad.reshape(total, heads, head_dim))
    query_grads, key_grads, value_grads, strength_grads = run_backward(
        queries, key_rows, values, strength_rows, persist, mixed_grad.reshape(total, mine), saved
    )
    strength_grad = strength_grads[:, :, 0].T
    projected_grad, conv_grad = mixer_pull((query_grads, key_grads, value_grads))
    projected_grad = projected_grad.astype(BF)
    logits_grad = (strength_grad * pad_rows * sigma_vals * (1.0 - sigma_vals)).astype(BF)
    mid_mine = lax.dynamic_slice_in_dim(mid_full, place * mine, mine, axis=1)
    mixer_grads = jnp.concatenate(
        [
            product_left(normed_full, projected_grad).astype(BF),
            product_left(out_full, mid_mine).astype(BF),
        ],
        axis=1,
    )
    shard_q, shard_k, shard_v, shard_o = rows_of(mixer_grads, width, 4)
    beta_grad = product_left(normed_full, logits_grad)
    normed_grad = scatter_seq(
        (product_right(projected_grad, w_qkv) + product_right(logits_grad, w_beta)).astype(BF)
    )
    input_from_norm, gain_first_grad = norm_first_pull(normed_grad.astype(F32))
    tokens_grad = residual_mid_grad + input_from_norm

    beta_spread = jnp.zeros((features, heads * width), F32)
    beta_spread = lax.dynamic_update_slice(beta_spread, beta_grad, (0, place * heads))
    conv_spread = jnp.zeros((3 * CONV, features), F32)
    conv_spread = lax.dynamic_update_slice(
        conv_spread, conv_grad.reshape(3 * CONV, mine), (0, place * mine)
    )
    pieces = [beta_spread, conv_spread, gain_first_grad, gain_second_grad, out_gain_grad]
    sums = lax.psum(jnp.concatenate([p.reshape(-1) for p in pieces]), ("dp", "seq"))
    ends = []
    for piece in pieces:
        ends.append((ends[-1] if ends else 0) + piece.size)
    beta_total = sums[: ends[0]].reshape(features, heads * width)
    wide = sums[ends[0] : ends[3]].reshape(3 * CONV + 2, features)
    own = lax.axis_index("dp") * width + place
    owned = norm1_gain.shape[0]
    wide = lax.dynamic_slice_in_dim(wide, own * owned, owned, axis=1)
    out_gain_total = sums[ends[3] :]
    return (
        output,
        tokens_grad,
        wide[3 * CONV],
        shard_q,
        shard_k,
        shard_v,
        wide[: 3 * CONV].reshape(3, CONV, owned),
        beta_total,
        out_gain_total,
        shard_o,
        wide[3 * CONV + 1],
        shard_gate,
        shard_up,
        shard_down.T,
    )


def solution(mesh):
    in_specs = (
        P(("dp", "seq"), None),
        P("dp", "seq"),
        P("dp", "seq"),
        P(("dp", "seq")),
        P(("dp", "seq"), None),
        P(("dp", "seq"), None),
        P(("dp", "seq"), None),
        P(None, None, ("dp", "seq")),
        P(),
        P(),
        P(("dp", "seq"), None),
        P(("dp", "seq")),
        P(("dp", "seq"), None),
        P(("dp", "seq"), None),
        P(None, ("dp", "seq")),
        P(("dp", "seq"), None),
    )
    out_specs = (
        P(("dp", "seq"), None),
        P(("dp", "seq"), None),
        P(("dp", "seq")),
        P(("dp", "seq"), None),
        P(("dp", "seq"), None),
        P(("dp", "seq"), None),
        P(None, None, ("dp", "seq")),
        P(),
        P(),
        P(("dp", "seq"), None),
        P(("dp", "seq")),
        P(("dp", "seq"), None),
        P(("dp", "seq"), None),
        P(None, ("dp", "seq")),
    )

    def layer(*arrays):
        head_count, hidden_width = arrays[8].shape[1], arrays[12].shape[1]
        width = mesh.shape["seq"]
        by_heads = head_count % width == 0 and hidden_width % width == 0
        local = local_heads if by_heads else local_sequence
        return jax.shard_map(
            local, mesh=mesh, in_specs=in_specs, out_specs=out_specs, check_vma=False
        )(*arrays)

    return layer
```

```python
import functools

import jax
import jax.numpy as jnp
from jax import lax
from jax.experimental import pallas as pl
from jax.experimental.pallas import tpu as pltpu
from jax.sharding import PartitionSpec as P

CONV = 4
BLOCK = 64


EPSILON = 1e-06
PRECISE = lax.Precision.HIGHEST


def from_behind(array, axis, by):
    length = lax.axis_size(axis)
    pairs = [(i, i + by) for i in range(length) if 0 <= i + by < length]
    return lax.ppermute(array, axis, pairs)


def product(left, right):
    return jnp.dot(left, right, preferred_element_type=jnp.float32)


def product_left(left, right):
    return lax.dot_general(
        left, right, (((0,), (0,)), ((), ())), preferred_element_type=jnp.float32
    )


def product_right(left, right):
    return lax.dot_general(
        left, right, (((1,), (1,)), ((), ())), preferred_element_type=jnp.float32
    )


def rounded(value):
    return lax.optimization_barrier(value.astype(jnp.bfloat16)).astype(jnp.float32)


def rms_norm(value, gain):
    return value * lax.rsqrt(jnp.mean(value * value, axis=-1, keepdims=True) + EPSILON) * gain


def block_parts(queries, key_rows, values, strength):
    keyed = key_rows * strength[..., None]
    block_len = key_rows.shape[1]
    lower_part = jnp.tril(jnp.einsum("hcd,hed->hce", keyed, key_rows, precision=PRECISE), -1)
    system = lower_part + jnp.eye(block_len, dtype=jnp.float32)
    weights = jax.scipy.linalg.solve_triangular(system, keyed, lower=True, unit_diagonal=True)
    updates = jax.scipy.linalg.solve_triangular(
        system, values * strength[..., None], lower=True, unit_diagonal=True
    )
    scores = jnp.tril(jnp.einsum("hcd,hed->hce", queries, key_rows, precision=PRECISE))
    return (weights, updates, scores)


def delta_step(state_now, inputs):
    queries, key_rows, values, strength, persist = inputs
    state_now = state_now * persist
    weights, updates, scores = block_parts(queries, key_rows, values, strength)
    corrected = updates - jnp.einsum("hcd,hde->hce", weights, state_now, precision=PRECISE)
    outputs = jnp.einsum("hcd,hde->hce", queries, state_now, precision=PRECISE) + jnp.einsum(
        "hce,hef->hcf", scores, corrected, precision=PRECISE
    )
    state_now = state_now + jnp.einsum("hcd,hce->hde", key_rows, corrected, precision=PRECISE)
    return (state_now, outputs)


def track_step(holding, inputs):
    state_now, transit = holding
    queries, key_rows, values, strength, persist = inputs
    state_now = state_now * persist
    transit = transit * persist
    weights, updates, scores = block_parts(queries, key_rows, values, strength)
    corrected = updates - jnp.einsum("hcd,hde->hce", weights, state_now, precision=PRECISE)
    outputs = jnp.einsum("hcd,hde->hce", queries, state_now, precision=PRECISE) + jnp.einsum(
        "hce,hef->hcf", scores, corrected, precision=PRECISE
    )
    leading = queries - jnp.einsum("hce,hed->hcd", scores, weights, precision=PRECISE)
    state_now = state_now + jnp.einsum("hcd,hce->hde", key_rows, corrected, precision=PRECISE)
    eraser = jnp.eye(key_rows.shape[2], dtype=jnp.float32) - jnp.einsum(
        "hcd,hce->hde", key_rows, weights, precision=PRECISE
    )
    return (
        (state_now, jnp.einsum("hde,hef->hdf", eraser, transit, precision=PRECISE)),
        (outputs, leading, transit),
    )


def advance(linear, offset_part, incoming):
    return jnp.einsum("hde,hef->hdf", linear, incoming, precision=PRECISE) + offset_part


def into_blocks(array):
    row_count, head_count, head_dim = array.shape
    return array.reshape(row_count // BLOCK, BLOCK, head_count, head_dim).transpose(0, 2, 1, 3)


def from_blocks(array):
    block_count, head_count, block_len, head_dim = array.shape
    return array.transpose(0, 2, 1, 3).reshape(block_count * block_len, head_count, head_dim)


def local_sequence(
    tokens,
    doc_starts,
    pad_mask,
    norm1_gain,
    query_weight,
    key_weight,
    value_weight,
    conv_weight,
    beta_weight,
    out_norm_gain,
    out_weight,
    norm2_gain,
    gate_weight,
    up_weight,
    down_weight,
    cotangent,
):
    row_count, features = tokens.shape
    head_count = beta_weight.shape[1]
    head_dim = out_norm_gain.shape[0]
    block_count = row_count // BLOCK
    w_query, w_key, w_value, w_out, conv_full, gain_first = (
        lax.all_gather(query_weight, ("dp", "seq"), axis=0, tiled=True),
        lax.all_gather(key_weight, ("dp", "seq"), axis=0, tiled=True),
        lax.all_gather(value_weight, ("dp", "seq"), axis=0, tiled=True),
        lax.all_gather(out_weight, ("dp", "seq"), axis=0, tiled=True),
        lax.all_gather(conv_weight, ("dp", "seq"), axis=2, tiled=True),
        lax.all_gather(norm1_gain, ("dp", "seq"), axis=0, tiled=True),
    )
    w_gate, w_up, w_down, gain_second = (
        lax.all_gather(gate_weight, ("dp", "seq"), axis=0, tiled=True),
        lax.all_gather(up_weight, ("dp", "seq"), axis=0, tiled=True),
        lax.all_gather(down_weight, ("dp", "seq"), axis=1, tiled=True),
        lax.all_gather(norm2_gain, ("dp", "seq"), axis=0, tiled=True),
    )
    seq_place = lax.axis_index("seq")
    positions = seq_place * row_count + jnp.arange(row_count, dtype=jnp.int32)
    starts = doc_starts[0]
    offsets = jnp.repeat(starts, BLOCK)
    persist = (
        starts != seq_place * row_count + BLOCK * jnp.arange(block_count, dtype=jnp.int32)
    ).astype(jnp.float32)
    pad_rows = pad_mask[0].astype(jnp.float32)[:, None]

    def mixer_in(extended, conv_taps):
        results = []
        for member in range(3):
            columns = extended[:, member * features : (member + 1) * features]
            summed = jnp.zeros((row_count, features), jnp.float32)
            for lagged in range(CONV):
                inside = (positions - lagged >= offsets).astype(jnp.float32)[:, None]
                summed = (
                    summed
                    + conv_taps[member, lagged]
                    * inside
                    * columns[CONV - 1 - lagged : CONV - 1 - lagged + row_count]
                )
            activated = jax.nn.silu(summed).reshape(row_count, head_count, head_dim)
            if member < 2:
                activated = activated * lax.rsqrt(
                    jnp.sum(activated * activated, axis=-1, keepdims=True) + EPSILON
                )
            if member == 0:
                activated = activated * head_dim ** (-0.5)
            results.append(activated)
        return tuple(results)

    residual_in = tokens.astype(jnp.float32)
    normed, norm_first_pull = jax.vjp(rms_norm, residual_in, gain_first.astype(jnp.float32))
    normed_low = normed.astype(jnp.bfloat16)
    projected = jnp.concatenate(
        [product(normed_low, w_query), product(normed_low, w_key), product(normed_low, w_value)],
        axis=1,
    ).astype(jnp.bfloat16)
    logits = product(normed_low, beta_weight)
    sigma_vals = jax.nn.sigmoid(logits)
    strength = sigma_vals * pad_rows
    rims = from_behind(projected[row_count - CONV + 1 :], "seq", 1)
    extended_in = jnp.concatenate([rims, projected], axis=0).astype(jnp.float32)
    (queries, key_rows, values), mixer_pull = jax.vjp(
        mixer_in, extended_in, conv_full.astype(jnp.float32)
    )
    query_blocks = into_blocks(rounded(queries))
    key_blocks = into_blocks(rounded(key_rows))
    value_blocks = into_blocks(rounded(values))
    strength_blocks = strength.reshape(block_count, BLOCK, head_count).transpose(0, 2, 1)
    zero_state = jnp.zeros((head_count, head_dim, head_dim), jnp.float32)
    identity = jnp.broadcast_to(
        jnp.eye(head_dim, dtype=jnp.float32), (head_count, head_dim, head_dim)
    )
    block_inputs = (query_blocks, key_blocks, value_blocks, strength_blocks, persist)
    (final_state, final_transit), (local_out, leading, transit) = lax.scan(
        track_step, (zero_state, identity), block_inputs
    )

    def forward_turn(turn_index, incoming):
        return from_behind(advance(final_transit, final_state, incoming), "seq", 1)

    start_state = lax.fori_loop(0, lax.axis_size("seq") - 1, forward_turn, zero_state)
    carried = jnp.einsum("nhde,hef->nhdf", transit, start_state, precision=PRECISE)
    mixed = from_blocks(
        local_out + jnp.einsum("nhcd,nhdf->nhcf", leading, carried, precision=PRECISE)
    )
    out_normed, out_norm_pull = jax.vjp(rms_norm, mixed, out_norm_gain.astype(jnp.float32))
    out_low = out_normed.reshape(row_count, features).astype(jnp.bfloat16)
    residual_mid = residual_in + product(out_low, w_out)
    normed_two, norm_second_pull = jax.vjp(rms_norm, residual_mid, gain_second.astype(jnp.float32))
    normed_two_low = normed_two.astype(jnp.bfloat16)
    gate_out = product(normed_two_low, w_gate)
    up_out = product(normed_two_low, w_up)
    hidden = (jax.nn.silu(gate_out) * up_out).astype(jnp.bfloat16)
    output = (residual_mid + product(hidden, w_down)).astype(jnp.bfloat16)
    grad_out = cotangent.astype(jnp.float32)
    down_grad = product_left(hidden, cotangent)
    hidden_grad = product_right(cotangent, w_down)
    gate_sigma = jax.nn.sigmoid(gate_out)
    gate_grad_low = (
        hidden_grad * up_out * gate_sigma * (1.0 + gate_out * (1.0 - gate_sigma))
    ).astype(jnp.bfloat16)
    up_grad_low = (hidden_grad * jax.nn.silu(gate_out)).astype(jnp.bfloat16)
    gate_grad = product_left(normed_two_low, gate_grad_low)
    up_grad = product_left(normed_two_low, up_grad_low)
    normed_two_grad = product_right(gate_grad_low, w_gate) + product_right(up_grad_low, w_up)
    mid_from_norm, gain_second_grad = norm_second_pull(normed_two_grad)
    residual_mid_grad = grad_out + mid_from_norm
    mid_low = residual_mid_grad.astype(jnp.bfloat16)
    out_grad = product_left(out_low, mid_low)
    out_normed_grad = product_right(mid_low, w_out).reshape(row_count, head_count, head_dim)
    mixed_grad, out_gain_grad = out_norm_pull(out_normed_grad)
    mixed_blocks = into_blocks(mixed_grad)
    pulled = jnp.einsum("nhcd,nhcf->nhdf", leading, mixed_blocks, precision=PRECISE)
    local_back = jnp.einsum("nhed,nhef->hdf", transit, pulled, precision=PRECISE)
    transit_turned = jnp.swapaxes(final_transit, 1, 2)

    def backward_turn(turn_index, incoming):
        return from_behind(advance(transit_turned, local_back, incoming), "seq", -1)

    end_grad = lax.fori_loop(0, lax.axis_size("seq") - 1, backward_turn, zero_state)

    def delta_local(query_in, key_in, value_in, strength_in):
        ending, outputs = lax.scan(
            jax.checkpoint(delta_step),
            start_state,
            (query_in, key_in, value_in, strength_in, persist),
        )
        return (outputs, ending)

    unused_out, delta_pull = jax.vjp(
        delta_local, query_blocks, key_blocks, value_blocks, strength_blocks
    )
    query_grad_blocks, key_grad_blocks, value_grad_blocks, strength_grad_blocks = delta_pull(
        (mixed_blocks, end_grad)
    )
    extended_grad, conv_grad = mixer_pull(
        (
            from_blocks(query_grad_blocks),
            from_blocks(key_grad_blocks),
            from_blocks(value_grad_blocks),
        )
    )
    rim_grad = from_behind(extended_grad[: CONV - 1], "seq", -1)
    projected_grad = jnp.concatenate(
        [extended_grad[CONV - 1 : row_count], extended_grad[row_count:] + rim_grad], axis=0
    ).astype(jnp.bfloat16)
    strength_grad = strength_grad_blocks.transpose(0, 2, 1).reshape(row_count, head_count)
    logits_grad = (strength_grad * pad_rows * sigma_vals * (1.0 - sigma_vals)).astype(jnp.bfloat16)
    part_query = projected_grad[:, :features]
    part_key = projected_grad[:, features : 2 * features]
    part_value = projected_grad[:, 2 * features :]
    query_grad = product_left(normed_low, part_query)
    key_grad = product_left(normed_low, part_key)
    value_grad = product_left(normed_low, part_value)
    beta_grad = product_left(normed_low, logits_grad)
    normed_grad = (
        product_right(part_query, w_query)
        + product_right(part_key, w_key)
        + product_right(part_value, w_value)
        + product_right(logits_grad, beta_weight)
    )
    input_from_norm, gain_first_grad = norm_first_pull(normed_grad)
    tokens_grad = residual_mid_grad + input_from_norm
    (
        shard_q,
        shard_k,
        shard_v,
        shard_o,
        shard_conv,
        shard_gain_one,
        shard_gate,
        shard_up,
        shard_down,
        shard_gain_two,
    ) = (
        lax.psum_scatter(query_grad, ("dp", "seq"), scatter_dimension=0, tiled=True),
        lax.psum_scatter(key_grad, ("dp", "seq"), scatter_dimension=0, tiled=True),
        lax.psum_scatter(value_grad, ("dp", "seq"), scatter_dimension=0, tiled=True),
        lax.psum_scatter(out_grad, ("dp", "seq"), scatter_dimension=0, tiled=True),
        lax.psum_scatter(conv_grad, ("dp", "seq"), scatter_dimension=2, tiled=True),
        lax.psum_scatter(gain_first_grad, ("dp", "seq"), scatter_dimension=0, tiled=True),
        lax.psum_scatter(gate_grad, ("dp", "seq"), scatter_dimension=0, tiled=True),
        lax.psum_scatter(up_grad, ("dp", "seq"), scatter_dimension=0, tiled=True),
        lax.psum_scatter(down_grad, ("dp", "seq"), scatter_dimension=1, tiled=True),
        lax.psum_scatter(gain_second_grad, ("dp", "seq"), scatter_dimension=0, tiled=True),
    )
    beta_total, out_gain_total = lax.psum((beta_grad, out_gain_grad), ("dp", "seq"))
    return (
        output,
        tokens_grad,
        shard_gain_one,
        shard_q,
        shard_k,
        shard_v,
        shard_conv,
        beta_total,
        out_gain_total,
        shard_o,
        shard_gain_two,
        shard_gate,
        shard_up,
        shard_down,
    )


F32 = jnp.float32
BF = jnp.bfloat16
NN=(((1,),(0,)),((),())); NT=(((1,),(1,)),((),())); TN=(((0,),(0,)),((),()))

def mm(a,b,dims=NN):
    return lax.dot_general(a,b,dims,preferred_element_type=F32)

def halves(a):
    high=a.astype(BF)
    return high,(a-high.astype(F32)).astype(BF)

def mm_lw(a,b,dims=NN):
    high,low=halves(b)
    return mm(a,high,dims)+mm(a,low,dims)

def mm_wl(a,b,dims=NN):
    high,low=halves(a)
    return mm(high,b,dims)+mm(low,b,dims)

def mm_ww(a,b,dims=NN):
    ah,al=halves(a); bh,bl=halves(b)
    return mm(ah,bh,dims)+(mm(al,bh,dims)+mm(ah,bl,dims))

def tile_masks(tile):
    row=lax.broadcasted_iota(jnp.int32,(tile,tile),0)
    col=lax.broadcasted_iota(jnp.int32,(tile,tile),1)
    return row,col

def delta_forward(heads,blocks,persist_ref,q_ref,k_ref,v_ref,brow_ref,o_ref,t_ref,w_ref,s_ref,f_ref,a_ref,u_buf,c_buf):
    hd=q_ref.shape[1]//heads
    tile=min(2*BLOCK,blocks*BLOCK); per=tile//BLOCK; tiles=blocks//per
    def first(index,carry):
        row,col=tile_masks(tile)
        same=(row//BLOCK)==(col//BLOCK)
        rows=pl.ds(pl.multiple_of(index*tile,tile),tile)
        eye=(row==col).astype(F32)
        ts=[];ls=[];ks=[];vs=[];bs=[]
        for h in range(heads):
            lanes=slice(h*hd,(h+1)*hd)
            k=k_ref[rows,lanes]; v=v_ref[rows,lanes]
            b=brow_ref[index,h:h+1,:]
            gram=mm(k,k,NT)
            bcol=jnp.sum(eye*b,axis=1,keepdims=True)
            low=jnp.where(same&(row>col),gram*bcol,0.0)
            ls.append(low); ks.append(k); vs.append(v); bs.append(b)
            ts.append(eye-jnp.where((row//2)==(col//2),low,0.0))
        size=2
        while size<BLOCK:
            cut=((row//(2*size))==(col//(2*size)))&((row//size)!=(col//size))
            mids=[mm_ww(jnp.where(cut,l,0.0),t) for l,t in zip(ls,ts)]
            ts=[t-mm_ww(t,m) for t,m in zip(ts,mids)]
            size*=2
        for h in range(heads):
            lanes=slice(h*hd,(h+1)*hd)
            t_ref[h,rows,:]=ts[h]
            tb=ts[h]*bs[h]
            wu=mm_wl(tb,jnp.concatenate([ks[h],vs[h]],axis=1))
            w_ref[rows,lanes]=wu[:,:hd]
            u_buf[rows,lanes]=wu[:,hd:]
            eyed=(lax.broadcasted_iota(jnp.int32,(hd,hd),0)==lax.broadcasted_iota(jnp.int32,(hd,hd),1)).astype(F32)
            for part in range(per):
                sub=slice(part*BLOCK,(part+1)*BLOCK)
                ab=mm_lw(ks[h][sub],wu[sub],TN)
                a_ref[h,index*per+part]=eyed-ab[:,:hd]
                c_buf[h,index*per+part]=ab[:,hd:]
        return carry
    lax.fori_loop(0,tiles,first,0)
    def chain(index,states):
        keep=persist_ref[index]
        new=[]
        for h in range(heads):
            s=states[h]*keep
            s_ref[h,index]=s
            new.append(mm_ww(a_ref[h,index],s)+c_buf[h,index])
        return tuple(new)
    lax.fori_loop(0,blocks,chain,tuple(jnp.zeros((hd,hd),F32) for _ in range(heads)))
    def last(index,carry):
        row,col=tile_masks(BLOCK)
        rows=pl.ds(pl.multiple_of(index*BLOCK,BLOCK),BLOCK)
        for h in range(heads):
            lanes=slice(h*hd,(h+1)*hd)
            q=q_ref[rows,lanes]; k=k_ref[rows,lanes]; s=s_ref[h,index]
            f=u_buf[rows,lanes]-mm_ww(w_ref[rows,lanes],s)
            p=jnp.where(row>=col,mm(q,k,NT),0.0)
            f_ref[rows,lanes]=f
            o_ref[rows,lanes]=mm_lw(q,s)+mm_ww(p,f)
        return carry
    lax.fori_loop(0,blocks,last,0)

def delta_backward(heads,blocks,persist_ref,q_ref,k_ref,v_ref,brow_ref,do_ref,t_ref,w_ref,s_ref,f_ref,a_ref,dq_ref,dk_ref,dv_ref,db_ref,y_buf,c_buf,g_buf):
    hd=q_ref.shape[1]//heads
    tile=min(2*BLOCK,blocks*BLOCK); per=tile//BLOCK
    def first(index,carry):
        row,col=tile_masks(BLOCK)
        rows=pl.ds(pl.multiple_of(index*BLOCK,BLOCK),BLOCK)
        for h in range(heads):
            lanes=slice(h*hd,(h+1)*hd)
            q=q_ref[rows,lanes]; k=k_ref[rows,lanes]; do=do_ref[rows,lanes]
            p=jnp.where(row>=col,mm(q,k,NT),0.0)
            y=mm_ww(p,do,TN)
            y_buf[rows,lanes]=y
            c_buf[h,index]=mm_lw(q,do,TN)-mm_ww(w_ref[rows,lanes],y,TN)
        return carry
    lax.fori_loop(0,blocks,first,0)
    def chain(step,grads):
        index=blocks-1-step
        keep=persist_ref[index]
        new=[]
        for h in range(heads):
            g=grads[h]
            g_buf[h,index]=g
            new.append((mm_ww(a_ref[h,index],g,TN)+c_buf[h,index])*keep)
        return tuple(new)
    lax.fori_loop(0,blocks,chain,tuple(jnp.zeros((hd,hd),F32) for _ in range(heads)))
    def last(index,carry):
        row,col=tile_masks(BLOCK)
        rows=pl.ds(pl.multiple_of(index*BLOCK,BLOCK),BLOCK)
        for h in range(heads):
            lanes=slice(h*hd,(h+1)*hd)
            q=q_ref[rows,lanes]; k=k_ref[rows,lanes]; v=v_ref[rows,lanes]; do=do_ref[rows,lanes]
            s=s_ref[h,index]; f=f_ref[rows,lanes]; g=g_buf[h,index]
            whole=brow_ref[index//per,h:h+1,:]
            part=index%per
            b=whole[:,:BLOCK]
            if per==2:
                b=jnp.where(part==0,whole[:,:BLOCK],whole[:,BLOCK:])
            bcol=jnp.sum(jnp.where(row==col,b,0.0),axis=1,keepdims=True)
            ttile=t_ref[h,rows,:]
            t=ttile[:,:BLOCK]
            if per==2:
                t=jnp.where(part==0,ttile[:,:BLOCK],ttile[:,BLOCK:])
            df=y_buf[rows,lanes]+mm_lw(k,g)
            dr=mm_ww(t,df,TN)
            dp=jnp.where(row>=col,mm_ww(do,f,NT),0.0)
            dl=jnp.where(row>col,-mm_ww(dr,f,NT),0.0)
            dq_ref[rows,lanes]=mm_ww(do,s,NT)+mm_wl(dp,k)
            dkb=mm_wl(dl,k)-mm_ww(dr,s,NT)
            dk=mm_wl(dp,q,TN)+mm_ww(f,g,NT)+mm_wl(dl*bcol,k,TN)+bcol*dkb
            dk_ref[rows,lanes]=dk
            dv_ref[rows,lanes]=bcol*dr
            kf=k.astype(F32); vf=v.astype(F32)
            db_ref[h,rows,:]=jnp.sum(dr*vf+dkb*kf,axis=1,keepdims=True)
        return carry
    lax.fori_loop(0,blocks,last,0)

def run_forward(q,k,v,strength,persist):
    rows,width=q.shape; heads=strength.shape[1]; hd=width//heads; blocks=rows//BLOCK
    tile=min(2*BLOCK,rows)
    brow=strength.reshape(rows//tile,tile,heads).transpose(0,2,1)
    shapes=lambda *s: jax.ShapeDtypeStruct(s,F32)
    vm=pl.BlockSpec(memory_space=pltpu.VMEM)
    outs=pl.pallas_call(functools.partial(delta_forward,heads,blocks),
        out_shape=(shapes(rows,width),shapes(heads,rows,tile),shapes(rows,width),shapes(heads,blocks,hd,hd),shapes(rows,width),shapes(heads,blocks,hd,hd)),
        in_specs=[pl.BlockSpec(memory_space=pltpu.SMEM)]+[vm]*4, out_specs=(vm,)*6,
        scratch_shapes=[pltpu.VMEM((rows,width),F32),pltpu.VMEM((heads,blocks,hd,hd),F32)],
        compiler_params=pltpu.CompilerParams(vmem_limit_bytes=40*2**20),
        )(persist,q,k,v,brow)
    return outs, brow

def run_backward(q,k,v,brow,persist,do,saved):
    t,w,s,f,a=saved
    rows,width=q.shape; heads=brow.shape[1]; hd=width//heads; blocks=rows//BLOCK
    shapes=lambda *s: jax.ShapeDtypeStruct(s,F32)
    vm=pl.BlockSpec(memory_space=pltpu.VMEM)
    return pl.pallas_call(functools.partial(delta_backward,heads,blocks),
        out_shape=(shapes(rows,width),)*3+(shapes(heads,rows,1),),
        in_specs=[pl.BlockSpec(memory_space=pltpu.SMEM)]+[vm]*10, out_specs=(vm,)*4,
        scratch_shapes=[pltpu.VMEM((rows,width),F32),pltpu.VMEM((heads,blocks,hd,hd),F32),pltpu.VMEM((heads,blocks,hd,hd),F32)],
        compiler_params=pltpu.CompilerParams(vmem_limit_bytes=40*2**20),
        )(persist,q,k,v,brow,do,t,w,s,f,a)


MESH = pl.DeviceIdType.MESH
ANY = pl.BlockSpec(memory_space=pl.ANY)
VMEM = pl.BlockSpec(memory_space=pltpu.VMEM)


def flipped(index, bit):
    size = 2**bit
    return index + (1 - 2 * ((index // size) % 2)) * size


def greet(peers):
    barrier = pltpu.get_barrier_semaphore()
    for axis, peer in peers:
        pl.semaphore_signal(barrier, inc=1, device_id={axis: peer}, device_id_type=MESH)
    pl.semaphore_wait(barrier, len(peers))


def others(axis, count):
    me = lax.axis_index(axis)
    return [(axis, lax.rem(me + step, count)) for step in range(1, count)]


def send(source, target, sends, recvs, slot, axis, peer):
    copy = pltpu.make_async_remote_copy(
        src_ref=source,
        dst_ref=target,
        send_sem=sends.at[slot],
        recv_sem=recvs.at[slot],
        device_id={axis: peer},
        device_id_type=MESH,
    )
    copy.start()
    return copy


def span(size, index, axis):
    piece = pl.ds(pl.multiple_of(index * size, size), size)
    return (piece, slice(None)) if axis == 0 else (slice(None), piece)


def start_exchange(pieces, count, sends, recvs, local, first=0):
    me = lax.axis_index("seq")
    started = []
    for number, (source, source_at, target, target_at) in enumerate(pieces):
        own = pltpu.make_async_copy(
            source.at[source_at(me)], target.at[target_at(me)], local.at[first // count + number]
        )
        own.start()
        started.append(own)
        for step in range(1, count):
            peer = lax.rem(me + step, count)
            slot = first + number * count + step
            started.append(
                send(
                    source.at[source_at(peer)], target.at[target_at(me)],
                    sends, recvs, slot, "seq", peer,
                )
            )
    return started


def wait_all(copies):
    for copy in copies:
        copy.wait()


def bit_orders(count):
    bits = list(range(count.bit_length() - 1))[::-1]
    other = bits[:]
    if len(bits) >= 3:
        other[0], other[1] = bits[1], bits[0]
    return [bits, other]


class Gather:
    def __init__(self, count, source, target, axis, sends, recvs, local, slot, local_slot):
        self.count, self.source, self.target, self.axis = count, source, target, axis
        self.sends, self.recvs, self.local = sends, recvs, local
        self.slot, self.local_slot = slot, local_slot
        self.me = lax.axis_index("seq")

    def piece(self, owner, half):
        rows, columns = self.source.shape
        part = rows // 2
        if self.axis == 0:
            return (pl.ds(pl.multiple_of(owner * rows + half * part, part), part), slice(None))
        return (
            pl.ds(half * part, part),
            pl.ds(pl.multiple_of(owner * columns, columns), columns),
        )

    def put(self, order, half, turn, known):
        owner = self.me
        for bit in known:
            owner = flipped(owner, bit)
        place = self.target.at[self.piece(owner, half)]
        part = self.source.shape[0] // 2
        source = place if known else self.source.at[pl.ds(half * part, part)]
        slot = self.slot + half * self.count + self.number(order, turn, known)
        self.copies[half, turn, known] = send(
            source, place, self.sends, self.recvs, slot, "seq", flipped(self.me, order[turn])
        )

    def number(self, order, turn, known):
        return 2**turn + sum(2 ** order.index(bit) for bit in known)

    def start(self):
        self.copies = {}
        self.own = pltpu.make_async_copy(
            self.source,
            self.target.at[
                span(self.source.shape[self.axis], self.me, self.axis)
            ],
            self.local.at[self.local_slot],
        )
        self.own.start()
        for half, order in enumerate(bit_orders(self.count)):
            for turn in range(len(order)):
                self.put(order, half, turn, ())

    def turns(self):
        return self.count.bit_length() - 1

    def forward(self, turn):
        orders = bit_orders(self.count)
        for before in range(2**turn):
            for half, order in enumerate(orders):
                known = tuple(order[i] for i in range(turn) if before // 2**i % 2)
                self.copies[half, turn, known].wait_recv()
                for later in range(turn + 1, len(order)):
                    self.put(order, half, later, known + (order[turn],))

    def finish(self):
        for copy in self.copies.values():
            copy.wait_send()
        self.own.wait()


def hypercube_peers(count):
    me = lax.axis_index("seq")
    return [("seq", flipped(me, bit)) for bit in range(count.bit_length() - 1)]


def gather_kernel(count, axis, source, target, sends, recvs, local):
    greet(hypercube_peers(count))
    gather = Gather(count, source, target, axis, sends, recvs, local, 0, 0)
    gather.start()
    for turn in range(gather.turns()):
        gather.forward(turn)
    gather.finish()


def comm_params(identity, limit=48):
    return pltpu.CompilerParams(
        collective_id=identity, has_side_effects=True, vmem_limit_bytes=limit * 2**20
    )


def gather_seq(array, count, axis, identity):
    shape = list(array.shape)
    shape[axis] *= count
    return pl.pallas_call(
        functools.partial(gather_kernel, count, axis),
        out_shape=jax.ShapeDtypeStruct(tuple(shape), array.dtype),
        in_specs=[ANY],
        out_specs=ANY,
        scratch_shapes=[
            pltpu.SemaphoreType.DMA((2 * count,)),
            pltpu.SemaphoreType.DMA((2 * count,)),
            pltpu.SemaphoreType.DMA((1,)),
        ],
        compiler_params=comm_params(identity),
    )(array)


def exchange_kernel(count, lanes, target_axis, source, target, sends, recvs, local):
    greet(others("seq", count))
    size = source.shape[0] // count
    width = target.shape[target_axis] // count
    wait_all(
        start_exchange(
            [
                (
                    source,
                    lambda i: (pl.ds(pl.multiple_of(i * size, size), size), slice(*lanes)),
                    target,
                    lambda i: span(width, i, target_axis),
                )
            ],
            count,
            sends,
            recvs,
            local,
        )
    )


def exchange_seq(array, count, lanes, target_axis, identity):
    shape = [array.shape[0] // count, lanes[1] - lanes[0]]
    shape[target_axis] *= count
    return pl.pallas_call(
        functools.partial(exchange_kernel, count, lanes, target_axis),
        out_shape=jax.ShapeDtypeStruct(tuple(shape), array.dtype),
        in_specs=[ANY],
        out_specs=ANY,
        scratch_shapes=[
            pltpu.SemaphoreType.DMA((count,)),
            pltpu.SemaphoreType.DMA((count,)),
            pltpu.SemaphoreType.DMA((1,)),
        ],
        compiler_params=comm_params(identity),
    )(array)


def scatter_kernel(count, part_ref, out_ref, landing, outgoing, total, sends, recvs):
    greet(hypercube_peers(count))
    me = lax.axis_index("seq")
    rows = out_ref.shape[0]
    half_rows = rows // 2
    bits = count.bit_length() - 1
    orders = [order[::-1] for order in bit_orders(count)]

    def rows_of(known, half):
        owner = me
        for bit in known:
            owner = flipped(owner, bit)
        return pl.ds(pl.multiple_of(owner * rows + half * half_rows, half_rows), half_rows)

    def subsets(order, turn):
        later = order[turn + 1 :]
        sets = [
            tuple(later[i] for i in range(len(later)) if code // 2**i % 2)
            for code in range(2 ** len(later))
        ]
        return sorted(sets, key=lambda known: [-(bit in known) for bit in later])

    def code_of(order, known):
        return sum(2**bit for bit in known)

    copies = {}
    for known_at in range(count // 2):
        for half, order in enumerate(orders):
            known = subsets(order, 0)[known_at]
            slot = half * count + code_of(order, known)
            copies[half, 0, known] = send(
                part_ref.at[rows_of((order[0],) + known, half)],
                landing.at[half, 0, code_of(order, known) // 2],
                sends, recvs, slot, "seq", flipped(me, order[0]),
            )
    for turn in range(bits):
        for known_at in range(2 ** (bits - turn - 1)):
            for half, order in enumerate(orders):
                known = subsets(order, turn)[known_at]
                code = code_of(order, known)
                copies[half, turn, known].wait_recv()
                came = landing[half, turn, code // 2].astype(F32)
                if turn == 0:
                    value = part_ref[rows_of(known, half), :].astype(F32) + came
                else:
                    value = total[half, code // 2] + came
                if turn == bits - 1:
                    out_ref[half * half_rows : (half + 1) * half_rows, :] = value
                elif order[turn + 1] in known:
                    rest = tuple(bit for bit in known if bit != order[turn + 1])
                    outgoing[half, code // 2] = value.astype(BF)
                    slot = half * count + (turn + 1) * 2 * count + code_of(order, rest)
                    copies[half, turn + 1, rest] = send(
                        outgoing.at[half, code // 2],
                        landing.at[half, turn + 1, code_of(order, rest) // 2],
                        sends, recvs, slot, "seq", flipped(me, order[turn + 1]),
                    )
                else:
                    total[half, code // 2] = value
    for copy in copies.values():
        copy.wait_send()


def scatter_seq(parts, count, identity):
    rows, columns = parts.shape[0] // count, parts.shape[1]
    bits = count.bit_length() - 1
    return pl.pallas_call(
        functools.partial(scatter_kernel, count),
        out_shape=jax.ShapeDtypeStruct((rows, columns), F32),
        in_specs=[VMEM],
        out_specs=VMEM,
        scratch_shapes=[
            pltpu.VMEM((2, bits, count // 2, rows // 2, columns), BF),
            pltpu.VMEM((2, count // 2, rows // 2, columns), BF),
            pltpu.VMEM((2, count // 2, rows // 2, columns), F32),
            pltpu.SemaphoreType.DMA((2 * bits * count,)),
            pltpu.SemaphoreType.DMA((2 * bits * count,)),
        ],
        compiler_params=comm_params(identity),
    )(parts)


def opening_kernel(count, depth, small, wq, wk, wv, wo, small_all, mixer, sends, recvs, local, near, far):
    greet(others("seq", count) + others("dp", depth))
    me, level = lax.axis_index("seq"), lax.axis_index("dp")
    mine = wq.shape[1] // count
    copies = [pltpu.make_async_copy(small, small_all.at[level * count + me], near.at[0])]
    copies[0].start()
    arriving = []
    for step in range(1, count):
        arriving.append(
            send(
                small, small_all.at[level * count + me],
                far.at[0], far.at[1], step, "seq", lax.rem(me + step, count),
            )
        )
    pieces = []
    for member, weight in enumerate((wq, wk, wv, wo)):
        pieces.append(
            (
                weight,
                lambda i: span(mine, i, 1),
                mixer,
                lambda i, member=member: (i, slice(None), slice(member * mine, (member + 1) * mine)),
            )
        )
    copies += arriving
    exchange = start_exchange(pieces, count, sends, recvs, local)
    wait_all(copies)
    plane = small_all.at[pl.ds(level * count, count)]
    levels = [
        send(plane, plane, far.at[2], far.at[3], step, "dp", lax.rem(level + step, depth))
        for step in range(1, depth)
    ]
    wait_all(exchange + levels)


def opening(count, depth, small, weights):
    rows, features = weights[0].shape
    slots = max(count, depth)
    return pl.pallas_call(
        functools.partial(opening_kernel, count, depth),
        out_shape=(
            jax.ShapeDtypeStruct((count * depth,) + small.shape, F32),
            jax.ShapeDtypeStruct((count, rows, 4 * features // count), BF),
        ),
        in_specs=[ANY] * 5,
        out_specs=(ANY, ANY),
        scratch_shapes=[
            pltpu.SemaphoreType.DMA((4 * count,)),
            pltpu.SemaphoreType.DMA((4 * count,)),
            pltpu.SemaphoreType.DMA((4,)),
            pltpu.SemaphoreType.DMA((1,)),
            pltpu.SemaphoreType.DMA((4, slots)),
        ],
        compiler_params=comm_params(1),
    )(small, *weights)


def second_kernel(count, gate, up, down, pair_rest, down_rest, normed, cotangent, hidden, normed_full, cotangent_full, sends, recvs, local, gather_sends, gather_recvs):
    greet(others("seq", count))
    rest = pair_rest.shape[1] // count
    main = (gate.shape[1] - pair_rest.shape[1] // 2) // count

    def piece(source, size, at):
        return (
            source,
            lambda i: span(size, i, 1),
            hidden,
            lambda i: (i, slice(None), slice(at, at + size)),
        )

    exchange = start_exchange(
        [
            piece(gate, main, 0),
            piece(up, main, main),
            piece(pair_rest, rest, 2 * main),
            piece(down, main, 2 * main + rest),
            piece(down_rest, rest, 3 * main + rest),
        ],
        count, sends, recvs, local,
    )
    gathers = [
        Gather(count, source, target, 0, gather_sends, gather_recvs, local, 2 * count * i, 5 + i)
        for i, (source, target) in enumerate(
            ((normed, normed_full), (cotangent, cotangent_full))
        )
    ]
    for gather in gathers:
        gather.start()
    for turn in range(gathers[0].turns()):
        for gather in gathers:
            gather.forward(turn)
    for gather in gathers:
        gather.finish()
    wait_all(exchange)


def second(count, gate, up, down, pair_rest, down_rest, normed, cotangent):
    rows = gate.shape[0]
    rest = pair_rest.shape[1] // count
    main = (gate.shape[1] - pair_rest.shape[1] // 2) // count
    whole = (normed.shape[0] * count, normed.shape[1])
    return pl.pallas_call(
        functools.partial(second_kernel, count),
        out_shape=(
            jax.ShapeDtypeStruct((count, rows, 3 * main + 2 * rest), BF),
            jax.ShapeDtypeStruct(whole, BF),
            jax.ShapeDtypeStruct(whole, BF),
        ),
        in_specs=[ANY] * 7,
        out_specs=(ANY,) * 3,
        scratch_shapes=[
            pltpu.SemaphoreType.DMA((5 * count,)),
            pltpu.SemaphoreType.DMA((5 * count,)),
            pltpu.SemaphoreType.DMA((7,)),
            pltpu.SemaphoreType.DMA((4 * count,)),
            pltpu.SemaphoreType.DMA((4 * count,)),
        ],
        compiler_params=comm_params(2),
    )(gate, up, down, pair_rest, down_rest, normed, cotangent)


def closing_kernel(count, sizes, source, *refs):
    targets, (sends, recvs, local) = refs[:-3], refs[-3:]
    greet(others("seq", count))
    rows = source.shape[0] // count
    pieces, at = [], 0
    for target, size in zip(targets, sizes):
        pieces.append(
            (
                source,
                lambda i, at=at, size=size: (
                    pl.ds(pl.multiple_of(i * rows, rows), rows),
                    slice(at, at + size),
                ),
                target,
                lambda i, size=size: span(size, i, 1),
            )
        )
        at += size
    wait_all(start_exchange(pieces, count, sends, recvs, local))


def closing(source, count, sizes, identity):
    rows, members = source.shape[0] // count, len(sizes)
    return pl.pallas_call(
        functools.partial(closing_kernel, count, sizes),
        out_shape=tuple(jax.ShapeDtypeStruct((rows, count * size), BF) for size in sizes),
        in_specs=[ANY],
        out_specs=(ANY,) * members,
        scratch_shapes=[
            pltpu.SemaphoreType.DMA((members * count,)),
            pltpu.SemaphoreType.DMA((members * count,)),
            pltpu.SemaphoreType.DMA((members,)),
        ],
        compiler_params=comm_params(identity),
    )(source)


def sums_kernel(count, depth, plane_ref, level_ref, total_ref, each_ref, plane_in, joined, level_in, sends, recvs):
    greet(others("seq", count) + others("dp", depth))
    me, level = lax.axis_index("seq"), lax.axis_index("dp")
    height = plane_ref.shape[0]
    plane_in[me] = plane_ref[...]
    wait_all(
        [
            send(
                plane_ref, plane_in.at[me], sends.at[0], recvs.at[0], step,
                "seq", lax.rem(me + step, count),
            )
            for step in range(1, count)
        ]
    )
    value = plane_in[0]
    for i in range(1, count):
        value = value + plane_in[i]
    joined[0:height] = value
    joined[height:] = level_ref[...]
    level_in[level] = joined[...]
    wait_all(
        [
            send(
                joined, level_in.at[level], sends.at[1], recvs.at[1], step,
                "dp", lax.rem(level + step, depth),
            )
            for step in range(1, depth)
        ]
    )
    value = level_in[0]
    for i in range(1, depth):
        value = value + level_in[i]
    total_ref[...] = value[0:height]
    joined[height:] = value[height:]
    each_ref[me] = value[height:]
    wait_all(
        [
            send(
                joined.at[pl.ds(height, level_ref.shape[0])], each_ref.at[me],
                sends.at[2], recvs.at[2], step, "seq", lax.rem(me + step, count),
            )
            for step in range(1, count)
        ]
    )


def small_sums(plane, level, count, depth):
    slots = max(count, depth)
    joined = (plane.shape[0] + level.shape[0], plane.shape[1])
    return pl.pallas_call(
        functools.partial(sums_kernel, count, depth),
        out_shape=(
            jax.ShapeDtypeStruct(plane.shape, F32),
            jax.ShapeDtypeStruct((count,) + level.shape, F32),
        ),
        in_specs=[VMEM, VMEM],
        out_specs=(VMEM, VMEM),
        scratch_shapes=[
            pltpu.VMEM((count,) + plane.shape, F32),
            pltpu.VMEM(joined, F32),
            pltpu.VMEM((depth,) + joined, F32),
            pltpu.SemaphoreType.DMA((3, slots)),
            pltpu.SemaphoreType.DMA((3, slots)),
        ],
        compiler_params=comm_params(3),
    )(plane, level)


def rest_and_main(hidden_width, count):
    main = hidden_width // (128 * count) * 128
    return hidden_width // count - main, main


def local_heads(
    tokens,
    doc_starts,
    pad_mask,
    norm1_gain,
    query_weight,
    key_weight,
    value_weight,
    conv_weight,
    beta_weight,
    out_norm_gain,
    out_weight,
    norm2_gain,
    gate_weight,
    up_weight,
    down_weight,
    cotangent,
):
    row_count, features = tokens.shape
    width = lax.axis_size("seq")
    place = lax.axis_index("seq")
    head_dim = out_norm_gain.shape[0]
    heads = beta_weight.shape[1] // width
    mine = heads * head_dim
    total = row_count * width
    block_total = total // BLOCK
    depth = lax.axis_size("dp")
    level = lax.axis_index("dp")
    owned = norm1_gain.shape[0]
    rest, main = rest_and_main(gate_weight.shape[1], width)
    lanes = max(owned, row_count)

    def across(array):
        return jnp.pad(array.astype(F32), ((0, 0), (0, lanes - array.shape[1])))

    small = jnp.concatenate(
        [
            across(norm1_gain[None]),
            across(norm2_gain[None]),
            across(conv_weight.reshape(3 * CONV, owned)),
            across(pad_mask),
            across(doc_starts),
        ],
        axis=0,
    )
    small_all, mixer_part = opening(
        width, depth, small, [query_weight, key_weight, value_weight, out_weight]
    )
    w_mixer = lax.all_gather(
        mixer_part.reshape(width * owned, 4 * mine), "dp", axis=0, tiled=True
    )
    wide = small_all[:, : 3 * CONV + 2, :owned].transpose(1, 0, 2).reshape(3 * CONV + 2, features)
    gain_first, gain_second = wide[0], wide[1]
    taps = lax.dynamic_slice_in_dim(wide[2:], place * mine, mine, axis=1).reshape(3, CONV, mine)
    marks = lax.dynamic_slice_in_dim(small_all[:, 3 * CONV + 2 :], level * width, width, axis=0)
    pad_rows = marks[:, 0, :row_count].reshape(-1)[:, None]
    starts = marks[:, 1, : doc_starts.shape[1]].reshape(-1).astype(jnp.int32)
    positions = jnp.arange(total, dtype=jnp.int32)
    offsets = jnp.repeat(starts, BLOCK)
    persist = (starts != BLOCK * jnp.arange(block_total, dtype=jnp.int32)).astype(F32)
    w_beta = lax.dynamic_slice_in_dim(beta_weight, place * heads, heads, axis=1)

    def mixer_in(projected, taps_in):
        padded = jnp.concatenate([jnp.zeros((CONV - 1, 3 * mine), F32), projected], axis=0)
        results = []
        for member in range(3):
            columns = padded[:, member * mine : (member + 1) * mine]
            summed = jnp.zeros((total, mine), F32)
            for lagged in range(CONV):
                inside = (positions - lagged >= offsets).astype(F32)[:, None]
                summed = (
                    summed
                    + taps_in[member, lagged]
                    * inside
                    * columns[CONV - 1 - lagged : CONV - 1 - lagged + total]
                )
            activated = jax.nn.silu(summed).reshape(total, heads, head_dim)
            if member < 2:
                activated = activated * lax.rsqrt(
                    jnp.sum(activated * activated, axis=-1, keepdims=True) + EPSILON
                )
            if member == 0:
                activated = activated * head_dim ** (-0.5)
            results.append(activated.reshape(total, mine))
        return tuple(results)

    residual_in = tokens.astype(F32)
    normed, norm_first_pull = jax.vjp(rms_norm, residual_in, gain_first)

    def ends(array):
        return array[:, main * width :].reshape(owned, width, rest)

    down_turned = down_weight.T
    pair_rest = jnp.concatenate([ends(gate_weight), ends(up_weight)], axis=2)
    down_rest = jnp.concatenate([ends(down_turned), jnp.zeros((owned, width, rest), BF)], axis=2)
    hidden_part, normed_full, cotangent_full = second(
        width,
        gate_weight,
        up_weight,
        down_turned,
        pair_rest.reshape(owned, -1),
        down_rest.reshape(owned, -1),
        normed.astype(BF),
        cotangent,
    )
    w_hidden = lax.all_gather(
        hidden_part.reshape(width * owned, -1), "dp", axis=0, tiled=True
    )
    pair_width = 2 * (main + rest)
    w_pair, w_down = w_hidden[:, :pair_width], w_hidden[:, pair_width:]
    w_qkv, w_out = w_mixer[:, : 3 * mine], w_mixer[:, 3 * mine :]
    w_out_rows = exchange_seq(w_mixer, width, (3 * mine, 4 * mine), 1, 4)
    projected = product(normed_full, w_qkv).astype(BF)
    logits = product(normed_full, w_beta)
    sigma_vals = jax.nn.sigmoid(logits)
    strength = sigma_vals * pad_rows
    (queries, key_rows, values), mixer_pull = jax.vjp(mixer_in, projected.astype(F32), taps)
    queries, key_rows, values = (a.astype(BF) for a in (queries, key_rows, values))
    (mixed, *saved), strength_rows = run_forward(queries, key_rows, values, strength, persist)
    out_normed, out_norm_pull = jax.vjp(
        rms_norm, mixed.reshape(total, heads, head_dim), out_norm_gain.astype(F32)
    )
    out_low = out_normed.reshape(total, mine).astype(BF)
    out_full = gather_seq(out_low, width, 1, 5)
    attended = exchange_seq(product(out_full, w_out), width, (0, mine), 1, 6)
    residual_mid = residual_in + attended
    normed_two, norm_second_pull = jax.vjp(rms_norm, residual_mid, gain_second)
    normed_two_full = gather_seq(normed_two.astype(BF), width, 0, 7)
    pair = product(normed_two_full, w_pair)
    tail = pair[:, 2 * main :]
    gate_out = jnp.concatenate([pair[:, :main], tail], axis=1)
    up_out = jnp.concatenate([pair[:, main : 2 * main], jnp.roll(tail, rest, axis=1)], axis=1)
    gate_sigma = jax.nn.sigmoid(gate_out)
    gate_silu = gate_out * gate_sigma
    hidden = (gate_silu * up_out).astype(BF)
    hidden_grad = product(cotangent_full, w_down)
    gate_grad_low = (
        hidden_grad * up_out * gate_sigma * (1.0 + gate_out * (1.0 - gate_sigma))
    ).astype(BF)
    up_grad_low = (hidden_grad * gate_silu).astype(BF)
    pair_grad_low = jnp.concatenate(
        [
            gate_grad_low[:, :main],
            up_grad_low[:, :main],
            gate_grad_low[:, main : main + rest],
            up_grad_low[:, main : main + rest],
        ],
        axis=1,
    )
    hidden_grads = jnp.concatenate(
        [
            product_left(normed_two_full, pair_grad_low).astype(BF),
            product_left(cotangent_full, hidden).astype(BF),
        ],
        axis=1,
    )
    two_parts = product_right(pair_grad_low, w_pair).astype(BF)
    hidden_grads, two_parts = lax.optimization_barrier((hidden_grads, two_parts))
    hidden_sums = lax.psum_scatter(hidden_grads, "dp", scatter_dimension=0, tiled=True)
    normed_two_grad = scatter_seq(two_parts, width, 8)
    added = scatter_seq(product_right(hidden, w_down).astype(BF), width, 9)
    output = (residual_mid + added).astype(BF)
    mid_from_norm, gain_second_grad = norm_second_pull(normed_two_grad)
    residual_mid_grad = cotangent.astype(F32) + mid_from_norm
    mid_full = gather_seq(residual_mid_grad.astype(BF), width, 0, 10)
    out_normed_grad = product_right(mid_full, w_out_rows)
    mixed_grad, out_gain_grad = out_norm_pull(out_normed_grad.reshape(total, heads, head_dim))
    query_grads, key_grads, value_grads, strength_grads = run_backward(
        queries, key_rows, values, strength_rows, persist, mixed_grad.reshape(total, mine), saved
    )
    strength_grad = strength_grads[:, :, 0].T
    projected_grad, conv_grad = mixer_pull((query_grads, key_grads, value_grads))
    projected_grad = projected_grad.astype(BF)
    logits_grad = (strength_grad * pad_rows * sigma_vals * (1.0 - sigma_vals)).astype(BF)
    mid_mine = lax.dynamic_slice_in_dim(mid_full, place * mine, mine, axis=1)
    mixer_grads = jnp.concatenate(
        [
            product_left(normed_full, projected_grad).astype(BF),
            product_left(out_full, mid_mine).astype(BF),
        ],
        axis=1,
    )
    mixer_grads, hidden_sums = lax.optimization_barrier((mixer_grads, hidden_sums))
    mixer_sums = lax.psum_scatter(mixer_grads, "dp", scatter_dimension=0, tiled=True)
    beta_grad = product_left(logits_grad, normed_full)
    normed_grad = scatter_seq(
        (product_right(projected_grad, w_qkv) + product_right(logits_grad, w_beta)).astype(BF),
        width,
        11,
    )
    input_from_norm, gain_first_grad = norm_first_pull(normed_grad)
    tokens_grad = residual_mid_grad + input_from_norm

    gain_row = jnp.pad(out_gain_grad[None], ((0, 0), (0, features - head_dim)))
    plane = jnp.concatenate([gain_first_grad[None], gain_second_grad[None], gain_row], axis=0)
    conv_rows = 3 * CONV * mine // features + 1
    conv_flat = jnp.pad(conv_grad.reshape(-1), (0, conv_rows * features - 3 * CONV * mine))
    levels = jnp.concatenate([beta_grad, conv_flat.reshape(conv_rows, features)], axis=0)
    plane = jnp.pad(plane, ((0, -plane.shape[0] % 8), (0, 0)))
    levels = jnp.pad(levels, ((0, -levels.shape[0] % 8), (0, 0)))
    sums, each = small_sums(plane, levels, width, depth)
    beta_total = each[:, :heads].reshape(width * heads, features).T
    conv_all = each[:, heads : heads + conv_rows].reshape(width, -1)[:, : 3 * CONV * mine]
    conv_all = conv_all.reshape(width, 3 * CONV, mine).transpose(1, 0, 2).reshape(-1, features)
    wide_sums = jnp.concatenate([sums[:2], conv_all], axis=0)
    own = level * width + place
    wide_own = lax.dynamic_slice_in_dim(wide_sums, own * owned, owned, axis=1)

    gate_main, up_main, pair_ends, down_main, down_ends = closing(
        hidden_sums, width, (main, main, 2 * rest, main, 2 * rest), 12
    )
    shard_q, shard_k, shard_v, shard_o = (
        a.astype(F32) for a in closing(mixer_sums, width, (mine,) * 4, 13)
    )

    def joined(front, back, at):
        back = back.reshape(owned, width, 2, rest)[:, :, at].reshape(owned, width * rest)
        return jnp.concatenate([front, back], axis=1).astype(F32)

    return (
        output,
        tokens_grad,
        wide_own[0],
        shard_q,
        shard_k,
        shard_v,
        wide_own[2:].reshape(3, CONV, owned),
        beta_total,
        sums[2, :head_dim],
        shard_o,
        wide_own[1],
        joined(gate_main, pair_ends, 0),
        joined(up_main, pair_ends, 1),
        joined(down_main, down_ends, 0).T,
    )


def solution(mesh):
    in_specs = (
        P(("dp", "seq"), None),
        P("dp", "seq"),
        P("dp", "seq"),
        P(("dp", "seq")),
        P(("dp", "seq"), None),
        P(("dp", "seq"), None),
        P(("dp", "seq"), None),
        P(None, None, ("dp", "seq")),
        P(),
        P(),
        P(("dp", "seq"), None),
        P(("dp", "seq")),
        P(("dp", "seq"), None),
        P(("dp", "seq"), None),
        P(None, ("dp", "seq")),
        P(("dp", "seq"), None),
    )
    out_specs = (
        P(("dp", "seq"), None),
        P(("dp", "seq"), None),
        P(("dp", "seq")),
        P(("dp", "seq"), None),
        P(("dp", "seq"), None),
        P(("dp", "seq"), None),
        P(None, None, ("dp", "seq")),
        P(),
        P(),
        P(("dp", "seq"), None),
        P(("dp", "seq")),
        P(("dp", "seq"), None),
        P(("dp", "seq"), None),
        P(None, ("dp", "seq")),
    )

    def layer(*arrays):
        head_count, hidden_width = arrays[8].shape[1], arrays[12].shape[1]
        width = mesh.shape["seq"]
        rest, main = rest_and_main(hidden_width, width)
        by_heads = head_count % width == 0 and rest == 64 and main > 0
        local = local_heads if by_heads else local_sequence
        return jax.shard_map(
            local, mesh=mesh, in_specs=in_specs, out_specs=out_specs, check_vma=False
        )(*arrays)

    return layer
```

```python
import functools

import jax
import jax.numpy as jnp
from jax import lax
from jax.experimental import pallas as pl
from jax.experimental.pallas import tpu as pltpu
from jax.sharding import PartitionSpec as P

CONV = 4
BLOCK = 64


EPSILON = 1e-06
PRECISE = lax.Precision.HIGHEST


def from_behind(array, axis, by):
    length = lax.axis_size(axis)
    pairs = [(i, i + by) for i in range(length) if 0 <= i + by < length]
    return lax.ppermute(array, axis, pairs)


def product(left, right):
    return jnp.dot(left, right, preferred_element_type=jnp.float32)


def product_left(left, right):
    return lax.dot_general(
        left, right, (((0,), (0,)), ((), ())), preferred_element_type=jnp.float32
    )


def product_right(left, right):
    return lax.dot_general(
        left, right, (((1,), (1,)), ((), ())), preferred_element_type=jnp.float32
    )


def rounded(value):
    return lax.optimization_barrier(value.astype(jnp.bfloat16)).astype(jnp.float32)


def rms_norm(value, gain):
    return value * lax.rsqrt(jnp.mean(value * value, axis=-1, keepdims=True) + EPSILON) * gain


def block_parts(queries, key_rows, values, strength):
    keyed = key_rows * strength[..., None]
    block_len = key_rows.shape[1]
    lower_part = jnp.tril(jnp.einsum("hcd,hed->hce", keyed, key_rows, precision=PRECISE), -1)
    system = lower_part + jnp.eye(block_len, dtype=jnp.float32)
    weights = jax.scipy.linalg.solve_triangular(system, keyed, lower=True, unit_diagonal=True)
    updates = jax.scipy.linalg.solve_triangular(
        system, values * strength[..., None], lower=True, unit_diagonal=True
    )
    scores = jnp.tril(jnp.einsum("hcd,hed->hce", queries, key_rows, precision=PRECISE))
    return (weights, updates, scores)


def delta_step(state_now, inputs):
    queries, key_rows, values, strength, persist = inputs
    state_now = state_now * persist
    weights, updates, scores = block_parts(queries, key_rows, values, strength)
    corrected = updates - jnp.einsum("hcd,hde->hce", weights, state_now, precision=PRECISE)
    outputs = jnp.einsum("hcd,hde->hce", queries, state_now, precision=PRECISE) + jnp.einsum(
        "hce,hef->hcf", scores, corrected, precision=PRECISE
    )
    state_now = state_now + jnp.einsum("hcd,hce->hde", key_rows, corrected, precision=PRECISE)
    return (state_now, outputs)


def track_step(holding, inputs):
    state_now, transit = holding
    queries, key_rows, values, strength, persist = inputs
    state_now = state_now * persist
    transit = transit * persist
    weights, updates, scores = block_parts(queries, key_rows, values, strength)
    corrected = updates - jnp.einsum("hcd,hde->hce", weights, state_now, precision=PRECISE)
    outputs = jnp.einsum("hcd,hde->hce", queries, state_now, precision=PRECISE) + jnp.einsum(
        "hce,hef->hcf", scores, corrected, precision=PRECISE
    )
    leading = queries - jnp.einsum("hce,hed->hcd", scores, weights, precision=PRECISE)
    state_now = state_now + jnp.einsum("hcd,hce->hde", key_rows, corrected, precision=PRECISE)
    eraser = jnp.eye(key_rows.shape[2], dtype=jnp.float32) - jnp.einsum(
        "hcd,hce->hde", key_rows, weights, precision=PRECISE
    )
    return (
        (state_now, jnp.einsum("hde,hef->hdf", eraser, transit, precision=PRECISE)),
        (outputs, leading, transit),
    )


def advance(linear, offset_part, incoming):
    return jnp.einsum("hde,hef->hdf", linear, incoming, precision=PRECISE) + offset_part


def into_blocks(array):
    row_count, head_count, head_dim = array.shape
    return array.reshape(row_count // BLOCK, BLOCK, head_count, head_dim).transpose(0, 2, 1, 3)


def from_blocks(array):
    block_count, head_count, block_len, head_dim = array.shape
    return array.transpose(0, 2, 1, 3).reshape(block_count * block_len, head_count, head_dim)


def local_sequence(
    tokens,
    doc_starts,
    pad_mask,
    norm1_gain,
    query_weight,
    key_weight,
    value_weight,
    conv_weight,
    beta_weight,
    out_norm_gain,
    out_weight,
    norm2_gain,
    gate_weight,
    up_weight,
    down_weight,
    cotangent,
):
    row_count, features = tokens.shape
    head_count = beta_weight.shape[1]
    head_dim = out_norm_gain.shape[0]
    block_count = row_count // BLOCK
    w_query, w_key, w_value, w_out, conv_full, gain_first = (
        lax.all_gather(query_weight, ("dp", "seq"), axis=0, tiled=True),
        lax.all_gather(key_weight, ("dp", "seq"), axis=0, tiled=True),
        lax.all_gather(value_weight, ("dp", "seq"), axis=0, tiled=True),
        lax.all_gather(out_weight, ("dp", "seq"), axis=0, tiled=True),
        lax.all_gather(conv_weight, ("dp", "seq"), axis=2, tiled=True),
        lax.all_gather(norm1_gain, ("dp", "seq"), axis=0, tiled=True),
    )
    w_gate, w_up, w_down, gain_second = (
        lax.all_gather(gate_weight, ("dp", "seq"), axis=0, tiled=True),
        lax.all_gather(up_weight, ("dp", "seq"), axis=0, tiled=True),
        lax.all_gather(down_weight, ("dp", "seq"), axis=1, tiled=True),
        lax.all_gather(norm2_gain, ("dp", "seq"), axis=0, tiled=True),
    )
    seq_place = lax.axis_index("seq")
    positions = seq_place * row_count + jnp.arange(row_count, dtype=jnp.int32)
    starts = doc_starts[0]
    offsets = jnp.repeat(starts, BLOCK)
    persist = (
        starts != seq_place * row_count + BLOCK * jnp.arange(block_count, dtype=jnp.int32)
    ).astype(jnp.float32)
    pad_rows = pad_mask[0].astype(jnp.float32)[:, None]

    def mixer_in(extended, conv_taps):
        results = []
        for member in range(3):
            columns = extended[:, member * features : (member + 1) * features]
            summed = jnp.zeros((row_count, features), jnp.float32)
            for lagged in range(CONV):
                inside = (positions - lagged >= offsets).astype(jnp.float32)[:, None]
                summed = (
                    summed
                    + conv_taps[member, lagged]
                    * inside
                    * columns[CONV - 1 - lagged : CONV - 1 - lagged + row_count]
                )
            activated = jax.nn.silu(summed).reshape(row_count, head_count, head_dim)
            if member < 2:
                activated = activated * lax.rsqrt(
                    jnp.sum(activated * activated, axis=-1, keepdims=True) + EPSILON
                )
            if member == 0:
                activated = activated * head_dim ** (-0.5)
            results.append(activated)
        return tuple(results)

    residual_in = tokens.astype(jnp.float32)
    normed, norm_first_pull = jax.vjp(rms_norm, residual_in, gain_first.astype(jnp.float32))
    normed_low = normed.astype(jnp.bfloat16)
    projected = jnp.concatenate(
        [product(normed_low, w_query), product(normed_low, w_key), product(normed_low, w_value)],
        axis=1,
    ).astype(jnp.bfloat16)
    logits = product(normed_low, beta_weight)
    sigma_vals = jax.nn.sigmoid(logits)
    strength = sigma_vals * pad_rows
    rims = from_behind(projected[row_count - CONV + 1 :], "seq", 1)
    extended_in = jnp.concatenate([rims, projected], axis=0).astype(jnp.float32)
    (queries, key_rows, values), mixer_pull = jax.vjp(
        mixer_in, extended_in, conv_full.astype(jnp.float32)
    )
    query_blocks = into_blocks(rounded(queries))
    key_blocks = into_blocks(rounded(key_rows))
    value_blocks = into_blocks(rounded(values))
    strength_blocks = strength.reshape(block_count, BLOCK, head_count).transpose(0, 2, 1)
    zero_state = jnp.zeros((head_count, head_dim, head_dim), jnp.float32)
    identity = jnp.broadcast_to(
        jnp.eye(head_dim, dtype=jnp.float32), (head_count, head_dim, head_dim)
    )
    block_inputs = (query_blocks, key_blocks, value_blocks, strength_blocks, persist)
    (final_state, final_transit), (local_out, leading, transit) = lax.scan(
        track_step, (zero_state, identity), block_inputs
    )

    def forward_turn(turn_index, incoming):
        return from_behind(advance(final_transit, final_state, incoming), "seq", 1)

    start_state = lax.fori_loop(0, lax.axis_size("seq") - 1, forward_turn, zero_state)
    carried = jnp.einsum("nhde,hef->nhdf", transit, start_state, precision=PRECISE)
    mixed = from_blocks(
        local_out + jnp.einsum("nhcd,nhdf->nhcf", leading, carried, precision=PRECISE)
    )
    out_normed, out_norm_pull = jax.vjp(rms_norm, mixed, out_norm_gain.astype(jnp.float32))
    out_low = out_normed.reshape(row_count, features).astype(jnp.bfloat16)
    residual_mid = residual_in + product(out_low, w_out)
    normed_two, norm_second_pull = jax.vjp(rms_norm, residual_mid, gain_second.astype(jnp.float32))
    normed_two_low = normed_two.astype(jnp.bfloat16)
    gate_out = product(normed_two_low, w_gate)
    up_out = product(normed_two_low, w_up)
    hidden = (jax.nn.silu(gate_out) * up_out).astype(jnp.bfloat16)
    output = (residual_mid + product(hidden, w_down)).astype(jnp.bfloat16)
    grad_out = cotangent.astype(jnp.float32)
    down_grad = product_left(hidden, cotangent)
    hidden_grad = product_right(cotangent, w_down)
    gate_sigma = jax.nn.sigmoid(gate_out)
    gate_grad_low = (
        hidden_grad * up_out * gate_sigma * (1.0 + gate_out * (1.0 - gate_sigma))
    ).astype(jnp.bfloat16)
    up_grad_low = (hidden_grad * jax.nn.silu(gate_out)).astype(jnp.bfloat16)
    gate_grad = product_left(normed_two_low, gate_grad_low)
    up_grad = product_left(normed_two_low, up_grad_low)
    normed_two_grad = product_right(gate_grad_low, w_gate) + product_right(up_grad_low, w_up)
    mid_from_norm, gain_second_grad = norm_second_pull(normed_two_grad)
    residual_mid_grad = grad_out + mid_from_norm
    mid_low = residual_mid_grad.astype(jnp.bfloat16)
    out_grad = product_left(out_low, mid_low)
    out_normed_grad = product_right(mid_low, w_out).reshape(row_count, head_count, head_dim)
    mixed_grad, out_gain_grad = out_norm_pull(out_normed_grad)
    mixed_blocks = into_blocks(mixed_grad)
    pulled = jnp.einsum("nhcd,nhcf->nhdf", leading, mixed_blocks, precision=PRECISE)
    local_back = jnp.einsum("nhed,nhef->hdf", transit, pulled, precision=PRECISE)
    transit_turned = jnp.swapaxes(final_transit, 1, 2)

    def backward_turn(turn_index, incoming):
        return from_behind(advance(transit_turned, local_back, incoming), "seq", -1)

    end_grad = lax.fori_loop(0, lax.axis_size("seq") - 1, backward_turn, zero_state)

    def delta_local(query_in, key_in, value_in, strength_in):
        ending, outputs = lax.scan(
            jax.checkpoint(delta_step),
            start_state,
            (query_in, key_in, value_in, strength_in, persist),
        )
        return (outputs, ending)

    unused_out, delta_pull = jax.vjp(
        delta_local, query_blocks, key_blocks, value_blocks, strength_blocks
    )
    query_grad_blocks, key_grad_blocks, value_grad_blocks, strength_grad_blocks = delta_pull(
        (mixed_blocks, end_grad)
    )
    extended_grad, conv_grad = mixer_pull(
        (
            from_blocks(query_grad_blocks),
            from_blocks(key_grad_blocks),
            from_blocks(value_grad_blocks),
        )
    )
    rim_grad = from_behind(extended_grad[: CONV - 1], "seq", -1)
    projected_grad = jnp.concatenate(
        [extended_grad[CONV - 1 : row_count], extended_grad[row_count:] + rim_grad], axis=0
    ).astype(jnp.bfloat16)
    strength_grad = strength_grad_blocks.transpose(0, 2, 1).reshape(row_count, head_count)
    logits_grad = (strength_grad * pad_rows * sigma_vals * (1.0 - sigma_vals)).astype(jnp.bfloat16)
    part_query = projected_grad[:, :features]
    part_key = projected_grad[:, features : 2 * features]
    part_value = projected_grad[:, 2 * features :]
    query_grad = product_left(normed_low, part_query)
    key_grad = product_left(normed_low, part_key)
    value_grad = product_left(normed_low, part_value)
    beta_grad = product_left(normed_low, logits_grad)
    normed_grad = (
        product_right(part_query, w_query)
        + product_right(part_key, w_key)
        + product_right(part_value, w_value)
        + product_right(logits_grad, beta_weight)
    )
    input_from_norm, gain_first_grad = norm_first_pull(normed_grad)
    tokens_grad = residual_mid_grad + input_from_norm
    (
        shard_q,
        shard_k,
        shard_v,
        shard_o,
        shard_conv,
        shard_gain_one,
        shard_gate,
        shard_up,
        shard_down,
        shard_gain_two,
    ) = (
        lax.psum_scatter(query_grad, ("dp", "seq"), scatter_dimension=0, tiled=True),
        lax.psum_scatter(key_grad, ("dp", "seq"), scatter_dimension=0, tiled=True),
        lax.psum_scatter(value_grad, ("dp", "seq"), scatter_dimension=0, tiled=True),
        lax.psum_scatter(out_grad, ("dp", "seq"), scatter_dimension=0, tiled=True),
        lax.psum_scatter(conv_grad, ("dp", "seq"), scatter_dimension=2, tiled=True),
        lax.psum_scatter(gain_first_grad, ("dp", "seq"), scatter_dimension=0, tiled=True),
        lax.psum_scatter(gate_grad, ("dp", "seq"), scatter_dimension=0, tiled=True),
        lax.psum_scatter(up_grad, ("dp", "seq"), scatter_dimension=0, tiled=True),
        lax.psum_scatter(down_grad, ("dp", "seq"), scatter_dimension=1, tiled=True),
        lax.psum_scatter(gain_second_grad, ("dp", "seq"), scatter_dimension=0, tiled=True),
    )
    beta_total, out_gain_total = lax.psum((beta_grad, out_gain_grad), ("dp", "seq"))
    return (
        output,
        tokens_grad,
        shard_gain_one,
        shard_q,
        shard_k,
        shard_v,
        shard_conv,
        beta_total,
        out_gain_total,
        shard_o,
        shard_gain_two,
        shard_gate,
        shard_up,
        shard_down,
    )


F32 = jnp.float32
BF = jnp.bfloat16
NN=(((1,),(0,)),((),())); NT=(((1,),(1,)),((),())); TN=(((0,),(0,)),((),()))

def mm(a,b,dims=NN):
    return lax.dot_general(a,b,dims,preferred_element_type=F32)

def halves(a):
    high=a.astype(BF)
    return high,(a-high.astype(F32)).astype(BF)

def mm_lw(a,b,dims=NN):
    high,low=halves(b)
    return mm(a,high,dims)+mm(a,low,dims)

def mm_wl(a,b,dims=NN):
    high,low=halves(a)
    return mm(high,b,dims)+mm(low,b,dims)

def mm_ww(a,b,dims=NN):
    ah,al=halves(a); bh,bl=halves(b)
    return mm(ah,bh,dims)+(mm(al,bh,dims)+mm(ah,bl,dims))

def tile_masks(tile):
    row=lax.broadcasted_iota(jnp.int32,(tile,tile),0)
    col=lax.broadcasted_iota(jnp.int32,(tile,tile),1)
    return row,col


MESH = pl.DeviceIdType.MESH
ANY = pl.BlockSpec(memory_space=pl.ANY)
VMEM = pl.BlockSpec(memory_space=pltpu.VMEM)
HBM = pl.BlockSpec(memory_space=pltpu.HBM)


def flipped(index, bit):
    size = 2**bit
    return index + (1 - 2 * ((index // size) % 2)) * size


def greet(peers):
    barrier = pltpu.get_barrier_semaphore()
    for axis, peer in peers:
        pl.semaphore_signal(barrier, inc=1, device_id={axis: peer}, device_id_type=MESH)
    pl.semaphore_wait(barrier, len(peers))


def others(axis, count):
    me = lax.axis_index(axis)
    return [(axis, lax.rem(me + step, count)) for step in range(1, count)]


def send(source, target, sends, recvs, slot, axis, peer):
    copy = pltpu.make_async_remote_copy(
        src_ref=source,
        dst_ref=target,
        send_sem=sends.at[slot],
        recv_sem=recvs.at[slot],
        device_id={axis: peer},
        device_id_type=MESH,
    )
    copy.start()
    return copy


def span(size, index, axis):
    piece = pl.ds(pl.multiple_of(index * size, size), size)
    return (piece, slice(None)) if axis == 0 else (slice(None), piece)


def start_exchange(pieces, count, sends, recvs, local, first=0):
    me = lax.axis_index("seq")
    started = []
    for number, (source, source_at, target, target_at) in enumerate(pieces):
        own = pltpu.make_async_copy(
            source.at[source_at(me)], target.at[target_at(me)], local.at[first // count + number]
        )
        own.start()
        started.append(own)
        for step in range(1, count):
            peer = lax.rem(me + step, count)
            slot = first + number * count + step
            started.append(
                send(
                    source.at[source_at(peer)], target.at[target_at(me)],
                    sends, recvs, slot, "seq", peer,
                )
            )
    return started


def wait_all(copies):
    for copy in copies:
        copy.wait()


def bit_orders(count):
    bits = list(range(count.bit_length() - 1))[::-1]
    other = bits[:]
    if len(bits) >= 3:
        other[0], other[1] = bits[1], bits[0]
    return [bits, other]


class Gather:
    def __init__(self, count, source, target, axis, sends, recvs, local, slot, local_slot):
        self.count, self.source, self.target, self.axis = count, source, target, axis
        self.sends, self.recvs, self.local = sends, recvs, local
        self.slot, self.local_slot = slot, local_slot
        self.me = lax.axis_index("seq")
        self.copies = {}

    def piece(self, owner, half):
        rows, columns = self.source.shape
        part = rows // 2
        if self.axis == 0:
            return (pl.ds(pl.multiple_of(owner * rows + half * part, part), part), slice(None))
        return (
            pl.ds(half * part, part),
            pl.ds(pl.multiple_of(owner * columns, columns), columns),
        )

    def put(self, order, half, turn, known):
        owner = self.me
        for bit in known:
            owner = flipped(owner, bit)
        place = self.target.at[self.piece(owner, half)]
        part = self.source.shape[0] // 2
        source = place if known else self.source.at[pl.ds(half * part, part)]
        slot = self.slot + half * self.count + self.number(order, turn, known)
        self.copies[half, turn, known] = send(
            source, place, self.sends, self.recvs, slot, "seq", flipped(self.me, order[turn])
        )

    def number(self, order, turn, known):
        return 2**turn + sum(2 ** order.index(bit) for bit in known)

    def start(self):
        self.start_own()
        for half in range(2):
            self.start_half(half)

    def start_own(self):
        self.own = pltpu.make_async_copy(
            self.source,
            self.target.at[
                span(self.source.shape[self.axis], self.me, self.axis)
            ],
            self.local.at[self.local_slot],
        )
        self.own.start()

    def start_half(self, half):
        order = bit_orders(self.count)[half]
        for turn in range(len(order)):
            self.put(order, half, turn, ())

    def turns(self):
        return self.count.bit_length() - 1

    def forward(self, turn):
        orders = bit_orders(self.count)
        for before in range(2**turn):
            for half, order in enumerate(orders):
                known = tuple(order[i] for i in range(turn) if before // 2**i % 2)
                self.copies[half, turn, known].wait_recv()
                for later in range(turn + 1, len(order)):
                    self.put(order, half, later, known + (order[turn],))

    def finish(self):
        for copy in self.copies.values():
            copy.wait_send()
        self.own.wait()


def hypercube_peers(count):
    me = lax.axis_index("seq")
    return [("seq", flipped(me, bit)) for bit in range(count.bit_length() - 1)]


def comm_params(identity, limit=48):
    return pltpu.CompilerParams(
        collective_id=identity, has_side_effects=True, vmem_limit_bytes=limit * 2**20
    )


def opening_kernel(
    count, depth, gain_one, gain_two, taps, pad, starts, wq, wk, wv, wo, small_all, mixer,
    small, sends, recvs, local, near, far,
):
    greet(others("seq", count) + others("dp", depth))
    me, level = lax.axis_index("seq"), lax.axis_index("dp")
    mine = wq.shape[1] // count
    pieces = []
    for member, weight in enumerate((wq, wk, wv, wo)):
        pieces.append(
            (
                weight,
                lambda i: span(mine, i, 1),
                mixer,
                lambda i, member=member: (i, slice(None), slice(member * mine, (member + 1) * mine)),
            )
        )
    exchange = start_exchange(pieces, count, sends, recvs, local)
    small[...] = jnp.zeros(small.shape, F32)
    owned = gain_one.shape[1]
    for member in range(3):
        small[member * CONV : (member + 1) * CONV, 0:owned] = taps[member].astype(F32)
    at = 3 * CONV
    for row, source in enumerate((gain_one, gain_two, pad, starts)):
        small[at + row : at + row + 1, 0 : source.shape[1]] = source[...].astype(F32)
    copies = [pltpu.make_async_copy(small, small_all.at[level * count + me], near.at[0])]
    copies[0].start()
    for step in range(1, count):
        copies.append(
            send(
                small, small_all.at[level * count + me],
                far.at[0], far.at[1], step, "seq", lax.rem(me + step, count),
            )
        )
    wait_all(copies)
    plane = small_all.at[pl.ds(level * count, count)]
    levels = [
        send(plane, plane, far.at[2], far.at[3], step, "dp", lax.rem(level + step, depth))
        for step in range(1, depth)
    ]
    wait_all(exchange + levels)


def opening(count, depth, small, weights):
    rows, features = weights[0].shape
    slots = max(count, depth)
    shape = (3 * CONV + 4, max(small[0].shape[1], small[3].shape[1]))
    return pl.pallas_call(
        functools.partial(opening_kernel, count, depth),
        out_shape=(
            jax.ShapeDtypeStruct((count * depth,) + shape, F32),
            jax.ShapeDtypeStruct((count, rows, 4 * features // count), BF),
        ),
        in_specs=[VMEM] * 5 + [HBM] * 4,
        out_specs=(HBM, HBM),
        scratch_shapes=[
            pltpu.VMEM(shape, F32),
            pltpu.SemaphoreType.DMA((4 * count,)),
            pltpu.SemaphoreType.DMA((4 * count,)),
            pltpu.SemaphoreType.DMA((4,)),
            pltpu.SemaphoreType.DMA((1,)),
            pltpu.SemaphoreType.DMA((4, slots)),
        ],
        compiler_params=comm_params(1),
    )(*small, *weights)


def second_kernel(count, gate, up, down, pair_rest, down_rest, normed, pair, last, normed_full, sends, recvs, local, gather_sends, gather_recvs):
    greet(others("seq", count))
    rest = pair_rest.shape[1] // count
    main = (gate.shape[1] - pair_rest.shape[1] // 2) // count

    def piece(source, size, target, at):
        return (
            source,
            lambda i: span(size, i, 1),
            target,
            lambda i: (i, slice(None), slice(at, at + size)),
        )

    exchange = start_exchange(
        [
            piece(down, main, last, 0),
            piece(down_rest, rest, last, main),
            piece(gate, main, pair, 0),
            piece(up, main, pair, main),
            piece(pair_rest, rest, pair, 2 * main),
        ],
        count, sends, recvs, local,
    )
    gather = Gather(count, normed, normed_full, 0, gather_sends, gather_recvs, local, 0, 5)
    gather.start()
    for turn in range(gather.turns()):
        gather.forward(turn)
    gather.finish()
    wait_all(exchange)


def second(count, gate, up, down, pair_rest, down_rest, normed):
    rows = gate.shape[0]
    rest = pair_rest.shape[1] // count
    main = (gate.shape[1] - pair_rest.shape[1] // 2) // count
    whole = (normed.shape[0] * count, normed.shape[1])
    return pl.pallas_call(
        functools.partial(second_kernel, count),
        out_shape=(
            jax.ShapeDtypeStruct((count, rows, 2 * main + rest), BF),
            jax.ShapeDtypeStruct((count, rows, main + rest), BF),
            jax.ShapeDtypeStruct(whole, BF),
        ),
        in_specs=[ANY] * 6,
        out_specs=(ANY,) * 3,
        scratch_shapes=[
            pltpu.SemaphoreType.DMA((5 * count,)),
            pltpu.SemaphoreType.DMA((5 * count,)),
            pltpu.SemaphoreType.DMA((6,)),
            pltpu.SemaphoreType.DMA((2 * count,)),
            pltpu.SemaphoreType.DMA((2 * count,)),
        ],
        compiler_params=comm_params(2),
    )(gate, up, down, pair_rest, down_rest, normed)


def closing_kernel(count, sizes, *refs):
    sources, targets, (sends, recvs, local) = refs[: len(sizes)], refs[len(sizes) : -3], refs[-3:]
    greet(others("seq", count))
    wait_all(start_exchange(row_pieces(sources, targets, sizes, count), count, sends, recvs, local))


def closing(sources, count, sizes, identity):
    shapes = row_shapes(sources, sizes, count)
    members = len(shapes)
    return pl.pallas_call(
        functools.partial(closing_kernel, count, sizes),
        out_shape=shapes,
        in_specs=[ANY] * len(sources),
        out_specs=(ANY,) * members,
        scratch_shapes=[
            pltpu.SemaphoreType.DMA((members * count,)),
            pltpu.SemaphoreType.DMA((members * count,)),
            pltpu.SemaphoreType.DMA((members,)),
        ],
        compiler_params=comm_params(identity),
    )(*sources)


def sums_kernel(count, depth, plane_ref, level_ref, total_ref, each_ref, plane_in, joined, level_in, sends, recvs):
    greet(others("seq", count) + others("dp", depth))
    me, level = lax.axis_index("seq"), lax.axis_index("dp")
    cut = plane_ref.shape[1]
    plane_in[me] = plane_ref[...]
    wait_all(
        [
            send(
                plane_ref, plane_in.at[me], sends.at[0], recvs.at[0], step,
                "seq", lax.rem(me + step, count),
            )
            for step in range(1, count)
        ]
    )
    value = plane_in[0]
    for i in range(1, count):
        value = value + plane_in[i]
    joined[:, 0:cut] = value
    joined[:, cut:] = level_ref[...]
    level_in[level] = joined[...]
    wait_all(
        [
            send(
                joined, level_in.at[level], sends.at[1], recvs.at[1], step,
                "dp", lax.rem(level + step, depth),
            )
            for step in range(1, depth)
        ]
    )
    value = level_in[0]
    for i in range(1, depth):
        value = value + level_in[i]
    total_ref[...] = value[:, 0:cut]
    joined[:, cut:] = value[:, cut:]
    each_ref[me] = value[:, cut:]
    wait_all(
        [
            send(
                joined.at[:, cut:], each_ref.at[me],
                sends.at[2], recvs.at[2], step, "seq", lax.rem(me + step, count),
            )
            for step in range(1, count)
        ]
    )


def small_sums(plane, level, count, depth):
    slots = max(count, depth)
    joined = (plane.shape[0], plane.shape[1] + level.shape[1])
    return pl.pallas_call(
        functools.partial(sums_kernel, count, depth),
        out_shape=(
            jax.ShapeDtypeStruct(plane.shape, F32),
            jax.ShapeDtypeStruct((count,) + level.shape, F32),
        ),
        in_specs=[VMEM, VMEM],
        out_specs=(VMEM, VMEM),
        scratch_shapes=[
            pltpu.VMEM((count,) + plane.shape, F32),
            pltpu.VMEM(joined, F32),
            pltpu.VMEM((depth,) + joined, F32),
            pltpu.SemaphoreType.DMA((3, slots)),
            pltpu.SemaphoreType.DMA((3, slots)),
        ],
        compiler_params=comm_params(3),
    )(plane, level)


class Scatter:
    def __init__(self, count, part, out, landing, outgoing, total, sends, recvs):
        self.count, self.part, self.out = count, part, out
        self.landing, self.outgoing, self.total = landing, outgoing, total
        self.sends, self.recvs = sends, recvs
        self.me = lax.axis_index("seq")
        self.rows = out.shape[0] // 2
        self.bits = count.bit_length() - 1
        self.orders = [order[::-1] for order in bit_orders(count)]
        self.copies = {}

    def rows_of(self, known, half):
        owner = self.me
        for bit in known:
            owner = flipped(owner, bit)
        size = self.rows
        return pl.ds(pl.multiple_of(owner * 2 * size + half * size, size), size)

    def place(self, order, turn, known):
        later = order[turn + 1 :]
        before = sum(self.count >> (t + 1) for t in range(turn))
        return before + sum(2**i for i, bit in enumerate(later) if bit in known)

    def subsets(self, order, turn):
        later = order[turn + 1 :]
        sets = [
            tuple(later[i] for i in range(len(later)) if code // 2**i % 2)
            for code in range(2 ** len(later))
        ]
        return sorted(sets, key=lambda known: [-(bit in known) for bit in later])

    def put(self, half, turn, known, source):
        order = self.orders[half]
        place = self.place(order, turn, known)
        self.copies[half, turn, known] = send(
            source,
            self.landing.at[half, place],
            self.sends,
            self.recvs,
            half * self.count + place,
            "seq",
            flipped(self.me, order[turn]),
        )

    def start(self):
        for at in range(self.count // 2):
            for half, order in enumerate(self.orders):
                known = self.subsets(order, 0)[at]
                self.put(half, 0, known, self.part.at[self.rows_of((order[0],) + known, half)])

    def turn(self, turn):
        for at in range(2 ** (self.bits - turn - 1)):
            for half, order in enumerate(self.orders):
                known = self.subsets(order, turn)[at]
                place = self.place(order, turn, known)
                self.copies[half, turn, known].wait_recv()
                came = self.landing[half, place].astype(F32)
                if turn == 0:
                    value = self.part[self.rows_of(known, half), :].astype(F32) + came
                else:
                    value = self.total[half, self.kept(order, turn - 1, known)] + came
                if turn == self.bits - 1:
                    self.out[half * self.rows : (half + 1) * self.rows, :] = value
                elif order[turn + 1] in known:
                    rest = tuple(bit for bit in known if bit != order[turn + 1])
                    next_place = self.place(order, turn + 1, rest) - self.count // 2
                    self.outgoing[half, next_place] = value.astype(BF)
                    self.put(half, turn + 1, rest, self.outgoing.at[half, next_place])
                else:
                    self.total[half, self.kept(order, turn, known)] = value

    def kept(self, order, turn, known):
        return sum(2**i for i, bit in enumerate(order[turn + 2 :]) if bit in known)

    def finish(self):
        for copy in self.copies.values():
            copy.wait_send()


def scatter_scratch(count, rows, columns):
    half = rows // 2
    return [
        pltpu.VMEM((2, count - 1, half, columns), BF),
        pltpu.VMEM((2, count // 2 - 1, half, columns), BF),
        pltpu.VMEM((2, count // 4, half, columns), F32),
        pltpu.SemaphoreType.DMA((2 * count,)),
        pltpu.SemaphoreType.DMA((2 * count,)),
    ]


def shifted_sum(window, taps_ref, member, lanes, keep):
    length = window.shape[0] - 8
    row = lax.broadcasted_iota(jnp.int32, (length, 1), 0)
    shifts = [window[8:]]
    for lagged in range(1, CONV):
        moved = pltpu.roll(window, lagged, 0)[8:]
        shifts.append(moved * jnp.where(row >= lagged, 1.0, keep))
    summed = shifts[0] * taps_ref[member * CONV : member * CONV + 1, lanes]
    for lagged in range(1, CONV):
        at = member * CONV + lagged
        summed = summed + shifts[lagged] * taps_ref[at : at + 1, lanes]
    return summed, shifts


def front_kernel(
    count, heads, persist_ref, x_ref, beta_ref, taps_ref, pad_ref, gain_ref, mixer_ref, g_ref,
    pre_ref, q_ref, k_ref, v_ref, brow_ref, sigma_ref, mixed_ref, t_ref, wide_ref, s_ref, f_ref, a_ref,
    full_ref, rows_ref, g_full_ref,
    w_ref, pre_buf, logit_buf, u_buf, c_buf, on_buf, sends, recvs, local, gather_sends, gather_recvs,
):
    total, features = x_ref.shape
    mine = on_buf.shape[1]
    weight = pltpu.make_async_copy(mixer_ref.at[:, 0 : 3 * mine], w_ref, local.at[2])
    weight.start()
    hd = mine // heads
    blocks = total // BLOCK
    tile = 2 * BLOCK
    greet(others("seq", count))
    exchange = start_exchange(
        [
            (
                mixer_ref,
                lambda i: (pl.ds(pl.multiple_of(i * mine, mine), mine), slice(3 * mine, 4 * mine)),
                rows_ref,
                lambda i: span(mine, i, 1),
            )
        ],
        count, sends, recvs, local,
    )
    beside = Gather(
        count, g_ref, g_full_ref, 0, gather_sends, gather_recvs, local, 2 * count, 3
    )
    beside.start()
    pre_buf[0:8, :] = jnp.zeros((8, 3 * mine), F32)
    chunk = 4 * BLOCK
    weight.wait()

    def project(index, carry):
        rows = pl.ds(pl.multiple_of(index * chunk, chunk), chunk)
        x = x_ref[rows, :]
        low = mm(x, w_ref[...]).astype(BF)
        pre_ref[rows, :] = low
        pre_buf[pl.ds(pl.multiple_of(index * chunk + 8, 8), chunk), :] = low.astype(F32)
        logit_buf[rows, :] = mm(x, beta_ref[...])
        return carry

    lax.fori_loop(0, total // chunk, project, 0)
    beside.forward(0)

    def convolve(index, carry):
        keep = persist_ref[index]
        rows = pl.ds(pl.multiple_of(index * BLOCK, BLOCK), BLOCK)
        for member, target in enumerate((q_ref, k_ref, v_ref)):
            for h in range(heads):
                lanes = slice(h * hd, (h + 1) * hd)
                there = slice(member * mine + h * hd, member * mine + (h + 1) * hd)
                window = pre_buf[pl.ds(pl.multiple_of(index * BLOCK, 8), BLOCK + 8), there]
                summed, _ = shifted_sum(window, taps_ref, member, lanes, keep)
                value = summed * jax.nn.sigmoid(summed)
                if member < 2:
                    norm = jnp.sum(value * value, axis=1, keepdims=True) + EPSILON
                    value = value * lax.rsqrt(norm)
                if member == 0:
                    value = value * hd ** (-0.5)
                target[rows, lanes] = value.astype(BF)
        return carry

    lax.fori_loop(0, blocks, convolve, 0)
    beside.forward(1)
    row, col = tile_masks(tile)
    eyed = (
        lax.broadcasted_iota(jnp.int32, (hd, hd), 0) == lax.broadcasted_iota(jnp.int32, (hd, hd), 1)
    ).astype(F32)

    def first(step, carry):
        same = (row // BLOCK) == (col // BLOCK)
        eye = (row == col).astype(F32)
        chains = [(2 * step + i, h) for i in range(2) for h in range(heads)]
        ts, ls, ks, vs, bs = [], [], [], [], []
        for index, h in chains:
            rows = pl.ds(pl.multiple_of(index * tile, tile), tile)
            lanes = slice(h * hd, (h + 1) * hd)
            k = k_ref[rows, lanes]
            logit = jnp.sum(eye * logit_buf[rows, h : h + 1], axis=0, keepdims=True)
            sigma = jax.nn.sigmoid(logit)
            b = sigma * pad_ref[pl.ds(index, 1), :]
            sigma_ref[index, h : h + 1, :] = sigma
            brow_ref[index, h : h + 1, :] = b
            bcol = jnp.sum(eye * b, axis=1, keepdims=True)
            low = jnp.where(same & (row > col), mm(k, k, NT) * bcol, 0.0)
            ls.append(low)
            ks.append(k)
            vs.append(v_ref[rows, lanes])
            bs.append(b)
            ts.append(eye - jnp.where((row // 2) == (col // 2), low, 0.0))
        size = 2
        while size < BLOCK:
            cut = ((row // (2 * size)) == (col // (2 * size))) & ((row // size) != (col // size))
            mids = [mm_ww(jnp.where(cut, l, 0.0), t) for l, t in zip(ls, ts)]
            ts = [t - mm_ww(t, m) for t, m in zip(ts, mids)]
            size *= 2
        for at, (index, h) in enumerate(chains):
            rows = pl.ds(pl.multiple_of(index * tile, tile), tile)
            lanes = slice(h * hd, (h + 1) * hd)
            t_ref[h, rows, :] = ts[at]
            wu = mm_wl(ts[at] * bs[at], jnp.concatenate([ks[at], vs[at]], axis=1))
            wide_ref[rows, lanes] = wu[:, :hd]
            u_buf[rows, lanes] = wu[:, hd:]
            for part in range(2):
                sub = slice(part * BLOCK, (part + 1) * BLOCK)
                ab = mm_lw(ks[at][sub], wu[sub], TN)
                a_ref[h, index * 2 + part] = eyed - ab[:, :hd]
                c_buf[h, index * 2 + part] = ab[:, hd:]
        return carry

    lax.fori_loop(0, blocks // 4, first, 0)
    for turn in range(2, beside.turns()):
        beside.forward(turn)

    def chain(index, states):
        keep = persist_ref[index]
        new = []
        for h in range(heads):
            s = states[h] * keep
            s_ref[h, index] = s
            new.append(mm_ww(a_ref[h, index], s) + c_buf[h, index])
        return tuple(new)

    lax.fori_loop(0, blocks, chain, tuple(jnp.zeros((hd, hd), F32) for _ in range(heads)))

    def last(step, carry):
        lower_row, lower_col = tile_masks(BLOCK)
        for part in range(2):
            index = 2 * step + part
            rows = pl.ds(pl.multiple_of(index * BLOCK, BLOCK), BLOCK)
            for h in range(heads):
                lanes = slice(h * hd, (h + 1) * hd)
                q, k, s = q_ref[rows, lanes], k_ref[rows, lanes], s_ref[h, index]
                f = u_buf[rows, lanes] - mm_ww(wide_ref[rows, lanes], s)
                p = jnp.where(lower_row >= lower_col, mm(q, k, NT), 0.0)
                f_ref[rows, lanes] = f
                mixed = mm_lw(q, s) + mm_ww(p, f)
                mixed_ref[rows, lanes] = mixed
                scale = lax.rsqrt(jnp.mean(mixed * mixed, axis=1, keepdims=True) + EPSILON)
                on_buf[rows, lanes] = (mixed * scale * gain_ref[0:1, :]).astype(BF)
        return carry

    gather = Gather(count, on_buf, full_ref, 1, gather_sends, gather_recvs, local, 0, 1)
    lax.fori_loop(0, blocks // 4, last, 0)
    gather.start_half(0)
    lax.fori_loop(blocks // 4, blocks // 2, last, 0)
    gather.start_half(1)
    gather.start_own()
    for turn in range(gather.turns()):
        gather.forward(turn)
    gather.finish()
    beside.finish()
    wait_all(exchange)


def front(count, heads, persist, x, w_mixer, w_beta, taps, pad, gain, g):
    total, features = x.shape
    mine = w_mixer.shape[1] // 4
    hd = mine // heads
    blocks, tiles = total // BLOCK, total // (2 * BLOCK)
    wide = jax.ShapeDtypeStruct((total, mine), F32)
    low = jax.ShapeDtypeStruct((total, mine), BF)
    strength = jax.ShapeDtypeStruct((tiles, heads, 2 * BLOCK), F32)
    states = jax.ShapeDtypeStruct((heads, blocks, hd, hd), F32)
    return pl.pallas_call(
        functools.partial(front_kernel, count, heads),
        out_shape=(
            jax.ShapeDtypeStruct((total, 3 * mine), BF),
            low, low, low, strength, strength, wide,
            jax.ShapeDtypeStruct((heads, total, 2 * BLOCK), F32),
            wide, states, wide, states,
            jax.ShapeDtypeStruct((total, mine * count), BF),
            jax.ShapeDtypeStruct((mine, features), BF),
            jax.ShapeDtypeStruct((total, features), BF),
        ),
        in_specs=[
            pl.BlockSpec(memory_space=pltpu.SMEM),
            VMEM, VMEM, VMEM, VMEM, VMEM, ANY, ANY,
        ],
        out_specs=(VMEM,) * 12 + (ANY,) * 3,
        scratch_shapes=[
            pltpu.VMEM((features, 3 * mine), BF),
            pltpu.VMEM((total + 8, 3 * mine), F32),
            pltpu.VMEM((total, w_beta.shape[1]), F32),
            pltpu.VMEM((total, mine), F32),
            pltpu.VMEM((heads, blocks, hd, hd), F32),
            pltpu.VMEM((total, mine), BF),
            pltpu.SemaphoreType.DMA((count,)),
            pltpu.SemaphoreType.DMA((count,)),
            pltpu.SemaphoreType.DMA((4,)),
            pltpu.SemaphoreType.DMA((4 * count,)),
            pltpu.SemaphoreType.DMA((4 * count,)),
        ],
        compiler_params=comm_params(4, 52),
    )(persist, x, w_beta, taps, pad, gain, w_mixer, g)


def middle_kernel(
    count, full_ref, mixer_ref, x_ref, gain_ref, mid_ref, normed_ref,
    w_ref, staged, landed, low_buf, sends, recvs, local, gather_sends, gather_recvs,
):
    me = lax.axis_index("seq")
    rows, features = x_ref.shape
    mine = w_ref.shape[1]
    weight = pltpu.make_async_copy(mixer_ref.at[:, 3 * mine : 4 * mine], w_ref, local.at[2])
    weight.start()
    greet(others("seq", count))
    weight.wait()
    copies = []
    for step in list(range(1, count)) + [0]:
        peer = lax.rem(me + step, count)
        at = pl.ds(pl.multiple_of(peer * rows, rows), rows)
        staged[step] = mm(full_ref[at, :], w_ref[...])
        target = landed.at[span(mine, me, 1)]
        if step:
            copies.append(send(staged.at[step], target, sends, recvs, step, "seq", peer))
        else:
            own = pltpu.make_async_copy(staged.at[0], target, local.at[0])
            own.start()
            copies.append(own)
    wait_all(copies)
    for at in range(0, rows, 16):
        part = slice(at, at + 16)
        value = x_ref[part, :].astype(F32) + landed[part, :]
        mid_ref[part, :] = value
        scale = lax.rsqrt(jnp.mean(value * value, axis=1, keepdims=True) + EPSILON)
        low_buf[part, :] = (value * scale * gain_ref[0:1, :]).astype(BF)
    gather = Gather(count, low_buf, normed_ref, 0, gather_sends, gather_recvs, local, 0, 1)
    gather.start()
    for turn in range(gather.turns()):
        gather.forward(turn)
    gather.finish()


def middle(count, full, w_mixer, x, gain):
    rows, features = x.shape
    mine = w_mixer.shape[1] // 4
    return pl.pallas_call(
        functools.partial(middle_kernel, count),
        out_shape=(
            jax.ShapeDtypeStruct((rows, features), F32),
            jax.ShapeDtypeStruct((rows * count, features), BF),
        ),
        in_specs=[VMEM, ANY, VMEM, VMEM],
        out_specs=(VMEM, ANY),
        scratch_shapes=[
            pltpu.VMEM((features, mine), BF),
            pltpu.VMEM((count, rows, mine), F32),
            pltpu.VMEM((rows, features), F32),
            pltpu.VMEM((rows, features), BF),
            pltpu.SemaphoreType.DMA((count,)),
            pltpu.SemaphoreType.DMA((count,)),
            pltpu.SemaphoreType.DMA((3,)),
            pltpu.SemaphoreType.DMA((2 * count,)),
            pltpu.SemaphoreType.DMA((2 * count,)),
        ],
        compiler_params=comm_params(5),
    )(full, w_mixer, x, gain)


def norm_backward(value_ref, grad_ref, beside_ref, gain_ref, out_ref, gain_out, low_ref=None):
    rows, features = out_ref.shape
    gain_out[...] = jnp.zeros((8, features), F32)
    for at in range(0, rows, 8):
        part = slice(at, at + 8)
        value = value_ref[part, :].astype(F32)
        scale = lax.rsqrt(jnp.mean(value * value, axis=1, keepdims=True) + EPSILON)
        unit = value * scale
        grad = grad_ref[part, :]
        gain_out[...] += grad * unit
        scaled = grad * gain_ref[0:1, :]
        mean = jnp.mean(scaled * unit, axis=1, keepdims=True)
        result = beside_ref[part, :].astype(F32) + scale * (scaled - unit * mean)
        out_ref[part, :] = result
        if low_ref is not None:
            half = (at // 16) * 16
            if at % 16 == 8:
                low_ref[half : half + 16, :] = out_ref[half : half + 16, :].astype(BF)


def reduce_kernel(
    count, part_ref, mid_ref, g_ref, gain_ref, grad_ref, gain_out, full_ref,
    summed, low_buf, landing, outgoing, kept, sends, recvs, local, gather_sends, gather_recvs,
):
    greet(hypercube_peers(count))
    scatter = Scatter(count, part_ref, summed, landing, outgoing, kept, sends, recvs)
    scatter.start()
    for turn in range(scatter.bits):
        scatter.turn(turn)
    norm_backward(mid_ref, summed, g_ref, gain_ref, grad_ref, gain_out, low_buf)
    gather = Gather(count, low_buf, full_ref, 0, gather_sends, gather_recvs, local, 0, 0)
    gather.start()
    for turn in range(gather.turns()):
        gather.forward(turn)
    gather.finish()
    scatter.finish()


def reduce_middle(count, parts, mid, g, gain):
    rows, features = mid.shape
    return pl.pallas_call(
        functools.partial(reduce_kernel, count),
        out_shape=(
            jax.ShapeDtypeStruct((rows, features), F32),
            jax.ShapeDtypeStruct((8, features), F32),
            jax.ShapeDtypeStruct((rows * count, features), BF),
        ),
        in_specs=[VMEM] * 4,
        out_specs=(VMEM, VMEM, ANY),
        scratch_shapes=[pltpu.VMEM((rows, features), F32), pltpu.VMEM((rows, features), BF)]
        + scatter_scratch(count, rows, features)
        + [
            pltpu.SemaphoreType.DMA((1,)),
            pltpu.SemaphoreType.DMA((2 * count,)),
            pltpu.SemaphoreType.DMA((2 * count,)),
        ],
        compiler_params=comm_params(6),
    )(parts, mid, g, gain)


def back_kernel(
    count, heads, sizes, persist_ref, full_ref, rows_ref, mixed_ref, gain_ref, taps_ref, pre_ref, q_ref, k_ref, v_ref,
    brow_ref, t_ref, wide_ref, s_ref, f_ref, a_ref, part_ref, done_ref,
    dpre_ref, dbeta_ref, taps_out, gain_out, added_ref, *refs,
):
    total, mine = mixed_ref.shape
    hd = mine // heads
    blocks = total // BLOCK
    targets, scratch = refs[: len(sizes)], refs[len(sizes) :]
    do_buf, y_buf, c_buf, g_buf, pre_buf, conv_buf = scratch[:6]
    landing, outgoing, kept, sends, recvs, pass_sends, pass_recvs, local = scratch[6:]
    greet(others("seq", count))
    scatter = Scatter(count, part_ref, added_ref, landing, outgoing, kept, sends, recvs)
    scatter.start()
    exchange = start_exchange(
        row_pieces([done_ref], targets, [sizes], count), count, pass_sends, pass_recvs, local
    )
    gain_out[...] = jnp.zeros((8, hd), F32)
    taps_out[...] = jnp.zeros((3 * CONV, 8, mine), F32)
    pre_buf[0:8, :] = jnp.zeros((8, 3 * mine), F32)
    conv_buf[total : total + 8, :] = jnp.zeros((8, 3 * mine), F32)
    chunk = 4 * BLOCK

    def heads_in(index, carry):
        rows = pl.ds(pl.multiple_of(index * chunk, chunk), chunk)
        pre_buf[pl.ds(pl.multiple_of(index * chunk + 8, 8), chunk), :] = pre_ref[rows, :].astype(F32)
        grad = mm(full_ref[rows, :], rows_ref[...], NT)
        for h in range(heads):
            lanes = slice(h * hd, (h + 1) * hd)
            mixed, don = mixed_ref[rows, lanes], grad[:, lanes]
            scale = lax.rsqrt(jnp.mean(mixed * mixed, axis=1, keepdims=True) + EPSILON)
            unit = mixed * scale
            gain_out[...] += jnp.sum((don * unit).reshape(chunk // 8, 8, hd), axis=0)
            scaled = don * gain_ref[0:1, :]
            mean = jnp.mean(scaled * unit, axis=1, keepdims=True)
            do_buf[rows, lanes] = scale * (scaled - unit * mean)
        return carry

    lax.fori_loop(0, total // chunk, heads_in, 0)
    row, col = tile_masks(BLOCK)

    def first(step, carry):
        for part in range(2):
            index = 2 * step + part
            rows = pl.ds(pl.multiple_of(index * BLOCK, BLOCK), BLOCK)
            for h in range(heads):
                lanes = slice(h * hd, (h + 1) * hd)
                q, k, do = q_ref[rows, lanes], k_ref[rows, lanes], do_buf[rows, lanes]
                p = jnp.where(row >= col, mm(q, k, NT), 0.0)
                y = mm_ww(p, do, TN)
                y_buf[rows, lanes] = y
                c_buf[h, index] = mm_lw(q, do, TN) - mm_ww(wide_ref[rows, lanes], y, TN)
        return carry

    lax.fori_loop(0, blocks // 2, first, 0)
    scatter.turn(0)

    def chain(step, grads):
        index = blocks - 1 - step
        keep = persist_ref[index]
        new = []
        for h in range(heads):
            g = grads[h]
            g_buf[h, index] = g
            new.append((mm_ww(a_ref[h, index], g, TN) + c_buf[h, index]) * keep)
        return tuple(new)

    lax.fori_loop(0, blocks, chain, tuple(jnp.zeros((hd, hd), F32) for _ in range(heads)))
    scatter.turn(1)

    def last(step, carry):
        for part in range(2):
            index = 2 * step + part
            keep = persist_ref[index]
            rows = pl.ds(pl.multiple_of(index * BLOCK, BLOCK), BLOCK)
            half = slice(part * BLOCK, (part + 1) * BLOCK)
            for h in range(heads):
                lanes = slice(h * hd, (h + 1) * hd)
                q, k, v = q_ref[rows, lanes], k_ref[rows, lanes], v_ref[rows, lanes]
                do, s, f, g = do_buf[rows, lanes], s_ref[h, index], f_ref[rows, lanes], g_buf[h, index]
                b = brow_ref[step, h : h + 1, half]
                bcol = jnp.sum(jnp.where(row == col, b, 0.0), axis=1, keepdims=True)
                t = t_ref[h, rows, half]
                df = y_buf[rows, lanes] + mm_lw(k, g)
                dr = mm_ww(t, df, TN)
                dp = jnp.where(row >= col, mm_ww(do, f, NT), 0.0)
                dl = jnp.where(row > col, -mm_ww(dr, f, NT), 0.0)
                dq = mm_ww(do, s, NT) + mm_wl(dp, k)
                dkb = mm_wl(dl, k) - mm_ww(dr, s, NT)
                dk = mm_wl(dp, q, TN) + mm_ww(f, g, NT) + mm_wl(dl * bcol, k, TN) + bcol * dkb
                dbeta = jnp.sum(dr * v.astype(F32) + dkb * k.astype(F32), axis=1, keepdims=True)
                dbeta_ref[step, h : h + 1, half] = jnp.sum(
                    jnp.where(row == col, dbeta, 0.0), axis=0, keepdims=True
                )
                for member, grad in enumerate((dq, dk, bcol * dr)):
                    there = slice(member * mine + h * hd, member * mine + (h + 1) * hd)
                    window = pre_buf[pl.ds(pl.multiple_of(index * BLOCK, 8), BLOCK + 8), there]
                    summed, shifts = shifted_sum(window, taps_ref, member, lanes, keep)
                    sigma = jax.nn.sigmoid(summed)
                    if member < 2:
                        value = summed * sigma
                        inverse = lax.rsqrt(jnp.sum(value * value, axis=1, keepdims=True) + EPSILON)
                        unit = value * inverse
                        along = jnp.sum(grad * unit, axis=1, keepdims=True)
                        grad = (grad - unit * along) * inverse
                    if member == 0:
                        grad = grad * hd ** (-0.5)
                    grad = grad * (sigma * (1.0 + summed * (1.0 - sigma)))
                    conv_buf[rows, there] = grad
                    for lagged in range(CONV):
                        taps_out[member * CONV + lagged, :, lanes] += jnp.sum(
                            (grad * shifts[lagged]).reshape(BLOCK // 8, 8, hd), axis=0
                        )
        return carry

    lax.fori_loop(0, blocks // 2, last, 0)
    scatter.turn(2)
    for turn in range(3, scatter.bits):
        scatter.turn(turn)

    def spread(index, carry):
        rows = pl.ds(pl.multiple_of(index * BLOCK, BLOCK), BLOCK)
        keep = persist_ref[jnp.minimum(index + 1, blocks - 1)]
        block_row = lax.broadcasted_iota(jnp.int32, (BLOCK, 1), 0)
        for member in range(3):
            there = slice(member * mine, (member + 1) * mine)
            window = conv_buf[pl.ds(pl.multiple_of(index * BLOCK, 8), BLOCK + 8), there]
            summed = window[:BLOCK] * taps_ref[member * CONV : member * CONV + 1, :]
            for lagged in range(1, CONV):
                at = member * CONV + lagged
                moved = pltpu.roll(window, BLOCK + 8 - lagged, 0)[:BLOCK]
                moved = moved * jnp.where(block_row < BLOCK - lagged, 1.0, keep)
                summed = summed + moved * taps_ref[at : at + 1, :]
            dpre_ref[rows, there] = summed.astype(BF)
        return carry

    lax.fori_loop(0, blocks, spread, 0)
    scatter.finish()
    wait_all(exchange)


def back(
    count, heads, sizes, persist, full, w_rows, mixed, gain, taps, pre, q, k, v, brow, saved, parts, done
):
    total, mine = mixed.shape
    hd = mine // heads
    blocks = total // BLOCK
    rows, features = total // count, full.shape[1]
    return pl.pallas_call(
        functools.partial(back_kernel, count, heads, sizes),
        out_shape=(
            jax.ShapeDtypeStruct((total, 3 * mine), BF),
            jax.ShapeDtypeStruct(brow.shape, F32),
            jax.ShapeDtypeStruct((3 * CONV, 8, mine), F32),
            jax.ShapeDtypeStruct((8, hd), F32),
            jax.ShapeDtypeStruct((rows, features), F32),
        )
        + row_shapes([done], [sizes], count),
        in_specs=[pl.BlockSpec(memory_space=pltpu.SMEM)] + [VMEM] * 16 + [ANY],
        out_specs=(VMEM,) * 5 + (ANY,) * len(sizes),
        scratch_shapes=[
            pltpu.VMEM((total, mine), F32),
            pltpu.VMEM((total, mine), F32),
            pltpu.VMEM((heads, blocks, hd, hd), F32),
            pltpu.VMEM((heads, blocks, hd, hd), F32),
            pltpu.VMEM((total + 8, 3 * mine), F32),
            pltpu.VMEM((total + 8, 3 * mine), F32),
        ]
        + scatter_scratch(count, rows, features)
        + [
            pltpu.SemaphoreType.DMA((len(sizes) * count,)),
            pltpu.SemaphoreType.DMA((len(sizes) * count,)),
            pltpu.SemaphoreType.DMA((len(sizes),)),
        ],
        compiler_params=comm_params(7, 56),
    )(persist, full, w_rows, mixed, gain, taps, pre, q, k, v, brow, *saved, parts, done)


def end_kernel(count, sizes, part_ref, x_ref, beside_ref, gain_ref, *refs):
    sources = refs[: len(sizes)]
    targets = refs[len(sizes) + 2 : len(sizes) + 2 + sum(len(w) for w in sizes)]
    grad_ref, gain_out = refs[len(sizes) : len(sizes) + 2]
    scratch = refs[len(sizes) + 2 + len(targets) :]
    summed, landing, outgoing, kept, sends, recvs, pass_sends, pass_recvs, local = scratch
    greet(others("seq", count))
    scatter = Scatter(count, part_ref, summed, landing, outgoing, kept, sends, recvs)
    scatter.start()
    exchange = start_exchange(row_pieces(sources, targets, sizes, count), count, pass_sends, pass_recvs, local)
    for turn in range(scatter.bits):
        scatter.turn(turn)
    norm_backward(x_ref, summed, beside_ref, gain_ref, grad_ref, gain_out)
    scatter.finish()
    wait_all(exchange)


def row_pieces(sources, targets, sizes, count):
    pieces = []
    for source, widths in zip(sources, sizes):
        rows, at = source.shape[0] // count, 0
        for size in widths:
            pieces.append(
                (
                    source,
                    lambda i, rows=rows, at=at, size=size: (
                        pl.ds(pl.multiple_of(i * rows, rows), rows),
                        slice(at, at + size),
                    ),
                    targets[len(pieces)],
                    lambda i, size=size: span(size, i, 1),
                )
            )
            at += size
    return pieces


def row_shapes(sources, sizes, count):
    return tuple(
        jax.ShapeDtypeStruct((source.shape[0] // count, count * size), BF)
        for source, widths in zip(sources, sizes)
        for size in widths
    )


def end(count, parts, x, beside, gain, sources, sizes):
    rows, features = x.shape
    shapes = row_shapes(sources, sizes, count)
    return pl.pallas_call(
        functools.partial(end_kernel, count, sizes),
        out_shape=(
            jax.ShapeDtypeStruct((rows, features), F32),
            jax.ShapeDtypeStruct((8, features), F32),
        )
        + shapes,
        in_specs=[VMEM] * 4 + [ANY] * len(sources),
        out_specs=(VMEM, VMEM) + (ANY,) * len(shapes),
        scratch_shapes=[pltpu.VMEM((rows, features), F32)]
        + scatter_scratch(count, rows, features)
        + [
            pltpu.SemaphoreType.DMA((len(shapes) * count,)),
            pltpu.SemaphoreType.DMA((len(shapes) * count,)),
            pltpu.SemaphoreType.DMA((len(shapes),)),
        ],
        compiler_params=comm_params(8),
    )(parts, x, beside, gain, *sources)


def rest_and_main(hidden_width, count):
    main = hidden_width // (128 * count) * 128
    return hidden_width // count - main, main


def local_heads(
    tokens,
    doc_starts,
    pad_mask,
    norm1_gain,
    query_weight,
    key_weight,
    value_weight,
    conv_weight,
    beta_weight,
    out_norm_gain,
    out_weight,
    norm2_gain,
    gate_weight,
    up_weight,
    down_weight,
    cotangent,
):
    row_count, features = tokens.shape
    width = lax.axis_size("seq")
    place = lax.axis_index("seq")
    head_dim = out_norm_gain.shape[0]
    heads = beta_weight.shape[1] // width
    mine = heads * head_dim
    total = row_count * width
    depth = lax.axis_size("dp")
    level = lax.axis_index("dp")
    owned = norm1_gain.shape[0]
    rest, main = rest_and_main(gate_weight.shape[1], width)
    small_all, mixer_part = opening(
        width,
        depth,
        [norm1_gain[None], norm2_gain[None], conv_weight, pad_mask, doc_starts],
        [query_weight, key_weight, value_weight, out_weight],
    )
    w_mixer = lax.all_gather(
        mixer_part.reshape(width * owned, 4 * mine), "dp", axis=0, tiled=True
    )
    wide = small_all[:, : 3 * CONV + 2, :owned].transpose(1, 0, 2).reshape(3 * CONV + 2, features)
    gain_first, gain_second = wide[3 * CONV], wide[3 * CONV + 1]
    taps = lax.dynamic_slice_in_dim(wide[: 3 * CONV], place * mine, mine, axis=1)
    marks = lax.dynamic_slice_in_dim(small_all[:, 3 * CONV + 2 :], level * width, width, axis=0)
    pad_rows = marks[:, 0, :row_count].reshape(-1, 2 * BLOCK)
    starts = marks[:, 1, : doc_starts.shape[1]].reshape(-1).astype(jnp.int32)
    begins = BLOCK * jnp.arange(total // BLOCK, dtype=jnp.int32)
    persist = (starts != begins).astype(F32)
    w_beta = lax.dynamic_slice_in_dim(beta_weight, place * heads, heads, axis=1)

    normed = rms_norm(tokens.astype(F32), gain_first)

    def ends(array):
        return array[:, main * width :].reshape(owned, width, rest)

    down_turned = down_weight.T
    pair_rest = jnp.concatenate([ends(gate_weight), ends(up_weight)], axis=2)
    down_rest = jnp.concatenate([ends(down_turned), jnp.zeros((owned, width, rest), BF)], axis=2)
    pair_part, down_part, normed_full = second(
        width,
        gate_weight,
        up_weight,
        down_turned,
        pair_rest.reshape(owned, -1),
        down_rest.reshape(owned, -1),
        normed.astype(BF),
    )
    w_down = lax.all_gather(down_part.reshape(width * owned, -1), "dp", axis=0, tiled=True)
    w_pair = lax.all_gather(pair_part.reshape(width * owned, -1), "dp", axis=0, tiled=True)
    w_qkv = w_mixer[:, : 3 * mine]
    beta_wide = jnp.pad(w_beta, ((0, 0), (0, 128 - heads)))
    head_gain = out_norm_gain.astype(F32)[None]
    (
        projected, queries, key_rows, values, strength, sigma_vals, mixed,
        *saved, out_full, w_out_rows, cotangent_full,
    ) = front(
        width, heads, persist, normed_full, w_mixer, beta_wide, taps, pad_rows, head_gain,
        cotangent,
    )
    residual_mid, normed_two_full = middle(width, out_full, w_mixer, tokens, gain_second[None])
    pair = product(normed_two_full, w_pair)
    tail = pair[:, 2 * main :]
    gate_out = jnp.concatenate([pair[:, :main], tail], axis=1)
    up_out = jnp.concatenate([pair[:, main : 2 * main], jnp.roll(tail, rest, axis=1)], axis=1)
    gate_sigma = jax.nn.sigmoid(gate_out)
    gate_silu = gate_out * gate_sigma
    hidden = (gate_silu * up_out).astype(BF)
    down_grads = product_left(cotangent_full, hidden).astype(BF)
    w_down, _ = lax.optimization_barrier((w_down, down_grads))
    down_sums = lax.psum_scatter(down_grads, "dp", scatter_dimension=0, tiled=True)
    hidden_grad = product(cotangent_full, w_down)
    gate_grad_low = (
        hidden_grad * up_out * gate_sigma * (1.0 + gate_out * (1.0 - gate_sigma))
    ).astype(BF)
    up_grad_low = (hidden_grad * gate_silu).astype(BF)
    pair_grad_low = jnp.concatenate(
        [
            gate_grad_low[:, :main],
            up_grad_low[:, :main],
            gate_grad_low[:, main : main + rest],
            up_grad_low[:, main : main + rest],
        ],
        axis=1,
    )
    two_parts = product_right(pair_grad_low, w_pair).astype(BF)
    pair_grads = product_left(normed_two_full, pair_grad_low).astype(BF)
    pair_sums = lax.psum_scatter(pair_grads, "dp", scatter_dimension=0, tiled=True)
    added_parts = product_right(hidden, w_down).astype(BF)
    residual_mid_grad, gain_second_rows, mid_full = reduce_middle(
        width, two_parts, residual_mid, cotangent, gain_second[None]
    )
    (
        projected_grad, strength_grads, conv_rows_grad, out_gain_rows, added,
        down_main, down_ends,
    ) = back(
        width, heads, (main, 2 * rest), persist, mid_full, w_out_rows, mixed, head_gain, taps, projected,
        queries, key_rows, values, strength, saved, added_parts, down_sums,
    )
    output = (residual_mid + added).astype(BF)
    gain_second_grad = jnp.sum(gain_second_rows, axis=0)
    out_gain_grad = jnp.sum(out_gain_rows, axis=0)
    conv_grad = jnp.sum(conv_rows_grad, axis=1)
    logits_grad = strength_grads * pad_rows[:, None] * sigma_vals * (1.0 - sigma_vals)
    logits_grad = logits_grad.transpose(1, 0, 2).reshape(heads, total).astype(BF)
    mid_mine = lax.dynamic_slice_in_dim(mid_full, place * mine, mine, axis=1)
    mixer_grads = jnp.concatenate(
        [
            product_left(normed_full, projected_grad).astype(BF),
            product_left(out_full, mid_mine).astype(BF),
        ],
        axis=1,
    )
    mixer_grads, pair_sums = lax.optimization_barrier((mixer_grads, pair_sums))
    mixer_sums = lax.psum_scatter(mixer_grads, "dp", scatter_dimension=0, tiled=True)
    beta_grad = product(logits_grad, normed_full)
    normed_parts = product_right(projected_grad, w_qkv) + lax.dot_general(
        logits_grad, w_beta, (((0,), (1,)), ((), ())), preferred_element_type=F32
    )
    (
        tokens_grad, gain_first_rows,
        gate_main, up_main, pair_ends,
    ) = end(
        width, normed_parts.astype(BF), tokens, residual_mid_grad, gain_first[None],
        [pair_sums], [(main, main, 2 * rest)],
    )
    gain_first_grad = jnp.sum(gain_first_rows, axis=0)

    gain_row = jnp.pad(out_gain_grad[None], ((0, 0), (0, features - head_dim)))
    plane = jnp.concatenate([gain_first_grad[None], gain_second_grad[None], gain_row], axis=0)
    conv_rows = -(-3 * CONV * mine // features)
    conv_flat = jnp.pad(conv_grad.reshape(-1), (0, conv_rows * features - 3 * CONV * mine))
    levels = jnp.concatenate([beta_grad, conv_flat.reshape(conv_rows, features)], axis=0)
    sums, each = small_sums(plane.reshape(8, -1), levels.reshape(8, -1), width, depth)
    sums = sums.reshape(3, features)
    each = each.reshape(width, heads + conv_rows, features)
    beta_total = each[:, :heads].reshape(width * heads, features).T
    conv_all = each[:, heads:].reshape(width, -1)[:, : 3 * CONV * mine]
    conv_all = conv_all.reshape(width, 3 * CONV, mine).transpose(1, 0, 2).reshape(-1, features)
    wide_sums = jnp.concatenate([sums[:2], conv_all], axis=0)
    own = level * width + place
    wide_own = lax.dynamic_slice_in_dim(wide_sums, own * owned, owned, axis=1)

    shard_q, shard_k, shard_v, shard_o = (
        a.astype(F32) for a in closing([mixer_sums], width, [(mine,) * 4], 13)
    )

    def joined(front, back, at):
        back = back.reshape(owned, width, 2, rest)[:, :, at].reshape(owned, width * rest)
        return jnp.concatenate([front, back], axis=1).astype(F32)

    return (
        output,
        tokens_grad,
        wide_own[0],
        shard_q,
        shard_k,
        shard_v,
        wide_own[2:].reshape(3, CONV, owned),
        beta_total,
        sums[2, :head_dim],
        shard_o,
        wide_own[1],
        joined(gate_main, pair_ends, 0),
        joined(up_main, pair_ends, 1),
        joined(down_main, down_ends, 0).T,
    )


def solution(mesh):
    in_specs = (
        P(("dp", "seq"), None),
        P("dp", "seq"),
        P("dp", "seq"),
        P(("dp", "seq")),
        P(("dp", "seq"), None),
        P(("dp", "seq"), None),
        P(("dp", "seq"), None),
        P(None, None, ("dp", "seq")),
        P(),
        P(),
        P(("dp", "seq"), None),
        P(("dp", "seq")),
        P(("dp", "seq"), None),
        P(("dp", "seq"), None),
        P(None, ("dp", "seq")),
        P(("dp", "seq"), None),
    )
    out_specs = (
        P(("dp", "seq"), None),
        P(("dp", "seq"), None),
        P(("dp", "seq")),
        P(("dp", "seq"), None),
        P(("dp", "seq"), None),
        P(("dp", "seq"), None),
        P(None, None, ("dp", "seq")),
        P(),
        P(),
        P(("dp", "seq"), None),
        P(("dp", "seq")),
        P(("dp", "seq"), None),
        P(("dp", "seq"), None),
        P(None, ("dp", "seq")),
    )

    def layer(*arrays):
        head_count, hidden_width = arrays[8].shape[1], arrays[12].shape[1]
        width = mesh.shape["seq"]
        rest, main = rest_and_main(hidden_width, width)
        by_heads = head_count % width == 0 and rest == 64 and main > 0
        by_heads = by_heads and width >= 4 and width & (width - 1) == 0
        local = local_heads if by_heads else local_sequence
        return jax.shard_map(
            local, mesh=mesh, in_specs=in_specs, out_specs=out_specs, check_vma=False
        )(*arrays)

    return layer
```

```python
import functools

import jax
import jax.numpy as jnp
from jax import lax
from jax.experimental import pallas as pl
from jax.experimental.pallas import tpu as pltpu
from jax.sharding import PartitionSpec as P

CONV = 4
BLOCK = 64


EPSILON = 1e-06
PRECISE = lax.Precision.HIGHEST


def from_behind(array, axis, by):
    length = lax.axis_size(axis)
    pairs = [(i, i + by) for i in range(length) if 0 <= i + by < length]
    return lax.ppermute(array, axis, pairs)


def product(left, right):
    return jnp.dot(left, right, preferred_element_type=jnp.float32)


def product_left(left, right):
    return lax.dot_general(
        left, right, (((0,), (0,)), ((), ())), preferred_element_type=jnp.float32
    )


def product_right(left, right):
    return lax.dot_general(
        left, right, (((1,), (1,)), ((), ())), preferred_element_type=jnp.float32
    )


def rounded(value):
    return lax.optimization_barrier(value.astype(jnp.bfloat16)).astype(jnp.float32)


def rms_norm(value, gain):
    return value * lax.rsqrt(jnp.mean(value * value, axis=-1, keepdims=True) + EPSILON) * gain


def block_parts(queries, key_rows, values, strength):
    keyed = key_rows * strength[..., None]
    block_len = key_rows.shape[1]
    lower_part = jnp.tril(jnp.einsum("hcd,hed->hce", keyed, key_rows, precision=PRECISE), -1)
    system = lower_part + jnp.eye(block_len, dtype=jnp.float32)
    weights = jax.scipy.linalg.solve_triangular(system, keyed, lower=True, unit_diagonal=True)
    updates = jax.scipy.linalg.solve_triangular(
        system, values * strength[..., None], lower=True, unit_diagonal=True
    )
    scores = jnp.tril(jnp.einsum("hcd,hed->hce", queries, key_rows, precision=PRECISE))
    return (weights, updates, scores)


def delta_step(state_now, inputs):
    queries, key_rows, values, strength, persist = inputs
    state_now = state_now * persist
    weights, updates, scores = block_parts(queries, key_rows, values, strength)
    corrected = updates - jnp.einsum("hcd,hde->hce", weights, state_now, precision=PRECISE)
    outputs = jnp.einsum("hcd,hde->hce", queries, state_now, precision=PRECISE) + jnp.einsum(
        "hce,hef->hcf", scores, corrected, precision=PRECISE
    )
    state_now = state_now + jnp.einsum("hcd,hce->hde", key_rows, corrected, precision=PRECISE)
    return (state_now, outputs)


def track_step(holding, inputs):
    state_now, transit = holding
    queries, key_rows, values, strength, persist = inputs
    state_now = state_now * persist
    transit = transit * persist
    weights, updates, scores = block_parts(queries, key_rows, values, strength)
    corrected = updates - jnp.einsum("hcd,hde->hce", weights, state_now, precision=PRECISE)
    outputs = jnp.einsum("hcd,hde->hce", queries, state_now, precision=PRECISE) + jnp.einsum(
        "hce,hef->hcf", scores, corrected, precision=PRECISE
    )
    leading = queries - jnp.einsum("hce,hed->hcd", scores, weights, precision=PRECISE)
    state_now = state_now + jnp.einsum("hcd,hce->hde", key_rows, corrected, precision=PRECISE)
    eraser = jnp.eye(key_rows.shape[2], dtype=jnp.float32) - jnp.einsum(
        "hcd,hce->hde", key_rows, weights, precision=PRECISE
    )
    return (
        (state_now, jnp.einsum("hde,hef->hdf", eraser, transit, precision=PRECISE)),
        (outputs, leading, transit),
    )


def advance(linear, offset_part, incoming):
    return jnp.einsum("hde,hef->hdf", linear, incoming, precision=PRECISE) + offset_part


def into_blocks(array):
    row_count, head_count, head_dim = array.shape
    return array.reshape(row_count // BLOCK, BLOCK, head_count, head_dim).transpose(0, 2, 1, 3)


def from_blocks(array):
    block_count, head_count, block_len, head_dim = array.shape
    return array.transpose(0, 2, 1, 3).reshape(block_count * block_len, head_count, head_dim)


def local_sequence(
    tokens,
    doc_starts,
    pad_mask,
    norm1_gain,
    query_weight,
    key_weight,
    value_weight,
    conv_weight,
    beta_weight,
    out_norm_gain,
    out_weight,
    norm2_gain,
    gate_weight,
    up_weight,
    down_weight,
    cotangent,
):
    row_count, features = tokens.shape
    head_count = beta_weight.shape[1]
    head_dim = out_norm_gain.shape[0]
    block_count = row_count // BLOCK
    w_query, w_key, w_value, w_out, conv_full, gain_first = (
        lax.all_gather(query_weight, ("dp", "seq"), axis=0, tiled=True),
        lax.all_gather(key_weight, ("dp", "seq"), axis=0, tiled=True),
        lax.all_gather(value_weight, ("dp", "seq"), axis=0, tiled=True),
        lax.all_gather(out_weight, ("dp", "seq"), axis=0, tiled=True),
        lax.all_gather(conv_weight, ("dp", "seq"), axis=2, tiled=True),
        lax.all_gather(norm1_gain, ("dp", "seq"), axis=0, tiled=True),
    )
    w_gate, w_up, w_down, gain_second = (
        lax.all_gather(gate_weight, ("dp", "seq"), axis=0, tiled=True),
        lax.all_gather(up_weight, ("dp", "seq"), axis=0, tiled=True),
        lax.all_gather(down_weight, ("dp", "seq"), axis=1, tiled=True),
        lax.all_gather(norm2_gain, ("dp", "seq"), axis=0, tiled=True),
    )
    seq_place = lax.axis_index("seq")
    positions = seq_place * row_count + jnp.arange(row_count, dtype=jnp.int32)
    starts = doc_starts[0]
    offsets = jnp.repeat(starts, BLOCK)
    persist = (
        starts != seq_place * row_count + BLOCK * jnp.arange(block_count, dtype=jnp.int32)
    ).astype(jnp.float32)
    pad_rows = pad_mask[0].astype(jnp.float32)[:, None]

    def mixer_in(extended, conv_taps):
        results = []
        for member in range(3):
            columns = extended[:, member * features : (member + 1) * features]
            summed = jnp.zeros((row_count, features), jnp.float32)
            for lagged in range(CONV):
                inside = (positions - lagged >= offsets).astype(jnp.float32)[:, None]
                summed = (
                    summed
                    + conv_taps[member, lagged]
                    * inside
                    * columns[CONV - 1 - lagged : CONV - 1 - lagged + row_count]
                )
            activated = jax.nn.silu(summed).reshape(row_count, head_count, head_dim)
            if member < 2:
                activated = activated * lax.rsqrt(
                    jnp.sum(activated * activated, axis=-1, keepdims=True) + EPSILON
                )
            if member == 0:
                activated = activated * head_dim ** (-0.5)
            results.append(activated)
        return tuple(results)

    residual_in = tokens.astype(jnp.float32)
    normed, norm_first_pull = jax.vjp(rms_norm, residual_in, gain_first.astype(jnp.float32))
    normed_low = normed.astype(jnp.bfloat16)
    projected = jnp.concatenate(
        [product(normed_low, w_query), product(normed_low, w_key), product(normed_low, w_value)],
        axis=1,
    ).astype(jnp.bfloat16)
    logits = product(normed_low, beta_weight)
    sigma_vals = jax.nn.sigmoid(logits)
    strength = sigma_vals * pad_rows
    rims = from_behind(projected[row_count - CONV + 1 :], "seq", 1)
    extended_in = jnp.concatenate([rims, projected], axis=0).astype(jnp.float32)
    (queries, key_rows, values), mixer_pull = jax.vjp(
        mixer_in, extended_in, conv_full.astype(jnp.float32)
    )
    query_blocks = into_blocks(rounded(queries))
    key_blocks = into_blocks(rounded(key_rows))
    value_blocks = into_blocks(rounded(values))
    strength_blocks = strength.reshape(block_count, BLOCK, head_count).transpose(0, 2, 1)
    zero_state = jnp.zeros((head_count, head_dim, head_dim), jnp.float32)
    identity = jnp.broadcast_to(
        jnp.eye(head_dim, dtype=jnp.float32), (head_count, head_dim, head_dim)
    )
    block_inputs = (query_blocks, key_blocks, value_blocks, strength_blocks, persist)
    (final_state, final_transit), (local_out, leading, transit) = lax.scan(
        track_step, (zero_state, identity), block_inputs
    )

    def forward_turn(turn_index, incoming):
        return from_behind(advance(final_transit, final_state, incoming), "seq", 1)

    start_state = lax.fori_loop(0, lax.axis_size("seq") - 1, forward_turn, zero_state)
    carried = jnp.einsum("nhde,hef->nhdf", transit, start_state, precision=PRECISE)
    mixed = from_blocks(
        local_out + jnp.einsum("nhcd,nhdf->nhcf", leading, carried, precision=PRECISE)
    )
    out_normed, out_norm_pull = jax.vjp(rms_norm, mixed, out_norm_gain.astype(jnp.float32))
    out_low = out_normed.reshape(row_count, features).astype(jnp.bfloat16)
    residual_mid = residual_in + product(out_low, w_out)
    normed_two, norm_second_pull = jax.vjp(rms_norm, residual_mid, gain_second.astype(jnp.float32))
    normed_two_low = normed_two.astype(jnp.bfloat16)
    gate_out = product(normed_two_low, w_gate)
    up_out = product(normed_two_low, w_up)
    hidden = (jax.nn.silu(gate_out) * up_out).astype(jnp.bfloat16)
    output = (residual_mid + product(hidden, w_down)).astype(jnp.bfloat16)
    grad_out = cotangent.astype(jnp.float32)
    down_grad = product_left(hidden, cotangent)
    hidden_grad = product_right(cotangent, w_down)
    gate_sigma = jax.nn.sigmoid(gate_out)
    gate_grad_low = (
        hidden_grad * up_out * gate_sigma * (1.0 + gate_out * (1.0 - gate_sigma))
    ).astype(jnp.bfloat16)
    up_grad_low = (hidden_grad * jax.nn.silu(gate_out)).astype(jnp.bfloat16)
    gate_grad = product_left(normed_two_low, gate_grad_low)
    up_grad = product_left(normed_two_low, up_grad_low)
    normed_two_grad = product_right(gate_grad_low, w_gate) + product_right(up_grad_low, w_up)
    mid_from_norm, gain_second_grad = norm_second_pull(normed_two_grad)
    residual_mid_grad = grad_out + mid_from_norm
    mid_low = residual_mid_grad.astype(jnp.bfloat16)
    out_grad = product_left(out_low, mid_low)
    out_normed_grad = product_right(mid_low, w_out).reshape(row_count, head_count, head_dim)
    mixed_grad, out_gain_grad = out_norm_pull(out_normed_grad)
    mixed_blocks = into_blocks(mixed_grad)
    pulled = jnp.einsum("nhcd,nhcf->nhdf", leading, mixed_blocks, precision=PRECISE)
    local_back = jnp.einsum("nhed,nhef->hdf", transit, pulled, precision=PRECISE)
    transit_turned = jnp.swapaxes(final_transit, 1, 2)

    def backward_turn(turn_index, incoming):
        return from_behind(advance(transit_turned, local_back, incoming), "seq", -1)

    end_grad = lax.fori_loop(0, lax.axis_size("seq") - 1, backward_turn, zero_state)

    def delta_local(query_in, key_in, value_in, strength_in):
        ending, outputs = lax.scan(
            jax.checkpoint(delta_step),
            start_state,
            (query_in, key_in, value_in, strength_in, persist),
        )
        return (outputs, ending)

    unused_out, delta_pull = jax.vjp(
        delta_local, query_blocks, key_blocks, value_blocks, strength_blocks
    )
    query_grad_blocks, key_grad_blocks, value_grad_blocks, strength_grad_blocks = delta_pull(
        (mixed_blocks, end_grad)
    )
    extended_grad, conv_grad = mixer_pull(
        (
            from_blocks(query_grad_blocks),
            from_blocks(key_grad_blocks),
            from_blocks(value_grad_blocks),
        )
    )
    rim_grad = from_behind(extended_grad[: CONV - 1], "seq", -1)
    projected_grad = jnp.concatenate(
        [extended_grad[CONV - 1 : row_count], extended_grad[row_count:] + rim_grad], axis=0
    ).astype(jnp.bfloat16)
    strength_grad = strength_grad_blocks.transpose(0, 2, 1).reshape(row_count, head_count)
    logits_grad = (strength_grad * pad_rows * sigma_vals * (1.0 - sigma_vals)).astype(jnp.bfloat16)
    part_query = projected_grad[:, :features]
    part_key = projected_grad[:, features : 2 * features]
    part_value = projected_grad[:, 2 * features :]
    query_grad = product_left(normed_low, part_query)
    key_grad = product_left(normed_low, part_key)
    value_grad = product_left(normed_low, part_value)
    beta_grad = product_left(normed_low, logits_grad)
    normed_grad = (
        product_right(part_query, w_query)
        + product_right(part_key, w_key)
        + product_right(part_value, w_value)
        + product_right(logits_grad, beta_weight)
    )
    input_from_norm, gain_first_grad = norm_first_pull(normed_grad)
    tokens_grad = residual_mid_grad + input_from_norm
    (
        shard_q,
        shard_k,
        shard_v,
        shard_o,
        shard_conv,
        shard_gain_one,
        shard_gate,
        shard_up,
        shard_down,
        shard_gain_two,
    ) = (
        lax.psum_scatter(query_grad, ("dp", "seq"), scatter_dimension=0, tiled=True),
        lax.psum_scatter(key_grad, ("dp", "seq"), scatter_dimension=0, tiled=True),
        lax.psum_scatter(value_grad, ("dp", "seq"), scatter_dimension=0, tiled=True),
        lax.psum_scatter(out_grad, ("dp", "seq"), scatter_dimension=0, tiled=True),
        lax.psum_scatter(conv_grad, ("dp", "seq"), scatter_dimension=2, tiled=True),
        lax.psum_scatter(gain_first_grad, ("dp", "seq"), scatter_dimension=0, tiled=True),
        lax.psum_scatter(gate_grad, ("dp", "seq"), scatter_dimension=0, tiled=True),
        lax.psum_scatter(up_grad, ("dp", "seq"), scatter_dimension=0, tiled=True),
        lax.psum_scatter(down_grad, ("dp", "seq"), scatter_dimension=1, tiled=True),
        lax.psum_scatter(gain_second_grad, ("dp", "seq"), scatter_dimension=0, tiled=True),
    )
    beta_total, out_gain_total = lax.psum((beta_grad, out_gain_grad), ("dp", "seq"))
    return (
        output,
        tokens_grad,
        shard_gain_one,
        shard_q,
        shard_k,
        shard_v,
        shard_conv,
        beta_total,
        out_gain_total,
        shard_o,
        shard_gain_two,
        shard_gate,
        shard_up,
        shard_down,
    )


F32 = jnp.float32
BF = jnp.bfloat16
NN=(((1,),(0,)),((),())); NT=(((1,),(1,)),((),())); TN=(((0,),(0,)),((),()))

def mm(a,b,dims=NN):
    return lax.dot_general(a,b,dims,preferred_element_type=F32)

def halves(a):
    high=a.astype(BF)
    return high,(a-high.astype(F32)).astype(BF)

def mm_lw(a,b,dims=NN):
    high,low=halves(b)
    return mm(a,high,dims)+mm(a,low,dims)

def mm_wl(a,b,dims=NN):
    high,low=halves(a)
    return mm(high,b,dims)+mm(low,b,dims)

def mm_ww(a,b,dims=NN):
    ah,al=halves(a); bh,bl=halves(b)
    return mm(ah,bh,dims)+(mm(al,bh,dims)+mm(ah,bl,dims))

def tile_masks(tile):
    row=lax.broadcasted_iota(jnp.int32,(tile,tile),0)
    col=lax.broadcasted_iota(jnp.int32,(tile,tile),1)
    return row,col


MESH = pl.DeviceIdType.MESH
ANY = pl.BlockSpec(memory_space=pl.ANY)
VMEM = pl.BlockSpec(memory_space=pltpu.VMEM)


def flipped(index, bit):
    size = 2**bit
    return index + (1 - 2 * ((index // size) % 2)) * size


def greet(peers):
    barrier = pltpu.get_barrier_semaphore()
    for axis, peer in peers:
        pl.semaphore_signal(barrier, inc=1, device_id={axis: peer}, device_id_type=MESH)
    pl.semaphore_wait(barrier, len(peers))


def others(axis, count):
    me = lax.axis_index(axis)
    return [(axis, lax.rem(me + step, count)) for step in range(1, count)]


def send(source, target, sends, recvs, slot, axis, peer):
    copy = pltpu.make_async_remote_copy(
        src_ref=source,
        dst_ref=target,
        send_sem=sends.at[slot],
        recv_sem=recvs.at[slot],
        device_id={axis: peer},
        device_id_type=MESH,
    )
    copy.start()
    return copy


def span(size, index, axis):
    piece = pl.ds(pl.multiple_of(index * size, size), size)
    return (piece, slice(None)) if axis == 0 else (slice(None), piece)


def start_exchange(pieces, count, sends, recvs, local, first=0):
    me = lax.axis_index("seq")
    started = []
    for number, (source, source_at, target, target_at) in enumerate(pieces):
        own = pltpu.make_async_copy(
            source.at[source_at(me)], target.at[target_at(me)], local.at[first // count + number]
        )
        own.start()
        started.append(own)
        for step in range(1, count):
            peer = lax.rem(me + step, count)
            slot = first + number * count + step
            started.append(
                send(
                    source.at[source_at(peer)], target.at[target_at(me)],
                    sends, recvs, slot, "seq", peer,
                )
            )
    return started


def wait_all(copies):
    for copy in copies:
        copy.wait()


def bit_orders(count):
    bits = list(range(count.bit_length() - 1))[::-1]
    other = bits[:]
    if len(bits) >= 3:
        other[0], other[1] = bits[1], bits[0]
    return [bits, other]


class Gather:
    def __init__(self, count, source, target, axis, sends, recvs, local, slot, local_slot):
        self.count, self.source, self.target, self.axis = count, source, target, axis
        self.sends, self.recvs, self.local = sends, recvs, local
        self.slot, self.local_slot = slot, local_slot
        self.me = lax.axis_index("seq")
        self.copies = {}

    def piece(self, owner, half):
        rows, columns = self.source.shape
        part = rows // 2
        if self.axis == 0:
            return (pl.ds(pl.multiple_of(owner * rows + half * part, part), part), slice(None))
        return (
            pl.ds(half * part, part),
            pl.ds(pl.multiple_of(owner * columns, columns), columns),
        )

    def put(self, order, half, turn, known):
        owner = self.me
        for bit in known:
            owner = flipped(owner, bit)
        place = self.target.at[self.piece(owner, half)]
        part = self.source.shape[0] // 2
        source = place if known else self.source.at[pl.ds(half * part, part)]
        slot = self.slot + half * self.count + self.number(order, turn, known)
        self.copies[half, turn, known] = send(
            source, place, self.sends, self.recvs, slot, "seq", flipped(self.me, order[turn])
        )

    def number(self, order, turn, known):
        return 2**turn + sum(2 ** order.index(bit) for bit in known)

    def start(self):
        self.start_own()
        for half in range(2):
            self.start_half(half)

    def start_own(self):
        self.own = pltpu.make_async_copy(
            self.source,
            self.target.at[
                span(self.source.shape[self.axis], self.me, self.axis)
            ],
            self.local.at[self.local_slot],
        )
        self.own.start()

    def start_half(self, half):
        order = bit_orders(self.count)[half]
        for turn in range(len(order)):
            self.put(order, half, turn, ())

    def turns(self):
        return self.count.bit_length() - 1

    def forward(self, turn):
        orders = bit_orders(self.count)
        for before in range(2**turn):
            for half, order in enumerate(orders):
                known = tuple(order[i] for i in range(turn) if before // 2**i % 2)
                self.copies[half, turn, known].wait_recv()
                for later in range(turn + 1, len(order)):
                    self.put(order, half, later, known + (order[turn],))

    def finish(self):
        for copy in self.copies.values():
            copy.wait_send()
        self.own.wait()


def hypercube_peers(count):
    me = lax.axis_index("seq")
    return [("seq", flipped(me, bit)) for bit in range(count.bit_length() - 1)]


def comm_params(identity, limit=48):
    return pltpu.CompilerParams(
        collective_id=identity, has_side_effects=True, vmem_limit_bytes=limit * 2**20
    )


def opening_kernel(count, wq, wk, wv, wo, mixer, sends, recvs, local):
    greet(others("seq", count))
    mine = wq.shape[1] // count
    pieces = []
    for member, weight in enumerate((wq, wk, wv, wo)):
        pieces.append(
            (
                weight,
                lambda i: span(mine, i, 1),
                mixer,
                lambda i, member=member: (i, slice(None), slice(member * mine, (member + 1) * mine)),
            )
        )
    wait_all(start_exchange(pieces, count, sends, recvs, local))


def opening(count, weights):
    rows, features = weights[0].shape
    return pl.pallas_call(
        functools.partial(opening_kernel, count),
        out_shape=jax.ShapeDtypeStruct((count, rows, 4 * features // count), BF),
        in_specs=[ANY] * 4,
        out_specs=ANY,
        scratch_shapes=[
            pltpu.SemaphoreType.DMA((4 * count,)),
            pltpu.SemaphoreType.DMA((4 * count,)),
            pltpu.SemaphoreType.DMA((4,)),
        ],
        compiler_params=comm_params(1, 60),
    )(*weights)


def second_kernel(
    count, depth, gain_one, gain_two, taps, pad, starts, x_ref, gate, up, down, pair_rest, down_rest,
    small_all, pair, last, normed_full,
    small, gain, normed, sends, recvs, local, gather_sends, gather_recvs, far,
):
    greet(others("seq", count) + others("dp", depth))
    me, level = lax.axis_index("seq"), lax.axis_index("dp")
    small[...] = jnp.zeros(small.shape, F32)
    owned, features = gain_one.shape[1], x_ref.shape[1]
    for member in range(3):
        small[member * CONV : (member + 1) * CONV, 0:owned] = taps[member].astype(F32)
    at = 3 * CONV
    for row, source in enumerate((gain_one, gain_two, pad, starts)):
        small[at + row : at + row + 1, 0 : source.shape[1]] = source[...].astype(F32)
    mine = level * count + me
    small_all[mine] = small[...]
    copies = [
        send(
            small, small_all.at[mine], far.at[0], far.at[1], step, "seq", lax.rem(me + step, count)
        )
        for step in range(1, count)
    ]
    rest = pair_rest.shape[1] // count
    main = (gate.shape[1] - pair_rest.shape[1] // 2) // count

    def piece(source, size, target, at):
        return (
            source,
            lambda i: span(size, i, 1),
            target,
            lambda i: (i, slice(None), slice(at, at + size)),
        )

    wait_all(copies)
    plane = small_all.at[pl.ds(level * count, count)]
    levels = [
        send(plane, plane, far.at[2], far.at[3], step, "dp", lax.rem(level + step, depth))
        for step in range(1, depth)
    ]
    exchange = start_exchange(
        [
            piece(gate, main, pair, 0),
            piece(up, main, pair, main),
            piece(pair_rest, rest, pair, 2 * main),
            piece(down, main, last, 0),
            piece(down_rest, rest, last, main),
        ],
        count, sends, recvs, local,
    )
    wait_all(levels)
    per = 128 // owned
    for tile in range(features // 128):
        row = small_all[tile * per, at : at + 1, :]
        for part in range(1, per):
            row = row + pltpu.roll(small_all[tile * per + part, at : at + 1, :], part * owned, 1)
        gain[0:1, tile * 128 : (tile + 1) * 128] = row
    for first in range(0, x_ref.shape[0], 16):
        part = slice(first, first + 16)
        value = x_ref[part, :].astype(F32)
        scale = lax.rsqrt(jnp.mean(value * value, axis=1, keepdims=True) + EPSILON)
        normed[part, :] = (value * scale * gain[0:1, :]).astype(BF)
    gather = Gather(count, normed, normed_full, 0, gather_sends, gather_recvs, local, 0, 5)
    gather.start()
    for turn in range(gather.turns()):
        gather.forward(turn)
    gather.finish()
    wait_all(exchange)


def second(count, depth, small, x, gate, up, down, pair_rest, down_rest):
    rows = gate.shape[0]
    rest = pair_rest.shape[1] // count
    main = (gate.shape[1] - pair_rest.shape[1] // 2) // count
    slots = max(count, depth)
    shape = (3 * CONV + 4, max(128, x.shape[0]))
    return pl.pallas_call(
        functools.partial(second_kernel, count, depth),
        out_shape=(
            jax.ShapeDtypeStruct((count * depth,) + shape, F32),
            jax.ShapeDtypeStruct((count, rows, 2 * main + rest), BF),
            jax.ShapeDtypeStruct((count, rows, main + rest), BF),
            jax.ShapeDtypeStruct((x.shape[0] * count, x.shape[1]), BF),
        ),
        in_specs=[VMEM] * 6 + [ANY] * 5,
        out_specs=(VMEM, ANY, ANY, ANY),
        scratch_shapes=[
            pltpu.VMEM(shape, F32),
            pltpu.VMEM((8, x.shape[1]), F32),
            pltpu.VMEM(x.shape, BF),
            pltpu.SemaphoreType.DMA((5 * count,)),
            pltpu.SemaphoreType.DMA((5 * count,)),
            pltpu.SemaphoreType.DMA((6,)),
            pltpu.SemaphoreType.DMA((2 * count,)),
            pltpu.SemaphoreType.DMA((2 * count,)),
            pltpu.SemaphoreType.DMA((4, slots)),
        ],
        compiler_params=comm_params(2),
    )(*small, x, gate, up, down, pair_rest, down_rest)


def closing_kernel(count, sizes, *refs):
    sources, targets, (sends, recvs, local) = refs[: len(sizes)], refs[len(sizes) : -3], refs[-3:]
    greet(others("seq", count))
    wait_all(start_exchange(row_pieces(sources, targets, sizes, count), count, sends, recvs, local))


def closing(sources, count, sizes, identity):
    shapes = row_shapes(sources, sizes, count)
    members = len(shapes)
    return pl.pallas_call(
        functools.partial(closing_kernel, count, sizes),
        out_shape=shapes,
        in_specs=[ANY] * len(sources),
        out_specs=(ANY,) * members,
        scratch_shapes=[
            pltpu.SemaphoreType.DMA((members * count,)),
            pltpu.SemaphoreType.DMA((members * count,)),
            pltpu.SemaphoreType.DMA((members,)),
        ],
        compiler_params=comm_params(identity),
    )(*sources)


def sums_kernel(count, depth, plane_ref, level_ref, total_ref, each_ref, plane_in, joined, level_in, sends, recvs):
    greet(others("seq", count) + others("dp", depth))
    me, level = lax.axis_index("seq"), lax.axis_index("dp")
    cut = plane_ref.shape[1]
    plane_in[me] = plane_ref[...]
    wait_all(
        [
            send(
                plane_ref, plane_in.at[me], sends.at[0], recvs.at[0], step,
                "seq", lax.rem(me + step, count),
            )
            for step in range(1, count)
        ]
    )
    value = plane_in[0]
    for i in range(1, count):
        value = value + plane_in[i]
    joined[:, 0:cut] = value
    joined[:, cut:] = level_ref[...]
    level_in[level] = joined[...]
    wait_all(
        [
            send(
                joined, level_in.at[level], sends.at[1], recvs.at[1], step,
                "dp", lax.rem(level + step, depth),
            )
            for step in range(1, depth)
        ]
    )
    value = level_in[0]
    for i in range(1, depth):
        value = value + level_in[i]
    total_ref[...] = value[:, 0:cut]
    joined[:, cut:] = value[:, cut:]
    each_ref[me] = value[:, cut:]
    wait_all(
        [
            send(
                joined.at[:, cut:], each_ref.at[me],
                sends.at[2], recvs.at[2], step, "seq", lax.rem(me + step, count),
            )
            for step in range(1, count)
        ]
    )


def small_sums(plane, level, count, depth):
    slots = max(count, depth)
    joined = (plane.shape[0], plane.shape[1] + level.shape[1])
    return pl.pallas_call(
        functools.partial(sums_kernel, count, depth),
        out_shape=(
            jax.ShapeDtypeStruct(plane.shape, F32),
            jax.ShapeDtypeStruct((count,) + level.shape, F32),
        ),
        in_specs=[VMEM, VMEM],
        out_specs=(VMEM, VMEM),
        scratch_shapes=[
            pltpu.VMEM((count,) + plane.shape, F32),
            pltpu.VMEM(joined, F32),
            pltpu.VMEM((depth,) + joined, F32),
            pltpu.SemaphoreType.DMA((3, slots)),
            pltpu.SemaphoreType.DMA((3, slots)),
        ],
        compiler_params=comm_params(3),
    )(plane, level)


class Scatter:
    def __init__(self, count, part, out, landing, outgoing, total, sends, recvs):
        self.count, self.part, self.out = count, part, out
        self.landing, self.outgoing, self.total = landing, outgoing, total
        self.sends, self.recvs = sends, recvs
        self.me = lax.axis_index("seq")
        self.rows = out.shape[0] // 2
        self.bits = count.bit_length() - 1
        self.orders = [order[::-1] for order in bit_orders(count)]
        self.copies = {}

    def rows_of(self, known, half):
        owner = self.me
        for bit in known:
            owner = flipped(owner, bit)
        size = self.rows
        return pl.ds(pl.multiple_of(owner * 2 * size + half * size, size), size)

    def place(self, order, turn, known):
        later = order[turn + 1 :]
        before = sum(self.count >> (t + 1) for t in range(turn))
        return before + sum(2**i for i, bit in enumerate(later) if bit in known)

    def subsets(self, order, turn):
        later = order[turn + 1 :]
        sets = [
            tuple(later[i] for i in range(len(later)) if code // 2**i % 2)
            for code in range(2 ** len(later))
        ]
        return sorted(sets, key=lambda known: [-(bit in known) for bit in later])

    def put(self, half, turn, known, source):
        order = self.orders[half]
        place = self.place(order, turn, known)
        self.copies[half, turn, known] = send(
            source,
            self.landing.at[half, place],
            self.sends,
            self.recvs,
            half * self.count + place,
            "seq",
            flipped(self.me, order[turn]),
        )

    def start(self):
        for at in range(self.count // 2):
            for half, order in enumerate(self.orders):
                known = self.subsets(order, 0)[at]
                self.put(half, 0, known, self.part.at[self.rows_of((order[0],) + known, half)])

    def turn(self, turn):
        for at in range(2 ** (self.bits - turn - 1)):
            for half, order in enumerate(self.orders):
                known = self.subsets(order, turn)[at]
                place = self.place(order, turn, known)
                self.copies[half, turn, known].wait_recv()
                came = self.landing[half, place].astype(F32)
                if turn == 0:
                    value = self.part[self.rows_of(known, half), :].astype(F32) + came
                else:
                    value = self.total[half, self.kept(order, turn - 1, known)] + came
                if turn == self.bits - 1:
                    self.out[half * self.rows : (half + 1) * self.rows, :] = value
                elif order[turn + 1] in known:
                    rest = tuple(bit for bit in known if bit != order[turn + 1])
                    next_place = self.place(order, turn + 1, rest) - self.count // 2
                    self.outgoing[half, next_place] = value.astype(BF)
                    self.put(half, turn + 1, rest, self.outgoing.at[half, next_place])
                else:
                    self.total[half, self.kept(order, turn, known)] = value

    def kept(self, order, turn, known):
        return sum(2**i for i, bit in enumerate(order[turn + 2 :]) if bit in known)

    def finish(self):
        for copy in self.copies.values():
            copy.wait_send()


def scatter_scratch(count, rows, columns):
    half = rows // 2
    return [
        pltpu.VMEM((2, count - 1, half, columns), BF),
        pltpu.VMEM((2, count // 2 - 1, half, columns), BF),
        pltpu.VMEM((2, count // 4, half, columns), F32),
        pltpu.SemaphoreType.DMA((2 * count,)),
        pltpu.SemaphoreType.DMA((2 * count,)),
    ]


def shifted_sum(window, taps_ref, member, lanes, keep):
    length = window.shape[0] - 8
    row = lax.broadcasted_iota(jnp.int32, (length, 1), 0)
    shifts = [window[8:]]
    for lagged in range(1, CONV):
        moved = pltpu.roll(window, lagged, 0)[8:]
        shifts.append(moved * jnp.where(row >= lagged, 1.0, keep))
    summed = shifts[0] * taps_ref[member * CONV : member * CONV + 1, lanes]
    for lagged in range(1, CONV):
        at = member * CONV + lagged
        summed = summed + shifts[lagged] * taps_ref[at : at + 1, lanes]
    return summed, shifts


def front_kernel(
    count, heads, persist_ref, x_ref, beta_ref, taps_ref, pad_ref, gain_ref, mixer_ref, g_ref,
    pre_ref, q_ref, k_ref, v_ref, brow_ref, sigma_ref, mixed_ref, t_ref, wide_ref, s_ref, f_ref, a_ref,
    full_ref, rows_ref, g_full_ref,
    w_ref, pre_buf, logit_buf, u_buf, c_buf, on_buf, sends, recvs, local, gather_sends, gather_recvs,
):
    total, features = x_ref.shape
    mine = on_buf.shape[1]
    weight = pltpu.make_async_copy(mixer_ref.at[:, 0 : 3 * mine], w_ref, local.at[2])
    weight.start()
    hd = mine // heads
    blocks = total // BLOCK
    tile = 2 * BLOCK
    greet(others("seq", count))
    exchange = start_exchange(
        [
            (
                mixer_ref,
                lambda i: (pl.ds(pl.multiple_of(i * mine, mine), mine), slice(3 * mine, 4 * mine)),
                rows_ref,
                lambda i: span(mine, i, 1),
            )
        ],
        count, sends, recvs, local,
    )
    beside = Gather(
        count, g_ref, g_full_ref, 0, gather_sends, gather_recvs, local, 2 * count, 3
    )
    beside.start()
    pre_buf[0:8, :] = jnp.zeros((8, 3 * mine), F32)
    chunk = 4 * BLOCK
    weight.wait()

    def project(index, carry):
        rows = pl.ds(pl.multiple_of(index * chunk, chunk), chunk)
        x = x_ref[rows, :]
        low = mm(x, w_ref[...]).astype(BF)
        pre_ref[rows, :] = low
        pre_buf[pl.ds(pl.multiple_of(index * chunk + 8, 8), chunk), :] = low.astype(F32)
        logit_buf[rows, :] = mm(x, beta_ref[...])
        return carry

    lax.fori_loop(0, total // chunk, project, 0)
    beside.forward(0)

    def convolve(index, carry):
        keep = persist_ref[index]
        rows = pl.ds(pl.multiple_of(index * BLOCK, BLOCK), BLOCK)
        for member, target in enumerate((q_ref, k_ref, v_ref)):
            for h in range(heads):
                lanes = slice(h * hd, (h + 1) * hd)
                there = slice(member * mine + h * hd, member * mine + (h + 1) * hd)
                window = pre_buf[pl.ds(pl.multiple_of(index * BLOCK, 8), BLOCK + 8), there]
                summed, _ = shifted_sum(window, taps_ref, member, lanes, keep)
                value = summed * jax.nn.sigmoid(summed)
                if member < 2:
                    norm = jnp.sum(value * value, axis=1, keepdims=True) + EPSILON
                    value = value * lax.rsqrt(norm)
                if member == 0:
                    value = value * hd ** (-0.5)
                target[rows, lanes] = value.astype(BF)
        return carry

    lax.fori_loop(0, blocks, convolve, 0)
    beside.forward(1)
    row, col = tile_masks(tile)
    eyed = (
        lax.broadcasted_iota(jnp.int32, (hd, hd), 0) == lax.broadcasted_iota(jnp.int32, (hd, hd), 1)
    ).astype(F32)

    def first(step, carry):
        same = (row // BLOCK) == (col // BLOCK)
        eye = (row == col).astype(F32)
        chains = [(2 * step + i, h) for i in range(2) for h in range(heads)]
        ts, ls, ks, vs, bs = [], [], [], [], []
        for index, h in chains:
            rows = pl.ds(pl.multiple_of(index * tile, tile), tile)
            lanes = slice(h * hd, (h + 1) * hd)
            k = k_ref[rows, lanes]
            logit = jnp.sum(eye * logit_buf[rows, h : h + 1], axis=0, keepdims=True)
            sigma = jax.nn.sigmoid(logit)
            b = sigma * pad_ref[pl.ds(index, 1), :]
            sigma_ref[index, h : h + 1, :] = sigma
            brow_ref[index, h : h + 1, :] = b
            bcol = jnp.sum(eye * b, axis=1, keepdims=True)
            low = jnp.where(same & (row > col), mm(k, k, NT) * bcol, 0.0)
            ls.append(low)
            ks.append(k)
            vs.append(v_ref[rows, lanes])
            bs.append(b)
            ts.append(eye - jnp.where((row // 2) == (col // 2), low, 0.0))
        size = 2
        while size < BLOCK:
            cut = ((row // (2 * size)) == (col // (2 * size))) & ((row // size) != (col // size))
            mids = [mm_ww(jnp.where(cut, l, 0.0), t) for l, t in zip(ls, ts)]
            ts = [t - mm_ww(t, m) for t, m in zip(ts, mids)]
            size *= 2
        for at, (index, h) in enumerate(chains):
            rows = pl.ds(pl.multiple_of(index * tile, tile), tile)
            lanes = slice(h * hd, (h + 1) * hd)
            t_ref[h, rows, :] = ts[at]
            wu = mm_wl(ts[at] * bs[at], jnp.concatenate([ks[at], vs[at]], axis=1))
            wide_ref[rows, lanes] = wu[:, :hd]
            u_buf[rows, lanes] = wu[:, hd:]
            for part in range(2):
                sub = slice(part * BLOCK, (part + 1) * BLOCK)
                ab = mm_lw(ks[at][sub], wu[sub], TN)
                a_ref[h, index * 2 + part] = eyed - ab[:, :hd]
                c_buf[h, index * 2 + part] = ab[:, hd:]
        return carry

    lax.fori_loop(0, blocks // 4, first, 0)
    for turn in range(2, beside.turns()):
        beside.forward(turn)

    def chain(index, states):
        keep = persist_ref[index]
        new = []
        for h in range(heads):
            s = states[h] * keep
            s_ref[h, index] = s
            new.append(mm_ww(a_ref[h, index], s) + c_buf[h, index])
        return tuple(new)

    lax.fori_loop(0, blocks, chain, tuple(jnp.zeros((hd, hd), F32) for _ in range(heads)))

    def last(step, carry):
        lower_row, lower_col = tile_masks(BLOCK)
        for part in range(2):
            index = 2 * step + part
            rows = pl.ds(pl.multiple_of(index * BLOCK, BLOCK), BLOCK)
            for h in range(heads):
                lanes = slice(h * hd, (h + 1) * hd)
                q, k, s = q_ref[rows, lanes], k_ref[rows, lanes], s_ref[h, index]
                f = u_buf[rows, lanes] - mm_ww(wide_ref[rows, lanes], s)
                p = jnp.where(lower_row >= lower_col, mm(q, k, NT), 0.0)
                f_ref[rows, lanes] = f
                mixed = mm_lw(q, s) + mm_ww(p, f)
                mixed_ref[rows, lanes] = mixed
                scale = lax.rsqrt(jnp.mean(mixed * mixed, axis=1, keepdims=True) + EPSILON)
                on_buf[rows, lanes] = (mixed * scale * gain_ref[0:1, :]).astype(BF)
        return carry

    gather = Gather(count, on_buf, full_ref, 1, gather_sends, gather_recvs, local, 0, 1)
    lax.fori_loop(0, blocks // 4, last, 0)
    gather.start_half(0)
    lax.fori_loop(blocks // 4, blocks // 2, last, 0)
    gather.start_half(1)
    gather.start_own()
    for turn in range(gather.turns()):
        gather.forward(turn)
    gather.finish()
    beside.finish()
    wait_all(exchange)


def front(count, heads, persist, x, w_mixer, w_beta, taps, pad, gain, g):
    total, features = x.shape
    mine = w_mixer.shape[1] // 4
    hd = mine // heads
    blocks, tiles = total // BLOCK, total // (2 * BLOCK)
    wide = jax.ShapeDtypeStruct((total, mine), F32)
    low = jax.ShapeDtypeStruct((total, mine), BF)
    strength = jax.ShapeDtypeStruct((tiles, heads, 2 * BLOCK), F32)
    states = jax.ShapeDtypeStruct((heads, blocks, hd, hd), F32)
    return pl.pallas_call(
        functools.partial(front_kernel, count, heads),
        out_shape=(
            jax.ShapeDtypeStruct((total, 3 * mine), BF),
            low, low, low, strength, strength, wide,
            jax.ShapeDtypeStruct((heads, total, 2 * BLOCK), F32),
            wide, states, wide, states,
            jax.ShapeDtypeStruct((total, mine * count), BF),
            jax.ShapeDtypeStruct((mine, features), BF),
            jax.ShapeDtypeStruct((total, features), BF),
        ),
        in_specs=[
            pl.BlockSpec(memory_space=pltpu.SMEM),
            VMEM, VMEM, VMEM, VMEM, VMEM, ANY, ANY,
        ],
        out_specs=(VMEM,) * 12 + (ANY,) * 3,
        scratch_shapes=[
            pltpu.VMEM((features, 3 * mine), BF),
            pltpu.VMEM((total + 8, 3 * mine), F32),
            pltpu.VMEM((total, w_beta.shape[1]), F32),
            pltpu.VMEM((total, mine), F32),
            pltpu.VMEM((heads, blocks, hd, hd), F32),
            pltpu.VMEM((total, mine), BF),
            pltpu.SemaphoreType.DMA((count,)),
            pltpu.SemaphoreType.DMA((count,)),
            pltpu.SemaphoreType.DMA((4,)),
            pltpu.SemaphoreType.DMA((4 * count,)),
            pltpu.SemaphoreType.DMA((4 * count,)),
        ],
        compiler_params=comm_params(4, 52),
    )(persist, x, w_beta, taps, pad, gain, w_mixer, g)


def middle_kernel(
    count, full_ref, mixer_ref, x_ref, gain_ref, mid_ref, normed_ref,
    w_ref, staged, landed, low_buf, sends, recvs, local, gather_sends, gather_recvs,
):
    me = lax.axis_index("seq")
    rows, features = x_ref.shape
    mine = w_ref.shape[1]
    weight = pltpu.make_async_copy(mixer_ref.at[:, 3 * mine : 4 * mine], w_ref, local.at[2])
    weight.start()
    greet(others("seq", count))
    weight.wait()
    copies = []
    for step in list(range(1, count)) + [0]:
        peer = lax.rem(me + step, count)
        at = pl.ds(pl.multiple_of(peer * rows, rows), rows)
        staged[step] = mm(full_ref[at, :], w_ref[...])
        target = landed.at[span(mine, me, 1)]
        if step:
            copies.append(send(staged.at[step], target, sends, recvs, step, "seq", peer))
        else:
            own = pltpu.make_async_copy(staged.at[0], target, local.at[0])
            own.start()
            copies.append(own)
    wait_all(copies)
    for at in range(0, rows, 16):
        part = slice(at, at + 16)
        value = x_ref[part, :].astype(F32) + landed[part, :]
        mid_ref[part, :] = value
        scale = lax.rsqrt(jnp.mean(value * value, axis=1, keepdims=True) + EPSILON)
        low_buf[part, :] = (value * scale * gain_ref[0:1, :]).astype(BF)
    gather = Gather(count, low_buf, normed_ref, 0, gather_sends, gather_recvs, local, 0, 1)
    gather.start()
    for turn in range(gather.turns()):
        gather.forward(turn)
    gather.finish()


def middle(count, full, w_mixer, x, gain):
    rows, features = x.shape
    mine = w_mixer.shape[1] // 4
    return pl.pallas_call(
        functools.partial(middle_kernel, count),
        out_shape=(
            jax.ShapeDtypeStruct((rows, features), F32),
            jax.ShapeDtypeStruct((rows * count, features), BF),
        ),
        in_specs=[VMEM, ANY, VMEM, VMEM],
        out_specs=(VMEM, ANY),
        scratch_shapes=[
            pltpu.VMEM((features, mine), BF),
            pltpu.VMEM((count, rows, mine), F32),
            pltpu.VMEM((rows, features), F32),
            pltpu.VMEM((rows, features), BF),
            pltpu.SemaphoreType.DMA((count,)),
            pltpu.SemaphoreType.DMA((count,)),
            pltpu.SemaphoreType.DMA((3,)),
            pltpu.SemaphoreType.DMA((2 * count,)),
            pltpu.SemaphoreType.DMA((2 * count,)),
        ],
        compiler_params=comm_params(5),
    )(full, w_mixer, x, gain)


def norm_backward(value_ref, grad_ref, beside_ref, gain_ref, out_ref, gain_out, low_ref=None):
    rows, features = out_ref.shape
    gain_out[...] = jnp.zeros((8, features), F32)
    for at in range(0, rows, 8):
        part = slice(at, at + 8)
        value = value_ref[part, :].astype(F32)
        scale = lax.rsqrt(jnp.mean(value * value, axis=1, keepdims=True) + EPSILON)
        unit = value * scale
        grad = grad_ref[part, :]
        gain_out[...] += grad * unit
        scaled = grad * gain_ref[0:1, :]
        mean = jnp.mean(scaled * unit, axis=1, keepdims=True)
        result = beside_ref[part, :].astype(F32) + scale * (scaled - unit * mean)
        out_ref[part, :] = result
        if low_ref is not None:
            half = (at // 16) * 16
            if at % 16 == 8:
                low_ref[half : half + 16, :] = out_ref[half : half + 16, :].astype(BF)


def reduce_kernel(
    count, part_ref, mid_ref, g_ref, gain_ref, grad_ref, gain_out, full_ref,
    summed, low_buf, landing, outgoing, kept, sends, recvs, local, gather_sends, gather_recvs,
):
    greet(hypercube_peers(count))
    scatter = Scatter(count, part_ref, summed, landing, outgoing, kept, sends, recvs)
    scatter.start()
    for turn in range(scatter.bits):
        scatter.turn(turn)
    norm_backward(mid_ref, summed, g_ref, gain_ref, grad_ref, gain_out, low_buf)
    gather = Gather(count, low_buf, full_ref, 0, gather_sends, gather_recvs, local, 0, 0)
    gather.start()
    for turn in range(gather.turns()):
        gather.forward(turn)
    gather.finish()
    scatter.finish()


def reduce_middle(count, parts, mid, g, gain):
    rows, features = mid.shape
    return pl.pallas_call(
        functools.partial(reduce_kernel, count),
        out_shape=(
            jax.ShapeDtypeStruct((rows, features), F32),
            jax.ShapeDtypeStruct((8, features), F32),
            jax.ShapeDtypeStruct((rows * count, features), BF),
        ),
        in_specs=[VMEM] * 4,
        out_specs=(VMEM, VMEM, ANY),
        scratch_shapes=[pltpu.VMEM((rows, features), F32), pltpu.VMEM((rows, features), BF)]
        + scatter_scratch(count, rows, features)
        + [
            pltpu.SemaphoreType.DMA((1,)),
            pltpu.SemaphoreType.DMA((2 * count,)),
            pltpu.SemaphoreType.DMA((2 * count,)),
        ],
        compiler_params=comm_params(6),
    )(parts, mid, g, gain)


def back_kernel(
    count, heads, sizes, persist_ref, full_ref, rows_ref, mixed_ref, gain_ref, taps_ref, pre_ref, q_ref, k_ref, v_ref,
    brow_ref, sigma_ref, pad_ref, t_ref, wide_ref, s_ref, f_ref, a_ref, part_ref, done_ref,
    dpre_ref, taps_out, gain_out, added_ref, *refs,
):
    total, mine = mixed_ref.shape
    hd = mine // heads
    blocks = total // BLOCK
    beta_lanes = dpre_ref.shape[1] - 3 * mine
    targets, scratch = refs[: len(sizes)], refs[len(sizes) :]
    do_buf, y_buf, c_buf, g_buf, pre_buf, conv_buf = scratch[:6]
    landing, outgoing, kept, sends, recvs, pass_sends, pass_recvs, local = scratch[6:]
    greet(others("seq", count))
    scatter = Scatter(count, part_ref, added_ref, landing, outgoing, kept, sends, recvs)
    scatter.start()
    exchange = start_exchange(
        row_pieces([done_ref], targets, [sizes], count), count, pass_sends, pass_recvs, local
    )
    gain_out[...] = jnp.zeros((8, hd), F32)
    taps_out[...] = jnp.zeros((3 * CONV, 8, mine), F32)
    pre_buf[0:8, :] = jnp.zeros((8, 3 * mine), F32)
    conv_buf[total : total + 8, :] = jnp.zeros((8, 3 * mine), F32)
    chunk = 4 * BLOCK

    def heads_in(index, carry):
        rows = pl.ds(pl.multiple_of(index * chunk, chunk), chunk)
        pre_buf[pl.ds(pl.multiple_of(index * chunk + 8, 8), chunk), :] = pre_ref[rows, :].astype(F32)
        grad = mm(full_ref[rows, :], rows_ref[...], NT)
        for h in range(heads):
            lanes = slice(h * hd, (h + 1) * hd)
            mixed, don = mixed_ref[rows, lanes], grad[:, lanes]
            scale = lax.rsqrt(jnp.mean(mixed * mixed, axis=1, keepdims=True) + EPSILON)
            unit = mixed * scale
            gain_out[...] += jnp.sum((don * unit).reshape(chunk // 8, 8, hd), axis=0)
            scaled = don * gain_ref[0:1, :]
            mean = jnp.mean(scaled * unit, axis=1, keepdims=True)
            do_buf[rows, lanes] = scale * (scaled - unit * mean)
        return carry

    lax.fori_loop(0, total // chunk, heads_in, 0)
    row, col = tile_masks(BLOCK)

    def first(step, carry):
        for part in range(2):
            index = 2 * step + part
            rows = pl.ds(pl.multiple_of(index * BLOCK, BLOCK), BLOCK)
            for h in range(heads):
                lanes = slice(h * hd, (h + 1) * hd)
                q, k, do = q_ref[rows, lanes], k_ref[rows, lanes], do_buf[rows, lanes]
                p = jnp.where(row >= col, mm(q, k, NT), 0.0)
                y = mm_ww(p, do, TN)
                y_buf[rows, lanes] = y
                c_buf[h, index] = mm_lw(q, do, TN) - mm_ww(wide_ref[rows, lanes], y, TN)
        return carry

    lax.fori_loop(0, blocks // 2, first, 0)
    scatter.turn(0)

    def chain(step, grads):
        index = blocks - 1 - step
        keep = persist_ref[index]
        new = []
        for h in range(heads):
            g = grads[h]
            g_buf[h, index] = g
            new.append((mm_ww(a_ref[h, index], g, TN) + c_buf[h, index]) * keep)
        return tuple(new)

    lax.fori_loop(0, blocks, chain, tuple(jnp.zeros((hd, hd), F32) for _ in range(heads)))
    scatter.turn(1)

    def last(step, carry):
        for part in range(2):
            index = 2 * step + part
            keep = persist_ref[index]
            rows = pl.ds(pl.multiple_of(index * BLOCK, BLOCK), BLOCK)
            half = slice(part * BLOCK, (part + 1) * BLOCK)
            lane = lax.broadcasted_iota(jnp.int32, (BLOCK, beta_lanes), 1)
            dlogits = jnp.zeros((BLOCK, beta_lanes), F32)
            for h in range(heads):
                lanes = slice(h * hd, (h + 1) * hd)
                q, k, v = q_ref[rows, lanes], k_ref[rows, lanes], v_ref[rows, lanes]
                do, s, f, g = do_buf[rows, lanes], s_ref[h, index], f_ref[rows, lanes], g_buf[h, index]
                b = brow_ref[step, h : h + 1, half]
                bcol = jnp.sum(jnp.where(row == col, b, 0.0), axis=1, keepdims=True)
                t = t_ref[h, rows, half]
                df = y_buf[rows, lanes] + mm_lw(k, g)
                dr = mm_ww(t, df, TN)
                dp = jnp.where(row >= col, mm_ww(do, f, NT), 0.0)
                dl = jnp.where(row > col, -mm_ww(dr, f, NT), 0.0)
                dq = mm_ww(do, s, NT) + mm_wl(dp, k)
                dkb = mm_wl(dl, k) - mm_ww(dr, s, NT)
                dk = mm_wl(dp, q, TN) + mm_ww(f, g, NT) + mm_wl(dl * bcol, k, TN) + bcol * dkb
                dbeta = jnp.sum(dr * v.astype(F32) + dkb * k.astype(F32), axis=1, keepdims=True)
                sigma = sigma_ref[step, h : h + 1, half]
                slope = pad_ref[pl.ds(step, 1), half] * sigma * (1.0 - sigma)
                slope = jnp.sum(jnp.where(row == col, slope, 0.0), axis=1, keepdims=True)
                dlogits = jnp.where(lane == h, dbeta * slope, dlogits)
                for member, grad in enumerate((dq, dk, bcol * dr)):
                    there = slice(member * mine + h * hd, member * mine + (h + 1) * hd)
                    window = pre_buf[pl.ds(pl.multiple_of(index * BLOCK, 8), BLOCK + 8), there]
                    summed, shifts = shifted_sum(window, taps_ref, member, lanes, keep)
                    sigma = jax.nn.sigmoid(summed)
                    if member < 2:
                        value = summed * sigma
                        inverse = lax.rsqrt(jnp.sum(value * value, axis=1, keepdims=True) + EPSILON)
                        unit = value * inverse
                        along = jnp.sum(grad * unit, axis=1, keepdims=True)
                        grad = (grad - unit * along) * inverse
                    if member == 0:
                        grad = grad * hd ** (-0.5)
                    grad = grad * (sigma * (1.0 + summed * (1.0 - sigma)))
                    conv_buf[rows, there] = grad
                    for lagged in range(CONV):
                        taps_out[member * CONV + lagged, :, lanes] += jnp.sum(
                            (grad * shifts[lagged]).reshape(BLOCK // 8, 8, hd), axis=0
                        )
            dpre_ref[rows, 3 * mine :] = dlogits.astype(BF)
        return carry

    lax.fori_loop(0, blocks // 2, last, 0)
    scatter.turn(2)
    for turn in range(3, scatter.bits):
        scatter.turn(turn)

    def spread(index, carry):
        rows = pl.ds(pl.multiple_of(index * BLOCK, BLOCK), BLOCK)
        keep = persist_ref[jnp.minimum(index + 1, blocks - 1)]
        block_row = lax.broadcasted_iota(jnp.int32, (BLOCK, 1), 0)
        for member in range(3):
            there = slice(member * mine, (member + 1) * mine)
            window = conv_buf[pl.ds(pl.multiple_of(index * BLOCK, 8), BLOCK + 8), there]
            summed = window[:BLOCK] * taps_ref[member * CONV : member * CONV + 1, :]
            for lagged in range(1, CONV):
                at = member * CONV + lagged
                moved = pltpu.roll(window, BLOCK + 8 - lagged, 0)[:BLOCK]
                moved = moved * jnp.where(block_row < BLOCK - lagged, 1.0, keep)
                summed = summed + moved * taps_ref[at : at + 1, :]
            dpre_ref[rows, there] = summed.astype(BF)
        return carry

    lax.fori_loop(0, blocks, spread, 0)
    scatter.finish()
    wait_all(exchange)


def back(
    count, heads, sizes, persist, full, w_rows, mixed, gain, taps, pre, q, k, v, strength, saved, parts, done
):
    total, mine = mixed.shape
    hd = mine // heads
    blocks = total // BLOCK
    rows, features = total // count, full.shape[1]
    return pl.pallas_call(
        functools.partial(back_kernel, count, heads, sizes),
        out_shape=(
            jax.ShapeDtypeStruct((total, 3 * mine + 128), BF),
            jax.ShapeDtypeStruct((3 * CONV, 8, mine), F32),
            jax.ShapeDtypeStruct((8, hd), F32),
            jax.ShapeDtypeStruct((rows, features), F32),
        )
        + row_shapes([done], [sizes], count),
        in_specs=[pl.BlockSpec(memory_space=pltpu.SMEM)] + [VMEM] * 18 + [ANY],
        out_specs=(VMEM,) * 4 + (ANY,) * len(sizes),
        scratch_shapes=[
            pltpu.VMEM((total, mine), F32),
            pltpu.VMEM((total, mine), F32),
            pltpu.VMEM((heads, blocks, hd, hd), F32),
            pltpu.VMEM((heads, blocks, hd, hd), F32),
            pltpu.VMEM((total + 8, 3 * mine), F32),
            pltpu.VMEM((total + 8, 3 * mine), F32),
        ]
        + scatter_scratch(count, rows, features)
        + [
            pltpu.SemaphoreType.DMA((len(sizes) * count,)),
            pltpu.SemaphoreType.DMA((len(sizes) * count,)),
            pltpu.SemaphoreType.DMA((len(sizes),)),
        ],
        compiler_params=comm_params(7, 56),
    )(persist, full, w_rows, mixed, gain, taps, pre, q, k, v, *strength, *saved, parts, done)


def end_kernel(count, sizes, part_ref, x_ref, beside_ref, gain_ref, *refs):
    sources = refs[: len(sizes)]
    targets = refs[len(sizes) + 2 : len(sizes) + 2 + sum(len(w) for w in sizes)]
    grad_ref, gain_out = refs[len(sizes) : len(sizes) + 2]
    scratch = refs[len(sizes) + 2 + len(targets) :]
    summed, landing, outgoing, kept, sends, recvs, pass_sends, pass_recvs, local = scratch
    greet(others("seq", count))
    scatter = Scatter(count, part_ref, summed, landing, outgoing, kept, sends, recvs)
    scatter.start()
    exchange = start_exchange(row_pieces(sources, targets, sizes, count), count, pass_sends, pass_recvs, local)
    for turn in range(scatter.bits):
        scatter.turn(turn)
    norm_backward(x_ref, summed, beside_ref, gain_ref, grad_ref, gain_out)
    scatter.finish()
    wait_all(exchange)


def row_pieces(sources, targets, sizes, count):
    pieces = []
    for source, widths in zip(sources, sizes):
        rows, at = source.shape[0] // count, 0
        for size in widths:
            pieces.append(
                (
                    source,
                    lambda i, rows=rows, at=at, size=size: (
                        pl.ds(pl.multiple_of(i * rows, rows), rows),
                        slice(at, at + size),
                    ),
                    targets[len(pieces)],
                    lambda i, size=size: span(size, i, 1),
                )
            )
            at += size
    return pieces


def row_shapes(sources, sizes, count):
    return tuple(
        jax.ShapeDtypeStruct((source.shape[0] // count, count * size), BF)
        for source, widths in zip(sources, sizes)
        for size in widths
    )


def end(count, parts, x, beside, gain, sources, sizes):
    rows, features = x.shape
    shapes = row_shapes(sources, sizes, count)
    return pl.pallas_call(
        functools.partial(end_kernel, count, sizes),
        out_shape=(
            jax.ShapeDtypeStruct((rows, features), F32),
            jax.ShapeDtypeStruct((8, features), F32),
        )
        + shapes,
        in_specs=[VMEM] * 4 + [ANY] * len(sources),
        out_specs=(VMEM, VMEM) + (ANY,) * len(shapes),
        scratch_shapes=[pltpu.VMEM((rows, features), F32)]
        + scatter_scratch(count, rows, features)
        + [
            pltpu.SemaphoreType.DMA((len(shapes) * count,)),
            pltpu.SemaphoreType.DMA((len(shapes) * count,)),
            pltpu.SemaphoreType.DMA((len(shapes),)),
        ],
        compiler_params=comm_params(8),
    )(parts, x, beside, gain, *sources)


def mixer_grads_kernel(x_ref, grad_ref, on_ref, out_ref, low_ref, beta_ref):
    wide = 3 * out_ref.shape[1]
    front = mm(x_ref[...], grad_ref[...], TN)
    low_ref[:, :wide] = front[:, :wide].astype(BF)
    beta_ref[...] = front[:, wide:]
    low_ref[:, wide:] = mm(on_ref[...], out_ref[...], TN).astype(BF)


def mixer_gradients(x, grad, on, out):
    total, features = x.shape
    beta = grad.shape[1] - 3 * out.shape[1]
    wide = grad.shape[1] - beta + out.shape[1]
    step = features // 4
    return pl.pallas_call(
        mixer_grads_kernel,
        grid=(features // step,),
        out_shape=(
            jax.ShapeDtypeStruct((features, wide), BF),
            jax.ShapeDtypeStruct((features, beta), F32),
        ),
        in_specs=[
            pl.BlockSpec((total, step), lambda i: (0, i)),
            pl.BlockSpec(grad.shape, lambda i: (0, 0)),
            pl.BlockSpec((total, step), lambda i: (0, i)),
            pl.BlockSpec(out.shape, lambda i: (0, 0)),
        ],
        out_specs=(
            pl.BlockSpec((step, wide), lambda i: (i, 0)),
            pl.BlockSpec((step, beta), lambda i: (i, 0)),
        ),
        compiler_params=pltpu.CompilerParams(vmem_limit_bytes=40 * 2**20),
        cost_estimate=pl.CostEstimate(
            flops=2 * total * features * (wide + beta),
            bytes_accessed=4 * total * features + 4 * features * wide,
            transcendentals=0,
        ),
    )(x, grad, on, out)


def rest_and_main(hidden_width, count):
    main = hidden_width // (128 * count) * 128
    return hidden_width // count - main, main


def local_heads(
    tokens,
    doc_starts,
    pad_mask,
    norm1_gain,
    query_weight,
    key_weight,
    value_weight,
    conv_weight,
    beta_weight,
    out_norm_gain,
    out_weight,
    norm2_gain,
    gate_weight,
    up_weight,
    down_weight,
    cotangent,
):
    row_count, features = tokens.shape
    width = lax.axis_size("seq")
    place = lax.axis_index("seq")
    head_dim = out_norm_gain.shape[0]
    heads = beta_weight.shape[1] // width
    mine = heads * head_dim
    total = row_count * width
    depth = lax.axis_size("dp")
    level = lax.axis_index("dp")
    owned = norm1_gain.shape[0]
    rest, main = rest_and_main(gate_weight.shape[1], width)
    mixer_part = opening(width, [query_weight, key_weight, value_weight, out_weight])
    w_mixer = lax.all_gather(
        mixer_part.reshape(width * owned, 4 * mine), "dp", axis=0, tiled=True
    )
    w_beta = lax.dynamic_slice_in_dim(beta_weight, place * heads, heads, axis=1)

    def ends(array):
        return array[:, main * width :].reshape(owned, width, rest)

    down_turned = down_weight.T
    pair_rest = jnp.concatenate([ends(gate_weight), ends(up_weight)], axis=2)
    down_rest = jnp.concatenate([ends(down_turned), jnp.zeros((owned, width, rest), BF)], axis=2)
    small_all, pair_part, down_part, normed_full = second(
        width,
        depth,
        [norm1_gain[None], norm2_gain[None], conv_weight, pad_mask, doc_starts],
        tokens,
        gate_weight,
        up_weight,
        down_turned,
        pair_rest.reshape(owned, -1),
        down_rest.reshape(owned, -1),
    )
    wide = small_all[:, : 3 * CONV + 2, :owned].transpose(1, 0, 2).reshape(3 * CONV + 2, features)
    gain_first, gain_second = wide[3 * CONV], wide[3 * CONV + 1]
    taps = lax.dynamic_slice_in_dim(wide[: 3 * CONV], place * mine, mine, axis=1)
    marks = lax.dynamic_slice_in_dim(small_all[:, 3 * CONV + 2 :], level * width, width, axis=0)
    pad_rows = marks[:, 0, :row_count].reshape(-1, 2 * BLOCK)
    starts = marks[:, 1, : doc_starts.shape[1]].reshape(-1).astype(jnp.int32)
    begins = BLOCK * jnp.arange(total // BLOCK, dtype=jnp.int32)
    persist = (starts != begins).astype(F32)
    w_down = lax.all_gather(down_part.reshape(width * owned, -1), "dp", axis=0, tiled=True)
    w_pair = lax.all_gather(pair_part.reshape(width * owned, -1), "dp", axis=0, tiled=True)
    beta_wide = jnp.pad(w_beta, ((0, 0), (0, 128 - heads)))
    w_front = jnp.concatenate([w_mixer[:, : 3 * mine], beta_wide], axis=1)
    head_gain = out_norm_gain.astype(F32)[None]
    (
        projected, queries, key_rows, values, strength, sigma_vals, mixed,
        *saved, out_full, w_out_rows, cotangent_full,
    ) = front(
        width, heads, persist, normed_full, w_mixer, beta_wide, taps, pad_rows, head_gain,
        cotangent,
    )
    residual_mid, normed_two_full = middle(width, out_full, w_mixer, tokens, gain_second[None])
    pair = product(normed_two_full, w_pair)
    tail = pair[:, 2 * main :]
    gate_out = jnp.concatenate([pair[:, :main], tail], axis=1)
    up_out = jnp.concatenate([pair[:, main : 2 * main], jnp.roll(tail, rest, axis=1)], axis=1)
    gate_sigma = jax.nn.sigmoid(gate_out)
    gate_silu = gate_out * gate_sigma
    hidden = (gate_silu * up_out).astype(BF)
    down_grads = product_left(cotangent_full, hidden).astype(BF)
    w_down, _ = lax.optimization_barrier((w_down, down_grads))
    down_sums = lax.psum_scatter(down_grads, "dp", scatter_dimension=0, tiled=True)
    hidden_grad = product(cotangent_full, w_down)
    gate_grad_low = (
        hidden_grad * up_out * gate_sigma * (1.0 + gate_out * (1.0 - gate_sigma))
    ).astype(BF)
    up_grad_low = (hidden_grad * gate_silu).astype(BF)
    pair_grad_low = jnp.concatenate(
        [
            gate_grad_low[:, :main],
            up_grad_low[:, :main],
            gate_grad_low[:, main : main + rest],
            up_grad_low[:, main : main + rest],
        ],
        axis=1,
    )
    two_parts = product_right(pair_grad_low, w_pair).astype(BF)
    pair_grads = product_left(normed_two_full, pair_grad_low).astype(BF)
    pair_sums = lax.psum_scatter(pair_grads, "dp", scatter_dimension=0, tiled=True)
    added_parts = product_right(hidden, w_down).astype(BF)
    residual_mid_grad, gain_second_rows, mid_full = reduce_middle(
        width, two_parts, residual_mid, cotangent, gain_second[None]
    )
    (
        projected_grad, conv_rows_grad, out_gain_rows, added,
        down_main, down_ends,
    ) = back(
        width, heads, (main, 2 * rest), persist, mid_full, w_out_rows, mixed, head_gain, taps, projected,
        queries, key_rows, values, (strength, sigma_vals, pad_rows), saved, added_parts, down_sums,
    )
    output = (residual_mid + added).astype(BF)
    gain_second_grad = jnp.sum(gain_second_rows, axis=0)
    out_gain_grad = jnp.sum(out_gain_rows, axis=0)
    conv_grad = jnp.sum(conv_rows_grad, axis=1)
    mid_mine = lax.dynamic_slice_in_dim(mid_full, place * mine, mine, axis=1)
    mixer_grads, beta_grads = mixer_gradients(normed_full, projected_grad, out_full, mid_mine)
    beta_grad = beta_grads[:, :heads].T
    mixer_grads, pair_sums = lax.optimization_barrier((mixer_grads, pair_sums))
    mixer_sums = lax.psum_scatter(mixer_grads, "dp", scatter_dimension=0, tiled=True)
    normed_parts = product_right(projected_grad, w_front).astype(BF)
    (
        tokens_grad, gain_first_rows,
        gate_main, up_main, pair_ends,
    ) = end(
        width, normed_parts, tokens, residual_mid_grad, gain_first[None],
        [pair_sums], [(main, main, 2 * rest)],
    )
    gain_first_grad = jnp.sum(gain_first_rows, axis=0)

    def joined(front, back, at):
        back = back.reshape(owned, width, 2, rest)[:, :, at].reshape(owned, width * rest)
        return jnp.concatenate([front, back], axis=1).astype(F32)

    shard_gate, shard_up, shard_down = (
        joined(gate_main, pair_ends, 0),
        joined(up_main, pair_ends, 1),
        joined(down_main, down_ends, 0).T,
    )
    gain_row = jnp.pad(out_gain_grad[None], ((0, 0), (0, features - head_dim)))
    plane = jnp.concatenate([gain_first_grad[None], gain_second_grad[None], gain_row], axis=0)
    conv_rows = -(-3 * CONV * mine // features)
    conv_flat = jnp.pad(conv_grad.reshape(-1), (0, conv_rows * features - 3 * CONV * mine))
    levels = jnp.concatenate([beta_grad, conv_flat.reshape(conv_rows, features)], axis=0)
    plane, shard_gate, shard_up, shard_down = lax.optimization_barrier(
        (plane.reshape(8, -1), shard_gate, shard_up, shard_down)
    )
    sums, each = small_sums(plane, levels.reshape(8, -1), width, depth)
    sums = sums.reshape(3, features)
    each = each.reshape(width, heads + conv_rows, features)
    beta_total = each[:, :heads].reshape(width * heads, features).T
    conv_all = each[:, heads:].reshape(width, -1)[:, : 3 * CONV * mine]
    conv_all = conv_all.reshape(width, 3 * CONV, mine).transpose(1, 0, 2).reshape(-1, features)
    wide_sums = jnp.concatenate([sums[:2], conv_all], axis=0)
    own = level * width + place
    wide_own = lax.dynamic_slice_in_dim(wide_sums, own * owned, owned, axis=1)

    shard_q, shard_k, shard_v, shard_o = (
        a.astype(F32) for a in closing([mixer_sums], width, [(mine,) * 4], 13)
    )

    return (
        output,
        tokens_grad,
        wide_own[0],
        shard_q,
        shard_k,
        shard_v,
        wide_own[2:].reshape(3, CONV, owned),
        beta_total,
        sums[2, :head_dim],
        shard_o,
        wide_own[1],
        shard_gate,
        shard_up,
        shard_down,
    )


def solution(mesh):
    in_specs = (
        P(("dp", "seq"), None),
        P("dp", "seq"),
        P("dp", "seq"),
        P(("dp", "seq")),
        P(("dp", "seq"), None),
        P(("dp", "seq"), None),
        P(("dp", "seq"), None),
        P(None, None, ("dp", "seq")),
        P(),
        P(),
        P(("dp", "seq"), None),
        P(("dp", "seq")),
        P(("dp", "seq"), None),
        P(("dp", "seq"), None),
        P(None, ("dp", "seq")),
        P(("dp", "seq"), None),
    )
    out_specs = (
        P(("dp", "seq"), None),
        P(("dp", "seq"), None),
        P(("dp", "seq")),
        P(("dp", "seq"), None),
        P(("dp", "seq"), None),
        P(("dp", "seq"), None),
        P(None, None, ("dp", "seq")),
        P(),
        P(),
        P(("dp", "seq"), None),
        P(("dp", "seq")),
        P(("dp", "seq"), None),
        P(("dp", "seq"), None),
        P(None, ("dp", "seq")),
    )

    def layer(*arrays):
        head_count, hidden_width = arrays[8].shape[1], arrays[12].shape[1]
        width = mesh.shape["seq"]
        rest, main = rest_and_main(hidden_width, width)
        by_heads = head_count % width == 0 and rest == 64 and main > 0
        by_heads = by_heads and width >= 4 and width & (width - 1) == 0
        by_heads = by_heads and 128 % (arrays[3].shape[0] // mesh.size) == 0
        local = local_heads if by_heads else local_sequence
        return jax.shard_map(
            local, mesh=mesh, in_specs=in_specs, out_specs=out_specs, check_vma=False
        )(*arrays)

    return layer
```

```python
import functools

import jax
import jax.numpy as jnp
from jax import lax
from jax.experimental import pallas as pl
from jax.experimental.pallas import tpu as pltpu
from jax.sharding import PartitionSpec as P

CONV = 4
BLOCK = 64


EPSILON = 1e-06
PRECISE = lax.Precision.HIGHEST


def from_behind(array, axis, by):
    length = lax.axis_size(axis)
    pairs = [(i, i + by) for i in range(length) if 0 <= i + by < length]
    return lax.ppermute(array, axis, pairs)


def product(left, right):
    return jnp.dot(left, right, preferred_element_type=jnp.float32)


def product_left(left, right):
    return lax.dot_general(
        left, right, (((0,), (0,)), ((), ())), preferred_element_type=jnp.float32
    )


def product_right(left, right):
    return lax.dot_general(
        left, right, (((1,), (1,)), ((), ())), preferred_element_type=jnp.float32
    )


def rounded(value):
    return lax.optimization_barrier(value.astype(jnp.bfloat16)).astype(jnp.float32)


def rms_norm(value, gain):
    return value * lax.rsqrt(jnp.mean(value * value, axis=-1, keepdims=True) + EPSILON) * gain


def block_parts(queries, key_rows, values, strength):
    keyed = key_rows * strength[..., None]
    block_len = key_rows.shape[1]
    lower_part = jnp.tril(jnp.einsum("hcd,hed->hce", keyed, key_rows, precision=PRECISE), -1)
    system = lower_part + jnp.eye(block_len, dtype=jnp.float32)
    weights = jax.scipy.linalg.solve_triangular(system, keyed, lower=True, unit_diagonal=True)
    updates = jax.scipy.linalg.solve_triangular(
        system, values * strength[..., None], lower=True, unit_diagonal=True
    )
    scores = jnp.tril(jnp.einsum("hcd,hed->hce", queries, key_rows, precision=PRECISE))
    return (weights, updates, scores)


def delta_step(state_now, inputs):
    queries, key_rows, values, strength, persist = inputs
    state_now = state_now * persist
    weights, updates, scores = block_parts(queries, key_rows, values, strength)
    corrected = updates - jnp.einsum("hcd,hde->hce", weights, state_now, precision=PRECISE)
    outputs = jnp.einsum("hcd,hde->hce", queries, state_now, precision=PRECISE) + jnp.einsum(
        "hce,hef->hcf", scores, corrected, precision=PRECISE
    )
    state_now = state_now + jnp.einsum("hcd,hce->hde", key_rows, corrected, precision=PRECISE)
    return (state_now, outputs)


def track_step(holding, inputs):
    state_now, transit = holding
    queries, key_rows, values, strength, persist = inputs
    state_now = state_now * persist
    transit = transit * persist
    weights, updates, scores = block_parts(queries, key_rows, values, strength)
    corrected = updates - jnp.einsum("hcd,hde->hce", weights, state_now, precision=PRECISE)
    outputs = jnp.einsum("hcd,hde->hce", queries, state_now, precision=PRECISE) + jnp.einsum(
        "hce,hef->hcf", scores, corrected, precision=PRECISE
    )
    leading = queries - jnp.einsum("hce,hed->hcd", scores, weights, precision=PRECISE)
    state_now = state_now + jnp.einsum("hcd,hce->hde", key_rows, corrected, precision=PRECISE)
    eraser = jnp.eye(key_rows.shape[2], dtype=jnp.float32) - jnp.einsum(
        "hcd,hce->hde", key_rows, weights, precision=PRECISE
    )
    return (
        (state_now, jnp.einsum("hde,hef->hdf", eraser, transit, precision=PRECISE)),
        (outputs, leading, transit),
    )


def advance(linear, offset_part, incoming):
    return jnp.einsum("hde,hef->hdf", linear, incoming, precision=PRECISE) + offset_part


def into_blocks(array):
    row_count, head_count, head_dim = array.shape
    return array.reshape(row_count // BLOCK, BLOCK, head_count, head_dim).transpose(0, 2, 1, 3)


def from_blocks(array):
    block_count, head_count, block_len, head_dim = array.shape
    return array.transpose(0, 2, 1, 3).reshape(block_count * block_len, head_count, head_dim)


def local_sequence(
    tokens,
    doc_starts,
    pad_mask,
    norm1_gain,
    query_weight,
    key_weight,
    value_weight,
    conv_weight,
    beta_weight,
    out_norm_gain,
    out_weight,
    norm2_gain,
    gate_weight,
    up_weight,
    down_weight,
    cotangent,
):
    row_count, features = tokens.shape
    head_count = beta_weight.shape[1]
    head_dim = out_norm_gain.shape[0]
    block_count = row_count // BLOCK
    w_query, w_key, w_value, w_out, conv_full, gain_first = (
        lax.all_gather(query_weight, ("dp", "seq"), axis=0, tiled=True),
        lax.all_gather(key_weight, ("dp", "seq"), axis=0, tiled=True),
        lax.all_gather(value_weight, ("dp", "seq"), axis=0, tiled=True),
        lax.all_gather(out_weight, ("dp", "seq"), axis=0, tiled=True),
        lax.all_gather(conv_weight, ("dp", "seq"), axis=2, tiled=True),
        lax.all_gather(norm1_gain, ("dp", "seq"), axis=0, tiled=True),
    )
    w_gate, w_up, w_down, gain_second = (
        lax.all_gather(gate_weight, ("dp", "seq"), axis=0, tiled=True),
        lax.all_gather(up_weight, ("dp", "seq"), axis=0, tiled=True),
        lax.all_gather(down_weight, ("dp", "seq"), axis=1, tiled=True),
        lax.all_gather(norm2_gain, ("dp", "seq"), axis=0, tiled=True),
    )
    seq_place = lax.axis_index("seq")
    positions = seq_place * row_count + jnp.arange(row_count, dtype=jnp.int32)
    starts = doc_starts[0]
    offsets = jnp.repeat(starts, BLOCK)
    persist = (
        starts != seq_place * row_count + BLOCK * jnp.arange(block_count, dtype=jnp.int32)
    ).astype(jnp.float32)
    pad_rows = pad_mask[0].astype(jnp.float32)[:, None]

    def mixer_in(extended, conv_taps):
        results = []
        for member in range(3):
            columns = extended[:, member * features : (member + 1) * features]
            summed = jnp.zeros((row_count, features), jnp.float32)
            for lagged in range(CONV):
                inside = (positions - lagged >= offsets).astype(jnp.float32)[:, None]
                summed = (
                    summed
                    + conv_taps[member, lagged]
                    * inside
                    * columns[CONV - 1 - lagged : CONV - 1 - lagged + row_count]
                )
            activated = jax.nn.silu(summed).reshape(row_count, head_count, head_dim)
            if member < 2:
                activated = activated * lax.rsqrt(
                    jnp.sum(activated * activated, axis=-1, keepdims=True) + EPSILON
                )
            if member == 0:
                activated = activated * head_dim ** (-0.5)
            results.append(activated)
        return tuple(results)

    residual_in = tokens.astype(jnp.float32)
    normed, norm_first_pull = jax.vjp(rms_norm, residual_in, gain_first.astype(jnp.float32))
    normed_low = normed.astype(jnp.bfloat16)
    projected = jnp.concatenate(
        [product(normed_low, w_query), product(normed_low, w_key), product(normed_low, w_value)],
        axis=1,
    ).astype(jnp.bfloat16)
    logits = product(normed_low, beta_weight)
    sigma_vals = jax.nn.sigmoid(logits)
    strength = sigma_vals * pad_rows
    rims = from_behind(projected[row_count - CONV + 1 :], "seq", 1)
    extended_in = jnp.concatenate([rims, projected], axis=0).astype(jnp.float32)
    (queries, key_rows, values), mixer_pull = jax.vjp(
        mixer_in, extended_in, conv_full.astype(jnp.float32)
    )
    query_blocks = into_blocks(rounded(queries))
    key_blocks = into_blocks(rounded(key_rows))
    value_blocks = into_blocks(rounded(values))
    strength_blocks = strength.reshape(block_count, BLOCK, head_count).transpose(0, 2, 1)
    zero_state = jnp.zeros((head_count, head_dim, head_dim), jnp.float32)
    identity = jnp.broadcast_to(
        jnp.eye(head_dim, dtype=jnp.float32), (head_count, head_dim, head_dim)
    )
    block_inputs = (query_blocks, key_blocks, value_blocks, strength_blocks, persist)
    (final_state, final_transit), (local_out, leading, transit) = lax.scan(
        track_step, (zero_state, identity), block_inputs
    )

    def forward_turn(turn_index, incoming):
        return from_behind(advance(final_transit, final_state, incoming), "seq", 1)

    start_state = lax.fori_loop(0, lax.axis_size("seq") - 1, forward_turn, zero_state)
    carried = jnp.einsum("nhde,hef->nhdf", transit, start_state, precision=PRECISE)
    mixed = from_blocks(
        local_out + jnp.einsum("nhcd,nhdf->nhcf", leading, carried, precision=PRECISE)
    )
    out_normed, out_norm_pull = jax.vjp(rms_norm, mixed, out_norm_gain.astype(jnp.float32))
    out_low = out_normed.reshape(row_count, features).astype(jnp.bfloat16)
    residual_mid = residual_in + product(out_low, w_out)
    normed_two, norm_second_pull = jax.vjp(rms_norm, residual_mid, gain_second.astype(jnp.float32))
    normed_two_low = normed_two.astype(jnp.bfloat16)
    gate_out = product(normed_two_low, w_gate)
    up_out = product(normed_two_low, w_up)
    hidden = (jax.nn.silu(gate_out) * up_out).astype(jnp.bfloat16)
    output = (residual_mid + product(hidden, w_down)).astype(jnp.bfloat16)
    grad_out = cotangent.astype(jnp.float32)
    down_grad = product_left(hidden, cotangent)
    hidden_grad = product_right(cotangent, w_down)
    gate_sigma = jax.nn.sigmoid(gate_out)
    gate_grad_low = (
        hidden_grad * up_out * gate_sigma * (1.0 + gate_out * (1.0 - gate_sigma))
    ).astype(jnp.bfloat16)
    up_grad_low = (hidden_grad * jax.nn.silu(gate_out)).astype(jnp.bfloat16)
    gate_grad = product_left(normed_two_low, gate_grad_low)
    up_grad = product_left(normed_two_low, up_grad_low)
    normed_two_grad = product_right(gate_grad_low, w_gate) + product_right(up_grad_low, w_up)
    mid_from_norm, gain_second_grad = norm_second_pull(normed_two_grad)
    residual_mid_grad = grad_out + mid_from_norm
    mid_low = residual_mid_grad.astype(jnp.bfloat16)
    out_grad = product_left(out_low, mid_low)
    out_normed_grad = product_right(mid_low, w_out).reshape(row_count, head_count, head_dim)
    mixed_grad, out_gain_grad = out_norm_pull(out_normed_grad)
    mixed_blocks = into_blocks(mixed_grad)
    pulled = jnp.einsum("nhcd,nhcf->nhdf", leading, mixed_blocks, precision=PRECISE)
    local_back = jnp.einsum("nhed,nhef->hdf", transit, pulled, precision=PRECISE)
    transit_turned = jnp.swapaxes(final_transit, 1, 2)

    def backward_turn(turn_index, incoming):
        return from_behind(advance(transit_turned, local_back, incoming), "seq", -1)

    end_grad = lax.fori_loop(0, lax.axis_size("seq") - 1, backward_turn, zero_state)

    def delta_local(query_in, key_in, value_in, strength_in):
        ending, outputs = lax.scan(
            jax.checkpoint(delta_step),
            start_state,
            (query_in, key_in, value_in, strength_in, persist),
        )
        return (outputs, ending)

    unused_out, delta_pull = jax.vjp(
        delta_local, query_blocks, key_blocks, value_blocks, strength_blocks
    )
    query_grad_blocks, key_grad_blocks, value_grad_blocks, strength_grad_blocks = delta_pull(
        (mixed_blocks, end_grad)
    )
    extended_grad, conv_grad = mixer_pull(
        (
            from_blocks(query_grad_blocks),
            from_blocks(key_grad_blocks),
            from_blocks(value_grad_blocks),
        )
    )
    rim_grad = from_behind(extended_grad[: CONV - 1], "seq", -1)
    projected_grad = jnp.concatenate(
        [extended_grad[CONV - 1 : row_count], extended_grad[row_count:] + rim_grad], axis=0
    ).astype(jnp.bfloat16)
    strength_grad = strength_grad_blocks.transpose(0, 2, 1).reshape(row_count, head_count)
    logits_grad = (strength_grad * pad_rows * sigma_vals * (1.0 - sigma_vals)).astype(jnp.bfloat16)
    part_query = projected_grad[:, :features]
    part_key = projected_grad[:, features : 2 * features]
    part_value = projected_grad[:, 2 * features :]
    query_grad = product_left(normed_low, part_query)
    key_grad = product_left(normed_low, part_key)
    value_grad = product_left(normed_low, part_value)
    beta_grad = product_left(normed_low, logits_grad)
    normed_grad = (
        product_right(part_query, w_query)
        + product_right(part_key, w_key)
        + product_right(part_value, w_value)
        + product_right(logits_grad, beta_weight)
    )
    input_from_norm, gain_first_grad = norm_first_pull(normed_grad)
    tokens_grad = residual_mid_grad + input_from_norm
    (
        shard_q,
        shard_k,
        shard_v,
        shard_o,
        shard_conv,
        shard_gain_one,
        shard_gate,
        shard_up,
        shard_down,
        shard_gain_two,
    ) = (
        lax.psum_scatter(query_grad, ("dp", "seq"), scatter_dimension=0, tiled=True),
        lax.psum_scatter(key_grad, ("dp", "seq"), scatter_dimension=0, tiled=True),
        lax.psum_scatter(value_grad, ("dp", "seq"), scatter_dimension=0, tiled=True),
        lax.psum_scatter(out_grad, ("dp", "seq"), scatter_dimension=0, tiled=True),
        lax.psum_scatter(conv_grad, ("dp", "seq"), scatter_dimension=2, tiled=True),
        lax.psum_scatter(gain_first_grad, ("dp", "seq"), scatter_dimension=0, tiled=True),
        lax.psum_scatter(gate_grad, ("dp", "seq"), scatter_dimension=0, tiled=True),
        lax.psum_scatter(up_grad, ("dp", "seq"), scatter_dimension=0, tiled=True),
        lax.psum_scatter(down_grad, ("dp", "seq"), scatter_dimension=1, tiled=True),
        lax.psum_scatter(gain_second_grad, ("dp", "seq"), scatter_dimension=0, tiled=True),
    )
    beta_total, out_gain_total = lax.psum((beta_grad, out_gain_grad), ("dp", "seq"))
    return (
        output,
        tokens_grad,
        shard_gain_one,
        shard_q,
        shard_k,
        shard_v,
        shard_conv,
        beta_total,
        out_gain_total,
        shard_o,
        shard_gain_two,
        shard_gate,
        shard_up,
        shard_down,
    )


F32 = jnp.float32
BF = jnp.bfloat16
NN=(((1,),(0,)),((),())); NT=(((1,),(1,)),((),())); TN=(((0,),(0,)),((),()))

def mm(a,b,dims=NN):
    return lax.dot_general(a,b,dims,preferred_element_type=F32)

def halves(a):
    high=a.astype(BF)
    return high,(a-high.astype(F32)).astype(BF)

def mm_lw(a,b,dims=NN):
    high,low=halves(b)
    return mm(a,high,dims)+mm(a,low,dims)

def mm_wl(a,b,dims=NN):
    high,low=halves(a)
    return mm(high,b,dims)+mm(low,b,dims)

def mm_ww(a,b,dims=NN):
    ah,al=halves(a); bh,bl=halves(b)
    return mm(ah,bh,dims)+(mm(al,bh,dims)+mm(ah,bl,dims))

def tile_masks(tile):
    row=lax.broadcasted_iota(jnp.int32,(tile,tile),0)
    col=lax.broadcasted_iota(jnp.int32,(tile,tile),1)
    return row,col


MESH = pl.DeviceIdType.MESH
ANY = pl.BlockSpec(memory_space=pl.ANY)
VMEM = pl.BlockSpec(memory_space=pltpu.VMEM)


def flipped(index, bit):
    size = 2**bit
    return index + (1 - 2 * ((index // size) % 2)) * size


def greet(peers):
    barrier = pltpu.get_barrier_semaphore()
    for axis, peer in peers:
        pl.semaphore_signal(barrier, inc=1, device_id={axis: peer}, device_id_type=MESH)
    pl.semaphore_wait(barrier, len(peers))


def others(axis, count):
    me = lax.axis_index(axis)
    return [(axis, lax.rem(me + step, count)) for step in range(1, count)]


def send(source, target, sends, recvs, slot, axis, peer):
    copy = pltpu.make_async_remote_copy(
        src_ref=source,
        dst_ref=target,
        send_sem=sends.at[slot],
        recv_sem=recvs.at[slot],
        device_id={axis: peer},
        device_id_type=MESH,
    )
    copy.start()
    return copy


def span(size, index, axis):
    piece = pl.ds(pl.multiple_of(index * size, size), size)
    return (piece, slice(None)) if axis == 0 else (slice(None), piece)


def start_exchange(pieces, count, sends, recvs, local, first=0):
    me = lax.axis_index("seq")
    started = []
    for number, (source, source_at, target, target_at) in enumerate(pieces):
        own = pltpu.make_async_copy(
            source.at[source_at(me)], target.at[target_at(me)], local.at[first // count + number]
        )
        own.start()
        started.append(own)
        for step in range(1, count):
            peer = lax.rem(me + step, count)
            slot = first + number * count + step
            started.append(
                send(
                    source.at[source_at(peer)], target.at[target_at(me)],
                    sends, recvs, slot, "seq", peer,
                )
            )
    return started


def wait_all(copies):
    for copy in copies:
        copy.wait()


def bit_orders(count):
    bits = list(range(count.bit_length() - 1))[::-1]
    other = bits[:]
    if len(bits) >= 3:
        other[0], other[1] = bits[1], bits[0]
    return [bits, other]


class Gather:
    def __init__(self, count, source, target, axis, sends, recvs, local, slot, local_slot):
        self.count, self.source, self.target, self.axis = count, source, target, axis
        self.sends, self.recvs, self.local = sends, recvs, local
        self.slot, self.local_slot = slot, local_slot
        self.me = lax.axis_index("seq")
        self.copies = {}

    def piece(self, owner, half):
        rows, columns = self.source.shape
        part = rows // 2
        if self.axis == 0:
            return (pl.ds(pl.multiple_of(owner * rows + half * part, part), part), slice(None))
        return (
            pl.ds(half * part, part),
            pl.ds(pl.multiple_of(owner * columns, columns), columns),
        )

    def put(self, order, half, turn, known):
        owner = self.me
        for bit in known:
            owner = flipped(owner, bit)
        place = self.target.at[self.piece(owner, half)]
        part = self.source.shape[0] // 2
        source = place if known else self.source.at[pl.ds(half * part, part)]
        slot = self.slot + half * self.count + self.number(order, turn, known)
        self.copies[half, turn, known] = send(
            source, place, self.sends, self.recvs, slot, "seq", flipped(self.me, order[turn])
        )

    def number(self, order, turn, known):
        return 2**turn + sum(2 ** order.index(bit) for bit in known)

    def start(self):
        self.start_own()
        for half in range(2):
            self.start_half(half)

    def start_own(self):
        self.own = pltpu.make_async_copy(
            self.source,
            self.target.at[
                span(self.source.shape[self.axis], self.me, self.axis)
            ],
            self.local.at[self.local_slot],
        )
        self.own.start()

    def start_half(self, half):
        order = bit_orders(self.count)[half]
        for turn in range(len(order)):
            self.put(order, half, turn, ())

    def turns(self):
        return self.count.bit_length() - 1

    def forward(self, turn):
        orders = bit_orders(self.count)
        for before in range(2**turn):
            for half, order in enumerate(orders):
                known = tuple(order[i] for i in range(turn) if before // 2**i % 2)
                self.copies[half, turn, known].wait_recv()
                for later in range(turn + 1, len(order)):
                    self.put(order, half, later, known + (order[turn],))

    def finish(self):
        for copy in self.copies.values():
            copy.wait_send()
        self.own.wait()


def hypercube_peers(count):
    me = lax.axis_index("seq")
    return [("seq", flipped(me, bit)) for bit in range(count.bit_length() - 1)]


def comm_params(identity, limit=48):
    return pltpu.CompilerParams(
        collective_id=identity, has_side_effects=True, vmem_limit_bytes=limit * 2**20
    )


def opening_kernel(count, wq, wk, wv, wo, mixer, sends, recvs, local):
    greet(others("seq", count))
    mine = wq.shape[1] // count
    pieces = []
    for member, weight in enumerate((wq, wk, wv, wo)):
        pieces.append(
            (
                weight,
                lambda i: span(mine, i, 1),
                mixer,
                lambda i, member=member: (i, slice(None), slice(member * mine, (member + 1) * mine)),
            )
        )
    wait_all(start_exchange(pieces, count, sends, recvs, local))


def opening(count, weights):
    rows, features = weights[0].shape
    return pl.pallas_call(
        functools.partial(opening_kernel, count),
        out_shape=jax.ShapeDtypeStruct((count, rows, 4 * features // count), BF),
        in_specs=[ANY] * 4,
        out_specs=ANY,
        scratch_shapes=[
            pltpu.SemaphoreType.DMA((4 * count,)),
            pltpu.SemaphoreType.DMA((4 * count,)),
            pltpu.SemaphoreType.DMA((4,)),
        ],
        compiler_params=comm_params(1, 60),
    )(*weights)


def second_kernel(
    count, depth, gain_one, gain_two, taps, pad, starts, x_ref, gate, up, down, pair_rest, down_rest,
    small_all, pair, last, normed_full,
    small, gain, normed, sends, recvs, local, gather_sends, gather_recvs, far,
):
    greet(others("seq", count) + others("dp", depth))
    me, level = lax.axis_index("seq"), lax.axis_index("dp")
    small[...] = jnp.zeros(small.shape, F32)
    owned, features = gain_one.shape[1], x_ref.shape[1]
    for member in range(3):
        small[member * CONV : (member + 1) * CONV, 0:owned] = taps[member].astype(F32)
    at = 3 * CONV
    for row, source in enumerate((gain_one, gain_two, pad, starts)):
        small[at + row : at + row + 1, 0 : source.shape[1]] = source[...].astype(F32)
    mine = level * count + me
    small_all[mine] = small[...]
    copies = [
        send(
            small, small_all.at[mine], far.at[0], far.at[1], step, "seq", lax.rem(me + step, count)
        )
        for step in range(1, count)
    ]
    rest = pair_rest.shape[1] // count
    main = (gate.shape[1] - pair_rest.shape[1] // 2) // count

    def piece(source, size, target, at):
        return (
            source,
            lambda i: span(size, i, 1),
            target,
            lambda i: (i, slice(None), slice(at, at + size)),
        )

    wait_all(copies)
    plane = small_all.at[pl.ds(level * count, count)]
    levels = [
        send(plane, plane, far.at[2], far.at[3], step, "dp", lax.rem(level + step, depth))
        for step in range(1, depth)
    ]
    rows = gate.shape[0]
    pieces = [
        piece(gate, main, pair, 0),
        piece(up, main, pair, main),
        piece(pair_rest, rest, pair, 2 * main),
    ]
    for tile in range(main // 128):
        pieces.append(
            (
                down,
                lambda i, tile=tile: (
                    slice(None), pl.ds(pl.multiple_of(i * main + tile * 128, 128), 128)
                ),
                last,
                lambda i, tile=tile: span(rows, tile * count + i, 0),
            )
        )
    folded = rows // 2
    pieces.append(
        (
            down_rest,
            lambda i: span(128, i, 1),
            last,
            lambda i: (
                pl.ds(pl.multiple_of(main // 128 * count * rows + i * folded, folded), folded),
                slice(None),
            ),
        )
    )
    exchange = start_exchange(pieces, count, sends, recvs, local)
    wait_all(levels)
    per = 128 // owned
    for tile in range(features // 128):
        row = small_all[tile * per, at : at + 1, :]
        for part in range(1, per):
            row = row + pltpu.roll(small_all[tile * per + part, at : at + 1, :], part * owned, 1)
        gain[0:1, tile * 128 : (tile + 1) * 128] = row
    for first in range(0, x_ref.shape[0], 16):
        part = slice(first, first + 16)
        value = x_ref[part, :].astype(F32)
        scale = lax.rsqrt(jnp.mean(value * value, axis=1, keepdims=True) + EPSILON)
        normed[part, :] = (value * scale * gain[0:1, :]).astype(BF)
    gather = Gather(count, normed, normed_full, 0, gather_sends, gather_recvs, local, 0, len(pieces))
    gather.start()
    for turn in range(gather.turns()):
        gather.forward(turn)
    gather.finish()
    wait_all(exchange)


def second(count, depth, small, x, gate, up, down, pair_rest, down_rest):
    rows = gate.shape[0]
    rest = pair_rest.shape[1] // count
    main = (gate.shape[1] - pair_rest.shape[1] // 2) // count
    slots = max(count, depth)
    members = 4 + main // 128
    shape = (3 * CONV + 4, max(128, x.shape[0]))
    return pl.pallas_call(
        functools.partial(second_kernel, count, depth),
        out_shape=(
            jax.ShapeDtypeStruct((count * depth,) + shape, F32),
            jax.ShapeDtypeStruct((count, rows, 2 * main + rest), BF),
            jax.ShapeDtypeStruct((count * rows * main // 128 + count * rows // 2, 128), BF),
            jax.ShapeDtypeStruct((x.shape[0] * count, x.shape[1]), BF),
        ),
        in_specs=[VMEM] * 6 + [ANY] * 5,
        out_specs=(VMEM, ANY, ANY, ANY),
        scratch_shapes=[
            pltpu.VMEM(shape, F32),
            pltpu.VMEM((8, x.shape[1]), F32),
            pltpu.VMEM(x.shape, BF),
            pltpu.SemaphoreType.DMA((members * count,)),
            pltpu.SemaphoreType.DMA((members * count,)),
            pltpu.SemaphoreType.DMA((members + 1,)),
            pltpu.SemaphoreType.DMA((2 * count,)),
            pltpu.SemaphoreType.DMA((2 * count,)),
            pltpu.SemaphoreType.DMA((4, slots)),
        ],
        compiler_params=comm_params(2),
    )(*small, x, gate, up, down, pair_rest, down_rest)


def closing_kernel(count, sizes, *refs):
    sources, targets, (sends, recvs, local) = refs[: len(sizes)], refs[len(sizes) : -3], refs[-3:]
    greet(others("seq", count))
    wait_all(start_exchange(row_pieces(sources, targets, sizes, count), count, sends, recvs, local))


def closing(sources, count, sizes, identity):
    shapes = row_shapes(sources, sizes, count)
    members = len(shapes)
    return pl.pallas_call(
        functools.partial(closing_kernel, count, sizes),
        out_shape=shapes,
        in_specs=[ANY] * len(sources),
        out_specs=(ANY,) * members,
        scratch_shapes=[
            pltpu.SemaphoreType.DMA((members * count,)),
            pltpu.SemaphoreType.DMA((members * count,)),
            pltpu.SemaphoreType.DMA((members,)),
        ],
        compiler_params=comm_params(identity),
    )(*sources)


def sums_kernel(count, depth, sizes, plane_ref, level_ref, source, total_ref, each_ref, *refs):
    targets, scratch = refs[: len(sizes)], refs[len(sizes) :]
    plane_in, joined, level_in, sends, recvs, pass_sends, pass_recvs, local = scratch
    greet(others("seq", count) + others("dp", depth))
    me, level = lax.axis_index("seq"), lax.axis_index("dp")
    cut = plane_ref.shape[1]
    plane_in[me] = plane_ref[...]
    wait_all(
        [
            send(
                plane_ref, plane_in.at[me], sends.at[0], recvs.at[0], step,
                "seq", lax.rem(me + step, count),
            )
            for step in range(1, count)
        ]
    )
    exchange = start_exchange(
        row_pieces([source], targets, [sizes], count), count, pass_sends, pass_recvs, local
    )
    value = plane_in[0]
    for i in range(1, count):
        value = value + plane_in[i]
    joined[:, 0:cut] = value
    joined[:, cut:] = level_ref[...]
    level_in[level] = joined[...]
    wait_all(
        [
            send(
                joined, level_in.at[level], sends.at[1], recvs.at[1], step,
                "dp", lax.rem(level + step, depth),
            )
            for step in range(1, depth)
        ]
    )
    value = level_in[0]
    for i in range(1, depth):
        value = value + level_in[i]
    total_ref[...] = value[:, 0:cut]
    joined[:, cut:] = value[:, cut:]
    each_ref[me] = value[:, cut:]
    wait_all(
        [
            send(
                joined.at[:, cut:], each_ref.at[me],
                sends.at[2], recvs.at[2], step, "seq", lax.rem(me + step, count),
            )
            for step in range(1, count)
        ]
    )
    wait_all(exchange)


def small_sums(plane, level, source, sizes, count, depth):
    shapes = row_shapes([source], [sizes], count)
    slots = max(count, depth)
    joined = (plane.shape[0], plane.shape[1] + level.shape[1])
    return pl.pallas_call(
        functools.partial(sums_kernel, count, depth, sizes),
        out_shape=(
            jax.ShapeDtypeStruct(plane.shape, F32),
            jax.ShapeDtypeStruct((count,) + level.shape, F32),
        )
        + shapes,
        in_specs=[VMEM, VMEM, ANY],
        out_specs=(VMEM, VMEM) + (ANY,) * len(shapes),
        scratch_shapes=[
            pltpu.VMEM((count,) + plane.shape, F32),
            pltpu.VMEM(joined, F32),
            pltpu.VMEM((depth,) + joined, F32),
            pltpu.SemaphoreType.DMA((3, slots)),
            pltpu.SemaphoreType.DMA((3, slots)),
            pltpu.SemaphoreType.DMA((len(sizes) * count,)),
            pltpu.SemaphoreType.DMA((len(sizes) * count,)),
            pltpu.SemaphoreType.DMA((len(sizes),)),
        ],
        compiler_params=comm_params(3),
    )(plane, level, source)


class Scatter:
    def __init__(self, count, part, out, landing, outgoing, total, sends, recvs):
        self.count, self.part, self.out = count, part, out
        self.landing, self.outgoing, self.total = landing, outgoing, total
        self.sends, self.recvs = sends, recvs
        self.me = lax.axis_index("seq")
        self.rows = out.shape[0] // 2
        self.bits = count.bit_length() - 1
        self.orders = [order[::-1] for order in bit_orders(count)]
        self.copies = {}

    def rows_of(self, known, half):
        owner = self.me
        for bit in known:
            owner = flipped(owner, bit)
        size = self.rows
        return pl.ds(pl.multiple_of(owner * 2 * size + half * size, size), size)

    def place(self, order, turn, known):
        later = order[turn + 1 :]
        before = sum(self.count >> (t + 1) for t in range(turn))
        return before + sum(2**i for i, bit in enumerate(later) if bit in known)

    def subsets(self, order, turn):
        later = order[turn + 1 :]
        sets = [
            tuple(later[i] for i in range(len(later)) if code // 2**i % 2)
            for code in range(2 ** len(later))
        ]
        return sorted(sets, key=lambda known: [-(bit in known) for bit in later])

    def put(self, half, turn, known, source):
        order = self.orders[half]
        place = self.place(order, turn, known)
        self.copies[half, turn, known] = send(
            source,
            self.landing.at[half, place],
            self.sends,
            self.recvs,
            half * self.count + place,
            "seq",
            flipped(self.me, order[turn]),
        )

    def start(self):
        for at in range(self.count // 2):
            for half, order in enumerate(self.orders):
                known = self.subsets(order, 0)[at]
                self.put(half, 0, known, self.part.at[self.rows_of((order[0],) + known, half)])

    def turn(self, turn):
        for at in range(2 ** (self.bits - turn - 1)):
            for half, order in enumerate(self.orders):
                known = self.subsets(order, turn)[at]
                place = self.place(order, turn, known)
                self.copies[half, turn, known].wait_recv()
                came = self.landing[half, place].astype(F32)
                if turn == 0:
                    value = self.part[self.rows_of(known, half), :].astype(F32) + came
                else:
                    value = self.total[half, self.kept(order, turn - 1, known)] + came
                if turn == self.bits - 1:
                    self.out[half * self.rows : (half + 1) * self.rows, :] = value
                elif order[turn + 1] in known:
                    rest = tuple(bit for bit in known if bit != order[turn + 1])
                    next_place = self.place(order, turn + 1, rest) - self.count // 2
                    self.outgoing[half, next_place] = value.astype(BF)
                    self.put(half, turn + 1, rest, self.outgoing.at[half, next_place])
                else:
                    self.total[half, self.kept(order, turn, known)] = value

    def kept(self, order, turn, known):
        return sum(2**i for i, bit in enumerate(order[turn + 2 :]) if bit in known)

    def finish(self):
        for copy in self.copies.values():
            copy.wait_send()


def scatter_scratch(count, rows, columns):
    half = rows // 2
    return [
        pltpu.VMEM((2, count - 1, half, columns), BF),
        pltpu.VMEM((2, count // 2 - 1, half, columns), BF),
        pltpu.VMEM((2, count // 4, half, columns), F32),
        pltpu.SemaphoreType.DMA((2 * count,)),
        pltpu.SemaphoreType.DMA((2 * count,)),
    ]


def shifted_sum(window, taps_ref, member, lanes, keep):
    length = window.shape[0] - 8
    row = lax.broadcasted_iota(jnp.int32, (length, 1), 0)
    shifts = [window[8:]]
    for lagged in range(1, CONV):
        moved = pltpu.roll(window, lagged, 0)[8:]
        shifts.append(moved * jnp.where(row >= lagged, 1.0, keep))
    summed = shifts[0] * taps_ref[member * CONV : member * CONV + 1, lanes]
    for lagged in range(1, CONV):
        at = member * CONV + lagged
        summed = summed + shifts[lagged] * taps_ref[at : at + 1, lanes]
    return summed, shifts


def front_kernel(
    count, heads, persist_ref, x_ref, beta_ref, taps_ref, pad_ref, gain_ref, mixer_ref, g_ref,
    pre_ref, q_ref, k_ref, v_ref, brow_ref, sigma_ref, mixed_ref, t_ref, wide_ref, s_ref, f_ref, a_ref,
    full_ref, rows_ref, g_full_ref,
    w_ref, pre_buf, logit_buf, u_buf, c_buf, on_buf, sends, recvs, local, gather_sends, gather_recvs,
):
    total, features = x_ref.shape
    mine = on_buf.shape[1]
    weight = pltpu.make_async_copy(mixer_ref.at[:, 0 : 3 * mine], w_ref, local.at[2])
    weight.start()
    hd = mine // heads
    blocks = total // BLOCK
    tile = 2 * BLOCK
    greet(others("seq", count))
    exchange = start_exchange(
        [
            (
                mixer_ref,
                lambda i: (pl.ds(pl.multiple_of(i * mine, mine), mine), slice(3 * mine, 4 * mine)),
                rows_ref,
                lambda i: span(mine, i, 1),
            )
        ],
        count, sends, recvs, local,
    )
    beside = Gather(
        count, g_ref, g_full_ref, 0, gather_sends, gather_recvs, local, 2 * count, 3
    )
    beside.start()
    pre_buf[0:8, :] = jnp.zeros((8, 3 * mine), F32)
    chunk = 4 * BLOCK
    weight.wait()

    def project(index, carry):
        rows = pl.ds(pl.multiple_of(index * chunk, chunk), chunk)
        x = x_ref[rows, :]
        low = mm(x, w_ref[...]).astype(BF)
        pre_ref[rows, :] = low
        pre_buf[pl.ds(pl.multiple_of(index * chunk + 8, 8), chunk), :] = low.astype(F32)
        logit_buf[rows, :] = mm(x, beta_ref[...])
        return carry

    lax.fori_loop(0, total // chunk, project, 0)
    beside.forward(0)

    def convolve(index, carry):
        keep = persist_ref[index]
        rows = pl.ds(pl.multiple_of(index * BLOCK, BLOCK), BLOCK)
        for member, target in enumerate((q_ref, k_ref, v_ref)):
            for h in range(heads):
                lanes = slice(h * hd, (h + 1) * hd)
                there = slice(member * mine + h * hd, member * mine + (h + 1) * hd)
                window = pre_buf[pl.ds(pl.multiple_of(index * BLOCK, 8), BLOCK + 8), there]
                summed, _ = shifted_sum(window, taps_ref, member, lanes, keep)
                value = summed * jax.nn.sigmoid(summed)
                if member < 2:
                    norm = jnp.sum(value * value, axis=1, keepdims=True) + EPSILON
                    value = value * lax.rsqrt(norm)
                if member == 0:
                    value = value * hd ** (-0.5)
                target[rows, lanes] = value.astype(BF)
        return carry

    lax.fori_loop(0, blocks, convolve, 0)
    beside.forward(1)
    row, col = tile_masks(tile)
    eyed = (
        lax.broadcasted_iota(jnp.int32, (hd, hd), 0) == lax.broadcasted_iota(jnp.int32, (hd, hd), 1)
    ).astype(F32)

    def first(step, carry):
        same = (row // BLOCK) == (col // BLOCK)
        eye = (row == col).astype(F32)
        chains = [(2 * step + i, h) for i in range(2) for h in range(heads)]
        ts, ls, ks, vs, bs = [], [], [], [], []
        for index, h in chains:
            rows = pl.ds(pl.multiple_of(index * tile, tile), tile)
            lanes = slice(h * hd, (h + 1) * hd)
            k = k_ref[rows, lanes]
            logit = jnp.sum(eye * logit_buf[rows, h : h + 1], axis=0, keepdims=True)
            sigma = jax.nn.sigmoid(logit)
            b = sigma * pad_ref[pl.ds(index, 1), :]
            sigma_ref[index, h : h + 1, :] = sigma
            brow_ref[index, h : h + 1, :] = b
            bcol = jnp.sum(eye * b, axis=1, keepdims=True)
            low = jnp.where(same & (row > col), mm(k, k, NT) * bcol, 0.0)
            ls.append(low)
            ks.append(k)
            vs.append(v_ref[rows, lanes])
            bs.append(b)
            ts.append(eye - jnp.where((row // 2) == (col // 2), low, 0.0))
        size = 2
        while size < BLOCK:
            cut = ((row // (2 * size)) == (col // (2 * size))) & ((row // size) != (col // size))
            mids = [mm_ww(jnp.where(cut, l, 0.0), t) for l, t in zip(ls, ts)]
            ts = [t - mm_ww(t, m) for t, m in zip(ts, mids)]
            size *= 2
        for at, (index, h) in enumerate(chains):
            rows = pl.ds(pl.multiple_of(index * tile, tile), tile)
            lanes = slice(h * hd, (h + 1) * hd)
            t_ref[h, rows, :] = ts[at]
            wu = mm_wl(ts[at] * bs[at], jnp.concatenate([ks[at], vs[at]], axis=1))
            wide_ref[rows, lanes] = wu[:, :hd]
            u_buf[rows, lanes] = wu[:, hd:]
            for part in range(2):
                sub = slice(part * BLOCK, (part + 1) * BLOCK)
                ab = mm_lw(ks[at][sub], wu[sub], TN)
                a_ref[h, index * 2 + part] = eyed - ab[:, :hd]
                c_buf[h, index * 2 + part] = ab[:, hd:]
        return carry

    lax.fori_loop(0, blocks // 4, first, 0)
    for turn in range(2, beside.turns()):
        beside.forward(turn)

    def chain(index, states):
        keep = persist_ref[index]
        new = []
        for h in range(heads):
            s = states[h] * keep
            s_ref[h, index] = s
            new.append(mm_ww(a_ref[h, index], s) + c_buf[h, index])
        return tuple(new)

    lax.fori_loop(0, blocks, chain, tuple(jnp.zeros((hd, hd), F32) for _ in range(heads)))

    def last(step, carry):
        lower_row, lower_col = tile_masks(BLOCK)
        for part in range(2):
            index = 2 * step + part
            rows = pl.ds(pl.multiple_of(index * BLOCK, BLOCK), BLOCK)
            for h in range(heads):
                lanes = slice(h * hd, (h + 1) * hd)
                q, k, s = q_ref[rows, lanes], k_ref[rows, lanes], s_ref[h, index]
                f = u_buf[rows, lanes] - mm_ww(wide_ref[rows, lanes], s)
                p = jnp.where(lower_row >= lower_col, mm(q, k, NT), 0.0)
                f_ref[rows, lanes] = f
                mixed = mm_lw(q, s) + mm_ww(p, f)
                mixed_ref[rows, lanes] = mixed
                scale = lax.rsqrt(jnp.mean(mixed * mixed, axis=1, keepdims=True) + EPSILON)
                on_buf[rows, lanes] = (mixed * scale * gain_ref[0:1, :]).astype(BF)
        return carry

    gather = Gather(count, on_buf, full_ref, 1, gather_sends, gather_recvs, local, 0, 1)
    lax.fori_loop(0, blocks // 4, last, 0)
    gather.start_half(0)
    lax.fori_loop(blocks // 4, blocks // 2, last, 0)
    gather.start_half(1)
    gather.start_own()
    for turn in range(gather.turns()):
        gather.forward(turn)
    gather.finish()
    beside.finish()
    wait_all(exchange)


def front(count, heads, persist, x, w_mixer, w_beta, taps, pad, gain, g):
    total, features = x.shape
    mine = w_mixer.shape[1] // 4
    hd = mine // heads
    blocks, tiles = total // BLOCK, total // (2 * BLOCK)
    wide = jax.ShapeDtypeStruct((total, mine), F32)
    low = jax.ShapeDtypeStruct((total, mine), BF)
    strength = jax.ShapeDtypeStruct((tiles, heads, 2 * BLOCK), F32)
    states = jax.ShapeDtypeStruct((heads, blocks, hd, hd), F32)
    return pl.pallas_call(
        functools.partial(front_kernel, count, heads),
        out_shape=(
            jax.ShapeDtypeStruct((total, 3 * mine), BF),
            low, low, low, strength, strength, wide,
            jax.ShapeDtypeStruct((heads, total, 2 * BLOCK), F32),
            wide, states, wide, states,
            jax.ShapeDtypeStruct((total, mine * count), BF),
            jax.ShapeDtypeStruct((mine, features), BF),
            jax.ShapeDtypeStruct((total, features), BF),
        ),
        in_specs=[
            pl.BlockSpec(memory_space=pltpu.SMEM),
            VMEM, VMEM, VMEM, VMEM, VMEM, ANY, ANY,
        ],
        out_specs=(VMEM,) * 12 + (ANY,) * 3,
        scratch_shapes=[
            pltpu.VMEM((features, 3 * mine), BF),
            pltpu.VMEM((total + 8, 3 * mine), F32),
            pltpu.VMEM((total, w_beta.shape[1]), F32),
            pltpu.VMEM((total, mine), F32),
            pltpu.VMEM((heads, blocks, hd, hd), F32),
            pltpu.VMEM((total, mine), BF),
            pltpu.SemaphoreType.DMA((count,)),
            pltpu.SemaphoreType.DMA((count,)),
            pltpu.SemaphoreType.DMA((4,)),
            pltpu.SemaphoreType.DMA((4 * count,)),
            pltpu.SemaphoreType.DMA((4 * count,)),
        ],
        compiler_params=comm_params(4, 52),
    )(persist, x, w_beta, taps, pad, gain, w_mixer, g)


def middle_kernel(
    count, full_ref, mixer_ref, x_ref, gain_ref, mid_ref, normed_ref,
    w_ref, staged, landed, low_buf, sends, recvs, local, gather_sends, gather_recvs,
):
    me = lax.axis_index("seq")
    rows, features = x_ref.shape
    mine = w_ref.shape[1]
    weight = pltpu.make_async_copy(mixer_ref.at[:, 3 * mine : 4 * mine], w_ref, local.at[2])
    weight.start()
    greet(others("seq", count))
    weight.wait()
    copies = []
    for step in list(range(1, count)) + [0]:
        peer = lax.rem(me + step, count)
        at = pl.ds(pl.multiple_of(peer * rows, rows), rows)
        staged[step] = mm(full_ref[at, :], w_ref[...])
        target = landed.at[span(mine, me, 1)]
        if step:
            copies.append(send(staged.at[step], target, sends, recvs, step, "seq", peer))
        else:
            own = pltpu.make_async_copy(staged.at[0], target, local.at[0])
            own.start()
            copies.append(own)
    wait_all(copies)
    for at in range(0, rows, 16):
        part = slice(at, at + 16)
        value = x_ref[part, :].astype(F32) + landed[part, :]
        mid_ref[part, :] = value
        scale = lax.rsqrt(jnp.mean(value * value, axis=1, keepdims=True) + EPSILON)
        low_buf[part, :] = (value * scale * gain_ref[0:1, :]).astype(BF)
    gather = Gather(count, low_buf, normed_ref, 0, gather_sends, gather_recvs, local, 0, 1)
    gather.start()
    for turn in range(gather.turns()):
        gather.forward(turn)
    gather.finish()


def middle(count, full, w_mixer, x, gain):
    rows, features = x.shape
    mine = w_mixer.shape[1] // 4
    return pl.pallas_call(
        functools.partial(middle_kernel, count),
        out_shape=(
            jax.ShapeDtypeStruct((rows, features), F32),
            jax.ShapeDtypeStruct((rows * count, features), BF),
        ),
        in_specs=[VMEM, ANY, VMEM, VMEM],
        out_specs=(VMEM, ANY),
        scratch_shapes=[
            pltpu.VMEM((features, mine), BF),
            pltpu.VMEM((count, rows, mine), F32),
            pltpu.VMEM((rows, features), F32),
            pltpu.VMEM((rows, features), BF),
            pltpu.SemaphoreType.DMA((count,)),
            pltpu.SemaphoreType.DMA((count,)),
            pltpu.SemaphoreType.DMA((3,)),
            pltpu.SemaphoreType.DMA((2 * count,)),
            pltpu.SemaphoreType.DMA((2 * count,)),
        ],
        compiler_params=comm_params(5),
    )(full, w_mixer, x, gain)


def norm_backward(value_ref, grad_ref, beside_ref, gain_ref, out_ref, gain_out, low_ref=None):
    rows, features = out_ref.shape
    gain_out[...] = jnp.zeros((8, features), F32)
    for at in range(0, rows, 8):
        part = slice(at, at + 8)
        value = value_ref[part, :].astype(F32)
        scale = lax.rsqrt(jnp.mean(value * value, axis=1, keepdims=True) + EPSILON)
        unit = value * scale
        grad = grad_ref[part, :]
        gain_out[...] += grad * unit
        scaled = grad * gain_ref[0:1, :]
        mean = jnp.mean(scaled * unit, axis=1, keepdims=True)
        result = beside_ref[part, :].astype(F32) + scale * (scaled - unit * mean)
        out_ref[part, :] = result
        if low_ref is not None:
            half = (at // 16) * 16
            if at % 16 == 8:
                low_ref[half : half + 16, :] = out_ref[half : half + 16, :].astype(BF)


def reduce_kernel(
    count, part_ref, mid_ref, g_ref, gain_ref, grad_ref, gain_out, full_ref,
    summed, low_buf, landing, outgoing, kept, sends, recvs, local, gather_sends, gather_recvs,
):
    greet(hypercube_peers(count))
    scatter = Scatter(count, part_ref, summed, landing, outgoing, kept, sends, recvs)
    scatter.start()
    for turn in range(scatter.bits):
        scatter.turn(turn)
    norm_backward(mid_ref, summed, g_ref, gain_ref, grad_ref, gain_out, low_buf)
    gather = Gather(count, low_buf, full_ref, 0, gather_sends, gather_recvs, local, 0, 0)
    gather.start()
    for turn in range(gather.turns()):
        gather.forward(turn)
    gather.finish()
    scatter.finish()


def reduce_middle(count, parts, mid, g, gain):
    rows, features = mid.shape
    return pl.pallas_call(
        functools.partial(reduce_kernel, count),
        out_shape=(
            jax.ShapeDtypeStruct((rows, features), F32),
            jax.ShapeDtypeStruct((8, features), F32),
            jax.ShapeDtypeStruct((rows * count, features), BF),
        ),
        in_specs=[VMEM] * 4,
        out_specs=(VMEM, VMEM, ANY),
        scratch_shapes=[pltpu.VMEM((rows, features), F32), pltpu.VMEM((rows, features), BF)]
        + scatter_scratch(count, rows, features)
        + [
            pltpu.SemaphoreType.DMA((1,)),
            pltpu.SemaphoreType.DMA((2 * count,)),
            pltpu.SemaphoreType.DMA((2 * count,)),
        ],
        compiler_params=comm_params(6),
    )(parts, mid, g, gain)


def back_kernel(
    count, heads, persist_ref, full_ref, rows_ref, mixed_ref, gain_ref, taps_ref, pre_ref, q_ref, k_ref, v_ref,
    brow_ref, sigma_ref, pad_ref, t_ref, wide_ref, s_ref, f_ref, a_ref, done_ref,
    dpre_ref, taps_out, gain_out, main_ref, ends_ref, *scratch,
):
    total, mine = mixed_ref.shape
    hd = mine // heads
    blocks = total // BLOCK
    beta_lanes = dpre_ref.shape[1] - 3 * mine
    do_buf, y_buf, c_buf, g_buf, pre_buf, conv_buf, pass_sends, pass_recvs, local = scratch
    greet(others("seq", count))
    exchange = start_exchange(
        folded_pieces(done_ref, main_ref, ends_ref, count), count, pass_sends, pass_recvs, local
    )
    gain_out[...] = jnp.zeros((8, hd), F32)
    taps_out[...] = jnp.zeros((3 * CONV, 8, mine), F32)
    pre_buf[0:8, :] = jnp.zeros((8, 3 * mine), F32)
    conv_buf[total : total + 8, :] = jnp.zeros((8, 3 * mine), F32)
    chunk = 4 * BLOCK

    def heads_in(index, carry):
        rows = pl.ds(pl.multiple_of(index * chunk, chunk), chunk)
        pre_buf[pl.ds(pl.multiple_of(index * chunk + 8, 8), chunk), :] = pre_ref[rows, :].astype(F32)
        grad = mm(full_ref[rows, :], rows_ref[...], NT)
        for h in range(heads):
            lanes = slice(h * hd, (h + 1) * hd)
            mixed, don = mixed_ref[rows, lanes], grad[:, lanes]
            scale = lax.rsqrt(jnp.mean(mixed * mixed, axis=1, keepdims=True) + EPSILON)
            unit = mixed * scale
            gain_out[...] += jnp.sum((don * unit).reshape(chunk // 8, 8, hd), axis=0)
            scaled = don * gain_ref[0:1, :]
            mean = jnp.mean(scaled * unit, axis=1, keepdims=True)
            do_buf[rows, lanes] = scale * (scaled - unit * mean)
        return carry

    lax.fori_loop(0, total // chunk, heads_in, 0)
    row, col = tile_masks(BLOCK)

    def first(step, carry):
        for part in range(2):
            index = 2 * step + part
            rows = pl.ds(pl.multiple_of(index * BLOCK, BLOCK), BLOCK)
            for h in range(heads):
                lanes = slice(h * hd, (h + 1) * hd)
                q, k, do = q_ref[rows, lanes], k_ref[rows, lanes], do_buf[rows, lanes]
                p = jnp.where(row >= col, mm(q, k, NT), 0.0)
                y = mm_ww(p, do, TN)
                y_buf[rows, lanes] = y
                c_buf[h, index] = mm_lw(q, do, TN) - mm_ww(wide_ref[rows, lanes], y, TN)
        return carry

    lax.fori_loop(0, blocks // 2, first, 0)

    def chain(step, grads):
        index = blocks - 1 - step
        keep = persist_ref[index]
        new = []
        for h in range(heads):
            g = grads[h]
            g_buf[h, index] = g
            new.append((mm_ww(a_ref[h, index], g, TN) + c_buf[h, index]) * keep)
        return tuple(new)

    lax.fori_loop(0, blocks, chain, tuple(jnp.zeros((hd, hd), F32) for _ in range(heads)))

    def last(step, carry):
        for part in range(2):
            index = 2 * step + part
            keep = persist_ref[index]
            rows = pl.ds(pl.multiple_of(index * BLOCK, BLOCK), BLOCK)
            half = slice(part * BLOCK, (part + 1) * BLOCK)
            lane = lax.broadcasted_iota(jnp.int32, (BLOCK, beta_lanes), 1)
            dlogits = jnp.zeros((BLOCK, beta_lanes), F32)
            for h in range(heads):
                lanes = slice(h * hd, (h + 1) * hd)
                q, k, v = q_ref[rows, lanes], k_ref[rows, lanes], v_ref[rows, lanes]
                do, s, f, g = do_buf[rows, lanes], s_ref[h, index], f_ref[rows, lanes], g_buf[h, index]
                b = brow_ref[step, h : h + 1, half]
                bcol = jnp.sum(jnp.where(row == col, b, 0.0), axis=1, keepdims=True)
                t = t_ref[h, rows, half]
                df = y_buf[rows, lanes] + mm_lw(k, g)
                dr = mm_ww(t, df, TN)
                dp = jnp.where(row >= col, mm_ww(do, f, NT), 0.0)
                dl = jnp.where(row > col, -mm_ww(dr, f, NT), 0.0)
                dq = mm_ww(do, s, NT) + mm_wl(dp, k)
                dkb = mm_wl(dl, k) - mm_ww(dr, s, NT)
                dk = mm_wl(dp, q, TN) + mm_ww(f, g, NT) + mm_wl(dl * bcol, k, TN) + bcol * dkb
                dbeta = jnp.sum(dr * v.astype(F32) + dkb * k.astype(F32), axis=1, keepdims=True)
                sigma = sigma_ref[step, h : h + 1, half]
                slope = pad_ref[pl.ds(step, 1), half] * sigma * (1.0 - sigma)
                slope = jnp.sum(jnp.where(row == col, slope, 0.0), axis=1, keepdims=True)
                dlogits = jnp.where(lane == h, dbeta * slope, dlogits)
                for member, grad in enumerate((dq, dk, bcol * dr)):
                    there = slice(member * mine + h * hd, member * mine + (h + 1) * hd)
                    window = pre_buf[pl.ds(pl.multiple_of(index * BLOCK, 8), BLOCK + 8), there]
                    summed, shifts = shifted_sum(window, taps_ref, member, lanes, keep)
                    sigma = jax.nn.sigmoid(summed)
                    if member < 2:
                        value = summed * sigma
                        inverse = lax.rsqrt(jnp.sum(value * value, axis=1, keepdims=True) + EPSILON)
                        unit = value * inverse
                        along = jnp.sum(grad * unit, axis=1, keepdims=True)
                        grad = (grad - unit * along) * inverse
                    if member == 0:
                        grad = grad * hd ** (-0.5)
                    grad = grad * (sigma * (1.0 + summed * (1.0 - sigma)))
                    conv_buf[rows, there] = grad
                    for lagged in range(CONV):
                        taps_out[member * CONV + lagged, :, lanes] += jnp.sum(
                            (grad * shifts[lagged]).reshape(BLOCK // 8, 8, hd), axis=0
                        )
            dpre_ref[rows, 3 * mine :] = dlogits.astype(BF)
        return carry

    lax.fori_loop(0, blocks // 2, last, 0)

    def spread(index, carry):
        rows = pl.ds(pl.multiple_of(index * BLOCK, BLOCK), BLOCK)
        keep = persist_ref[jnp.minimum(index + 1, blocks - 1)]
        block_row = lax.broadcasted_iota(jnp.int32, (BLOCK, 1), 0)
        for member in range(3):
            there = slice(member * mine, (member + 1) * mine)
            window = conv_buf[pl.ds(pl.multiple_of(index * BLOCK, 8), BLOCK + 8), there]
            summed = window[:BLOCK] * taps_ref[member * CONV : member * CONV + 1, :]
            for lagged in range(1, CONV):
                at = member * CONV + lagged
                moved = pltpu.roll(window, BLOCK + 8 - lagged, 0)[:BLOCK]
                moved = moved * jnp.where(block_row < BLOCK - lagged, 1.0, keep)
                summed = summed + moved * taps_ref[at : at + 1, :]
            dpre_ref[rows, there] = summed.astype(BF)
        return carry

    lax.fori_loop(0, blocks, spread, 0)
    wait_all(exchange)


def back(
    count, heads, persist, full, w_rows, mixed, gain, taps, pre, q, k, v, strength, saved, done, main
):
    total, mine = mixed.shape
    hd = mine // heads
    blocks = total // BLOCK
    owned = done.shape[0] // (count * main // 128 + count // 2)
    members = main // 128 + 1
    return pl.pallas_call(
        functools.partial(back_kernel, count, heads),
        out_shape=(
            jax.ShapeDtypeStruct((total, 3 * mine + 128), BF),
            jax.ShapeDtypeStruct((3 * CONV, 8, mine), F32),
            jax.ShapeDtypeStruct((8, hd), F32),
            jax.ShapeDtypeStruct((owned, count * main), BF),
            jax.ShapeDtypeStruct((owned // 2, count * 128), BF),
        ),
        in_specs=[pl.BlockSpec(memory_space=pltpu.SMEM)] + [VMEM] * 17 + [ANY],
        out_specs=(VMEM,) * 3 + (ANY,) * 2,
        scratch_shapes=[
            pltpu.VMEM((total, mine), F32),
            pltpu.VMEM((total, mine), F32),
            pltpu.VMEM((heads, blocks, hd, hd), F32),
            pltpu.VMEM((heads, blocks, hd, hd), F32),
            pltpu.VMEM((total + 8, 3 * mine), F32),
            pltpu.VMEM((total + 8, 3 * mine), F32),
            pltpu.SemaphoreType.DMA((members * count,)),
            pltpu.SemaphoreType.DMA((members * count,)),
            pltpu.SemaphoreType.DMA((members,)),
        ],
        compiler_params=comm_params(7, 56),
    )(persist, full, w_rows, mixed, gain, taps, pre, q, k, v, *strength, *saved, done)


def end_kernel(
    count, part_ref, added_ref, x_ref, mid_ref, beside_ref, gain_ref,
    grad_ref, gain_out, out_ref, summed, added, *scratch
):
    greet(hypercube_peers(count))
    scatter = Scatter(count, part_ref, summed, *scratch[:5])
    beside = Scatter(count, added_ref, added, *scratch[5:])
    scatter.start()
    beside.start()
    for turn in range(scatter.bits):
        scatter.turn(turn)
        beside.turn(turn)
    norm_backward(x_ref, summed, beside_ref, gain_ref, grad_ref, gain_out)
    for at in range(0, out_ref.shape[0], 16):
        part = slice(at, at + 16)
        out_ref[part, :] = (mid_ref[part, :] + added[part, :]).astype(BF)
    scatter.finish()
    beside.finish()


def folded_pieces(source, main_ref, ends_ref, count):
    main = main_ref.shape[1] // count
    rows, half = main_ref.shape[0], ends_ref.shape[0]
    pieces = []
    for tile in range(main // 128):
        pieces.append(
            (
                source,
                lambda i, tile=tile: span(rows, tile * count + i, 0),
                main_ref,
                lambda i, tile=tile: (
                    slice(None), pl.ds(pl.multiple_of(i * main + tile * 128, 128), 128)
                ),
            )
        )
    pieces.append(
        (
            source,
            lambda i: (
                pl.ds(pl.multiple_of(main // 128 * count * rows + i * half, half), half),
                slice(None),
            ),
            ends_ref,
            lambda i: span(128, i, 1),
        )
    )
    return pieces


def row_pieces(sources, targets, sizes, count):
    pieces = []
    for source, widths in zip(sources, sizes):
        rows, at = source.shape[0] // count, 0
        for size in widths:
            pieces.append(
                (
                    source,
                    lambda i, rows=rows, at=at, size=size: (
                        pl.ds(pl.multiple_of(i * rows, rows), rows),
                        slice(at, at + size),
                    ),
                    targets[len(pieces)],
                    lambda i, size=size: span(size, i, 1),
                )
            )
            at += size
    return pieces


def row_shapes(sources, sizes, count):
    return tuple(
        jax.ShapeDtypeStruct((source.shape[0] // count, count * size), BF)
        for source, widths in zip(sources, sizes)
        for size in widths
    )


def end(count, parts, added, x, mid, beside, gain):
    rows, features = x.shape
    return pl.pallas_call(
        functools.partial(end_kernel, count),
        out_shape=(
            jax.ShapeDtypeStruct((rows, features), F32),
            jax.ShapeDtypeStruct((8, features), F32),
            jax.ShapeDtypeStruct((rows, features), BF),
        ),
        in_specs=[VMEM] * 6,
        out_specs=(VMEM,) * 3,
        scratch_shapes=[pltpu.VMEM((rows, features), F32)] * 2
        + scatter_scratch(count, rows, features)
        + scatter_scratch(count, rows, features),
        compiler_params=comm_params(8),
    )(parts, added, x, mid, beside, gain)


def hidden_grads_kernel(count, rest, g_ref, pair_ref, down_ref, low_ref, w_ref):
    main = w_ref.shape[1] - 128
    lane = lax.broadcasted_iota(jnp.int32, (1, 128), 1)

    @pl.when(pl.program_id(0) == 0)
    def assemble():
        depth = down_ref.shape[0]
        level = w_ref.shape[0] // depth
        rows = level // count
        for z in range(depth):
            at = z * level
            for tile in range(main // 128):
                w_ref[at : at + level, tile * 128 : (tile + 1) * 128] = down_ref[
                    z, tile * level : (tile + 1) * level, :
                ]
            for i in range(count):
                start = main // 128 * level + i * (rows // 2)
                pair = down_ref[z, start : start + rows // 2, :].astype(F32)
                for part in range(2):
                    piece = pair if part == 0 else pltpu.roll(pair, rest, 1)
                    first = at + i * rows + part * (rows // 2)
                    w_ref[first : first + rows // 2, main:] = jnp.where(
                        lane < rest, piece, 0.0
                    ).astype(BF)

    grad = mm(g_ref[...], w_ref[...])

    def slopes(gate, up, grad):
        sigma = jax.nn.sigmoid(gate)
        return grad * up * sigma * (1.0 + gate * (1.0 - sigma)), grad * (gate * sigma)

    dgate, dup = slopes(pair_ref[:, :main], pair_ref[:, main : 2 * main], grad[:, :main])
    low_ref[:, :main] = dgate.astype(BF)
    low_ref[:, main : 2 * main] = dup.astype(BF)
    tail = pair_ref[:, 2 * main :]
    dgate, dup = slopes(tail, pltpu.roll(tail, rest, 1), grad[:, main:])
    low_ref[:, 2 * main :] = jnp.where(lane < rest, dgate, pltpu.roll(dup, rest, 1)).astype(BF)


def hidden_gradients(count, rest, g, pair, down):
    total, features = g.shape
    main = (pair.shape[1] - 2 * rest) // 2
    step = total // 4
    return pl.pallas_call(
        functools.partial(hidden_grads_kernel, count, rest),
        grid=(total // step,),
        out_shape=(
            jax.ShapeDtypeStruct(pair.shape, BF),
            jax.ShapeDtypeStruct((features, main + 128), BF),
        ),
        in_specs=[
            pl.BlockSpec((step, features), lambda i: (i, 0)),
            pl.BlockSpec((step, pair.shape[1]), lambda i: (i, 0)),
            pl.BlockSpec(down.shape, lambda i: (0, 0, 0)),
        ],
        out_specs=(
            pl.BlockSpec((step, pair.shape[1]), lambda i: (i, 0)),
            pl.BlockSpec((features, main + 128), lambda i: (0, 0)),
        ),
        compiler_params=pltpu.CompilerParams(vmem_limit_bytes=40 * 2**20),
        cost_estimate=pl.CostEstimate(
            flops=2 * total * features * (main + 128),
            bytes_accessed=2 * total * features + 6 * total * pair.shape[1],
            transcendentals=total * pair.shape[1] // 2,
        ),
    )(g, pair, down)


def down_grads_kernel(count, rest, g_ref, hidden_ref, out_ref):
    grad = mm(g_ref[...], hidden_ref[...], TN)
    level = grad.shape[0]
    main = grad.shape[1] - 128
    rows = level // count
    lane = lax.broadcasted_iota(jnp.int32, (1, 128), 1)
    for tile in range(main // 128):
        out_ref[tile * level : (tile + 1) * level, :] = grad[:, tile * 128 : (tile + 1) * 128].astype(BF)
    for i in range(count):
        at = i * rows
        front = grad[at : at + rows // 2, main:]
        later = pltpu.roll(grad[at + rows // 2 : at + rows, main:], rest, 1)
        start = main // 128 * level + i * (rows // 2)
        out_ref[start : start + rows // 2, :] = jnp.where(lane < rest, front, later).astype(BF)


def down_gradients(count, depth, rest, g, hidden):
    total, features = g.shape
    width = hidden.shape[1]
    level = features // depth
    high = (width - 128) // 128 * level + level // 2
    return pl.pallas_call(
        functools.partial(down_grads_kernel, count, rest),
        grid=(depth,),
        out_shape=jax.ShapeDtypeStruct((depth * high, 128), BF),
        in_specs=[
            pl.BlockSpec((total, level), lambda i: (0, i)),
            pl.BlockSpec((total, width), lambda i: (0, 0)),
        ],
        out_specs=pl.BlockSpec((high, 128), lambda i: (i, 0)),
        compiler_params=pltpu.CompilerParams(vmem_limit_bytes=40 * 2**20),
        cost_estimate=pl.CostEstimate(
            flops=2 * total * features * width,
            bytes_accessed=2 * total * (features + width) + 2 * features * width,
            transcendentals=0,
        ),
    )(g, hidden)


def mixer_grads_kernel(x_ref, grad_ref, on_ref, out_ref, low_ref, beta_ref):
    wide = 3 * out_ref.shape[1]
    front = mm(x_ref[...], grad_ref[:, :wide], TN)
    low_ref[:, :wide] = front.astype(BF)
    beta_ref[...] = mm(grad_ref[:, wide:], x_ref[...], TN)[: beta_ref.shape[0]]
    low_ref[:, wide:] = mm(on_ref[...], out_ref[...], TN).astype(BF)


def mixer_gradients(x, grad, on, out):
    total, features = x.shape
    beta = grad.shape[1] - 3 * out.shape[1]
    wide = grad.shape[1] - beta + out.shape[1]
    step = features // 4
    return pl.pallas_call(
        mixer_grads_kernel,
        grid=(features // step,),
        out_shape=(
            jax.ShapeDtypeStruct((features, wide), BF),
            jax.ShapeDtypeStruct((8, features), F32),
        ),
        in_specs=[
            pl.BlockSpec((total, step), lambda i: (0, i)),
            pl.BlockSpec(grad.shape, lambda i: (0, 0)),
            pl.BlockSpec((total, step), lambda i: (0, i)),
            pl.BlockSpec(out.shape, lambda i: (0, 0)),
        ],
        out_specs=(
            pl.BlockSpec((step, wide), lambda i: (i, 0)),
            pl.BlockSpec((8, step), lambda i: (0, i)),
        ),
        compiler_params=pltpu.CompilerParams(vmem_limit_bytes=40 * 2**20),
        cost_estimate=pl.CostEstimate(
            flops=2 * total * features * (wide + beta),
            bytes_accessed=4 * total * features + 4 * features * wide,
            transcendentals=0,
        ),
    )(x, grad, on, out)


def rest_and_main(hidden_width, count):
    main = hidden_width // (128 * count) * 128
    return hidden_width // count - main, main


def local_heads(
    tokens,
    doc_starts,
    pad_mask,
    norm1_gain,
    query_weight,
    key_weight,
    value_weight,
    conv_weight,
    beta_weight,
    out_norm_gain,
    out_weight,
    norm2_gain,
    gate_weight,
    up_weight,
    down_weight,
    cotangent,
):
    row_count, features = tokens.shape
    width = lax.axis_size("seq")
    place = lax.axis_index("seq")
    head_dim = out_norm_gain.shape[0]
    heads = beta_weight.shape[1] // width
    mine = heads * head_dim
    total = row_count * width
    depth = lax.axis_size("dp")
    level = lax.axis_index("dp")
    owned = norm1_gain.shape[0]
    rest, main = rest_and_main(gate_weight.shape[1], width)
    mixer_part = opening(width, [query_weight, key_weight, value_weight, out_weight])
    w_mixer = lax.all_gather(
        mixer_part.reshape(width * owned, 4 * mine), "dp", axis=0, tiled=True
    )
    w_beta = lax.dynamic_slice_in_dim(beta_weight, place * heads, heads, axis=1)

    def ends(array):
        return array[:, main * width :].reshape(owned, width, rest)

    down_turned = down_weight.T
    pair_rest = jnp.concatenate([ends(gate_weight), ends(up_weight)], axis=2)
    down_rest = ends(down_turned).reshape(2, owned // 2, width, rest).transpose(1, 2, 0, 3)
    small_all, pair_part, down_part, normed_full = second(
        width,
        depth,
        [norm1_gain[None], norm2_gain[None], conv_weight, pad_mask, doc_starts],
        tokens,
        gate_weight,
        up_weight,
        down_turned,
        pair_rest.reshape(owned, -1),
        down_rest.reshape(owned // 2, -1),
    )
    wide = small_all[:, : 3 * CONV + 2, :owned].transpose(1, 0, 2).reshape(3 * CONV + 2, features)
    gain_first, gain_second = wide[3 * CONV], wide[3 * CONV + 1]
    taps = lax.dynamic_slice_in_dim(wide[: 3 * CONV], place * mine, mine, axis=1)
    marks = lax.dynamic_slice_in_dim(small_all[:, 3 * CONV + 2 :], level * width, width, axis=0)
    pad_rows = marks[:, 0, :row_count].reshape(-1, 2 * BLOCK)
    starts = marks[:, 1, : doc_starts.shape[1]].reshape(-1).astype(jnp.int32)
    begins = BLOCK * jnp.arange(total // BLOCK, dtype=jnp.int32)
    persist = (starts != begins).astype(F32)
    down_tiles = lax.all_gather(down_part, "dp", axis=0)
    w_pair = lax.all_gather(pair_part.reshape(width * owned, -1), "dp", axis=0, tiled=True)
    beta_wide = jnp.pad(w_beta, ((0, 0), (0, 128 - heads)))
    w_front = jnp.concatenate([w_mixer[:, : 3 * mine], beta_wide], axis=1)
    head_gain = out_norm_gain.astype(F32)[None]
    (
        projected, queries, key_rows, values, strength, sigma_vals, mixed,
        *saved, out_full, w_out_rows, cotangent_full,
    ) = front(
        width, heads, persist, normed_full, w_mixer, beta_wide, taps, pad_rows, head_gain,
        cotangent,
    )
    residual_mid, normed_two_full = middle(width, out_full, w_mixer, tokens, gain_second[None])
    normed_two_full, w_front = lax.optimization_barrier((normed_two_full, w_front))
    pair = product(normed_two_full, w_pair)
    tail = pair[:, 2 * main :]
    gate_out = jnp.concatenate([pair[:, :main], tail], axis=1)
    up_out = jnp.concatenate([pair[:, main : 2 * main], jnp.roll(tail, rest, axis=1)], axis=1)
    gate_sigma = jax.nn.sigmoid(gate_out)
    gate_silu = gate_out * gate_sigma
    hidden = (gate_silu * up_out).astype(BF)
    down_grads = down_gradients(width, depth, rest, cotangent_full, hidden)
    down_tiles, _ = lax.optimization_barrier((down_tiles, down_grads))
    down_sums = lax.psum_scatter(down_grads, "dp", scatter_dimension=0, tiled=True)
    pair_grad_low, w_down = hidden_gradients(width, rest, cotangent_full, pair, down_tiles)
    two_parts = product_right(pair_grad_low, w_pair).astype(BF)
    pair_grads = product_left(normed_two_full, pair_grad_low).astype(BF)
    pair_sums = lax.psum_scatter(pair_grads, "dp", scatter_dimension=0, tiled=True)
    residual_mid_grad, gain_second_rows, mid_full = reduce_middle(
        width, two_parts, residual_mid, cotangent, gain_second[None]
    )
    projected_grad, conv_rows_grad, out_gain_rows, down_main, down_ends = back(
        width, heads, persist, mid_full, w_out_rows, mixed, head_gain, taps, projected,
        queries, key_rows, values, (strength, sigma_vals, pad_rows), saved, down_sums, main,
    )
    gain_second_grad = jnp.sum(gain_second_rows, axis=0)
    out_gain_grad = jnp.sum(out_gain_rows, axis=0)
    conv_grad = jnp.sum(conv_rows_grad, axis=1)
    mid_mine = lax.dynamic_slice_in_dim(mid_full, place * mine, mine, axis=1)
    mixer_grads, beta_grads = mixer_gradients(normed_full, projected_grad, out_full, mid_mine)
    beta_grad = beta_grads[:heads]
    mixer_sums = lax.psum_scatter(mixer_grads, "dp", scatter_dimension=0, tiled=True)
    normed_parts = product_right(projected_grad, w_front).astype(BF)
    hidden, normed_parts = lax.optimization_barrier((hidden, normed_parts))
    added_parts = product_right(hidden, w_down).astype(BF)
    tokens_grad, gain_first_rows, output = end(
        width, normed_parts, added_parts, tokens, residual_mid, residual_mid_grad, gain_first[None]
    )
    gain_first_grad = jnp.sum(gain_first_rows, axis=0)

    gain_row = jnp.pad(out_gain_grad[None], ((0, 0), (0, features - head_dim)))
    plane = jnp.concatenate([gain_first_grad[None], gain_second_grad[None], gain_row], axis=0)
    conv_rows = -(-3 * CONV * mine // features)
    conv_flat = jnp.pad(conv_grad.reshape(-1), (0, conv_rows * features - 3 * CONV * mine))
    levels = jnp.concatenate([beta_grad, conv_flat.reshape(conv_rows, features)], axis=0)
    sums, each, gate_main, up_main, pair_ends = small_sums(
        plane.reshape(8, -1), levels.reshape(8, -1), pair_sums, (main, main, 2 * rest), width, depth
    )
    def joined(front, back, at):
        back = back.reshape(owned, width, 2, rest)[:, :, at].reshape(owned, width * rest)
        return jnp.concatenate([front, back], axis=1).astype(F32)

    down_back = down_ends.reshape(owned // 2, width, 2, rest).transpose(2, 0, 1, 3)
    down_back = down_back.reshape(owned, width * rest)
    shard_gate, shard_up, shard_down = (
        joined(gate_main, pair_ends, 0),
        joined(up_main, pair_ends, 1),
        jnp.concatenate([down_main, down_back], axis=1).astype(F32).T,
    )
    sums = sums.reshape(3, features)
    each = each.reshape(width, heads + conv_rows, features)
    beta_total = each[:, :heads].reshape(width * heads, features).T
    conv_all = each[:, heads:].reshape(width, -1)[:, : 3 * CONV * mine]
    conv_all = conv_all.reshape(width, 3 * CONV, mine).transpose(1, 0, 2).reshape(-1, features)
    wide_sums = jnp.concatenate([sums[:2], conv_all], axis=0)
    own = level * width + place
    wide_own = lax.dynamic_slice_in_dim(wide_sums, own * owned, owned, axis=1)

    shard_q, shard_k, shard_v, shard_o = (
        a.astype(F32) for a in closing([mixer_sums], width, [(mine,) * 4], 13)
    )

    return (
        output,
        tokens_grad,
        wide_own[0],
        shard_q,
        shard_k,
        shard_v,
        wide_own[2:].reshape(3, CONV, owned),
        beta_total,
        sums[2, :head_dim],
        shard_o,
        wide_own[1],
        shard_gate,
        shard_up,
        shard_down,
    )


def solution(mesh):
    in_specs = (
        P(("dp", "seq"), None),
        P("dp", "seq"),
        P("dp", "seq"),
        P(("dp", "seq")),
        P(("dp", "seq"), None),
        P(("dp", "seq"), None),
        P(("dp", "seq"), None),
        P(None, None, ("dp", "seq")),
        P(),
        P(),
        P(("dp", "seq"), None),
        P(("dp", "seq")),
        P(("dp", "seq"), None),
        P(("dp", "seq"), None),
        P(None, ("dp", "seq")),
        P(("dp", "seq"), None),
    )
    out_specs = (
        P(("dp", "seq"), None),
        P(("dp", "seq"), None),
        P(("dp", "seq")),
        P(("dp", "seq"), None),
        P(("dp", "seq"), None),
        P(("dp", "seq"), None),
        P(None, None, ("dp", "seq")),
        P(),
        P(),
        P(("dp", "seq"), None),
        P(("dp", "seq")),
        P(("dp", "seq"), None),
        P(("dp", "seq"), None),
        P(None, ("dp", "seq")),
    )

    def layer(*arrays):
        head_count, hidden_width = arrays[8].shape[1], arrays[12].shape[1]
        width = mesh.shape["seq"]
        rest, main = rest_and_main(hidden_width, width)
        by_heads = head_count % width == 0 and rest == 64 and main > 0
        by_heads = by_heads and width >= 4 and width & (width - 1) == 0 and head_count // width <= 8
        by_heads = by_heads and arrays[3].shape[0] // mesh.size % 32 == 0
        by_heads = by_heads and 128 % (arrays[3].shape[0] // mesh.size) == 0
        local = local_heads if by_heads else local_sequence
        return jax.shard_map(
            local, mesh=mesh, in_specs=in_specs, out_specs=out_specs, check_vma=False
        )(*arrays)

    return layer
```

```python
import functools

import jax
import jax.numpy as jnp
from jax import lax
from jax.experimental import pallas as pl
from jax.experimental.pallas import tpu as pltpu
from jax.sharding import PartitionSpec as P

CONV = 4
BLOCK = 64


EPSILON = 1e-06
PRECISE = lax.Precision.HIGHEST


def from_behind(array, axis, by):
    length = lax.axis_size(axis)
    pairs = [(i, i + by) for i in range(length) if 0 <= i + by < length]
    return lax.ppermute(array, axis, pairs)


def product(left, right):
    return jnp.dot(left, right, preferred_element_type=jnp.float32)


def product_left(left, right):
    return lax.dot_general(
        left, right, (((0,), (0,)), ((), ())), preferred_element_type=jnp.float32
    )


def product_right(left, right):
    return lax.dot_general(
        left, right, (((1,), (1,)), ((), ())), preferred_element_type=jnp.float32
    )


def rounded(value):
    return lax.optimization_barrier(value.astype(jnp.bfloat16)).astype(jnp.float32)


def rms_norm(value, gain):
    return value * lax.rsqrt(jnp.mean(value * value, axis=-1, keepdims=True) + EPSILON) * gain


def block_parts(queries, key_rows, values, strength):
    keyed = key_rows * strength[..., None]
    block_len = key_rows.shape[1]
    lower_part = jnp.tril(jnp.einsum("hcd,hed->hce", keyed, key_rows, precision=PRECISE), -1)
    system = lower_part + jnp.eye(block_len, dtype=jnp.float32)
    weights = jax.scipy.linalg.solve_triangular(system, keyed, lower=True, unit_diagonal=True)
    updates = jax.scipy.linalg.solve_triangular(
        system, values * strength[..., None], lower=True, unit_diagonal=True
    )
    scores = jnp.tril(jnp.einsum("hcd,hed->hce", queries, key_rows, precision=PRECISE))
    return (weights, updates, scores)


def delta_step(state_now, inputs):
    queries, key_rows, values, strength, persist = inputs
    state_now = state_now * persist
    weights, updates, scores = block_parts(queries, key_rows, values, strength)
    corrected = updates - jnp.einsum("hcd,hde->hce", weights, state_now, precision=PRECISE)
    outputs = jnp.einsum("hcd,hde->hce", queries, state_now, precision=PRECISE) + jnp.einsum(
        "hce,hef->hcf", scores, corrected, precision=PRECISE
    )
    state_now = state_now + jnp.einsum("hcd,hce->hde", key_rows, corrected, precision=PRECISE)
    return (state_now, outputs)


def track_step(holding, inputs):
    state_now, transit = holding
    queries, key_rows, values, strength, persist = inputs
    state_now = state_now * persist
    transit = transit * persist
    weights, updates, scores = block_parts(queries, key_rows, values, strength)
    corrected = updates - jnp.einsum("hcd,hde->hce", weights, state_now, precision=PRECISE)
    outputs = jnp.einsum("hcd,hde->hce", queries, state_now, precision=PRECISE) + jnp.einsum(
        "hce,hef->hcf", scores, corrected, precision=PRECISE
    )
    leading = queries - jnp.einsum("hce,hed->hcd", scores, weights, precision=PRECISE)
    state_now = state_now + jnp.einsum("hcd,hce->hde", key_rows, corrected, precision=PRECISE)
    eraser = jnp.eye(key_rows.shape[2], dtype=jnp.float32) - jnp.einsum(
        "hcd,hce->hde", key_rows, weights, precision=PRECISE
    )
    return (
        (state_now, jnp.einsum("hde,hef->hdf", eraser, transit, precision=PRECISE)),
        (outputs, leading, transit),
    )


def advance(linear, offset_part, incoming):
    return jnp.einsum("hde,hef->hdf", linear, incoming, precision=PRECISE) + offset_part


def into_blocks(array):
    row_count, head_count, head_dim = array.shape
    return array.reshape(row_count // BLOCK, BLOCK, head_count, head_dim).transpose(0, 2, 1, 3)


def from_blocks(array):
    block_count, head_count, block_len, head_dim = array.shape
    return array.transpose(0, 2, 1, 3).reshape(block_count * block_len, head_count, head_dim)


def local_sequence(
    tokens,
    doc_starts,
    pad_mask,
    norm1_gain,
    query_weight,
    key_weight,
    value_weight,
    conv_weight,
    beta_weight,
    out_norm_gain,
    out_weight,
    norm2_gain,
    gate_weight,
    up_weight,
    down_weight,
    cotangent,
):
    row_count, features = tokens.shape
    head_count = beta_weight.shape[1]
    head_dim = out_norm_gain.shape[0]
    block_count = row_count // BLOCK
    w_query, w_key, w_value, w_out, conv_full, gain_first = (
        lax.all_gather(query_weight, ("dp", "seq"), axis=0, tiled=True),
        lax.all_gather(key_weight, ("dp", "seq"), axis=0, tiled=True),
        lax.all_gather(value_weight, ("dp", "seq"), axis=0, tiled=True),
        lax.all_gather(out_weight, ("dp", "seq"), axis=0, tiled=True),
        lax.all_gather(conv_weight, ("dp", "seq"), axis=2, tiled=True),
        lax.all_gather(norm1_gain, ("dp", "seq"), axis=0, tiled=True),
    )
    w_gate, w_up, w_down, gain_second = (
        lax.all_gather(gate_weight, ("dp", "seq"), axis=0, tiled=True),
        lax.all_gather(up_weight, ("dp", "seq"), axis=0, tiled=True),
        lax.all_gather(down_weight, ("dp", "seq"), axis=1, tiled=True),
        lax.all_gather(norm2_gain, ("dp", "seq"), axis=0, tiled=True),
    )
    seq_place = lax.axis_index("seq")
    positions = seq_place * row_count + jnp.arange(row_count, dtype=jnp.int32)
    starts = doc_starts[0]
    offsets = jnp.repeat(starts, BLOCK)
    persist = (
        starts != seq_place * row_count + BLOCK * jnp.arange(block_count, dtype=jnp.int32)
    ).astype(jnp.float32)
    pad_rows = pad_mask[0].astype(jnp.float32)[:, None]

    def mixer_in(extended, conv_taps):
        results = []
        for member in range(3):
            columns = extended[:, member * features : (member + 1) * features]
            summed = jnp.zeros((row_count, features), jnp.float32)
            for lagged in range(CONV):
                inside = (positions - lagged >= offsets).astype(jnp.float32)[:, None]
                summed = (
                    summed
                    + conv_taps[member, lagged]
                    * inside
                    * columns[CONV - 1 - lagged : CONV - 1 - lagged + row_count]
                )
            activated = jax.nn.silu(summed).reshape(row_count, head_count, head_dim)
            if member < 2:
                activated = activated * lax.rsqrt(
                    jnp.sum(activated * activated, axis=-1, keepdims=True) + EPSILON
                )
            if member == 0:
                activated = activated * head_dim ** (-0.5)
            results.append(activated)
        return tuple(results)

    residual_in = tokens.astype(jnp.float32)
    normed, norm_first_pull = jax.vjp(rms_norm, residual_in, gain_first.astype(jnp.float32))
    normed_low = normed.astype(jnp.bfloat16)
    projected = jnp.concatenate(
        [product(normed_low, w_query), product(normed_low, w_key), product(normed_low, w_value)],
        axis=1,
    ).astype(jnp.bfloat16)
    logits = product(normed_low, beta_weight)
    sigma_vals = jax.nn.sigmoid(logits)
    strength = sigma_vals * pad_rows
    rims = from_behind(projected[row_count - CONV + 1 :], "seq", 1)
    extended_in = jnp.concatenate([rims, projected], axis=0).astype(jnp.float32)
    (queries, key_rows, values), mixer_pull = jax.vjp(
        mixer_in, extended_in, conv_full.astype(jnp.float32)
    )
    query_blocks = into_blocks(rounded(queries))
    key_blocks = into_blocks(rounded(key_rows))
    value_blocks = into_blocks(rounded(values))
    strength_blocks = strength.reshape(block_count, BLOCK, head_count).transpose(0, 2, 1)
    zero_state = jnp.zeros((head_count, head_dim, head_dim), jnp.float32)
    identity = jnp.broadcast_to(
        jnp.eye(head_dim, dtype=jnp.float32), (head_count, head_dim, head_dim)
    )
    block_inputs = (query_blocks, key_blocks, value_blocks, strength_blocks, persist)
    (final_state, final_transit), (local_out, leading, transit) = lax.scan(
        track_step, (zero_state, identity), block_inputs
    )

    def forward_turn(turn_index, incoming):
        return from_behind(advance(final_transit, final_state, incoming), "seq", 1)

    start_state = lax.fori_loop(0, lax.axis_size("seq") - 1, forward_turn, zero_state)
    carried = jnp.einsum("nhde,hef->nhdf", transit, start_state, precision=PRECISE)
    mixed = from_blocks(
        local_out + jnp.einsum("nhcd,nhdf->nhcf", leading, carried, precision=PRECISE)
    )
    out_normed, out_norm_pull = jax.vjp(rms_norm, mixed, out_norm_gain.astype(jnp.float32))
    out_low = out_normed.reshape(row_count, features).astype(jnp.bfloat16)
    residual_mid = residual_in + product(out_low, w_out)
    normed_two, norm_second_pull = jax.vjp(rms_norm, residual_mid, gain_second.astype(jnp.float32))
    normed_two_low = normed_two.astype(jnp.bfloat16)
    gate_out = product(normed_two_low, w_gate)
    up_out = product(normed_two_low, w_up)
    hidden = (jax.nn.silu(gate_out) * up_out).astype(jnp.bfloat16)
    output = (residual_mid + product(hidden, w_down)).astype(jnp.bfloat16)
    grad_out = cotangent.astype(jnp.float32)
    down_grad = product_left(hidden, cotangent)
    hidden_grad = product_right(cotangent, w_down)
    gate_sigma = jax.nn.sigmoid(gate_out)
    gate_grad_low = (
        hidden_grad * up_out * gate_sigma * (1.0 + gate_out * (1.0 - gate_sigma))
    ).astype(jnp.bfloat16)
    up_grad_low = (hidden_grad * jax.nn.silu(gate_out)).astype(jnp.bfloat16)
    gate_grad = product_left(normed_two_low, gate_grad_low)
    up_grad = product_left(normed_two_low, up_grad_low)
    normed_two_grad = product_right(gate_grad_low, w_gate) + product_right(up_grad_low, w_up)
    mid_from_norm, gain_second_grad = norm_second_pull(normed_two_grad)
    residual_mid_grad = grad_out + mid_from_norm
    mid_low = residual_mid_grad.astype(jnp.bfloat16)
    out_grad = product_left(out_low, mid_low)
    out_normed_grad = product_right(mid_low, w_out).reshape(row_count, head_count, head_dim)
    mixed_grad, out_gain_grad = out_norm_pull(out_normed_grad)
    mixed_blocks = into_blocks(mixed_grad)
    pulled = jnp.einsum("nhcd,nhcf->nhdf", leading, mixed_blocks, precision=PRECISE)
    local_back = jnp.einsum("nhed,nhef->hdf", transit, pulled, precision=PRECISE)
    transit_turned = jnp.swapaxes(final_transit, 1, 2)

    def backward_turn(turn_index, incoming):
        return from_behind(advance(transit_turned, local_back, incoming), "seq", -1)

    end_grad = lax.fori_loop(0, lax.axis_size("seq") - 1, backward_turn, zero_state)

    def delta_local(query_in, key_in, value_in, strength_in):
        ending, outputs = lax.scan(
            jax.checkpoint(delta_step),
            start_state,
            (query_in, key_in, value_in, strength_in, persist),
        )
        return (outputs, ending)

    unused_out, delta_pull = jax.vjp(
        delta_local, query_blocks, key_blocks, value_blocks, strength_blocks
    )
    query_grad_blocks, key_grad_blocks, value_grad_blocks, strength_grad_blocks = delta_pull(
        (mixed_blocks, end_grad)
    )
    extended_grad, conv_grad = mixer_pull(
        (
            from_blocks(query_grad_blocks),
            from_blocks(key_grad_blocks),
            from_blocks(value_grad_blocks),
        )
    )
    rim_grad = from_behind(extended_grad[: CONV - 1], "seq", -1)
    projected_grad = jnp.concatenate(
        [extended_grad[CONV - 1 : row_count], extended_grad[row_count:] + rim_grad], axis=0
    ).astype(jnp.bfloat16)
    strength_grad = strength_grad_blocks.transpose(0, 2, 1).reshape(row_count, head_count)
    logits_grad = (strength_grad * pad_rows * sigma_vals * (1.0 - sigma_vals)).astype(jnp.bfloat16)
    part_query = projected_grad[:, :features]
    part_key = projected_grad[:, features : 2 * features]
    part_value = projected_grad[:, 2 * features :]
    query_grad = product_left(normed_low, part_query)
    key_grad = product_left(normed_low, part_key)
    value_grad = product_left(normed_low, part_value)
    beta_grad = product_left(normed_low, logits_grad)
    normed_grad = (
        product_right(part_query, w_query)
        + product_right(part_key, w_key)
        + product_right(part_value, w_value)
        + product_right(logits_grad, beta_weight)
    )
    input_from_norm, gain_first_grad = norm_first_pull(normed_grad)
    tokens_grad = residual_mid_grad + input_from_norm
    (
        shard_q,
        shard_k,
        shard_v,
        shard_o,
        shard_conv,
        shard_gain_one,
        shard_gate,
        shard_up,
        shard_down,
        shard_gain_two,
    ) = (
        lax.psum_scatter(query_grad, ("dp", "seq"), scatter_dimension=0, tiled=True),
        lax.psum_scatter(key_grad, ("dp", "seq"), scatter_dimension=0, tiled=True),
        lax.psum_scatter(value_grad, ("dp", "seq"), scatter_dimension=0, tiled=True),
        lax.psum_scatter(out_grad, ("dp", "seq"), scatter_dimension=0, tiled=True),
        lax.psum_scatter(conv_grad, ("dp", "seq"), scatter_dimension=2, tiled=True),
        lax.psum_scatter(gain_first_grad, ("dp", "seq"), scatter_dimension=0, tiled=True),
        lax.psum_scatter(gate_grad, ("dp", "seq"), scatter_dimension=0, tiled=True),
        lax.psum_scatter(up_grad, ("dp", "seq"), scatter_dimension=0, tiled=True),
        lax.psum_scatter(down_grad, ("dp", "seq"), scatter_dimension=1, tiled=True),
        lax.psum_scatter(gain_second_grad, ("dp", "seq"), scatter_dimension=0, tiled=True),
    )
    beta_total, out_gain_total = lax.psum((beta_grad, out_gain_grad), ("dp", "seq"))
    return (
        output,
        tokens_grad,
        shard_gain_one,
        shard_q,
        shard_k,
        shard_v,
        shard_conv,
        beta_total,
        out_gain_total,
        shard_o,
        shard_gain_two,
        shard_gate,
        shard_up,
        shard_down,
    )


F32 = jnp.float32
BF = jnp.bfloat16
NN=(((1,),(0,)),((),())); NT=(((1,),(1,)),((),())); TN=(((0,),(0,)),((),()))

def mm(a,b,dims=NN):
    return lax.dot_general(a,b,dims,preferred_element_type=F32)

def halves(a):
    high=a.astype(BF)
    return high,(a-high.astype(F32)).astype(BF)

def mm_lw(a,b,dims=NN):
    high,low=halves(b)
    return mm(a,high,dims)+mm(a,low,dims)

def mm_wl(a,b,dims=NN):
    high,low=halves(a)
    return mm(high,b,dims)+mm(low,b,dims)

def mm_ww(a,b,dims=NN):
    ah,al=halves(a); bh,bl=halves(b)
    return mm(ah,bh,dims)+(mm(al,bh,dims)+mm(ah,bl,dims))

def tile_masks(tile):
    row=lax.broadcasted_iota(jnp.int32,(tile,tile),0)
    col=lax.broadcasted_iota(jnp.int32,(tile,tile),1)
    return row,col


MESH = pl.DeviceIdType.MESH
ANY = pl.BlockSpec(memory_space=pl.ANY)
VMEM = pl.BlockSpec(memory_space=pltpu.VMEM)


def flipped(index, bit):
    size = 2**bit
    return index + (1 - 2 * ((index // size) % 2)) * size


def greet(peers):
    barrier = pltpu.get_barrier_semaphore()
    for axis, peer in peers:
        pl.semaphore_signal(barrier, inc=1, device_id={axis: peer}, device_id_type=MESH)
    pl.semaphore_wait(barrier, len(peers))


def others(axis, count):
    me = lax.axis_index(axis)
    return [(axis, lax.rem(me + step, count)) for step in range(1, count)]


def send(source, target, sends, recvs, slot, axis, peer):
    copy = pltpu.make_async_remote_copy(
        src_ref=source,
        dst_ref=target,
        send_sem=sends.at[slot],
        recv_sem=recvs.at[slot],
        device_id={axis: peer},
        device_id_type=MESH,
    )
    copy.start()
    return copy


def span(size, index, axis):
    piece = pl.ds(pl.multiple_of(index * size, size), size)
    return (piece, slice(None)) if axis == 0 else (slice(None), piece)


def start_exchange(pieces, count, sends, recvs, local, first=0):
    me = lax.axis_index("seq")
    started = []
    for number, (source, source_at, target, target_at) in enumerate(pieces):
        own = pltpu.make_async_copy(
            source.at[source_at(me)], target.at[target_at(me)], local.at[first // count + number]
        )
        own.start()
        started.append(own)
        for step in range(1, count):
            peer = lax.rem(me + step, count)
            slot = first + number * count + step
            started.append(
                send(
                    source.at[source_at(peer)], target.at[target_at(me)],
                    sends, recvs, slot, "seq", peer,
                )
            )
    return started


def wait_all(copies):
    for copy in copies:
        copy.wait()


def bit_orders(count):
    bits = list(range(count.bit_length() - 1))[::-1]
    other = bits[:]
    if len(bits) >= 3:
        other[0], other[1] = bits[1], bits[0]
    return [bits, other]


class Gather:
    def __init__(self, count, source, target, axis, sends, recvs, local, slot, local_slot):
        self.count, self.source, self.target, self.axis = count, source, target, axis
        self.sends, self.recvs, self.local = sends, recvs, local
        self.slot, self.local_slot = slot, local_slot
        self.me = lax.axis_index("seq")
        self.copies = {}

    def piece(self, owner, half):
        rows, columns = self.source.shape
        part = rows // 2
        if self.axis == 0:
            return (pl.ds(pl.multiple_of(owner * rows + half * part, part), part), slice(None))
        return (
            pl.ds(half * part, part),
            pl.ds(pl.multiple_of(owner * columns, columns), columns),
        )

    def put(self, order, half, turn, known):
        owner = self.me
        for bit in known:
            owner = flipped(owner, bit)
        place = self.target.at[self.piece(owner, half)]
        part = self.source.shape[0] // 2
        source = place if known else self.source.at[pl.ds(half * part, part)]
        slot = self.slot + half * self.count + self.number(order, turn, known)
        self.copies[half, turn, known] = send(
            source, place, self.sends, self.recvs, slot, "seq", flipped(self.me, order[turn])
        )

    def number(self, order, turn, known):
        return 2**turn + sum(2 ** order.index(bit) for bit in known)

    def start(self):
        self.start_own()
        for half in range(2):
            self.start_half(half)

    def start_own(self):
        self.own = pltpu.make_async_copy(
            self.source,
            self.target.at[
                span(self.source.shape[self.axis], self.me, self.axis)
            ],
            self.local.at[self.local_slot],
        )
        self.own.start()

    def start_half(self, half):
        order = bit_orders(self.count)[half]
        for turn in range(len(order)):
            self.put(order, half, turn, ())

    def turns(self):
        return self.count.bit_length() - 1

    def forward(self, turn):
        orders = bit_orders(self.count)
        for before in range(2**turn):
            for half, order in enumerate(orders):
                known = tuple(order[i] for i in range(turn) if before // 2**i % 2)
                self.copies[half, turn, known].wait_recv()
                for later in range(turn + 1, len(order)):
                    self.put(order, half, later, known + (order[turn],))

    def finish(self):
        for copy in self.copies.values():
            copy.wait_send()
        self.own.wait()


class LineGather:
    def __init__(self, depth, source, target, chunks, sems, local):
        self.depth, self.source, self.target, self.chunks = depth, source, target, chunks
        self.sems, self.local = sems, local
        self.level = lax.axis_index("dp")
        self.rows = target.shape[0] // depth

    def copy(self, block, chunk, distance, up, source=None):
        part = self.rows // self.chunks
        at = pl.multiple_of(block * self.rows + chunk * part, part)
        place = self.target.at[pl.ds(at, part)]
        way = 0 if up else 2
        return pltpu.make_async_remote_copy(
            src_ref=place if source is None else source.at[pl.ds(chunk * part, part)],
            dst_ref=place,
            send_sem=self.sems.at[way, distance * self.chunks + chunk],
            recv_sem=self.sems.at[way + 1, distance * self.chunks + chunk],
            device_id={"dp": self.level + 1 if up else self.level - 1},
            device_id_type=MESH,
        )

    def start(self):
        level = self.level
        for chunk in range(self.chunks):

            @pl.when(level < self.depth - 1)
            def up():
                self.copy(level, chunk, 0, True, self.source).start()

            @pl.when(level > 0)
            def down():
                self.copy(level, chunk, 0, False, self.source).start()

        if self.source is not None:
            self.own = pltpu.make_async_copy(
                self.source,
                self.target.at[pl.ds(pl.multiple_of(level * self.rows, self.rows), self.rows)],
                self.local,
            )
            self.own.start()

    def forward(self, distance, chunks=None):
        level, last = self.level, self.depth - 1
        for chunk in range(self.chunks) if chunks is None else chunks:

            @pl.when(level - distance >= 0)
            def from_below():
                self.copy(level - distance, chunk, distance - 1, True).wait_recv()

                @pl.when(level < last)
                def hand_on():
                    self.copy(level - distance, chunk, distance, True).start()

            @pl.when(level + distance <= last)
            def from_above():
                self.copy(level + distance, chunk, distance - 1, False).wait_recv()

                @pl.when(level > 0)
                def hand_on():
                    self.copy(level + distance, chunk, distance, False).start()

    def finish(self):
        level, last = self.level, self.depth - 1
        for distance in range(last):
            for chunk in range(self.chunks):

                @pl.when((level - distance >= 0) & (level < last))
                def up():
                    self.copy(level - distance, chunk, distance, True).wait_send()

                @pl.when((level + distance <= last) & (level > 0))
                def down():
                    self.copy(level + distance, chunk, distance, False).wait_send()

        if self.source is not None:
            self.own.wait()


def hypercube_peers(count):
    me = lax.axis_index("seq")
    return [("seq", flipped(me, bit)) for bit in range(count.bit_length() - 1)]


def comm_params(identity, limit=48):
    return pltpu.CompilerParams(
        collective_id=identity, has_side_effects=True, vmem_limit_bytes=limit * 2**20
    )


def start_kernel(
    count, depth, main, gain_one, gain_two, taps, pad, starts, x_ref, wq, wk, wv, wo, gate, up, down,
    small_all, mixer, pair, last, normed_full,
    small, gain, normed, tails, pair_rest, down_rest, sends, recvs, local, gather_sends, gather_recvs, far,
    mixer_sends, mixer_recvs, mixer_local, line_sems, tail_sems,
):
    rest = gate.shape[1] // count - main
    loads = [
        pltpu.make_async_copy(weight.at[:, main * count :], tails.at[i], tail_sems.at[i])
        for i, weight in enumerate((gate, up, down))
    ]
    for load in loads:
        load.start()
    greet(others("seq", count) + others("dp", depth))
    me, level = lax.axis_index("seq"), lax.axis_index("dp")
    mine, height = wq.shape[1] // count, wq.shape[0]
    small[...] = jnp.zeros(small.shape, F32)
    owned, features = gain_one.shape[1], x_ref.shape[1]
    for member in range(3):
        small[member * CONV : (member + 1) * CONV, 0:owned] = taps[member].astype(F32)
    at = 3 * CONV
    for row, source in enumerate((gain_one, gain_two, pad, starts)):
        small[at + row : at + row + 1, 0 : source.shape[1]] = source[...].astype(F32)
    place = me * depth + level
    small_all[place] = small[...]
    levels = [
        send(
            small, small_all.at[place], far.at[0], far.at[1], step, "dp", lax.rem(level + step, depth)
        )
        for step in range(1, depth)
    ]
    first_exchange = start_exchange(
        [
            (
                weight,
                lambda i: span(mine, i, 1),
                mixer,
                lambda i, member=member: (
                    pl.ds(pl.multiple_of((level * count + i) * height, height), height),
                    slice(member * mine, (member + 1) * mine),
                ),
            )
            for member, weight in enumerate((wq, wk, wv, wo))
        ],
        count, mixer_sends, mixer_recvs, mixer_local,
    )
    wait_all(levels)
    block = small_all.at[pl.ds(me * depth, depth)]
    copies = [
        send(block, block, far.at[2], far.at[3], step, "seq", lax.rem(me + step, count))
        for step in range(1, count)
    ]
    wait_all(first_exchange)
    line = LineGather(depth, None, mixer, 2, line_sems, None)
    line.start()
    for load in loads:
        load.wait()
    lane = lax.broadcasted_iota(jnp.int32, (1, 128), 1)
    half = height // 2
    for i in range(count):
        tile = slice(i // 2 * 128, (i // 2 + 1) * 128)
        gate_tile, up_tile, down_tile = (tails[j, :, tile].astype(F32) for j in range(3))
        if i % 2:
            gate_tile = pltpu.roll(gate_tile, rest, 1)
            top, bottom = pltpu.roll(down_tile[:half], rest, 1), down_tile[half:]
        else:
            up_tile = pltpu.roll(up_tile, rest, 1)
            top, bottom = down_tile[:half], pltpu.roll(down_tile[half:], rest, 1)
        there = slice(i * 128, (i + 1) * 128)
        pair_rest[:, there] = jnp.where(lane < rest, gate_tile, up_tile).astype(BF)
        down_rest[:, there] = jnp.where(lane < rest, top, bottom).astype(BF)
    wait_all(copies)
    per = 128 // owned
    for tile in range(features // 128):
        row = jnp.zeros((1, 128), F32)
        for part in range(per):
            owner = tile * per + part
            piece = small_all[owner % count * depth + owner // count, at : at + 1, :]
            row = row + (pltpu.roll(piece, part * owned, 1) if part else piece)
        gain[0:1, tile * 128 : (tile + 1) * 128] = row
    for first in range(0, x_ref.shape[0], 16):
        part = slice(first, first + 16)
        value = x_ref[part, :].astype(F32)
        scale = lax.rsqrt(jnp.mean(value * value, axis=1, keepdims=True) + EPSILON)
        normed[part, :] = (value * scale * gain[0:1, :]).astype(BF)
    pieces = [
        (
            source,
            lambda i, size=size: span(size, i, 1),
            pair,
            lambda i, size=size, at=at: (i, slice(None), slice(at, at + size)),
        )
        for source, size, at in ((gate, main, 0), (up, main, main), (pair_rest, 128, 2 * main))
    ]
    for tile in range(main // 128):
        pieces.append(
            (
                down,
                lambda i, tile=tile: (
                    slice(None), pl.ds(pl.multiple_of(i * main + tile * 128, 128), 128)
                ),
                last,
                lambda i, tile=tile: span(height, tile * count + i, 0),
            )
        )
    pieces.append(
        (
            down_rest,
            lambda i: span(128, i, 1),
            last,
            lambda i: (
                pl.ds(pl.multiple_of(main // 128 * count * height + i * half, half), half),
                slice(None),
            ),
        )
    )
    gather = Gather(
        count, normed, normed_full, 0, gather_sends, gather_recvs, local, 0, len(pieces)
    )
    gather.start()
    exchange = start_exchange(pieces, count, sends, recvs, local)
    line.forward(1, (0,))
    gather.forward(0)
    line.forward(1, (1,))
    gather.forward(1)
    line.forward(2, (0,))
    for turn in range(2, gather.turns()):
        gather.forward(turn)
    line.forward(2, (1,))
    for distance in range(3, depth):
        line.forward(distance)
    gather.finish()
    wait_all(exchange)
    line.finish()


def start(count, depth, main, small, x, mixer, gate, up, down):
    rows = gate.shape[0]
    rest = gate.shape[1] // count - main
    slots = max(count, depth)
    members = 4 + main // 128
    shape = (3 * CONV + 4, max(128, x.shape[0]))
    whole = jax.ShapeDtypeStruct((x.shape[0] * count, x.shape[1]), BF)
    return pl.pallas_call(
        functools.partial(start_kernel, count, depth, main),
        out_shape=(
            jax.ShapeDtypeStruct((count * depth,) + shape, F32),
            jax.ShapeDtypeStruct((x.shape[1], 4 * x.shape[1] // count), BF),
            jax.ShapeDtypeStruct((count, rows, 2 * main + 128), BF),
            jax.ShapeDtypeStruct((count * rows * main // 128 + count * rows // 2, 128), BF),
            whole,
        ),
        in_specs=[VMEM] * 6 + [ANY] * 7,
        out_specs=(VMEM,) + (ANY,) * 4,
        scratch_shapes=[
            pltpu.VMEM(shape, F32),
            pltpu.VMEM((8, x.shape[1]), F32),
            pltpu.VMEM(x.shape, BF),
            pltpu.VMEM((3, rows, rest * count), BF),
            pltpu.VMEM((rows, 128 * count), BF),
            pltpu.VMEM((rows // 2, 128 * count), BF),
            pltpu.SemaphoreType.DMA((members * count,)),
            pltpu.SemaphoreType.DMA((members * count,)),
            pltpu.SemaphoreType.DMA((members + 1,)),
            pltpu.SemaphoreType.DMA((2 * count,)),
            pltpu.SemaphoreType.DMA((2 * count,)),
            pltpu.SemaphoreType.DMA((4, slots)),
            pltpu.SemaphoreType.DMA((4 * count,)),
            pltpu.SemaphoreType.DMA((4 * count,)),
            pltpu.SemaphoreType.DMA((4,)),
            pltpu.SemaphoreType.DMA((4, 2 * depth)),
            pltpu.SemaphoreType.DMA((3,)),
        ],
        compiler_params=comm_params(2, 60),
    )(*small, x, *mixer, gate, up, down)


def closing_kernel(count, sizes, *refs):
    sources, targets, (sends, recvs, local) = refs[: len(sizes)], refs[len(sizes) : -3], refs[-3:]
    greet(others("seq", count))
    wait_all(start_exchange(row_pieces(sources, targets, sizes, count), count, sends, recvs, local))


def closing(sources, count, sizes, identity):
    shapes = row_shapes(sources, sizes, count)
    members = len(shapes)
    return pl.pallas_call(
        functools.partial(closing_kernel, count, sizes),
        out_shape=shapes,
        in_specs=[ANY] * len(sources),
        out_specs=(ANY,) * members,
        scratch_shapes=[
            pltpu.SemaphoreType.DMA((members * count,)),
            pltpu.SemaphoreType.DMA((members * count,)),
            pltpu.SemaphoreType.DMA((members,)),
        ],
        compiler_params=comm_params(identity),
    )(*sources)


def sums_kernel(count, depth, sizes, plane_ref, level_ref, source, total_ref, each_ref, *refs):
    targets, scratch = refs[: len(sizes)], refs[len(sizes) :]
    plane_in, joined, level_in, sends, recvs, pass_sends, pass_recvs, local = scratch
    greet(others("seq", count) + others("dp", depth))
    me, level = lax.axis_index("seq"), lax.axis_index("dp")
    cut = plane_ref.shape[1]
    plane_in[me] = plane_ref[...]
    wait_all(
        [
            send(
                plane_ref, plane_in.at[me], sends.at[0], recvs.at[0], step,
                "seq", lax.rem(me + step, count),
            )
            for step in range(1, count)
        ]
    )
    exchange = start_exchange(
        row_pieces([source], targets, [sizes], count), count, pass_sends, pass_recvs, local
    )
    value = plane_in[0]
    for i in range(1, count):
        value = value + plane_in[i]
    joined[:, 0:cut] = value
    joined[:, cut:] = level_ref[...]
    level_in[level] = joined[...]
    wait_all(
        [
            send(
                joined, level_in.at[level], sends.at[1], recvs.at[1], step,
                "dp", lax.rem(level + step, depth),
            )
            for step in range(1, depth)
        ]
    )
    value = level_in[0]
    for i in range(1, depth):
        value = value + level_in[i]
    total_ref[...] = value[:, 0:cut]
    joined[:, cut:] = value[:, cut:]
    each_ref[me] = value[:, cut:]
    wait_all(
        [
            send(
                joined.at[:, cut:], each_ref.at[me],
                sends.at[2], recvs.at[2], step, "seq", lax.rem(me + step, count),
            )
            for step in range(1, count)
        ]
    )
    wait_all(exchange)


def small_sums(plane, level, source, sizes, count, depth):
    shapes = row_shapes([source], [sizes], count)
    slots = max(count, depth)
    joined = (plane.shape[0], plane.shape[1] + level.shape[1])
    return pl.pallas_call(
        functools.partial(sums_kernel, count, depth, sizes),
        out_shape=(
            jax.ShapeDtypeStruct(plane.shape, F32),
            jax.ShapeDtypeStruct((count,) + level.shape, F32),
        )
        + shapes,
        in_specs=[VMEM, VMEM, ANY],
        out_specs=(VMEM, VMEM) + (ANY,) * len(shapes),
        scratch_shapes=[
            pltpu.VMEM((count,) + plane.shape, F32),
            pltpu.VMEM(joined, F32),
            pltpu.VMEM((depth,) + joined, F32),
            pltpu.SemaphoreType.DMA((3, slots)),
            pltpu.SemaphoreType.DMA((3, slots)),
            pltpu.SemaphoreType.DMA((len(sizes) * count,)),
            pltpu.SemaphoreType.DMA((len(sizes) * count,)),
            pltpu.SemaphoreType.DMA((len(sizes),)),
        ],
        compiler_params=comm_params(3),
    )(plane, level, source)


class Scatter:
    def __init__(self, count, part, out, landing, outgoing, total, sends, recvs):
        self.count, self.part, self.out = count, part, out
        self.landing, self.outgoing, self.total = landing, outgoing, total
        self.sends, self.recvs = sends, recvs
        self.me = lax.axis_index("seq")
        self.rows = out.shape[0] // 2
        self.bits = count.bit_length() - 1
        self.orders = [order[::-1] for order in bit_orders(count)]
        self.copies = {}

    def rows_of(self, known, half):
        owner = self.me
        for bit in known:
            owner = flipped(owner, bit)
        size = self.rows
        return pl.ds(pl.multiple_of(owner * 2 * size + half * size, size), size)

    def place(self, order, turn, known):
        later = order[turn + 1 :]
        before = sum(self.count >> (t + 1) for t in range(turn))
        return before + sum(2**i for i, bit in enumerate(later) if bit in known)

    def subsets(self, order, turn):
        later = order[turn + 1 :]
        sets = [
            tuple(later[i] for i in range(len(later)) if code // 2**i % 2)
            for code in range(2 ** len(later))
        ]
        return sorted(sets, key=lambda known: [-(bit in known) for bit in later])

    def put(self, half, turn, known, source):
        order = self.orders[half]
        place = self.place(order, turn, known)
        self.copies[half, turn, known] = send(
            source,
            self.landing.at[half, place],
            self.sends,
            self.recvs,
            half * self.count + place,
            "seq",
            flipped(self.me, order[turn]),
        )

    def start(self):
        for at in range(self.count // 2):
            for half, order in enumerate(self.orders):
                known = self.subsets(order, 0)[at]
                self.put(half, 0, known, self.part.at[self.rows_of((order[0],) + known, half)])

    def turn(self, turn):
        for at in range(2 ** (self.bits - turn - 1)):
            for half, order in enumerate(self.orders):
                known = self.subsets(order, turn)[at]
                place = self.place(order, turn, known)
                self.copies[half, turn, known].wait_recv()
                came = self.landing[half, place].astype(F32)
                if turn == 0:
                    value = self.part[self.rows_of(known, half), :].astype(F32) + came
                else:
                    value = self.total[half, self.kept(order, turn - 1, known)] + came
                if turn == self.bits - 1:
                    self.out[half * self.rows : (half + 1) * self.rows, :] = value
                elif order[turn + 1] in known:
                    rest = tuple(bit for bit in known if bit != order[turn + 1])
                    next_place = self.place(order, turn + 1, rest) - self.count // 2
                    self.outgoing[half, next_place] = value.astype(BF)
                    self.put(half, turn + 1, rest, self.outgoing.at[half, next_place])
                else:
                    self.total[half, self.kept(order, turn, known)] = value

    def kept(self, order, turn, known):
        return sum(2**i for i, bit in enumerate(order[turn + 2 :]) if bit in known)

    def finish(self):
        for copy in self.copies.values():
            copy.wait_send()


def scatter_scratch(count, rows, columns):
    half = rows // 2
    return [
        pltpu.VMEM((2, count - 1, half, columns), BF),
        pltpu.VMEM((2, count // 2 - 1, half, columns), BF),
        pltpu.VMEM((2, count // 4, half, columns), F32),
        pltpu.SemaphoreType.DMA((2 * count,)),
        pltpu.SemaphoreType.DMA((2 * count,)),
    ]


def shifted_sum(window, taps_ref, member, lanes, keep):
    length = window.shape[0] - 8
    row = lax.broadcasted_iota(jnp.int32, (length, 1), 0)
    shifts = [window[8:]]
    for lagged in range(1, CONV):
        moved = pltpu.roll(window, lagged, 0)[8:]
        shifts.append(moved * jnp.where(row >= lagged, 1.0, keep))
    summed = shifts[0] * taps_ref[member * CONV : member * CONV + 1, lanes]
    for lagged in range(1, CONV):
        at = member * CONV + lagged
        summed = summed + shifts[lagged] * taps_ref[at : at + 1, lanes]
    return summed, shifts


def front_kernel(
    count, heads, persist_ref, x_ref, beta_ref, taps_ref, pad_ref, gain_ref, mixer_ref, g_ref,
    pre_ref, q_ref, k_ref, v_ref, brow_ref, sigma_ref, mixed_ref, t_ref, wide_ref, s_ref, f_ref, a_ref,
    full_ref, rows_ref, g_full_ref,
    w_ref, pre_buf, logit_buf, u_buf, c_buf, on_buf, sends, recvs, local, gather_sends, gather_recvs,
):
    total, features = x_ref.shape
    mine = on_buf.shape[1]
    weight = pltpu.make_async_copy(mixer_ref.at[:, 0 : 3 * mine], w_ref, local.at[2])
    weight.start()
    hd = mine // heads
    blocks = total // BLOCK
    tile = 2 * BLOCK
    greet(others("seq", count))
    exchange = start_exchange(
        [
            (
                mixer_ref,
                lambda i: (pl.ds(pl.multiple_of(i * mine, mine), mine), slice(3 * mine, 4 * mine)),
                rows_ref,
                lambda i: span(mine, i, 1),
            )
        ],
        count, sends, recvs, local,
    )
    beside = Gather(
        count, g_ref, g_full_ref, 0, gather_sends, gather_recvs, local, 2 * count, 3
    )
    beside.start()
    pre_buf[0:8, :] = jnp.zeros((8, 3 * mine), F32)
    chunk = 4 * BLOCK
    weight.wait()

    def project(index, carry):
        rows = pl.ds(pl.multiple_of(index * chunk, chunk), chunk)
        x = x_ref[rows, :]
        low = mm(x, w_ref[...]).astype(BF)
        pre_ref[rows, :] = low
        pre_buf[pl.ds(pl.multiple_of(index * chunk + 8, 8), chunk), :] = low.astype(F32)
        logit_buf[rows, :] = mm(x, beta_ref[...])
        return carry

    lax.fori_loop(0, total // chunk, project, 0)

    def convolve(index, carry):
        keep = persist_ref[index]
        rows = pl.ds(pl.multiple_of(index * BLOCK, BLOCK), BLOCK)
        for member, target in enumerate((q_ref, k_ref, v_ref)):
            for h in range(heads):
                lanes = slice(h * hd, (h + 1) * hd)
                there = slice(member * mine + h * hd, member * mine + (h + 1) * hd)
                window = pre_buf[pl.ds(pl.multiple_of(index * BLOCK, 8), BLOCK + 8), there]
                summed, _ = shifted_sum(window, taps_ref, member, lanes, keep)
                value = summed * jax.nn.sigmoid(summed)
                if member < 2:
                    norm = jnp.sum(value * value, axis=1, keepdims=True) + EPSILON
                    value = value * lax.rsqrt(norm)
                if member == 0:
                    value = value * hd ** (-0.5)
                target[rows, lanes] = value.astype(BF)
        return carry

    lax.fori_loop(0, blocks, convolve, 0)
    beside.forward(0)
    row, col = tile_masks(tile)
    eyed = (
        lax.broadcasted_iota(jnp.int32, (hd, hd), 0) == lax.broadcasted_iota(jnp.int32, (hd, hd), 1)
    ).astype(F32)

    def first(step, carry):
        same = (row // BLOCK) == (col // BLOCK)
        eye = (row == col).astype(F32)
        chains = [(2 * step + i, h) for i in range(2) for h in range(heads)]
        ts, ls, ks, vs, bs = [], [], [], [], []
        for index, h in chains:
            rows = pl.ds(pl.multiple_of(index * tile, tile), tile)
            lanes = slice(h * hd, (h + 1) * hd)
            k = k_ref[rows, lanes]
            logit = jnp.sum(eye * logit_buf[rows, h : h + 1], axis=0, keepdims=True)
            sigma = jax.nn.sigmoid(logit)
            b = sigma * pad_ref[pl.ds(index, 1), :]
            sigma_ref[index, h : h + 1, :] = sigma
            brow_ref[index, h : h + 1, :] = b
            bcol = jnp.sum(eye * b, axis=1, keepdims=True)
            low = jnp.where(same & (row > col), mm(k, k, NT) * bcol, 0.0)
            ls.append(low)
            ks.append(k)
            vs.append(v_ref[rows, lanes])
            bs.append(b)
            ts.append(eye - jnp.where((row // 2) == (col // 2), low, 0.0))
        size = 2
        while size < BLOCK:
            cut = ((row // (2 * size)) == (col // (2 * size))) & ((row // size) != (col // size))
            mids = [mm_ww(jnp.where(cut, l, 0.0), t) for l, t in zip(ls, ts)]
            ts = [t - mm_ww(t, m) for t, m in zip(ts, mids)]
            size *= 2
        for at, (index, h) in enumerate(chains):
            rows = pl.ds(pl.multiple_of(index * tile, tile), tile)
            lanes = slice(h * hd, (h + 1) * hd)
            t_ref[h, rows, :] = ts[at]
            wu = mm_wl(ts[at] * bs[at], jnp.concatenate([ks[at], vs[at]], axis=1))
            wide_ref[rows, lanes] = wu[:, :hd]
            u_buf[rows, lanes] = wu[:, hd:]
            for part in range(2):
                sub = slice(part * BLOCK, (part + 1) * BLOCK)
                ab = mm_lw(ks[at][sub], wu[sub], TN)
                a_ref[h, index * 2 + part] = eyed - ab[:, :hd]
                c_buf[h, index * 2 + part] = ab[:, hd:]
        return carry

    lax.fori_loop(0, blocks // 4, first, 0)
    beside.forward(1)

    def chain(index, states):
        keep = persist_ref[index]
        new = []
        for h in range(heads):
            s = states[h] * keep
            s_ref[h, index] = s
            new.append(mm_ww(a_ref[h, index], s) + c_buf[h, index])
        return tuple(new)

    lax.fori_loop(0, blocks, chain, tuple(jnp.zeros((hd, hd), F32) for _ in range(heads)))

    def last(step, carry):
        lower_row, lower_col = tile_masks(BLOCK)
        for part in range(2):
            index = 2 * step + part
            rows = pl.ds(pl.multiple_of(index * BLOCK, BLOCK), BLOCK)
            for h in range(heads):
                lanes = slice(h * hd, (h + 1) * hd)
                q, k, s = q_ref[rows, lanes], k_ref[rows, lanes], s_ref[h, index]
                f = u_buf[rows, lanes] - mm_ww(wide_ref[rows, lanes], s)
                p = jnp.where(lower_row >= lower_col, mm(q, k, NT), 0.0)
                f_ref[rows, lanes] = f
                mixed = mm_lw(q, s) + mm_ww(p, f)
                mixed_ref[rows, lanes] = mixed
                scale = lax.rsqrt(jnp.mean(mixed * mixed, axis=1, keepdims=True) + EPSILON)
                on_buf[rows, lanes] = (mixed * scale * gain_ref[0:1, :]).astype(BF)
        return carry

    for turn in range(2, beside.turns()):
        beside.forward(turn)
    gather = Gather(count, on_buf, full_ref, 1, gather_sends, gather_recvs, local, 0, 1)
    lax.fori_loop(0, blocks // 4, last, 0)
    gather.start_half(0)
    lax.fori_loop(blocks // 4, blocks // 2, last, 0)
    gather.start_half(1)
    gather.start_own()
    for turn in range(gather.turns()):
        gather.forward(turn)
    gather.finish()
    beside.finish()
    wait_all(exchange)


def front(count, heads, persist, x, w_mixer, w_beta, taps, pad, gain, g):
    total, features = x.shape
    mine = w_mixer.shape[1] // 4
    hd = mine // heads
    blocks, tiles = total // BLOCK, total // (2 * BLOCK)
    wide = jax.ShapeDtypeStruct((total, mine), F32)
    low = jax.ShapeDtypeStruct((total, mine), BF)
    strength = jax.ShapeDtypeStruct((tiles, heads, 2 * BLOCK), F32)
    states = jax.ShapeDtypeStruct((heads, blocks, hd, hd), F32)
    return pl.pallas_call(
        functools.partial(front_kernel, count, heads),
        out_shape=(
            jax.ShapeDtypeStruct((total, 3 * mine), BF),
            low, low, low, strength, strength, wide,
            jax.ShapeDtypeStruct((heads, total, 2 * BLOCK), F32),
            wide, states, wide, states,
            jax.ShapeDtypeStruct((total, mine * count), BF),
            jax.ShapeDtypeStruct((mine, features), BF),
            jax.ShapeDtypeStruct((total, features), BF),
        ),
        in_specs=[
            pl.BlockSpec(memory_space=pltpu.SMEM),
            VMEM, VMEM, VMEM, VMEM, VMEM, ANY, ANY,
        ],
        out_specs=(VMEM,) * 12 + (ANY,) * 3,
        scratch_shapes=[
            pltpu.VMEM((features, 3 * mine), BF),
            pltpu.VMEM((total + 8, 3 * mine), F32),
            pltpu.VMEM((total, w_beta.shape[1]), F32),
            pltpu.VMEM((total, mine), F32),
            pltpu.VMEM((heads, blocks, hd, hd), F32),
            pltpu.VMEM((total, mine), BF),
            pltpu.SemaphoreType.DMA((count,)),
            pltpu.SemaphoreType.DMA((count,)),
            pltpu.SemaphoreType.DMA((4,)),
            pltpu.SemaphoreType.DMA((4 * count,)),
            pltpu.SemaphoreType.DMA((4 * count,)),
        ],
        compiler_params=comm_params(4, 52),
    )(persist, x, w_beta, taps, pad, gain, w_mixer, g)


def middle_kernel(
    count, full_ref, mixer_ref, x_ref, gain_ref, mid_ref, normed_ref,
    w_ref, staged, landed, low_buf, sends, recvs, local, gather_sends, gather_recvs,
):
    me = lax.axis_index("seq")
    rows, features = x_ref.shape
    mine = w_ref.shape[1]
    weight = pltpu.make_async_copy(mixer_ref.at[:, 3 * mine : 4 * mine], w_ref, local.at[2])
    weight.start()
    greet(others("seq", count))
    weight.wait()
    copies = []
    for step in list(range(1, count)) + [0]:
        peer = lax.rem(me + step, count)
        at = pl.ds(pl.multiple_of(peer * rows, rows), rows)
        staged[step] = mm(full_ref[at, :], w_ref[...])
        target = landed.at[span(mine, me, 1)]
        if step:
            copies.append(send(staged.at[step], target, sends, recvs, step, "seq", peer))
        else:
            own = pltpu.make_async_copy(staged.at[0], target, local.at[0])
            own.start()
            copies.append(own)
    wait_all(copies)
    for at in range(0, rows, 16):
        part = slice(at, at + 16)
        value = x_ref[part, :].astype(F32) + landed[part, :]
        mid_ref[part, :] = value
        scale = lax.rsqrt(jnp.mean(value * value, axis=1, keepdims=True) + EPSILON)
        low_buf[part, :] = (value * scale * gain_ref[0:1, :]).astype(BF)
    gather = Gather(count, low_buf, normed_ref, 0, gather_sends, gather_recvs, local, 0, 1)
    gather.start()
    for turn in range(gather.turns()):
        gather.forward(turn)
    gather.finish()


def middle(count, full, w_mixer, x, gain):
    rows, features = x.shape
    mine = w_mixer.shape[1] // 4
    return pl.pallas_call(
        functools.partial(middle_kernel, count),
        out_shape=(
            jax.ShapeDtypeStruct((rows, features), F32),
            jax.ShapeDtypeStruct((rows * count, features), BF),
        ),
        in_specs=[VMEM, ANY, VMEM, VMEM],
        out_specs=(VMEM, ANY),
        scratch_shapes=[
            pltpu.VMEM((features, mine), BF),
            pltpu.VMEM((count, rows, mine), F32),
            pltpu.VMEM((rows, features), F32),
            pltpu.VMEM((rows, features), BF),
            pltpu.SemaphoreType.DMA((count,)),
            pltpu.SemaphoreType.DMA((count,)),
            pltpu.SemaphoreType.DMA((3,)),
            pltpu.SemaphoreType.DMA((2 * count,)),
            pltpu.SemaphoreType.DMA((2 * count,)),
        ],
        compiler_params=comm_params(5),
    )(full, w_mixer, x, gain)


def norm_backward(value_ref, grad_ref, beside_ref, gain_ref, out_ref, gain_out, low_ref=None):
    rows, features = out_ref.shape
    gain_out[...] = jnp.zeros((8, features), F32)
    for at in range(0, rows, 8):
        part = slice(at, at + 8)
        value = value_ref[part, :].astype(F32)
        scale = lax.rsqrt(jnp.mean(value * value, axis=1, keepdims=True) + EPSILON)
        unit = value * scale
        grad = grad_ref[part, :]
        gain_out[...] += grad * unit
        scaled = grad * gain_ref[0:1, :]
        mean = jnp.mean(scaled * unit, axis=1, keepdims=True)
        result = beside_ref[part, :].astype(F32) + scale * (scaled - unit * mean)
        out_ref[part, :] = result
        if low_ref is not None:
            half = (at // 16) * 16
            if at % 16 == 8:
                low_ref[half : half + 16, :] = out_ref[half : half + 16, :].astype(BF)


def reduce_kernel(
    count, part_ref, mid_ref, g_ref, gain_ref, grad_ref, gain_out, full_ref,
    summed, low_buf, landing, outgoing, kept, sends, recvs, local, gather_sends, gather_recvs,
):
    greet(hypercube_peers(count))
    scatter = Scatter(count, part_ref, summed, landing, outgoing, kept, sends, recvs)
    scatter.start()
    for turn in range(scatter.bits):
        scatter.turn(turn)
    norm_backward(mid_ref, summed, g_ref, gain_ref, grad_ref, gain_out, low_buf)
    gather = Gather(count, low_buf, full_ref, 0, gather_sends, gather_recvs, local, 0, 0)
    gather.start()
    for turn in range(gather.turns()):
        gather.forward(turn)
    gather.finish()
    scatter.finish()


def reduce_middle(count, parts, mid, g, gain):
    rows, features = mid.shape
    return pl.pallas_call(
        functools.partial(reduce_kernel, count),
        out_shape=(
            jax.ShapeDtypeStruct((rows, features), F32),
            jax.ShapeDtypeStruct((8, features), F32),
            jax.ShapeDtypeStruct((rows * count, features), BF),
        ),
        in_specs=[VMEM] * 4,
        out_specs=(VMEM, VMEM, ANY),
        scratch_shapes=[pltpu.VMEM((rows, features), F32), pltpu.VMEM((rows, features), BF)]
        + scatter_scratch(count, rows, features)
        + [
            pltpu.SemaphoreType.DMA((1,)),
            pltpu.SemaphoreType.DMA((2 * count,)),
            pltpu.SemaphoreType.DMA((2 * count,)),
        ],
        compiler_params=comm_params(6),
    )(parts, mid, g, gain)


def back_kernel(
    count, heads, persist_ref, full_ref, rows_ref, mixed_ref, gain_ref, taps_ref, pre_ref, q_ref, k_ref, v_ref,
    brow_ref, sigma_ref, pad_ref, t_ref, wide_ref, s_ref, f_ref, a_ref, done_ref,
    dpre_ref, taps_out, gain_out, main_ref, ends_ref, *scratch,
):
    total, mine = mixed_ref.shape
    hd = mine // heads
    blocks = total // BLOCK
    beta_lanes = dpre_ref.shape[1] - 3 * mine
    do_buf, y_buf, c_buf, g_buf, pre_buf, conv_buf, pass_sends, pass_recvs, local = scratch
    greet(others("seq", count))
    exchange = start_exchange(
        folded_pieces(done_ref, main_ref, ends_ref, count), count, pass_sends, pass_recvs, local
    )
    gain_out[...] = jnp.zeros((8, hd), F32)
    taps_out[...] = jnp.zeros((3 * CONV, 8, mine), F32)
    pre_buf[0:8, :] = jnp.zeros((8, 3 * mine), F32)
    conv_buf[total : total + 8, :] = jnp.zeros((8, 3 * mine), F32)
    chunk = 4 * BLOCK

    def heads_in(index, carry):
        rows = pl.ds(pl.multiple_of(index * chunk, chunk), chunk)
        pre_buf[pl.ds(pl.multiple_of(index * chunk + 8, 8), chunk), :] = pre_ref[rows, :].astype(F32)
        grad = mm(full_ref[rows, :], rows_ref[...], NT)
        for h in range(heads):
            lanes = slice(h * hd, (h + 1) * hd)
            mixed, don = mixed_ref[rows, lanes], grad[:, lanes]
            scale = lax.rsqrt(jnp.mean(mixed * mixed, axis=1, keepdims=True) + EPSILON)
            unit = mixed * scale
            gain_out[...] += jnp.sum((don * unit).reshape(chunk // 8, 8, hd), axis=0)
            scaled = don * gain_ref[0:1, :]
            mean = jnp.mean(scaled * unit, axis=1, keepdims=True)
            do_buf[rows, lanes] = scale * (scaled - unit * mean)
        return carry

    lax.fori_loop(0, total // chunk, heads_in, 0)
    row, col = tile_masks(BLOCK)

    def first(step, carry):
        for part in range(2):
            index = 2 * step + part
            rows = pl.ds(pl.multiple_of(index * BLOCK, BLOCK), BLOCK)
            for h in range(heads):
                lanes = slice(h * hd, (h + 1) * hd)
                q, k, do = q_ref[rows, lanes], k_ref[rows, lanes], do_buf[rows, lanes]
                p = jnp.where(row >= col, mm(q, k, NT), 0.0)
                y = mm_ww(p, do, TN)
                y_buf[rows, lanes] = y
                c_buf[h, index] = mm_lw(q, do, TN) - mm_ww(wide_ref[rows, lanes], y, TN)
        return carry

    lax.fori_loop(0, blocks // 2, first, 0)

    def chain(step, grads):
        index = blocks - 1 - step
        keep = persist_ref[index]
        new = []
        for h in range(heads):
            g = grads[h]
            g_buf[h, index] = g
            new.append((mm_ww(a_ref[h, index], g, TN) + c_buf[h, index]) * keep)
        return tuple(new)

    lax.fori_loop(0, blocks, chain, tuple(jnp.zeros((hd, hd), F32) for _ in range(heads)))

    def last(step, carry):
        for part in range(2):
            index = 2 * step + part
            keep = persist_ref[index]
            rows = pl.ds(pl.multiple_of(index * BLOCK, BLOCK), BLOCK)
            half = slice(part * BLOCK, (part + 1) * BLOCK)
            lane = lax.broadcasted_iota(jnp.int32, (BLOCK, beta_lanes), 1)
            dlogits = jnp.zeros((BLOCK, beta_lanes), F32)
            for h in range(heads):
                lanes = slice(h * hd, (h + 1) * hd)
                q, k, v = q_ref[rows, lanes], k_ref[rows, lanes], v_ref[rows, lanes]
                do, s, f, g = do_buf[rows, lanes], s_ref[h, index], f_ref[rows, lanes], g_buf[h, index]
                b = brow_ref[step, h : h + 1, half]
                bcol = jnp.sum(jnp.where(row == col, b, 0.0), axis=1, keepdims=True)
                t = t_ref[h, rows, half]
                df = y_buf[rows, lanes] + mm_lw(k, g)
                dr = mm_ww(t, df, TN)
                dp = jnp.where(row >= col, mm_ww(do, f, NT), 0.0)
                dl = jnp.where(row > col, -mm_ww(dr, f, NT), 0.0)
                dq = mm_ww(do, s, NT) + mm_wl(dp, k)
                dkb = mm_wl(dl, k) - mm_ww(dr, s, NT)
                dk = mm_wl(dp, q, TN) + mm_ww(f, g, NT) + mm_wl(dl * bcol, k, TN) + bcol * dkb
                dbeta = jnp.sum(dr * v.astype(F32) + dkb * k.astype(F32), axis=1, keepdims=True)
                sigma = sigma_ref[step, h : h + 1, half]
                slope = pad_ref[pl.ds(step, 1), half] * sigma * (1.0 - sigma)
                slope = jnp.sum(jnp.where(row == col, slope, 0.0), axis=1, keepdims=True)
                dlogits = jnp.where(lane == h, dbeta * slope, dlogits)
                for member, grad in enumerate((dq, dk, bcol * dr)):
                    there = slice(member * mine + h * hd, member * mine + (h + 1) * hd)
                    window = pre_buf[pl.ds(pl.multiple_of(index * BLOCK, 8), BLOCK + 8), there]
                    summed, shifts = shifted_sum(window, taps_ref, member, lanes, keep)
                    sigma = jax.nn.sigmoid(summed)
                    if member < 2:
                        value = summed * sigma
                        inverse = lax.rsqrt(jnp.sum(value * value, axis=1, keepdims=True) + EPSILON)
                        unit = value * inverse
                        along = jnp.sum(grad * unit, axis=1, keepdims=True)
                        grad = (grad - unit * along) * inverse
                    if member == 0:
                        grad = grad * hd ** (-0.5)
                    grad = grad * (sigma * (1.0 + summed * (1.0 - sigma)))
                    conv_buf[rows, there] = grad
                    for lagged in range(CONV):
                        taps_out[member * CONV + lagged, :, lanes] += jnp.sum(
                            (grad * shifts[lagged]).reshape(BLOCK // 8, 8, hd), axis=0
                        )
            dpre_ref[rows, 3 * mine :] = dlogits.astype(BF)
        return carry

    lax.fori_loop(0, blocks // 2, last, 0)

    def spread(index, carry):
        rows = pl.ds(pl.multiple_of(index * BLOCK, BLOCK), BLOCK)
        keep = persist_ref[jnp.minimum(index + 1, blocks - 1)]
        block_row = lax.broadcasted_iota(jnp.int32, (BLOCK, 1), 0)
        for member in range(3):
            there = slice(member * mine, (member + 1) * mine)
            window = conv_buf[pl.ds(pl.multiple_of(index * BLOCK, 8), BLOCK + 8), there]
            summed = window[:BLOCK] * taps_ref[member * CONV : member * CONV + 1, :]
            for lagged in range(1, CONV):
                at = member * CONV + lagged
                moved = pltpu.roll(window, BLOCK + 8 - lagged, 0)[:BLOCK]
                moved = moved * jnp.where(block_row < BLOCK - lagged, 1.0, keep)
                summed = summed + moved * taps_ref[at : at + 1, :]
            dpre_ref[rows, there] = summed.astype(BF)
        return carry

    lax.fori_loop(0, blocks, spread, 0)
    wait_all(exchange)


def back(
    count, heads, persist, full, w_rows, mixed, gain, taps, pre, q, k, v, strength, saved, done, main
):
    total, mine = mixed.shape
    hd = mine // heads
    blocks = total // BLOCK
    owned = done.shape[0] // (count * main // 128 + count // 2)
    members = main // 128 + 1
    return pl.pallas_call(
        functools.partial(back_kernel, count, heads),
        out_shape=(
            jax.ShapeDtypeStruct((total, 3 * mine + 128), BF),
            jax.ShapeDtypeStruct((3 * CONV, 8, mine), F32),
            jax.ShapeDtypeStruct((8, hd), F32),
            jax.ShapeDtypeStruct((owned, count * main), BF),
            jax.ShapeDtypeStruct((owned // 2, count * 128), BF),
        ),
        in_specs=[pl.BlockSpec(memory_space=pltpu.SMEM)] + [VMEM] * 17 + [ANY],
        out_specs=(VMEM,) * 3 + (ANY,) * 2,
        scratch_shapes=[
            pltpu.VMEM((total, mine), F32),
            pltpu.VMEM((total, mine), F32),
            pltpu.VMEM((heads, blocks, hd, hd), F32),
            pltpu.VMEM((heads, blocks, hd, hd), F32),
            pltpu.VMEM((total + 8, 3 * mine), F32),
            pltpu.VMEM((total + 8, 3 * mine), F32),
            pltpu.SemaphoreType.DMA((members * count,)),
            pltpu.SemaphoreType.DMA((members * count,)),
            pltpu.SemaphoreType.DMA((members,)),
        ],
        compiler_params=comm_params(7, 56),
    )(persist, full, w_rows, mixed, gain, taps, pre, q, k, v, *strength, *saved, done)


def end_kernel(
    count, part_ref, added_ref, x_ref, mid_ref, beside_ref, gain_ref,
    grad_ref, gain_out, out_ref, summed, added, *scratch
):
    greet(hypercube_peers(count))
    scatter = Scatter(count, part_ref, summed, *scratch[:5])
    beside = Scatter(count, added_ref, added, *scratch[5:])
    scatter.start()
    beside.start()
    for turn in range(scatter.bits):
        scatter.turn(turn)
        beside.turn(turn)
    norm_backward(x_ref, summed, beside_ref, gain_ref, grad_ref, gain_out)
    for at in range(0, out_ref.shape[0], 16):
        part = slice(at, at + 16)
        out_ref[part, :] = (mid_ref[part, :] + added[part, :]).astype(BF)
    scatter.finish()
    beside.finish()


def folded_pieces(source, main_ref, ends_ref, count):
    main = main_ref.shape[1] // count
    rows, half = main_ref.shape[0], ends_ref.shape[0]
    pieces = []
    for tile in range(main // 128):
        pieces.append(
            (
                source,
                lambda i, tile=tile: span(rows, tile * count + i, 0),
                main_ref,
                lambda i, tile=tile: (
                    slice(None), pl.ds(pl.multiple_of(i * main + tile * 128, 128), 128)
                ),
            )
        )
    pieces.append(
        (
            source,
            lambda i: (
                pl.ds(pl.multiple_of(main // 128 * count * rows + i * half, half), half),
                slice(None),
            ),
            ends_ref,
            lambda i: span(128, i, 1),
        )
    )
    return pieces


def row_pieces(sources, targets, sizes, count):
    pieces = []
    for source, widths in zip(sources, sizes):
        rows, at = source.shape[0] // count, 0
        for size in widths:
            pieces.append(
                (
                    source,
                    lambda i, rows=rows, at=at, size=size: (
                        pl.ds(pl.multiple_of(i * rows, rows), rows),
                        slice(at, at + size),
                    ),
                    targets[len(pieces)],
                    lambda i, size=size: span(size, i, 1),
                )
            )
            at += size
    return pieces


def row_shapes(sources, sizes, count):
    return tuple(
        jax.ShapeDtypeStruct((source.shape[0] // count, count * size), BF)
        for source, widths in zip(sources, sizes)
        for size in widths
    )


def end(count, parts, added, x, mid, beside, gain):
    rows, features = x.shape
    return pl.pallas_call(
        functools.partial(end_kernel, count),
        out_shape=(
            jax.ShapeDtypeStruct((rows, features), F32),
            jax.ShapeDtypeStruct((8, features), F32),
            jax.ShapeDtypeStruct((rows, features), BF),
        ),
        in_specs=[VMEM] * 6,
        out_specs=(VMEM,) * 3,
        scratch_shapes=[pltpu.VMEM((rows, features), F32)] * 2
        + scatter_scratch(count, rows, features)
        + scatter_scratch(count, rows, features),
        compiler_params=comm_params(8),
    )(parts, added, x, mid, beside, gain)


def hidden_grads_kernel(count, rest, g_ref, pair_ref, down_ref, low_ref, w_ref):
    main = w_ref.shape[1] - 128
    lane = lax.broadcasted_iota(jnp.int32, (1, 128), 1)

    @pl.when(pl.program_id(0) == 0)
    def assemble():
        depth = down_ref.shape[0]
        level = w_ref.shape[0] // depth
        rows = level // count
        for z in range(depth):
            at = z * level
            for tile in range(main // 128):
                w_ref[at : at + level, tile * 128 : (tile + 1) * 128] = down_ref[
                    z, tile * level : (tile + 1) * level, :
                ]
            for i in range(count):
                start = main // 128 * level + i * (rows // 2)
                pair = down_ref[z, start : start + rows // 2, :].astype(F32)
                for part in range(2):
                    piece = pair if part == 0 else pltpu.roll(pair, rest, 1)
                    first = at + i * rows + part * (rows // 2)
                    w_ref[first : first + rows // 2, main:] = jnp.where(
                        lane < rest, piece, 0.0
                    ).astype(BF)

    grad = mm(g_ref[...], w_ref[...])

    def slopes(gate, up, grad):
        sigma = jax.nn.sigmoid(gate)
        return grad * up * sigma * (1.0 + gate * (1.0 - sigma)), grad * (gate * sigma)

    dgate, dup = slopes(pair_ref[:, :main], pair_ref[:, main : 2 * main], grad[:, :main])
    low_ref[:, :main] = dgate.astype(BF)
    low_ref[:, main : 2 * main] = dup.astype(BF)
    tail = pair_ref[:, 2 * main :]
    dgate, dup = slopes(tail, pltpu.roll(tail, rest, 1), grad[:, main:])
    low_ref[:, 2 * main :] = jnp.where(lane < rest, dgate, pltpu.roll(dup, rest, 1)).astype(BF)


def hidden_gradients(count, rest, g, pair, down):
    total, features = g.shape
    main = (pair.shape[1] - 2 * rest) // 2
    step = total // 4
    return pl.pallas_call(
        functools.partial(hidden_grads_kernel, count, rest),
        grid=(total // step,),
        out_shape=(
            jax.ShapeDtypeStruct(pair.shape, BF),
            jax.ShapeDtypeStruct((features, main + 128), BF),
        ),
        in_specs=[
            pl.BlockSpec((step, features), lambda i: (i, 0)),
            pl.BlockSpec((step, pair.shape[1]), lambda i: (i, 0)),
            pl.BlockSpec(down.shape, lambda i: (0, 0, 0)),
        ],
        out_specs=(
            pl.BlockSpec((step, pair.shape[1]), lambda i: (i, 0)),
            pl.BlockSpec((features, main + 128), lambda i: (0, 0)),
        ),
        compiler_params=pltpu.CompilerParams(vmem_limit_bytes=40 * 2**20),
        cost_estimate=pl.CostEstimate(
            flops=2 * total * features * (main + 128),
            bytes_accessed=2 * total * features + 6 * total * pair.shape[1],
            transcendentals=total * pair.shape[1] // 2,
        ),
    )(g, pair, down)


def down_grads_kernel(count, rest, g_ref, hidden_ref, out_ref):
    grad = mm(g_ref[...], hidden_ref[...], TN)
    level = grad.shape[0]
    main = grad.shape[1] - 128
    rows = level // count
    lane = lax.broadcasted_iota(jnp.int32, (1, 128), 1)
    for tile in range(main // 128):
        out_ref[tile * level : (tile + 1) * level, :] = grad[:, tile * 128 : (tile + 1) * 128].astype(BF)
    for i in range(count):
        at = i * rows
        front = grad[at : at + rows // 2, main:]
        later = pltpu.roll(grad[at + rows // 2 : at + rows, main:], rest, 1)
        start = main // 128 * level + i * (rows // 2)
        out_ref[start : start + rows // 2, :] = jnp.where(lane < rest, front, later).astype(BF)


def down_gradients(count, depth, rest, g, hidden):
    total, features = g.shape
    width = hidden.shape[1]
    level = features // depth
    high = (width - 128) // 128 * level + level // 2
    return pl.pallas_call(
        functools.partial(down_grads_kernel, count, rest),
        grid=(depth,),
        out_shape=jax.ShapeDtypeStruct((depth * high, 128), BF),
        in_specs=[
            pl.BlockSpec((total, level), lambda i: (0, i)),
            pl.BlockSpec((total, width), lambda i: (0, 0)),
        ],
        out_specs=pl.BlockSpec((high, 128), lambda i: (i, 0)),
        compiler_params=pltpu.CompilerParams(vmem_limit_bytes=40 * 2**20),
        cost_estimate=pl.CostEstimate(
            flops=2 * total * features * width,
            bytes_accessed=2 * total * (features + width) + 2 * features * width,
            transcendentals=0,
        ),
    )(g, hidden)


def mixer_grads_kernel(x_ref, grad_ref, on_ref, out_ref, low_ref, beta_ref):
    wide = 3 * out_ref.shape[1]
    front = mm(x_ref[...], grad_ref[:, :wide], TN)
    low_ref[:, :wide] = front.astype(BF)
    beta_ref[...] = mm(grad_ref[:, wide:], x_ref[...], TN)[: beta_ref.shape[0]]
    low_ref[:, wide:] = mm(on_ref[...], out_ref[...], TN).astype(BF)


def mixer_gradients(x, grad, on, out):
    total, features = x.shape
    beta = grad.shape[1] - 3 * out.shape[1]
    wide = grad.shape[1] - beta + out.shape[1]
    step = features // 4
    return pl.pallas_call(
        mixer_grads_kernel,
        grid=(features // step,),
        out_shape=(
            jax.ShapeDtypeStruct((features, wide), BF),
            jax.ShapeDtypeStruct((8, features), F32),
        ),
        in_specs=[
            pl.BlockSpec((total, step), lambda i: (0, i)),
            pl.BlockSpec(grad.shape, lambda i: (0, 0)),
            pl.BlockSpec((total, step), lambda i: (0, i)),
            pl.BlockSpec(out.shape, lambda i: (0, 0)),
        ],
        out_specs=(
            pl.BlockSpec((step, wide), lambda i: (i, 0)),
            pl.BlockSpec((8, step), lambda i: (0, i)),
        ),
        compiler_params=pltpu.CompilerParams(vmem_limit_bytes=40 * 2**20),
        cost_estimate=pl.CostEstimate(
            flops=2 * total * features * (wide + beta),
            bytes_accessed=4 * total * features + 4 * features * wide,
            transcendentals=0,
        ),
    )(x, grad, on, out)


def rest_and_main(hidden_width, count):
    main = hidden_width // (128 * count) * 128
    return hidden_width // count - main, main


def local_heads(
    tokens,
    doc_starts,
    pad_mask,
    norm1_gain,
    query_weight,
    key_weight,
    value_weight,
    conv_weight,
    beta_weight,
    out_norm_gain,
    out_weight,
    norm2_gain,
    gate_weight,
    up_weight,
    down_weight,
    cotangent,
):
    row_count, features = tokens.shape
    width = lax.axis_size("seq")
    place = lax.axis_index("seq")
    head_dim = out_norm_gain.shape[0]
    heads = beta_weight.shape[1] // width
    mine = heads * head_dim
    total = row_count * width
    depth = lax.axis_size("dp")
    level = lax.axis_index("dp")
    owned = norm1_gain.shape[0]
    rest, main = rest_and_main(gate_weight.shape[1], width)
    w_beta = lax.dynamic_slice_in_dim(beta_weight, place * heads, heads, axis=1)

    small_all, w_mixer, pair_part, down_part, normed_full = start(
        width,
        depth,
        main,
        [norm1_gain[None], norm2_gain[None], conv_weight, pad_mask, doc_starts],
        tokens,
        [query_weight, key_weight, value_weight, out_weight],
        gate_weight,
        up_weight,
        down_weight.T,
    )
    w_pair = lax.all_gather(pair_part.reshape(width * owned, -1), "dp", axis=0, tiled=True)
    down_tiles = lax.all_gather(down_part, "dp", axis=0)
    small_all = small_all.reshape(width, depth, -1, small_all.shape[2])
    wide = small_all[:, :, : 3 * CONV + 2, :owned].transpose(2, 1, 0, 3)
    wide = wide.reshape(3 * CONV + 2, features)
    gain_first, gain_second = wide[3 * CONV], wide[3 * CONV + 1]
    taps = lax.dynamic_slice_in_dim(wide[: 3 * CONV], place * mine, mine, axis=1)
    marks = lax.dynamic_index_in_dim(small_all[:, :, 3 * CONV + 2 :], level, 1, keepdims=False)
    pad_rows = marks[:, 0, :row_count].reshape(-1, 2 * BLOCK)
    starts = marks[:, 1, : doc_starts.shape[1]].reshape(-1).astype(jnp.int32)
    begins = BLOCK * jnp.arange(total // BLOCK, dtype=jnp.int32)
    persist = (starts != begins).astype(F32)
    beta_wide = jnp.pad(w_beta, ((0, 0), (0, 128 - heads)))
    w_front = jnp.concatenate([w_mixer[:, : 3 * mine], beta_wide], axis=1)
    head_gain = out_norm_gain.astype(F32)[None]
    (
        projected, queries, key_rows, values, strength, sigma_vals, mixed,
        *saved, out_full, w_out_rows, cotangent_full,
    ) = front(
        width, heads, persist, normed_full, w_mixer, beta_wide, taps, pad_rows, head_gain,
        cotangent,
    )
    residual_mid, normed_two_full = middle(width, out_full, w_mixer, tokens, gain_second[None])
    normed_two_full, w_front = lax.optimization_barrier((normed_two_full, w_front))
    pair = product(normed_two_full, w_pair)
    tail = pair[:, 2 * main :]
    gate_out = jnp.concatenate([pair[:, :main], tail], axis=1)
    up_out = jnp.concatenate([pair[:, main : 2 * main], jnp.roll(tail, rest, axis=1)], axis=1)
    gate_sigma = jax.nn.sigmoid(gate_out)
    gate_silu = gate_out * gate_sigma
    hidden = (gate_silu * up_out).astype(BF)
    down_grads = down_gradients(width, depth, rest, cotangent_full, hidden)
    down_tiles, _ = lax.optimization_barrier((down_tiles, down_grads))
    down_sums = lax.psum_scatter(down_grads, "dp", scatter_dimension=0, tiled=True)
    pair_grad_low, w_down = hidden_gradients(width, rest, cotangent_full, pair, down_tiles)
    two_parts = product_right(pair_grad_low, w_pair).astype(BF)
    pair_grads = product_left(normed_two_full, pair_grad_low).astype(BF)
    pair_grads, two_parts = lax.optimization_barrier((pair_grads, two_parts))
    pair_sums = lax.psum_scatter(pair_grads, "dp", scatter_dimension=0, tiled=True)
    residual_mid_grad, gain_second_rows, mid_full = reduce_middle(
        width, two_parts, residual_mid, cotangent, gain_second[None]
    )
    projected_grad, conv_rows_grad, out_gain_rows, down_main, down_ends = back(
        width, heads, persist, mid_full, w_out_rows, mixed, head_gain, taps, projected,
        queries, key_rows, values, (strength, sigma_vals, pad_rows), saved, down_sums, main,
    )
    gain_second_grad = jnp.sum(gain_second_rows, axis=0)
    out_gain_grad = jnp.sum(out_gain_rows, axis=0)
    conv_grad = jnp.sum(conv_rows_grad, axis=1)
    mid_mine = lax.dynamic_slice_in_dim(mid_full, place * mine, mine, axis=1)
    mixer_grads, beta_grads = mixer_gradients(normed_full, projected_grad, out_full, mid_mine)
    beta_grad = beta_grads[:heads]
    mixer_sums = lax.psum_scatter(mixer_grads, "dp", scatter_dimension=0, tiled=True)
    normed_parts = product_right(projected_grad, w_front).astype(BF)
    hidden, normed_parts = lax.optimization_barrier((hidden, normed_parts))
    added_parts = product_right(hidden, w_down).astype(BF)
    tokens_grad, gain_first_rows, output = end(
        width, normed_parts, added_parts, tokens, residual_mid, residual_mid_grad, gain_first[None]
    )
    gain_first_grad = jnp.sum(gain_first_rows, axis=0)

    gain_row = jnp.pad(out_gain_grad[None], ((0, 0), (0, features - head_dim)))
    plane = jnp.concatenate([gain_first_grad[None], gain_second_grad[None], gain_row], axis=0)
    conv_rows = -(-3 * CONV * mine // features)
    conv_flat = jnp.pad(conv_grad.reshape(-1), (0, conv_rows * features - 3 * CONV * mine))
    levels = jnp.concatenate([beta_grad, conv_flat.reshape(conv_rows, features)], axis=0)
    sums, each, gate_main, up_main, pair_ends = small_sums(
        plane.reshape(8, -1), levels.reshape(8, -1), pair_sums, (main, main, 2 * rest), width, depth
    )
    def joined(front, back, at):
        back = back.reshape(owned, width, 2, rest)[:, :, at].reshape(owned, width * rest)
        return jnp.concatenate([front, back], axis=1).astype(F32)

    down_back = down_ends.reshape(owned // 2, width, 2, rest).transpose(2, 0, 1, 3)
    down_back = down_back.reshape(owned, width * rest)
    shard_gate, shard_up, shard_down = (
        joined(gate_main, pair_ends, 0),
        joined(up_main, pair_ends, 1),
        jnp.concatenate([down_main, down_back], axis=1).astype(F32).T,
    )
    sums = sums.reshape(3, features)
    each = each.reshape(width, heads + conv_rows, features)
    beta_total = each[:, :heads].reshape(width * heads, features).T
    conv_all = each[:, heads:].reshape(width, -1)[:, : 3 * CONV * mine]
    conv_all = conv_all.reshape(width, 3 * CONV, mine).transpose(1, 0, 2).reshape(-1, features)
    wide_sums = jnp.concatenate([sums[:2], conv_all], axis=0)
    own = level * width + place
    wide_own = lax.dynamic_slice_in_dim(wide_sums, own * owned, owned, axis=1)

    mixer_sums, gate_main = lax.optimization_barrier((mixer_sums, gate_main))
    shard_q, shard_k, shard_v, shard_o = (
        a.astype(F32) for a in closing([mixer_sums], width, [(mine,) * 4], 13)
    )

    return (
        output,
        tokens_grad,
        wide_own[0],
        shard_q,
        shard_k,
        shard_v,
        wide_own[2:].reshape(3, CONV, owned),
        beta_total,
        sums[2, :head_dim],
        shard_o,
        wide_own[1],
        shard_gate,
        shard_up,
        shard_down,
    )


def solution(mesh):
    in_specs = (
        P(("dp", "seq"), None),
        P("dp", "seq"),
        P("dp", "seq"),
        P(("dp", "seq")),
        P(("dp", "seq"), None),
        P(("dp", "seq"), None),
        P(("dp", "seq"), None),
        P(None, None, ("dp", "seq")),
        P(),
        P(),
        P(("dp", "seq"), None),
        P(("dp", "seq")),
        P(("dp", "seq"), None),
        P(("dp", "seq"), None),
        P(None, ("dp", "seq")),
        P(("dp", "seq"), None),
    )
    out_specs = (
        P(("dp", "seq"), None),
        P(("dp", "seq"), None),
        P(("dp", "seq")),
        P(("dp", "seq"), None),
        P(("dp", "seq"), None),
        P(("dp", "seq"), None),
        P(None, None, ("dp", "seq")),
        P(),
        P(),
        P(("dp", "seq"), None),
        P(("dp", "seq")),
        P(("dp", "seq"), None),
        P(("dp", "seq"), None),
        P(None, ("dp", "seq")),
    )

    def layer(*arrays):
        head_count, hidden_width = arrays[8].shape[1], arrays[12].shape[1]
        width = mesh.shape["seq"]
        rest, main = rest_and_main(hidden_width, width)
        by_heads = head_count % width == 0 and rest == 64 and main > 0
        by_heads = by_heads and width >= 4 and width & (width - 1) == 0 and head_count // width <= 8
        by_heads = by_heads and arrays[3].shape[0] // mesh.size % 32 == 0
        by_heads = by_heads and 128 % (arrays[3].shape[0] // mesh.size) == 0
        local = local_heads if by_heads else local_sequence
        return jax.shard_map(
            local, mesh=mesh, in_specs=in_specs, out_specs=out_specs, check_vma=False
        )(*arrays)

    return layer
```

```python
import functools

import jax
import jax.numpy as jnp
from jax import lax
from jax.experimental import pallas as pl
from jax.experimental.pallas import tpu as pltpu
from jax.sharding import PartitionSpec as P

CONV = 4
BLOCK = 64


EPSILON = 1e-06
PRECISE = lax.Precision.HIGHEST


def from_behind(array, axis, by):
    length = lax.axis_size(axis)
    pairs = [(i, i + by) for i in range(length) if 0 <= i + by < length]
    return lax.ppermute(array, axis, pairs)


def product(left, right):
    return jnp.dot(left, right, preferred_element_type=jnp.float32)


def product_left(left, right):
    return lax.dot_general(
        left, right, (((0,), (0,)), ((), ())), preferred_element_type=jnp.float32
    )


def product_right(left, right):
    return lax.dot_general(
        left, right, (((1,), (1,)), ((), ())), preferred_element_type=jnp.float32
    )


def rounded(value):
    return lax.optimization_barrier(value.astype(jnp.bfloat16)).astype(jnp.float32)


def rms_norm(value, gain):
    return value * lax.rsqrt(jnp.mean(value * value, axis=-1, keepdims=True) + EPSILON) * gain


def block_parts(queries, key_rows, values, strength):
    keyed = key_rows * strength[..., None]
    block_len = key_rows.shape[1]
    lower_part = jnp.tril(jnp.einsum("hcd,hed->hce", keyed, key_rows, precision=PRECISE), -1)
    system = lower_part + jnp.eye(block_len, dtype=jnp.float32)
    weights = jax.scipy.linalg.solve_triangular(system, keyed, lower=True, unit_diagonal=True)
    updates = jax.scipy.linalg.solve_triangular(
        system, values * strength[..., None], lower=True, unit_diagonal=True
    )
    scores = jnp.tril(jnp.einsum("hcd,hed->hce", queries, key_rows, precision=PRECISE))
    return (weights, updates, scores)


def delta_step(state_now, inputs):
    queries, key_rows, values, strength, persist = inputs
    state_now = state_now * persist
    weights, updates, scores = block_parts(queries, key_rows, values, strength)
    corrected = updates - jnp.einsum("hcd,hde->hce", weights, state_now, precision=PRECISE)
    outputs = jnp.einsum("hcd,hde->hce", queries, state_now, precision=PRECISE) + jnp.einsum(
        "hce,hef->hcf", scores, corrected, precision=PRECISE
    )
    state_now = state_now + jnp.einsum("hcd,hce->hde", key_rows, corrected, precision=PRECISE)
    return (state_now, outputs)


def track_step(holding, inputs):
    state_now, transit = holding
    queries, key_rows, values, strength, persist = inputs
    state_now = state_now * persist
    transit = transit * persist
    weights, updates, scores = block_parts(queries, key_rows, values, strength)
    corrected = updates - jnp.einsum("hcd,hde->hce", weights, state_now, precision=PRECISE)
    outputs = jnp.einsum("hcd,hde->hce", queries, state_now, precision=PRECISE) + jnp.einsum(
        "hce,hef->hcf", scores, corrected, precision=PRECISE
    )
    leading = queries - jnp.einsum("hce,hed->hcd", scores, weights, precision=PRECISE)
    state_now = state_now + jnp.einsum("hcd,hce->hde", key_rows, corrected, precision=PRECISE)
    eraser = jnp.eye(key_rows.shape[2], dtype=jnp.float32) - jnp.einsum(
        "hcd,hce->hde", key_rows, weights, precision=PRECISE
    )
    return (
        (state_now, jnp.einsum("hde,hef->hdf", eraser, transit, precision=PRECISE)),
        (outputs, leading, transit),
    )


def advance(linear, offset_part, incoming):
    return jnp.einsum("hde,hef->hdf", linear, incoming, precision=PRECISE) + offset_part


def into_blocks(array):
    row_count, head_count, head_dim = array.shape
    return array.reshape(row_count // BLOCK, BLOCK, head_count, head_dim).transpose(0, 2, 1, 3)


def from_blocks(array):
    block_count, head_count, block_len, head_dim = array.shape
    return array.transpose(0, 2, 1, 3).reshape(block_count * block_len, head_count, head_dim)


def local_sequence(
    tokens,
    doc_starts,
    pad_mask,
    norm1_gain,
    query_weight,
    key_weight,
    value_weight,
    conv_weight,
    beta_weight,
    out_norm_gain,
    out_weight,
    norm2_gain,
    gate_weight,
    up_weight,
    down_weight,
    cotangent,
):
    row_count, features = tokens.shape
    head_count = beta_weight.shape[1]
    head_dim = out_norm_gain.shape[0]
    block_count = row_count // BLOCK
    w_query, w_key, w_value, w_out, conv_full, gain_first = (
        lax.all_gather(query_weight, ("dp", "seq"), axis=0, tiled=True),
        lax.all_gather(key_weight, ("dp", "seq"), axis=0, tiled=True),
        lax.all_gather(value_weight, ("dp", "seq"), axis=0, tiled=True),
        lax.all_gather(out_weight, ("dp", "seq"), axis=0, tiled=True),
        lax.all_gather(conv_weight, ("dp", "seq"), axis=2, tiled=True),
        lax.all_gather(norm1_gain, ("dp", "seq"), axis=0, tiled=True),
    )
    w_gate, w_up, w_down, gain_second = (
        lax.all_gather(gate_weight, ("dp", "seq"), axis=0, tiled=True),
        lax.all_gather(up_weight, ("dp", "seq"), axis=0, tiled=True),
        lax.all_gather(down_weight, ("dp", "seq"), axis=1, tiled=True),
        lax.all_gather(norm2_gain, ("dp", "seq"), axis=0, tiled=True),
    )
    seq_place = lax.axis_index("seq")
    positions = seq_place * row_count + jnp.arange(row_count, dtype=jnp.int32)
    starts = doc_starts[0]
    offsets = jnp.repeat(starts, BLOCK)
    persist = (
        starts != seq_place * row_count + BLOCK * jnp.arange(block_count, dtype=jnp.int32)
    ).astype(jnp.float32)
    pad_rows = pad_mask[0].astype(jnp.float32)[:, None]

    def mixer_in(extended, conv_taps):
        results = []
        for member in range(3):
            columns = extended[:, member * features : (member + 1) * features]
            summed = jnp.zeros((row_count, features), jnp.float32)
            for lagged in range(CONV):
                inside = (positions - lagged >= offsets).astype(jnp.float32)[:, None]
                summed = (
                    summed
                    + conv_taps[member, lagged]
                    * inside
                    * columns[CONV - 1 - lagged : CONV - 1 - lagged + row_count]
                )
            activated = jax.nn.silu(summed).reshape(row_count, head_count, head_dim)
            if member < 2:
                activated = activated * lax.rsqrt(
                    jnp.sum(activated * activated, axis=-1, keepdims=True) + EPSILON
                )
            if member == 0:
                activated = activated * head_dim ** (-0.5)
            results.append(activated)
        return tuple(results)

    residual_in = tokens.astype(jnp.float32)
    normed, norm_first_pull = jax.vjp(rms_norm, residual_in, gain_first.astype(jnp.float32))
    normed_low = normed.astype(jnp.bfloat16)
    projected = jnp.concatenate(
        [product(normed_low, w_query), product(normed_low, w_key), product(normed_low, w_value)],
        axis=1,
    ).astype(jnp.bfloat16)
    logits = product(normed_low, beta_weight)
    sigma_vals = jax.nn.sigmoid(logits)
    strength = sigma_vals * pad_rows
    rims = from_behind(projected[row_count - CONV + 1 :], "seq", 1)
    extended_in = jnp.concatenate([rims, projected], axis=0).astype(jnp.float32)
    (queries, key_rows, values), mixer_pull = jax.vjp(
        mixer_in, extended_in, conv_full.astype(jnp.float32)
    )
    query_blocks = into_blocks(rounded(queries))
    key_blocks = into_blocks(rounded(key_rows))
    value_blocks = into_blocks(rounded(values))
    strength_blocks = strength.reshape(block_count, BLOCK, head_count).transpose(0, 2, 1)
    zero_state = jnp.zeros((head_count, head_dim, head_dim), jnp.float32)
    identity = jnp.broadcast_to(
        jnp.eye(head_dim, dtype=jnp.float32), (head_count, head_dim, head_dim)
    )
    block_inputs = (query_blocks, key_blocks, value_blocks, strength_blocks, persist)
    (final_state, final_transit), (local_out, leading, transit) = lax.scan(
        track_step, (zero_state, identity), block_inputs
    )

    def forward_turn(turn_index, incoming):
        return from_behind(advance(final_transit, final_state, incoming), "seq", 1)

    start_state = lax.fori_loop(0, lax.axis_size("seq") - 1, forward_turn, zero_state)
    carried = jnp.einsum("nhde,hef->nhdf", transit, start_state, precision=PRECISE)
    mixed = from_blocks(
        local_out + jnp.einsum("nhcd,nhdf->nhcf", leading, carried, precision=PRECISE)
    )
    out_normed, out_norm_pull = jax.vjp(rms_norm, mixed, out_norm_gain.astype(jnp.float32))
    out_low = out_normed.reshape(row_count, features).astype(jnp.bfloat16)
    residual_mid = residual_in + product(out_low, w_out)
    normed_two, norm_second_pull = jax.vjp(rms_norm, residual_mid, gain_second.astype(jnp.float32))
    normed_two_low = normed_two.astype(jnp.bfloat16)
    gate_out = product(normed_two_low, w_gate)
    up_out = product(normed_two_low, w_up)
    hidden = (jax.nn.silu(gate_out) * up_out).astype(jnp.bfloat16)
    output = (residual_mid + product(hidden, w_down)).astype(jnp.bfloat16)
    grad_out = cotangent.astype(jnp.float32)
    down_grad = product_left(hidden, cotangent)
    hidden_grad = product_right(cotangent, w_down)
    gate_sigma = jax.nn.sigmoid(gate_out)
    gate_grad_low = (
        hidden_grad * up_out * gate_sigma * (1.0 + gate_out * (1.0 - gate_sigma))
    ).astype(jnp.bfloat16)
    up_grad_low = (hidden_grad * jax.nn.silu(gate_out)).astype(jnp.bfloat16)
    gate_grad = product_left(normed_two_low, gate_grad_low)
    up_grad = product_left(normed_two_low, up_grad_low)
    normed_two_grad = product_right(gate_grad_low, w_gate) + product_right(up_grad_low, w_up)
    mid_from_norm, gain_second_grad = norm_second_pull(normed_two_grad)
    residual_mid_grad = grad_out + mid_from_norm
    mid_low = residual_mid_grad.astype(jnp.bfloat16)
    out_grad = product_left(out_low, mid_low)
    out_normed_grad = product_right(mid_low, w_out).reshape(row_count, head_count, head_dim)
    mixed_grad, out_gain_grad = out_norm_pull(out_normed_grad)
    mixed_blocks = into_blocks(mixed_grad)
    pulled = jnp.einsum("nhcd,nhcf->nhdf", leading, mixed_blocks, precision=PRECISE)
    local_back = jnp.einsum("nhed,nhef->hdf", transit, pulled, precision=PRECISE)
    transit_turned = jnp.swapaxes(final_transit, 1, 2)

    def backward_turn(turn_index, incoming):
        return from_behind(advance(transit_turned, local_back, incoming), "seq", -1)

    end_grad = lax.fori_loop(0, lax.axis_size("seq") - 1, backward_turn, zero_state)

    def delta_local(query_in, key_in, value_in, strength_in):
        ending, outputs = lax.scan(
            jax.checkpoint(delta_step),
            start_state,
            (query_in, key_in, value_in, strength_in, persist),
        )
        return (outputs, ending)

    unused_out, delta_pull = jax.vjp(
        delta_local, query_blocks, key_blocks, value_blocks, strength_blocks
    )
    query_grad_blocks, key_grad_blocks, value_grad_blocks, strength_grad_blocks = delta_pull(
        (mixed_blocks, end_grad)
    )
    extended_grad, conv_grad = mixer_pull(
        (
            from_blocks(query_grad_blocks),
            from_blocks(key_grad_blocks),
            from_blocks(value_grad_blocks),
        )
    )
    rim_grad = from_behind(extended_grad[: CONV - 1], "seq", -1)
    projected_grad = jnp.concatenate(
        [extended_grad[CONV - 1 : row_count], extended_grad[row_count:] + rim_grad], axis=0
    ).astype(jnp.bfloat16)
    strength_grad = strength_grad_blocks.transpose(0, 2, 1).reshape(row_count, head_count)
    logits_grad = (strength_grad * pad_rows * sigma_vals * (1.0 - sigma_vals)).astype(jnp.bfloat16)
    part_query = projected_grad[:, :features]
    part_key = projected_grad[:, features : 2 * features]
    part_value = projected_grad[:, 2 * features :]
    query_grad = product_left(normed_low, part_query)
    key_grad = product_left(normed_low, part_key)
    value_grad = product_left(normed_low, part_value)
    beta_grad = product_left(normed_low, logits_grad)
    normed_grad = (
        product_right(part_query, w_query)
        + product_right(part_key, w_key)
        + product_right(part_value, w_value)
        + product_right(logits_grad, beta_weight)
    )
    input_from_norm, gain_first_grad = norm_first_pull(normed_grad)
    tokens_grad = residual_mid_grad + input_from_norm
    (
        shard_q,
        shard_k,
        shard_v,
        shard_o,
        shard_conv,
        shard_gain_one,
        shard_gate,
        shard_up,
        shard_down,
        shard_gain_two,
    ) = (
        lax.psum_scatter(query_grad, ("dp", "seq"), scatter_dimension=0, tiled=True),
        lax.psum_scatter(key_grad, ("dp", "seq"), scatter_dimension=0, tiled=True),
        lax.psum_scatter(value_grad, ("dp", "seq"), scatter_dimension=0, tiled=True),
        lax.psum_scatter(out_grad, ("dp", "seq"), scatter_dimension=0, tiled=True),
        lax.psum_scatter(conv_grad, ("dp", "seq"), scatter_dimension=2, tiled=True),
        lax.psum_scatter(gain_first_grad, ("dp", "seq"), scatter_dimension=0, tiled=True),
        lax.psum_scatter(gate_grad, ("dp", "seq"), scatter_dimension=0, tiled=True),
        lax.psum_scatter(up_grad, ("dp", "seq"), scatter_dimension=0, tiled=True),
        lax.psum_scatter(down_grad, ("dp", "seq"), scatter_dimension=1, tiled=True),
        lax.psum_scatter(gain_second_grad, ("dp", "seq"), scatter_dimension=0, tiled=True),
    )
    beta_total, out_gain_total = lax.psum((beta_grad, out_gain_grad), ("dp", "seq"))
    return (
        output,
        tokens_grad,
        shard_gain_one,
        shard_q,
        shard_k,
        shard_v,
        shard_conv,
        beta_total,
        out_gain_total,
        shard_o,
        shard_gain_two,
        shard_gate,
        shard_up,
        shard_down,
    )


F32 = jnp.float32
BF = jnp.bfloat16
NN=(((1,),(0,)),((),())); NT=(((1,),(1,)),((),())); TN=(((0,),(0,)),((),()))

def mm(a,b,dims=NN):
    return lax.dot_general(a,b,dims,preferred_element_type=F32)

def halves(a):
    high=a.astype(BF)
    return high,(a-high.astype(F32)).astype(BF)

def mm_lw(a,b,dims=NN):
    high,low=halves(b)
    return mm(a,high,dims)+mm(a,low,dims)

def mm_wl(a,b,dims=NN):
    high,low=halves(a)
    return mm(high,b,dims)+mm(low,b,dims)

def mm_ww(a,b,dims=NN):
    ah,al=halves(a); bh,bl=halves(b)
    return mm(ah,bh,dims)+(mm(al,bh,dims)+mm(ah,bl,dims))

def tile_masks(tile):
    row=lax.broadcasted_iota(jnp.int32,(tile,tile),0)
    col=lax.broadcasted_iota(jnp.int32,(tile,tile),1)
    return row,col


MESH = pl.DeviceIdType.MESH
ANY = pl.BlockSpec(memory_space=pl.ANY)
VMEM = pl.BlockSpec(memory_space=pltpu.VMEM)


def flipped(index, bit):
    size = 2**bit
    return index + (1 - 2 * ((index // size) % 2)) * size


def greet(peers):
    barrier = pltpu.get_barrier_semaphore()
    for axis, peer in peers:
        pl.semaphore_signal(barrier, inc=1, device_id={axis: peer}, device_id_type=MESH)
    pl.semaphore_wait(barrier, len(peers))


def others(axis, count):
    me = lax.axis_index(axis)
    return [(axis, lax.rem(me + step, count)) for step in range(1, count)]


def send(source, target, sends, recvs, slot, axis, peer):
    copy = pltpu.make_async_remote_copy(
        src_ref=source,
        dst_ref=target,
        send_sem=sends.at[slot],
        recv_sem=recvs.at[slot],
        device_id={axis: peer},
        device_id_type=MESH,
    )
    copy.start()
    return copy


def span(size, index, axis):
    piece = pl.ds(pl.multiple_of(index * size, size), size)
    return (piece, slice(None)) if axis == 0 else (slice(None), piece)


def start_exchange(pieces, count, sends, recvs, local, first=0):
    me = lax.axis_index("seq")
    started = []
    for number, (source, source_at, target, target_at) in enumerate(pieces):
        own = pltpu.make_async_copy(
            source.at[source_at(me)], target.at[target_at(me)], local.at[first // count + number]
        )
        own.start()
        started.append(own)
        for step in range(1, count):
            peer = lax.rem(me + step, count)
            slot = first + number * count + step
            started.append(
                send(
                    source.at[source_at(peer)], target.at[target_at(me)],
                    sends, recvs, slot, "seq", peer,
                )
            )
    return started


def wait_all(copies):
    for copy in copies:
        copy.wait()


def bit_orders(count):
    bits = list(range(count.bit_length() - 1))[::-1]
    other = bits[:]
    if len(bits) >= 3:
        other[0], other[1] = bits[1], bits[0]
    return [bits, other]


class Gather:
    def __init__(self, count, source, target, axis, sends, recvs, local, slot, local_slot):
        self.count, self.source, self.target, self.axis = count, source, target, axis
        self.sends, self.recvs, self.local = sends, recvs, local
        self.slot, self.local_slot = slot, local_slot
        self.me = lax.axis_index("seq")
        self.copies = {}

    def piece(self, owner, half):
        rows, columns = self.source.shape
        part = rows // 2
        if self.axis == 0:
            return (pl.ds(pl.multiple_of(owner * rows + half * part, part), part), slice(None))
        return (
            pl.ds(half * part, part),
            pl.ds(pl.multiple_of(owner * columns, columns), columns),
        )

    def put(self, order, half, turn, known):
        owner = self.me
        for bit in known:
            owner = flipped(owner, bit)
        place = self.target.at[self.piece(owner, half)]
        part = self.source.shape[0] // 2
        source = place if known else self.source.at[pl.ds(half * part, part)]
        slot = self.slot + half * self.count + self.number(order, turn, known)
        self.copies[half, turn, known] = send(
            source, place, self.sends, self.recvs, slot, "seq", flipped(self.me, order[turn])
        )

    def number(self, order, turn, known):
        return 2**turn + sum(2 ** order.index(bit) for bit in known)

    def start(self):
        self.start_own()
        for half in range(2):
            self.start_half(half)

    def start_own(self):
        self.own = pltpu.make_async_copy(
            self.source,
            self.target.at[
                span(self.source.shape[self.axis], self.me, self.axis)
            ],
            self.local.at[self.local_slot],
        )
        self.own.start()

    def start_half(self, half):
        order = bit_orders(self.count)[half]
        for turn in range(len(order)):
            self.put(order, half, turn, ())

    def turns(self):
        return self.count.bit_length() - 1

    def forward(self, turn):
        orders = bit_orders(self.count)
        for before in range(2**turn):
            for half, order in enumerate(orders):
                known = tuple(order[i] for i in range(turn) if before // 2**i % 2)
                self.copies[half, turn, known].wait_recv()
                for later in range(turn + 1, len(order)):
                    self.put(order, half, later, known + (order[turn],))

    def finish(self):
        for copy in self.copies.values():
            copy.wait_send()
        self.own.wait()


class LineGather:
    def __init__(self, depth, target, chunks, sems):
        self.depth, self.target, self.chunks = depth, target, chunks
        self.sems = sems
        self.level = lax.axis_index("dp")
        self.rows = target.shape[0] // depth

    def copy(self, block, chunk, distance, up):
        part = self.target.shape[1] // self.chunks
        at = pl.multiple_of(block * self.rows, self.rows)
        place = self.target.at[pl.ds(at, self.rows), pl.ds(chunk * part, part)]
        way = 0 if up else 2
        return pltpu.make_async_remote_copy(
            src_ref=place,
            dst_ref=place,
            send_sem=self.sems.at[way, distance * self.chunks + chunk],
            recv_sem=self.sems.at[way + 1, distance * self.chunks + chunk],
            device_id={"dp": self.level + 1 if up else self.level - 1},
            device_id_type=MESH,
        )

    def start(self, chunks):
        level = self.level
        for chunk in chunks:

            @pl.when(level < self.depth - 1)
            def up():
                self.copy(level, chunk, 0, True).start()

            @pl.when(level > 0)
            def down():
                self.copy(level, chunk, 0, False).start()

    def forward(self, distance, chunks=None):
        level, last = self.level, self.depth - 1
        for chunk in range(self.chunks) if chunks is None else chunks:

            @pl.when(level - distance >= 0)
            def from_below():
                self.copy(level - distance, chunk, distance - 1, True).wait_recv()

                @pl.when(level < last)
                def hand_on():
                    self.copy(level - distance, chunk, distance, True).start()

            @pl.when(level + distance <= last)
            def from_above():
                self.copy(level + distance, chunk, distance - 1, False).wait_recv()

                @pl.when(level > 0)
                def hand_on():
                    self.copy(level + distance, chunk, distance, False).start()

    def finish(self):
        level, last = self.level, self.depth - 1
        for distance in range(last):
            for chunk in range(self.chunks):

                @pl.when((level - distance >= 0) & (level < last))
                def up():
                    self.copy(level - distance, chunk, distance, True).wait_send()

                @pl.when((level + distance <= last) & (level > 0))
                def down():
                    self.copy(level + distance, chunk, distance, False).wait_send()


def hypercube_peers(count):
    me = lax.axis_index("seq")
    return [("seq", flipped(me, bit)) for bit in range(count.bit_length() - 1)]


def comm_params(identity, limit=48):
    return pltpu.CompilerParams(
        collective_id=identity, has_side_effects=True, vmem_limit_bytes=limit * 2**20
    )


def start_kernel(
    count, depth, main, gain_one, gain_two, taps, pad, starts, x_ref, wq, wk, wv, wo, gate, up, down,
    small_all, mixer, native, pair, down_rest, normed_full,
    small, gain, normed, tails, pair_rest, sends, recvs, local, gather_sends, gather_recvs, far,
    mixer_sends, mixer_recvs, mixer_local, line_sems, tail_sems, early_sems,
):
    rest = gate.shape[1] // count - main
    loads = [
        pltpu.make_async_copy(weight.at[:, main * count :], tails.at[i], tail_sems.at[i])
        for i, weight in enumerate((gate, up, down))
    ]
    for load in loads:
        load.start()
    greet(others("seq", count) + others("dp", depth))
    me, level = lax.axis_index("seq"), lax.axis_index("dp")
    mine, height = wq.shape[1] // count, wq.shape[0]
    early = LineGather(depth, native, 1, early_sems)
    own = pltpu.make_async_copy(
        wo, native.at[pl.ds(pl.multiple_of(level * height, height), height)], tail_sems.at[3]
    )
    own.start()
    own.wait()
    small[...] = jnp.zeros(small.shape, F32)
    owned, features = gain_one.shape[1], x_ref.shape[1]
    for member in range(3):
        small[member * CONV : (member + 1) * CONV, 0:owned] = taps[member].astype(F32)
    at = 3 * CONV
    for row, source in enumerate((gain_one, gain_two, pad, starts)):
        small[at + row : at + row + 1, 0 : source.shape[1]] = source[...].astype(F32)
    place = me * depth + level
    small_all[place] = small[...]
    levels = [
        send(
            small, small_all.at[place], far.at[0], far.at[1], step, "dp", lax.rem(level + step, depth)
        )
        for step in range(1, depth)
    ]
    places = [
        (
            weight,
            lambda i: span(mine, i, 1),
            mixer,
            lambda i, member=member: (
                pl.ds(pl.multiple_of((level * count + i) * height, height), height),
                slice(member * mine, (member + 1) * mine),
            ),
        )
        for member, weight in enumerate((wq, wk, wv))
    ]
    first_exchange = start_exchange(places, count, mixer_sends, mixer_recvs, mixer_local)
    early.start((0,))
    wait_all(levels)
    block = small_all.at[pl.ds(me * depth, depth)]
    copies = [
        send(block, block, far.at[2], far.at[3], step, "seq", lax.rem(me + step, count))
        for step in range(1, count)
    ]
    line = LineGather(depth, mixer, 3, line_sems)
    for member in range(3):
        wait_all(first_exchange[member * count : (member + 1) * count])
        line.start((member,))
    for load in loads:
        load.wait()
    lane = lax.broadcasted_iota(jnp.int32, (1, 128), 1)
    half = height // 2
    for i in range(count):
        tile = slice(i // 2 * 128, (i // 2 + 1) * 128)
        gate_tile, up_tile, down_tile = (tails[j, :, tile].astype(F32) for j in range(3))
        if i % 2:
            gate_tile = pltpu.roll(gate_tile, rest, 1)
            top, bottom = pltpu.roll(down_tile[:half], rest, 1), down_tile[half:]
        else:
            up_tile = pltpu.roll(up_tile, rest, 1)
            top, bottom = down_tile[:half], pltpu.roll(down_tile[half:], rest, 1)
        there = slice(i * 128, (i + 1) * 128)
        pair_rest[:, there] = jnp.where(lane < rest, gate_tile, up_tile).astype(BF)
        down_rest[:, there] = jnp.where(lane < rest, top, bottom).astype(BF)
    wait_all(copies)
    per = 128 // owned
    for tile in range(features // 128):
        row = jnp.zeros((1, 128), F32)
        for part in range(per):
            owner = tile * per + part
            piece = small_all[owner % count * depth + owner // count, at : at + 1, :]
            row = row + (pltpu.roll(piece, part * owned, 1) if part else piece)
        gain[0:1, tile * 128 : (tile + 1) * 128] = row
    for first in range(0, x_ref.shape[0], 16):
        part = slice(first, first + 16)
        value = x_ref[part, :].astype(F32)
        scale = lax.rsqrt(jnp.mean(value * value, axis=1, keepdims=True) + EPSILON)
        normed[part, :] = (value * scale * gain[0:1, :]).astype(BF)
    pieces = [
        (
            source,
            lambda i, size=size: span(size, i, 1),
            pair,
            lambda i, size=size, at=at: (i, slice(None), slice(at, at + size)),
        )
        for source, size, at in ((gate, main, 0), (up, main, main), (pair_rest, 128, 2 * main))
    ]
    gather = Gather(
        count, normed, normed_full, 0, gather_sends, gather_recvs, local, 0, len(pieces)
    )
    gather.start()
    exchange = start_exchange(pieces, count, sends, recvs, local)
    early.forward(1)
    line.forward(1, (0, 1))
    early.forward(2)
    gather.forward(0)
    line.forward(1, (2,))
    gather.forward(1)
    line.forward(2, (0, 1))
    for turn in range(2, gather.turns()):
        gather.forward(turn)
    line.forward(2, (2,))
    for distance in range(3, depth):
        line.forward(distance)
    gather.finish()
    for distance in range(3, depth):
        early.forward(distance)
    wait_all(exchange)
    line.finish()
    early.finish()


def start(count, depth, main, small, x, mixer, gate, up, down):
    rows = gate.shape[0]
    rest = gate.shape[1] // count - main
    slots = max(count, depth)
    members = 3
    shape = (3 * CONV + 4, max(128, x.shape[0]))
    whole = jax.ShapeDtypeStruct((x.shape[0] * count, x.shape[1]), BF)
    return pl.pallas_call(
        functools.partial(start_kernel, count, depth, main),
        out_shape=(
            jax.ShapeDtypeStruct((count * depth,) + shape, F32),
            jax.ShapeDtypeStruct((x.shape[1], 3 * x.shape[1] // count), BF),
            jax.ShapeDtypeStruct((depth * rows, x.shape[1]), BF),
            jax.ShapeDtypeStruct((count, rows, 2 * main + 128), BF),
            jax.ShapeDtypeStruct((rows // 2, 128 * count), BF),
            whole,
        ),
        in_specs=[VMEM] * 6 + [ANY] * 7,
        out_specs=(VMEM, ANY, ANY, ANY, VMEM, ANY),
        scratch_shapes=[
            pltpu.VMEM(shape, F32),
            pltpu.VMEM((8, x.shape[1]), F32),
            pltpu.VMEM(x.shape, BF),
            pltpu.VMEM((3, rows, rest * count), BF),
            pltpu.VMEM((rows, 128 * count), BF),
            pltpu.SemaphoreType.DMA((members * count,)),
            pltpu.SemaphoreType.DMA((members * count,)),
            pltpu.SemaphoreType.DMA((members + 1,)),
            pltpu.SemaphoreType.DMA((2 * count,)),
            pltpu.SemaphoreType.DMA((2 * count,)),
            pltpu.SemaphoreType.DMA((4, slots)),
            pltpu.SemaphoreType.DMA((4 * count,)),
            pltpu.SemaphoreType.DMA((4 * count,)),
            pltpu.SemaphoreType.DMA((4,)),
            pltpu.SemaphoreType.DMA((4, 3 * depth)),
            pltpu.SemaphoreType.DMA((4,)),
            pltpu.SemaphoreType.DMA((4, depth)),
        ],
        compiler_params=comm_params(2, 60),
    )(*small, x, *mixer, gate, up, down)


def closing_kernel(count, sizes, *refs):
    sources, targets, (sends, recvs, local) = refs[: len(sizes)], refs[len(sizes) : -3], refs[-3:]
    greet(others("seq", count))
    wait_all(start_exchange(row_pieces(sources, targets, sizes, count), count, sends, recvs, local))


def closing(sources, count, sizes, identity):
    shapes = row_shapes(sources, sizes, count)
    members = len(shapes)
    return pl.pallas_call(
        functools.partial(closing_kernel, count, sizes),
        out_shape=shapes,
        in_specs=[ANY] * len(sources),
        out_specs=(ANY,) * members,
        scratch_shapes=[
            pltpu.SemaphoreType.DMA((members * count,)),
            pltpu.SemaphoreType.DMA((members * count,)),
            pltpu.SemaphoreType.DMA((members,)),
        ],
        compiler_params=comm_params(identity),
    )(*sources)


def sums_kernel(count, depth, sizes, plane_ref, level_ref, source, total_ref, each_ref, *refs):
    targets, scratch = refs[: len(sizes)], refs[len(sizes) :]
    plane_in, joined, level_in, sends, recvs, pass_sends, pass_recvs, local = scratch
    greet(others("seq", count) + others("dp", depth))
    me, level = lax.axis_index("seq"), lax.axis_index("dp")
    cut = plane_ref.shape[1]
    plane_in[me] = plane_ref[...]
    wait_all(
        [
            send(
                plane_ref, plane_in.at[me], sends.at[0], recvs.at[0], step,
                "seq", lax.rem(me + step, count),
            )
            for step in range(1, count)
        ]
    )
    exchange = start_exchange(
        row_pieces([source], targets, [sizes], count), count, pass_sends, pass_recvs, local
    )
    value = plane_in[0]
    for i in range(1, count):
        value = value + plane_in[i]
    joined[:, 0:cut] = value
    joined[:, cut:] = level_ref[...]
    level_in[level] = joined[...]
    wait_all(
        [
            send(
                joined, level_in.at[level], sends.at[1], recvs.at[1], step,
                "dp", lax.rem(level + step, depth),
            )
            for step in range(1, depth)
        ]
    )
    value = level_in[0]
    for i in range(1, depth):
        value = value + level_in[i]
    total_ref[...] = value[:, 0:cut]
    joined[:, cut:] = value[:, cut:]
    each_ref[me] = value[:, cut:]
    wait_all(
        [
            send(
                joined.at[:, cut:], each_ref.at[me],
                sends.at[2], recvs.at[2], step, "seq", lax.rem(me + step, count),
            )
            for step in range(1, count)
        ]
    )
    wait_all(exchange)


def small_sums(plane, level, source, sizes, count, depth):
    shapes = row_shapes([source], [sizes], count)
    slots = max(count, depth)
    joined = (plane.shape[0], plane.shape[1] + level.shape[1])
    return pl.pallas_call(
        functools.partial(sums_kernel, count, depth, sizes),
        out_shape=(
            jax.ShapeDtypeStruct(plane.shape, F32),
            jax.ShapeDtypeStruct((count,) + level.shape, F32),
        )
        + shapes,
        in_specs=[VMEM, VMEM, ANY],
        out_specs=(VMEM, VMEM) + (ANY,) * len(shapes),
        scratch_shapes=[
            pltpu.VMEM((count,) + plane.shape, F32),
            pltpu.VMEM(joined, F32),
            pltpu.VMEM((depth,) + joined, F32),
            pltpu.SemaphoreType.DMA((3, slots)),
            pltpu.SemaphoreType.DMA((3, slots)),
            pltpu.SemaphoreType.DMA((len(sizes) * count,)),
            pltpu.SemaphoreType.DMA((len(sizes) * count,)),
            pltpu.SemaphoreType.DMA((len(sizes),)),
        ],
        compiler_params=comm_params(3),
    )(plane, level, source)


class Scatter:
    def __init__(self, count, part, out, landing, outgoing, total, sends, recvs):
        self.count, self.part, self.out = count, part, out
        self.landing, self.outgoing, self.total = landing, outgoing, total
        self.sends, self.recvs = sends, recvs
        self.me = lax.axis_index("seq")
        self.rows = out.shape[0] // 2
        self.bits = count.bit_length() - 1
        self.orders = [order[::-1] for order in bit_orders(count)]
        self.copies = {}

    def rows_of(self, known, half):
        owner = self.me
        for bit in known:
            owner = flipped(owner, bit)
        size = self.rows
        return pl.ds(pl.multiple_of(owner * 2 * size + half * size, size), size)

    def place(self, order, turn, known):
        later = order[turn + 1 :]
        before = sum(self.count >> (t + 1) for t in range(turn))
        return before + sum(2**i for i, bit in enumerate(later) if bit in known)

    def subsets(self, order, turn):
        later = order[turn + 1 :]
        sets = [
            tuple(later[i] for i in range(len(later)) if code // 2**i % 2)
            for code in range(2 ** len(later))
        ]
        return sorted(sets, key=lambda known: [-(bit in known) for bit in later])

    def put(self, half, turn, known, source):
        order = self.orders[half]
        place = self.place(order, turn, known)
        self.copies[half, turn, known] = send(
            source,
            self.landing.at[half, place],
            self.sends,
            self.recvs,
            half * self.count + place,
            "seq",
            flipped(self.me, order[turn]),
        )

    def start(self):
        for at in range(self.count // 2):
            for half, order in enumerate(self.orders):
                known = self.subsets(order, 0)[at]
                self.put(half, 0, known, self.part.at[self.rows_of((order[0],) + known, half)])

    def turn(self, turn):
        for at in range(2 ** (self.bits - turn - 1)):
            for half, order in enumerate(self.orders):
                known = self.subsets(order, turn)[at]
                place = self.place(order, turn, known)
                self.copies[half, turn, known].wait_recv()
                came = self.landing[half, place].astype(F32)
                if turn == 0:
                    value = self.part[self.rows_of(known, half), :].astype(F32) + came
                else:
                    value = self.total[half, self.kept(order, turn - 1, known)] + came
                if turn == self.bits - 1:
                    self.out[half * self.rows : (half + 1) * self.rows, :] = value
                elif order[turn + 1] in known:
                    rest = tuple(bit for bit in known if bit != order[turn + 1])
                    next_place = self.place(order, turn + 1, rest) - self.count // 2
                    self.outgoing[half, next_place] = value.astype(BF)
                    self.put(half, turn + 1, rest, self.outgoing.at[half, next_place])
                else:
                    self.total[half, self.kept(order, turn, known)] = value

    def kept(self, order, turn, known):
        return sum(2**i for i, bit in enumerate(order[turn + 2 :]) if bit in known)

    def finish(self):
        for copy in self.copies.values():
            copy.wait_send()


def scatter_scratch(count, rows, columns):
    half = rows // 2
    return [
        pltpu.VMEM((2, count - 1, half, columns), BF),
        pltpu.VMEM((2, count // 2 - 1, half, columns), BF),
        pltpu.VMEM((2, count // 4, half, columns), F32),
        pltpu.SemaphoreType.DMA((2 * count,)),
        pltpu.SemaphoreType.DMA((2 * count,)),
    ]


def shifted_sum(window, taps_ref, member, lanes, keep):
    length = window.shape[0] - 8
    row = lax.broadcasted_iota(jnp.int32, (length, 1), 0)
    shifts = [window[8:]]
    for lagged in range(1, CONV):
        moved = pltpu.roll(window, lagged, 0)[8:]
        shifts.append(moved * jnp.where(row >= lagged, 1.0, keep))
    summed = shifts[0] * taps_ref[member * CONV : member * CONV + 1, lanes]
    for lagged in range(1, CONV):
        at = member * CONV + lagged
        summed = summed + shifts[lagged] * taps_ref[at : at + 1, lanes]
    return summed, shifts


def front_kernel(
    count, depth, heads, main, persist_ref, x_ref, w_ref, beta_ref, taps_ref, pad_ref, gain_ref, own_ref, g_ref, down_ref, ends_ref,
    pre_ref, q_ref, k_ref, v_ref, brow_ref, sigma_ref, mixed_ref, t_ref, wide_ref, s_ref, f_ref, a_ref,
    full_ref, columns_ref, rows_ref, g_full_ref, tiles_ref,
    pre_buf, logit_buf, u_buf, c_buf, on_buf, local, gather_sends, gather_recvs, sends, recvs, row_sends, row_recvs, row_local,
    tile_sends, tile_recvs, tile_local,
):
    total, features = x_ref.shape
    mine = on_buf.shape[1]
    hd = mine // heads
    blocks = total // BLOCK
    tile = 2 * BLOCK
    greet(others("seq", count))
    height = columns_ref.shape[0] // (depth * count)
    first_exchange = start_exchange(
        [
            (
                own_ref,
                lambda i, z=z: (slice(z * height, (z + 1) * height), span(mine, i, 1)[1]),
                columns_ref,
                lambda i, z=z: span(height, z * count + i, 0),
            )
            for z in range(depth)
        ],
        count, sends, recvs, local,
    )
    beside = Gather(
        count, g_ref, g_full_ref, 0, gather_sends, gather_recvs, local, 2 * count, depth
    )
    beside.start()
    pre_buf[0:8, :] = jnp.zeros((8, 3 * mine), F32)
    chunk = 4 * BLOCK

    def project(index, carry):
        rows = pl.ds(pl.multiple_of(index * chunk, chunk), chunk)
        x = x_ref[rows, :]
        low = mm(x, w_ref[...]).astype(BF)
        pre_ref[rows, :] = low
        pre_buf[pl.ds(pl.multiple_of(index * chunk + 8, 8), chunk), :] = low.astype(F32)
        logit_buf[rows, :] = mm(x, beta_ref[...])
        return carry

    lax.fori_loop(0, total // chunk, project, 0)

    def convolve(index, carry):
        keep = persist_ref[index]
        rows = pl.ds(pl.multiple_of(index * BLOCK, BLOCK), BLOCK)
        for member, target in enumerate((q_ref, k_ref, v_ref)):
            for h in range(heads):
                lanes = slice(h * hd, (h + 1) * hd)
                there = slice(member * mine + h * hd, member * mine + (h + 1) * hd)
                window = pre_buf[pl.ds(pl.multiple_of(index * BLOCK, 8), BLOCK + 8), there]
                summed, _ = shifted_sum(window, taps_ref, member, lanes, keep)
                value = summed * jax.nn.sigmoid(summed)
                if member < 2:
                    norm = jnp.sum(value * value, axis=1, keepdims=True) + EPSILON
                    value = value * lax.rsqrt(norm)
                if member == 0:
                    value = value * hd ** (-0.5)
                target[rows, lanes] = value.astype(BF)
        return carry

    lax.fori_loop(0, blocks, convolve, 0)
    beside.forward(0)
    wait_all(first_exchange)
    tiles = start_exchange(
        [
            (target, target_at, source, source_at)
            for source, source_at, target, target_at in folded_pieces(tiles_ref, down_ref, ends_ref, count, main)
        ],
        count, tile_sends, tile_recvs, tile_local,
    )
    exchange = start_exchange(
        [(columns_ref, lambda i: span(mine, i, 0), rows_ref, lambda i: span(mine, i, 1))],
        count, row_sends, row_recvs, row_local,
    )
    row, col = tile_masks(tile)
    eyed = (
        lax.broadcasted_iota(jnp.int32, (hd, hd), 0) == lax.broadcasted_iota(jnp.int32, (hd, hd), 1)
    ).astype(F32)

    def first(step, carry):
        same = (row // BLOCK) == (col // BLOCK)
        eye = (row == col).astype(F32)
        chains = [(2 * step + i, h) for i in range(2) for h in range(heads)]
        ts, ls, ks, vs, bs = [], [], [], [], []
        for index, h in chains:
            rows = pl.ds(pl.multiple_of(index * tile, tile), tile)
            lanes = slice(h * hd, (h + 1) * hd)
            k = k_ref[rows, lanes]
            logit = jnp.sum(eye * logit_buf[rows, h : h + 1], axis=0, keepdims=True)
            sigma = jax.nn.sigmoid(logit)
            b = sigma * pad_ref[pl.ds(index, 1), :]
            sigma_ref[index, h : h + 1, :] = sigma
            brow_ref[index, h : h + 1, :] = b
            bcol = jnp.sum(eye * b, axis=1, keepdims=True)
            low = jnp.where(same & (row > col), mm(k, k, NT) * bcol, 0.0)
            ls.append(low)
            ks.append(k)
            vs.append(v_ref[rows, lanes])
            bs.append(b)
            ts.append(eye - jnp.where((row // 2) == (col // 2), low, 0.0))
        size = 2
        while size < BLOCK:
            cut = ((row // (2 * size)) == (col // (2 * size))) & ((row // size) != (col // size))
            mids = [mm_ww(jnp.where(cut, l, 0.0), t) for l, t in zip(ls, ts)]
            ts = [t - mm_ww(t, m) for t, m in zip(ts, mids)]
            size *= 2
        for at, (index, h) in enumerate(chains):
            rows = pl.ds(pl.multiple_of(index * tile, tile), tile)
            lanes = slice(h * hd, (h + 1) * hd)
            t_ref[h, rows, :] = ts[at]
            wu = mm_wl(ts[at] * bs[at], jnp.concatenate([ks[at], vs[at]], axis=1))
            wide_ref[rows, lanes] = wu[:, :hd]
            u_buf[rows, lanes] = wu[:, hd:]
            for part in range(2):
                sub = slice(part * BLOCK, (part + 1) * BLOCK)
                ab = mm_lw(ks[at][sub], wu[sub], TN)
                a_ref[h, index * 2 + part] = eyed - ab[:, :hd]
                c_buf[h, index * 2 + part] = ab[:, hd:]
        return carry

    lax.fori_loop(0, blocks // 4, first, 0)
    beside.forward(1)

    def chain(index, states):
        keep = persist_ref[index]
        new = []
        for h in range(heads):
            s = states[h] * keep
            s_ref[h, index] = s
            new.append(mm_ww(a_ref[h, index], s) + c_buf[h, index])
        return tuple(new)

    lax.fori_loop(0, blocks, chain, tuple(jnp.zeros((hd, hd), F32) for _ in range(heads)))

    def last(step, carry):
        lower_row, lower_col = tile_masks(BLOCK)
        for part in range(2):
            index = 2 * step + part
            rows = pl.ds(pl.multiple_of(index * BLOCK, BLOCK), BLOCK)
            for h in range(heads):
                lanes = slice(h * hd, (h + 1) * hd)
                q, k, s = q_ref[rows, lanes], k_ref[rows, lanes], s_ref[h, index]
                f = u_buf[rows, lanes] - mm_ww(wide_ref[rows, lanes], s)
                p = jnp.where(lower_row >= lower_col, mm(q, k, NT), 0.0)
                f_ref[rows, lanes] = f
                mixed = mm_lw(q, s) + mm_ww(p, f)
                mixed_ref[rows, lanes] = mixed
                scale = lax.rsqrt(jnp.mean(mixed * mixed, axis=1, keepdims=True) + EPSILON)
                on_buf[rows, lanes] = (mixed * scale * gain_ref[0:1, :]).astype(BF)
        return carry

    for turn in range(2, beside.turns()):
        beside.forward(turn)
    gather = Gather(count, on_buf, full_ref, 1, gather_sends, gather_recvs, local, 0, depth + 1)
    lax.fori_loop(0, blocks // 4, last, 0)
    gather.start_half(0)
    lax.fori_loop(blocks // 4, blocks // 2, last, 0)
    gather.start_half(1)
    gather.start_own()
    for turn in range(gather.turns()):
        gather.forward(turn)
    gather.finish()
    beside.finish()
    wait_all(exchange)
    wait_all(tiles)


def front(count, depth, heads, main, persist, x, w_qkv, w_beta, taps, pad, gain, own, g, down, ends):
    total, features = x.shape
    mine = features // count
    hd = mine // heads
    blocks, tiles = total // BLOCK, total // (2 * BLOCK)
    wide = jax.ShapeDtypeStruct((total, mine), F32)
    low = jax.ShapeDtypeStruct((total, mine), BF)
    strength = jax.ShapeDtypeStruct((tiles, heads, 2 * BLOCK), F32)
    states = jax.ShapeDtypeStruct((heads, blocks, hd, hd), F32)
    return pl.pallas_call(
        functools.partial(front_kernel, count, depth, heads, main),
        out_shape=(
            jax.ShapeDtypeStruct((total, 3 * mine), BF),
            low, low, low, strength, strength, wide,
            jax.ShapeDtypeStruct((heads, total, 2 * BLOCK), F32),
            wide, states, wide, states,
            jax.ShapeDtypeStruct((total, mine * count), BF),
            jax.ShapeDtypeStruct((features, mine), BF),
            jax.ShapeDtypeStruct((mine, features), BF),
            jax.ShapeDtypeStruct((total, features), BF),
            jax.ShapeDtypeStruct((count * down.shape[0] * main // 128 + count * ends.shape[0], 128), BF),
        ),
        in_specs=[
            pl.BlockSpec(memory_space=pltpu.SMEM),
            VMEM, VMEM, VMEM, VMEM, VMEM, VMEM, ANY, ANY, ANY, ANY,
        ],
        out_specs=(VMEM,) * 12 + (ANY,) * 5,
        scratch_shapes=[
            pltpu.VMEM((total + 8, 3 * mine), F32),
            pltpu.VMEM((total, w_beta.shape[1]), F32),
            pltpu.VMEM((total, mine), F32),
            pltpu.VMEM((heads, blocks, hd, hd), F32),
            pltpu.VMEM((total, mine), BF),
            pltpu.SemaphoreType.DMA((depth + 2,)),
            pltpu.SemaphoreType.DMA((4 * count,)),
            pltpu.SemaphoreType.DMA((4 * count,)),
            pltpu.SemaphoreType.DMA((depth * count,)),
            pltpu.SemaphoreType.DMA((depth * count,)),
            pltpu.SemaphoreType.DMA((count,)),
            pltpu.SemaphoreType.DMA((count,)),
            pltpu.SemaphoreType.DMA((1,)),
            pltpu.SemaphoreType.DMA(((main // 128 + 1) * count,)),
            pltpu.SemaphoreType.DMA(((main // 128 + 1) * count,)),
            pltpu.SemaphoreType.DMA((main // 128 + 1,)),
        ],
        compiler_params=comm_params(4, 52),
    )(persist, x, w_qkv, w_beta, taps, pad, gain, own, g, down, ends)


def middle_kernel(
    count, full_ref, w_ref, x_ref, gain_ref, mid_ref, normed_ref,
    staged, landed, low_buf, sends, recvs, local, gather_sends, gather_recvs,
):
    me = lax.axis_index("seq")
    rows, features = x_ref.shape
    mine = w_ref.shape[1]
    greet(others("seq", count))
    copies = []
    for step in list(range(1, count)) + [0]:
        peer = lax.rem(me + step, count)
        at = pl.ds(pl.multiple_of(peer * rows, rows), rows)
        staged[step] = mm(full_ref[at, :], w_ref[...])
        target = landed.at[span(mine, me, 1)]
        if step:
            copies.append(send(staged.at[step], target, sends, recvs, step, "seq", peer))
        else:
            own = pltpu.make_async_copy(staged.at[0], target, local.at[0])
            own.start()
            copies.append(own)
    wait_all(copies)
    for at in range(0, rows, 16):
        part = slice(at, at + 16)
        value = x_ref[part, :].astype(F32) + landed[part, :]
        mid_ref[part, :] = value
        scale = lax.rsqrt(jnp.mean(value * value, axis=1, keepdims=True) + EPSILON)
        low_buf[part, :] = (value * scale * gain_ref[0:1, :]).astype(BF)
    gather = Gather(count, low_buf, normed_ref, 0, gather_sends, gather_recvs, local, 0, 1)
    gather.start()
    for turn in range(gather.turns()):
        gather.forward(turn)
    gather.finish()


def middle(count, full, w_out, x, gain):
    rows, features = x.shape
    mine = w_out.shape[1]
    return pl.pallas_call(
        functools.partial(middle_kernel, count),
        out_shape=(
            jax.ShapeDtypeStruct((rows, features), F32),
            jax.ShapeDtypeStruct((rows * count, features), BF),
        ),
        in_specs=[VMEM] * 4,
        out_specs=(VMEM, ANY),
        scratch_shapes=[
            pltpu.VMEM((count, rows, mine), F32),
            pltpu.VMEM((rows, features), F32),
            pltpu.VMEM((rows, features), BF),
            pltpu.SemaphoreType.DMA((count,)),
            pltpu.SemaphoreType.DMA((count,)),
            pltpu.SemaphoreType.DMA((3,)),
            pltpu.SemaphoreType.DMA((2 * count,)),
            pltpu.SemaphoreType.DMA((2 * count,)),
        ],
        compiler_params=comm_params(5),
    )(full, w_out, x, gain)


def norm_backward(value_ref, grad_ref, beside_ref, gain_ref, out_ref, gain_out, low_ref=None):
    rows, features = out_ref.shape
    gain_out[...] = jnp.zeros((8, features), F32)
    for at in range(0, rows, 8):
        part = slice(at, at + 8)
        value = value_ref[part, :].astype(F32)
        scale = lax.rsqrt(jnp.mean(value * value, axis=1, keepdims=True) + EPSILON)
        unit = value * scale
        grad = grad_ref[part, :]
        gain_out[...] += grad * unit
        scaled = grad * gain_ref[0:1, :]
        mean = jnp.mean(scaled * unit, axis=1, keepdims=True)
        result = beside_ref[part, :].astype(F32) + scale * (scaled - unit * mean)
        out_ref[part, :] = result
        if low_ref is not None:
            half = (at // 16) * 16
            if at % 16 == 8:
                low_ref[half : half + 16, :] = out_ref[half : half + 16, :].astype(BF)


def reduce_kernel(
    count, part_ref, mid_ref, g_ref, gain_ref, grad_ref, gain_out, full_ref,
    summed, low_buf, landing, outgoing, kept, sends, recvs, local, gather_sends, gather_recvs,
):
    greet(hypercube_peers(count))
    scatter = Scatter(count, part_ref, summed, landing, outgoing, kept, sends, recvs)
    scatter.start()
    for turn in range(scatter.bits):
        scatter.turn(turn)
    norm_backward(mid_ref, summed, g_ref, gain_ref, grad_ref, gain_out, low_buf)
    gather = Gather(count, low_buf, full_ref, 0, gather_sends, gather_recvs, local, 0, 0)
    gather.start()
    for turn in range(gather.turns()):
        gather.forward(turn)
    gather.finish()
    scatter.finish()


def reduce_middle(count, parts, mid, g, gain):
    rows, features = mid.shape
    return pl.pallas_call(
        functools.partial(reduce_kernel, count),
        out_shape=(
            jax.ShapeDtypeStruct((rows, features), F32),
            jax.ShapeDtypeStruct((8, features), F32),
            jax.ShapeDtypeStruct((rows * count, features), BF),
        ),
        in_specs=[VMEM] * 4,
        out_specs=(VMEM, VMEM, ANY),
        scratch_shapes=[pltpu.VMEM((rows, features), F32), pltpu.VMEM((rows, features), BF)]
        + scatter_scratch(count, rows, features)
        + [
            pltpu.SemaphoreType.DMA((1,)),
            pltpu.SemaphoreType.DMA((2 * count,)),
            pltpu.SemaphoreType.DMA((2 * count,)),
        ],
        compiler_params=comm_params(6),
    )(parts, mid, g, gain)


def back_kernel(
    count, heads, persist_ref, full_ref, rows_ref, mixed_ref, gain_ref, taps_ref, pre_ref, q_ref, k_ref, v_ref,
    brow_ref, sigma_ref, pad_ref, t_ref, wide_ref, s_ref, f_ref, a_ref, done_ref,
    dpre_ref, taps_out, gain_out, main_ref, ends_ref, *scratch,
):
    total, mine = mixed_ref.shape
    hd = mine // heads
    blocks = total // BLOCK
    beta_lanes = dpre_ref.shape[1] - 3 * mine
    do_buf, y_buf, c_buf, g_buf, pre_buf, conv_buf, pass_sends, pass_recvs, local = scratch
    greet(others("seq", count))
    exchange = start_exchange(
        folded_pieces(done_ref, main_ref, ends_ref, count), count, pass_sends, pass_recvs, local
    )
    gain_out[...] = jnp.zeros((8, hd), F32)
    taps_out[...] = jnp.zeros((3 * CONV, 8, mine), F32)
    pre_buf[0:8, :] = jnp.zeros((8, 3 * mine), F32)
    conv_buf[total : total + 8, :] = jnp.zeros((8, 3 * mine), F32)
    chunk = 4 * BLOCK

    def heads_in(index, carry):
        rows = pl.ds(pl.multiple_of(index * chunk, chunk), chunk)
        pre_buf[pl.ds(pl.multiple_of(index * chunk + 8, 8), chunk), :] = pre_ref[rows, :].astype(F32)
        grad = mm(full_ref[rows, :], rows_ref[...], NT)
        for h in range(heads):
            lanes = slice(h * hd, (h + 1) * hd)
            mixed, don = mixed_ref[rows, lanes], grad[:, lanes]
            scale = lax.rsqrt(jnp.mean(mixed * mixed, axis=1, keepdims=True) + EPSILON)
            unit = mixed * scale
            gain_out[...] += jnp.sum((don * unit).reshape(chunk // 8, 8, hd), axis=0)
            scaled = don * gain_ref[0:1, :]
            mean = jnp.mean(scaled * unit, axis=1, keepdims=True)
            do_buf[rows, lanes] = scale * (scaled - unit * mean)
        return carry

    lax.fori_loop(0, total // chunk, heads_in, 0)
    row, col = tile_masks(BLOCK)

    def first(step, carry):
        for part in range(2):
            index = 2 * step + part
            rows = pl.ds(pl.multiple_of(index * BLOCK, BLOCK), BLOCK)
            for h in range(heads):
                lanes = slice(h * hd, (h + 1) * hd)
                q, k, do = q_ref[rows, lanes], k_ref[rows, lanes], do_buf[rows, lanes]
                p = jnp.where(row >= col, mm(q, k, NT), 0.0)
                y = mm_ww(p, do, TN)
                y_buf[rows, lanes] = y
                c_buf[h, index] = mm_lw(q, do, TN) - mm_ww(wide_ref[rows, lanes], y, TN)
        return carry

    lax.fori_loop(0, blocks // 2, first, 0)

    def chain(step, grads):
        index = blocks - 1 - step
        keep = persist_ref[index]
        new = []
        for h in range(heads):
            g = grads[h]
            g_buf[h, index] = g
            new.append((mm_ww(a_ref[h, index], g, TN) + c_buf[h, index]) * keep)
        return tuple(new)

    lax.fori_loop(0, blocks, chain, tuple(jnp.zeros((hd, hd), F32) for _ in range(heads)))

    def last(step, carry):
        for part in range(2):
            index = 2 * step + part
            keep = persist_ref[index]
            rows = pl.ds(pl.multiple_of(index * BLOCK, BLOCK), BLOCK)
            half = slice(part * BLOCK, (part + 1) * BLOCK)
            lane = lax.broadcasted_iota(jnp.int32, (BLOCK, beta_lanes), 1)
            dlogits = jnp.zeros((BLOCK, beta_lanes), F32)
            for h in range(heads):
                lanes = slice(h * hd, (h + 1) * hd)
                q, k, v = q_ref[rows, lanes], k_ref[rows, lanes], v_ref[rows, lanes]
                do, s, f, g = do_buf[rows, lanes], s_ref[h, index], f_ref[rows, lanes], g_buf[h, index]
                b = brow_ref[step, h : h + 1, half]
                bcol = jnp.sum(jnp.where(row == col, b, 0.0), axis=1, keepdims=True)
                t = t_ref[h, rows, half]
                df = y_buf[rows, lanes] + mm_lw(k, g)
                dr = mm_ww(t, df, TN)
                dp = jnp.where(row >= col, mm_ww(do, f, NT), 0.0)
                dl = jnp.where(row > col, -mm_ww(dr, f, NT), 0.0)
                dq = mm_ww(do, s, NT) + mm_wl(dp, k)
                dkb = mm_wl(dl, k) - mm_ww(dr, s, NT)
                dk = mm_wl(dp, q, TN) + mm_ww(f, g, NT) + mm_wl(dl * bcol, k, TN) + bcol * dkb
                dbeta = jnp.sum(dr * v.astype(F32) + dkb * k.astype(F32), axis=1, keepdims=True)
                sigma = sigma_ref[step, h : h + 1, half]
                slope = pad_ref[pl.ds(step, 1), half] * sigma * (1.0 - sigma)
                slope = jnp.sum(jnp.where(row == col, slope, 0.0), axis=1, keepdims=True)
                dlogits = jnp.where(lane == h, dbeta * slope, dlogits)
                for member, grad in enumerate((dq, dk, bcol * dr)):
                    there = slice(member * mine + h * hd, member * mine + (h + 1) * hd)
                    window = pre_buf[pl.ds(pl.multiple_of(index * BLOCK, 8), BLOCK + 8), there]
                    summed, shifts = shifted_sum(window, taps_ref, member, lanes, keep)
                    sigma = jax.nn.sigmoid(summed)
                    if member < 2:
                        value = summed * sigma
                        inverse = lax.rsqrt(jnp.sum(value * value, axis=1, keepdims=True) + EPSILON)
                        unit = value * inverse
                        along = jnp.sum(grad * unit, axis=1, keepdims=True)
                        grad = (grad - unit * along) * inverse
                    if member == 0:
                        grad = grad * hd ** (-0.5)
                    grad = grad * (sigma * (1.0 + summed * (1.0 - sigma)))
                    conv_buf[rows, there] = grad
                    for lagged in range(CONV):
                        taps_out[member * CONV + lagged, :, lanes] += jnp.sum(
                            (grad * shifts[lagged]).reshape(BLOCK // 8, 8, hd), axis=0
                        )
            dpre_ref[rows, 3 * mine :] = dlogits.astype(BF)
        return carry

    lax.fori_loop(0, blocks // 2, last, 0)

    def spread(index, carry):
        rows = pl.ds(pl.multiple_of(index * BLOCK, BLOCK), BLOCK)
        keep = persist_ref[jnp.minimum(index + 1, blocks - 1)]
        block_row = lax.broadcasted_iota(jnp.int32, (BLOCK, 1), 0)
        for member in range(3):
            there = slice(member * mine, (member + 1) * mine)
            window = conv_buf[pl.ds(pl.multiple_of(index * BLOCK, 8), BLOCK + 8), there]
            summed = window[:BLOCK] * taps_ref[member * CONV : member * CONV + 1, :]
            for lagged in range(1, CONV):
                at = member * CONV + lagged
                moved = pltpu.roll(window, BLOCK + 8 - lagged, 0)[:BLOCK]
                moved = moved * jnp.where(block_row < BLOCK - lagged, 1.0, keep)
                summed = summed + moved * taps_ref[at : at + 1, :]
            dpre_ref[rows, there] = summed.astype(BF)
        return carry

    lax.fori_loop(0, blocks, spread, 0)
    wait_all(exchange)


def back(
    count, heads, persist, full, w_rows, mixed, gain, taps, pre, q, k, v, strength, saved, done, main
):
    total, mine = mixed.shape
    hd = mine // heads
    blocks = total // BLOCK
    owned = done.shape[0] // (count * main // 128 + count // 2)
    members = main // 128 + 1
    return pl.pallas_call(
        functools.partial(back_kernel, count, heads),
        out_shape=(
            jax.ShapeDtypeStruct((total, 3 * mine + 128), BF),
            jax.ShapeDtypeStruct((3 * CONV, 8, mine), F32),
            jax.ShapeDtypeStruct((8, hd), F32),
            jax.ShapeDtypeStruct((owned, count * main), BF),
            jax.ShapeDtypeStruct((owned // 2, count * 128), BF),
        ),
        in_specs=[pl.BlockSpec(memory_space=pltpu.SMEM)] + [VMEM] * 17 + [ANY],
        out_specs=(VMEM,) * 3 + (ANY,) * 2,
        scratch_shapes=[
            pltpu.VMEM((total, mine), F32),
            pltpu.VMEM((total, mine), F32),
            pltpu.VMEM((heads, blocks, hd, hd), F32),
            pltpu.VMEM((heads, blocks, hd, hd), F32),
            pltpu.VMEM((total + 8, 3 * mine), F32),
            pltpu.VMEM((total + 8, 3 * mine), F32),
            pltpu.SemaphoreType.DMA((members * count,)),
            pltpu.SemaphoreType.DMA((members * count,)),
            pltpu.SemaphoreType.DMA((members,)),
        ],
        compiler_params=comm_params(7, 56),
    )(persist, full, w_rows, mixed, gain, taps, pre, q, k, v, *strength, *saved, done)


def end_kernel(
    count, part_ref, added_ref, x_ref, mid_ref, beside_ref, gain_ref,
    grad_ref, gain_out, out_ref, summed, added, *scratch
):
    greet(hypercube_peers(count))
    scatter = Scatter(count, part_ref, summed, *scratch[:5])
    beside = Scatter(count, added_ref, added, *scratch[5:])
    scatter.start()
    beside.start()
    for turn in range(scatter.bits):
        scatter.turn(turn)
        beside.turn(turn)
    norm_backward(x_ref, summed, beside_ref, gain_ref, grad_ref, gain_out)
    for at in range(0, out_ref.shape[0], 16):
        part = slice(at, at + 16)
        out_ref[part, :] = (mid_ref[part, :] + added[part, :]).astype(BF)
    scatter.finish()
    beside.finish()


def folded_pieces(source, main_ref, ends_ref, count, main=None):
    main = main_ref.shape[1] // count if main is None else main
    rows, half = main_ref.shape[0], ends_ref.shape[0]
    pieces = []
    for tile in range(main // 128):
        pieces.append(
            (
                source,
                lambda i, tile=tile: span(rows, tile * count + i, 0),
                main_ref,
                lambda i, tile=tile: (
                    slice(None), pl.ds(pl.multiple_of(i * main + tile * 128, 128), 128)
                ),
            )
        )
    pieces.append(
        (
            source,
            lambda i: (
                pl.ds(pl.multiple_of(main // 128 * count * rows + i * half, half), half),
                slice(None),
            ),
            ends_ref,
            lambda i: span(128, i, 1),
        )
    )
    return pieces


def row_pieces(sources, targets, sizes, count):
    pieces = []
    for source, widths in zip(sources, sizes):
        rows, at = source.shape[0] // count, 0
        for size in widths:
            pieces.append(
                (
                    source,
                    lambda i, rows=rows, at=at, size=size: (
                        pl.ds(pl.multiple_of(i * rows, rows), rows),
                        slice(at, at + size),
                    ),
                    targets[len(pieces)],
                    lambda i, size=size: span(size, i, 1),
                )
            )
            at += size
    return pieces


def row_shapes(sources, sizes, count):
    return tuple(
        jax.ShapeDtypeStruct((source.shape[0] // count, count * size), BF)
        for source, widths in zip(sources, sizes)
        for size in widths
    )


def end(count, parts, added, x, mid, beside, gain):
    rows, features = x.shape
    return pl.pallas_call(
        functools.partial(end_kernel, count),
        out_shape=(
            jax.ShapeDtypeStruct((rows, features), F32),
            jax.ShapeDtypeStruct((8, features), F32),
            jax.ShapeDtypeStruct((rows, features), BF),
        ),
        in_specs=[VMEM] * 6,
        out_specs=(VMEM,) * 3,
        scratch_shapes=[pltpu.VMEM((rows, features), F32)] * 2
        + scatter_scratch(count, rows, features)
        + scatter_scratch(count, rows, features),
        compiler_params=comm_params(8),
    )(parts, added, x, mid, beside, gain)


def hidden_grads_kernel(count, rest, g_ref, pair_ref, down_ref, low_ref, w_ref):
    main = w_ref.shape[1] - 128
    lane = lax.broadcasted_iota(jnp.int32, (1, 128), 1)

    @pl.when(pl.program_id(0) == 0)
    def assemble():
        depth = down_ref.shape[0]
        level = w_ref.shape[0] // depth
        rows = level // count
        for z in range(depth):
            at = z * level
            for tile in range(main // 128):
                w_ref[at : at + level, tile * 128 : (tile + 1) * 128] = down_ref[
                    z, tile * level : (tile + 1) * level, :
                ]
            for i in range(count):
                start = main // 128 * level + i * (rows // 2)
                pair = down_ref[z, start : start + rows // 2, :].astype(F32)
                for part in range(2):
                    piece = pair if part == 0 else pltpu.roll(pair, rest, 1)
                    first = at + i * rows + part * (rows // 2)
                    w_ref[first : first + rows // 2, main:] = jnp.where(
                        lane < rest, piece, 0.0
                    ).astype(BF)

    grad = mm(g_ref[...], w_ref[...])

    def slopes(gate, up, grad):
        sigma = jax.nn.sigmoid(gate)
        return grad * up * sigma * (1.0 + gate * (1.0 - sigma)), grad * (gate * sigma)

    dgate, dup = slopes(pair_ref[:, :main], pair_ref[:, main : 2 * main], grad[:, :main])
    low_ref[:, :main] = dgate.astype(BF)
    low_ref[:, main : 2 * main] = dup.astype(BF)
    tail = pair_ref[:, 2 * main :]
    dgate, dup = slopes(tail, pltpu.roll(tail, rest, 1), grad[:, main:])
    low_ref[:, 2 * main :] = jnp.where(lane < rest, dgate, pltpu.roll(dup, rest, 1)).astype(BF)


def hidden_gradients(count, rest, g, pair, down):
    total, features = g.shape
    main = (pair.shape[1] - 2 * rest) // 2
    step = total // 4
    return pl.pallas_call(
        functools.partial(hidden_grads_kernel, count, rest),
        grid=(total // step,),
        out_shape=(
            jax.ShapeDtypeStruct(pair.shape, BF),
            jax.ShapeDtypeStruct((features, main + 128), BF),
        ),
        in_specs=[
            pl.BlockSpec((step, features), lambda i: (i, 0)),
            pl.BlockSpec((step, pair.shape[1]), lambda i: (i, 0)),
            pl.BlockSpec(down.shape, lambda i: (0, 0, 0)),
        ],
        out_specs=(
            pl.BlockSpec((step, pair.shape[1]), lambda i: (i, 0)),
            pl.BlockSpec((features, main + 128), lambda i: (0, 0)),
        ),
        compiler_params=pltpu.CompilerParams(vmem_limit_bytes=40 * 2**20),
        cost_estimate=pl.CostEstimate(
            flops=2 * total * features * (main + 128),
            bytes_accessed=2 * total * features + 6 * total * pair.shape[1],
            transcendentals=total * pair.shape[1] // 2,
        ),
    )(g, pair, down)


def down_grads_kernel(count, rest, g_ref, hidden_ref, out_ref):
    grad = mm(g_ref[...], hidden_ref[...], TN)
    level = grad.shape[0]
    main = grad.shape[1] - 128
    rows = level // count
    lane = lax.broadcasted_iota(jnp.int32, (1, 128), 1)
    for tile in range(main // 128):
        out_ref[tile * level : (tile + 1) * level, :] = grad[:, tile * 128 : (tile + 1) * 128].astype(BF)
    for i in range(count):
        at = i * rows
        front = grad[at : at + rows // 2, main:]
        later = pltpu.roll(grad[at + rows // 2 : at + rows, main:], rest, 1)
        start = main // 128 * level + i * (rows // 2)
        out_ref[start : start + rows // 2, :] = jnp.where(lane < rest, front, later).astype(BF)


def down_gradients(count, depth, rest, g, hidden):
    total, features = g.shape
    width = hidden.shape[1]
    level = features // depth
    high = (width - 128) // 128 * level + level // 2
    return pl.pallas_call(
        functools.partial(down_grads_kernel, count, rest),
        grid=(depth,),
        out_shape=jax.ShapeDtypeStruct((depth * high, 128), BF),
        in_specs=[
            pl.BlockSpec((total, level), lambda i: (0, i)),
            pl.BlockSpec((total, width), lambda i: (0, 0)),
        ],
        out_specs=pl.BlockSpec((high, 128), lambda i: (i, 0)),
        compiler_params=pltpu.CompilerParams(vmem_limit_bytes=40 * 2**20),
        cost_estimate=pl.CostEstimate(
            flops=2 * total * features * width,
            bytes_accessed=2 * total * (features + width) + 2 * features * width,
            transcendentals=0,
        ),
    )(g, hidden)


def mixer_grads_kernel(x_ref, grad_ref, on_ref, out_ref, low_ref, beta_ref):
    wide = 3 * out_ref.shape[1]
    front = mm(x_ref[...], grad_ref[:, :wide], TN)
    low_ref[:, :wide] = front.astype(BF)
    beta_ref[...] = mm(grad_ref[:, wide:], x_ref[...], TN)[: beta_ref.shape[0]]
    low_ref[:, wide:] = mm(on_ref[...], out_ref[...], TN).astype(BF)


def mixer_gradients(x, grad, on, out):
    total, features = x.shape
    beta = grad.shape[1] - 3 * out.shape[1]
    wide = grad.shape[1] - beta + out.shape[1]
    step = features // 4
    return pl.pallas_call(
        mixer_grads_kernel,
        grid=(features // step,),
        out_shape=(
            jax.ShapeDtypeStruct((features, wide), BF),
            jax.ShapeDtypeStruct((8, features), F32),
        ),
        in_specs=[
            pl.BlockSpec((total, step), lambda i: (0, i)),
            pl.BlockSpec(grad.shape, lambda i: (0, 0)),
            pl.BlockSpec((total, step), lambda i: (0, i)),
            pl.BlockSpec(out.shape, lambda i: (0, 0)),
        ],
        out_specs=(
            pl.BlockSpec((step, wide), lambda i: (i, 0)),
            pl.BlockSpec((8, step), lambda i: (0, i)),
        ),
        compiler_params=pltpu.CompilerParams(vmem_limit_bytes=40 * 2**20),
        cost_estimate=pl.CostEstimate(
            flops=2 * total * features * (wide + beta),
            bytes_accessed=4 * total * features + 4 * features * wide,
            transcendentals=0,
        ),
    )(x, grad, on, out)


def rest_and_main(hidden_width, count):
    main = hidden_width // (128 * count) * 128
    return hidden_width // count - main, main


def local_heads(
    tokens,
    doc_starts,
    pad_mask,
    norm1_gain,
    query_weight,
    key_weight,
    value_weight,
    conv_weight,
    beta_weight,
    out_norm_gain,
    out_weight,
    norm2_gain,
    gate_weight,
    up_weight,
    down_weight,
    cotangent,
):
    row_count, features = tokens.shape
    width = lax.axis_size("seq")
    place = lax.axis_index("seq")
    head_dim = out_norm_gain.shape[0]
    heads = beta_weight.shape[1] // width
    mine = heads * head_dim
    total = row_count * width
    depth = lax.axis_size("dp")
    level = lax.axis_index("dp")
    owned = norm1_gain.shape[0]
    rest, main = rest_and_main(gate_weight.shape[1], width)
    w_beta = lax.dynamic_slice_in_dim(beta_weight, place * heads, heads, axis=1)

    small_all, w_qkv, out_native, pair_part, down_rest, normed_full = start(
        width,
        depth,
        main,
        [norm1_gain[None], norm2_gain[None], conv_weight, pad_mask, doc_starts],
        tokens,
        [query_weight, key_weight, value_weight, out_weight],
        gate_weight,
        up_weight,
        down_weight.T,
    )
    w_pair = lax.all_gather(pair_part.reshape(width * owned, -1), "dp", axis=0, tiled=True)
    small_all = small_all.reshape(width, depth, -1, small_all.shape[2])
    wide = small_all[:, :, : 3 * CONV + 2, :owned].transpose(2, 1, 0, 3)
    wide = wide.reshape(3 * CONV + 2, features)
    gain_first, gain_second = wide[3 * CONV], wide[3 * CONV + 1]
    taps = lax.dynamic_slice_in_dim(wide[: 3 * CONV], place * mine, mine, axis=1)
    marks = lax.dynamic_index_in_dim(small_all[:, :, 3 * CONV + 2 :], level, 1, keepdims=False)
    pad_rows = marks[:, 0, :row_count].reshape(-1, 2 * BLOCK)
    starts = marks[:, 1, : doc_starts.shape[1]].reshape(-1).astype(jnp.int32)
    begins = BLOCK * jnp.arange(total // BLOCK, dtype=jnp.int32)
    persist = (starts != begins).astype(F32)
    beta_wide = jnp.pad(w_beta, ((0, 0), (0, 128 - heads)))
    w_front = jnp.concatenate([w_qkv, beta_wide], axis=1)
    head_gain = out_norm_gain.astype(F32)[None]
    (
        projected, queries, key_rows, values, strength, sigma_vals, mixed,
        *saved, out_full, w_out, w_out_rows, cotangent_full, down_part,
    ) = front(
        width, depth, heads, main, persist, normed_full, w_qkv, beta_wide, taps, pad_rows, head_gain,
        out_native, cotangent, down_weight.T, down_rest,
    )
    down_tiles = lax.all_gather(down_part, "dp", axis=0)
    residual_mid, normed_two_full = middle(width, out_full, w_out, tokens, gain_second[None])
    normed_two_full, w_front = lax.optimization_barrier((normed_two_full, w_front))
    pair = product(normed_two_full, w_pair)
    tail = pair[:, 2 * main :]
    gate_out = jnp.concatenate([pair[:, :main], tail], axis=1)
    up_out = jnp.concatenate([pair[:, main : 2 * main], jnp.roll(tail, rest, axis=1)], axis=1)
    gate_sigma = jax.nn.sigmoid(gate_out)
    gate_silu = gate_out * gate_sigma
    hidden = (gate_silu * up_out).astype(BF)
    down_grads = down_gradients(width, depth, rest, cotangent_full, hidden)
    down_tiles, _ = lax.optimization_barrier((down_tiles, down_grads))
    down_sums = lax.psum_scatter(down_grads, "dp", scatter_dimension=0, tiled=True)
    pair_grad_low, w_down = hidden_gradients(width, rest, cotangent_full, pair, down_tiles)
    two_parts = product_right(pair_grad_low, w_pair).astype(BF)
    pair_grads = product_left(normed_two_full, pair_grad_low).astype(BF)
    pair_grads, two_parts = lax.optimization_barrier((pair_grads, two_parts))
    pair_sums = lax.psum_scatter(pair_grads, "dp", scatter_dimension=0, tiled=True)
    residual_mid_grad, gain_second_rows, mid_full = reduce_middle(
        width, two_parts, residual_mid, cotangent, gain_second[None]
    )
    projected_grad, conv_rows_grad, out_gain_rows, down_main, down_ends = back(
        width, heads, persist, mid_full, w_out_rows, mixed, head_gain, taps, projected,
        queries, key_rows, values, (strength, sigma_vals, pad_rows), saved, down_sums, main,
    )
    gain_second_grad = jnp.sum(gain_second_rows, axis=0)
    out_gain_grad = jnp.sum(out_gain_rows, axis=0)
    conv_grad = jnp.sum(conv_rows_grad, axis=1)
    mid_mine = lax.dynamic_slice_in_dim(mid_full, place * mine, mine, axis=1)
    mixer_grads, beta_grads = mixer_gradients(normed_full, projected_grad, out_full, mid_mine)
    beta_grad = beta_grads[:heads]
    mixer_sums = lax.psum_scatter(mixer_grads, "dp", scatter_dimension=0, tiled=True)
    normed_parts = product_right(projected_grad, w_front).astype(BF)
    hidden, normed_parts = lax.optimization_barrier((hidden, normed_parts))
    added_parts = product_right(hidden, w_down).astype(BF)
    tokens_grad, gain_first_rows, output = end(
        width, normed_parts, added_parts, tokens, residual_mid, residual_mid_grad, gain_first[None]
    )
    gain_first_grad = jnp.sum(gain_first_rows, axis=0)

    gain_row = jnp.pad(out_gain_grad[None], ((0, 0), (0, features - head_dim)))
    plane = jnp.concatenate([gain_first_grad[None], gain_second_grad[None], gain_row], axis=0)
    conv_rows = -(-3 * CONV * mine // features)
    conv_flat = jnp.pad(conv_grad.reshape(-1), (0, conv_rows * features - 3 * CONV * mine))
    levels = jnp.concatenate([beta_grad, conv_flat.reshape(conv_rows, features)], axis=0)
    sums, each, gate_main, up_main, pair_ends = small_sums(
        plane.reshape(8, -1), levels.reshape(8, -1), pair_sums, (main, main, 2 * rest), width, depth
    )
    def joined(front, back, at):
        back = back.reshape(owned, width, 2, rest)[:, :, at].reshape(owned, width * rest)
        return jnp.concatenate([front, back], axis=1).astype(F32)

    down_back = down_ends.reshape(owned // 2, width, 2, rest).transpose(2, 0, 1, 3)
    down_back = down_back.reshape(owned, width * rest)
    shard_gate, shard_up, shard_down = (
        joined(gate_main, pair_ends, 0),
        joined(up_main, pair_ends, 1),
        jnp.concatenate([down_main, down_back], axis=1).astype(F32).T,
    )
    sums = sums.reshape(3, features)
    each = each.reshape(width, heads + conv_rows, features)
    beta_total = each[:, :heads].reshape(width * heads, features).T
    conv_all = each[:, heads:].reshape(width, -1)[:, : 3 * CONV * mine]
    conv_all = conv_all.reshape(width, 3 * CONV, mine).transpose(1, 0, 2).reshape(-1, features)
    wide_sums = jnp.concatenate([sums[:2], conv_all], axis=0)
    own = level * width + place
    wide_own = lax.dynamic_slice_in_dim(wide_sums, own * owned, owned, axis=1)

    mixer_sums, gate_main = lax.optimization_barrier((mixer_sums, gate_main))
    shard_q, shard_k, shard_v, shard_o = (
        a.astype(F32) for a in closing([mixer_sums], width, [(mine,) * 4], 13)
    )

    return (
        output,
        tokens_grad,
        wide_own[0],
        shard_q,
        shard_k,
        shard_v,
        wide_own[2:].reshape(3, CONV, owned),
        beta_total,
        sums[2, :head_dim],
        shard_o,
        wide_own[1],
        shard_gate,
        shard_up,
        shard_down,
    )


def solution(mesh):
    in_specs = (
        P(("dp", "seq"), None),
        P("dp", "seq"),
        P("dp", "seq"),
        P(("dp", "seq")),
        P(("dp", "seq"), None),
        P(("dp", "seq"), None),
        P(("dp", "seq"), None),
        P(None, None, ("dp", "seq")),
        P(),
        P(),
        P(("dp", "seq"), None),
        P(("dp", "seq")),
        P(("dp", "seq"), None),
        P(("dp", "seq"), None),
        P(None, ("dp", "seq")),
        P(("dp", "seq"), None),
    )
    out_specs = (
        P(("dp", "seq"), None),
        P(("dp", "seq"), None),
        P(("dp", "seq")),
        P(("dp", "seq"), None),
        P(("dp", "seq"), None),
        P(("dp", "seq"), None),
        P(None, None, ("dp", "seq")),
        P(),
        P(),
        P(("dp", "seq"), None),
        P(("dp", "seq")),
        P(("dp", "seq"), None),
        P(("dp", "seq"), None),
        P(None, ("dp", "seq")),
    )

    def layer(*arrays):
        head_count, hidden_width = arrays[8].shape[1], arrays[12].shape[1]
        width = mesh.shape["seq"]
        rest, main = rest_and_main(hidden_width, width)
        by_heads = head_count % width == 0 and rest == 64 and main > 0
        by_heads = by_heads and width >= 4 and width & (width - 1) == 0 and head_count // width <= 8
        by_heads = by_heads and arrays[3].shape[0] // mesh.size % 32 == 0
        by_heads = by_heads and 128 % (arrays[3].shape[0] // mesh.size) == 0
        local = local_heads if by_heads else local_sequence
        return jax.shard_map(
            local, mesh=mesh, in_specs=in_specs, out_specs=out_specs, check_vma=False
        )(*arrays)

    return layer
```

```python
import functools

import jax
import jax.numpy as jnp
from jax import lax
from jax.experimental import pallas as pl
from jax.experimental.pallas import tpu as pltpu
from jax.sharding import PartitionSpec as P

CONV = 4
BLOCK = 64


EPSILON = 1e-06
PRECISE = lax.Precision.HIGHEST


def from_behind(array, axis, by):
    length = lax.axis_size(axis)
    pairs = [(i, i + by) for i in range(length) if 0 <= i + by < length]
    return lax.ppermute(array, axis, pairs)


def product(left, right):
    return jnp.dot(left, right, preferred_element_type=jnp.float32)


def product_left(left, right):
    return lax.dot_general(
        left, right, (((0,), (0,)), ((), ())), preferred_element_type=jnp.float32
    )


def product_right(left, right):
    return lax.dot_general(
        left, right, (((1,), (1,)), ((), ())), preferred_element_type=jnp.float32
    )


def rounded(value):
    return lax.optimization_barrier(value.astype(jnp.bfloat16)).astype(jnp.float32)


def rms_norm(value, gain):
    return value * lax.rsqrt(jnp.mean(value * value, axis=-1, keepdims=True) + EPSILON) * gain


def block_parts(queries, key_rows, values, strength):
    keyed = key_rows * strength[..., None]
    block_len = key_rows.shape[1]
    lower_part = jnp.tril(jnp.einsum("hcd,hed->hce", keyed, key_rows, precision=PRECISE), -1)
    system = lower_part + jnp.eye(block_len, dtype=jnp.float32)
    weights = jax.scipy.linalg.solve_triangular(system, keyed, lower=True, unit_diagonal=True)
    updates = jax.scipy.linalg.solve_triangular(
        system, values * strength[..., None], lower=True, unit_diagonal=True
    )
    scores = jnp.tril(jnp.einsum("hcd,hed->hce", queries, key_rows, precision=PRECISE))
    return (weights, updates, scores)


def delta_step(state_now, inputs):
    queries, key_rows, values, strength, persist = inputs
    state_now = state_now * persist
    weights, updates, scores = block_parts(queries, key_rows, values, strength)
    corrected = updates - jnp.einsum("hcd,hde->hce", weights, state_now, precision=PRECISE)
    outputs = jnp.einsum("hcd,hde->hce", queries, state_now, precision=PRECISE) + jnp.einsum(
        "hce,hef->hcf", scores, corrected, precision=PRECISE
    )
    state_now = state_now + jnp.einsum("hcd,hce->hde", key_rows, corrected, precision=PRECISE)
    return (state_now, outputs)


def track_step(holding, inputs):
    state_now, transit = holding
    queries, key_rows, values, strength, persist = inputs
    state_now = state_now * persist
    transit = transit * persist
    weights, updates, scores = block_parts(queries, key_rows, values, strength)
    corrected = updates - jnp.einsum("hcd,hde->hce", weights, state_now, precision=PRECISE)
    outputs = jnp.einsum("hcd,hde->hce", queries, state_now, precision=PRECISE) + jnp.einsum(
        "hce,hef->hcf", scores, corrected, precision=PRECISE
    )
    leading = queries - jnp.einsum("hce,hed->hcd", scores, weights, precision=PRECISE)
    state_now = state_now + jnp.einsum("hcd,hce->hde", key_rows, corrected, precision=PRECISE)
    eraser = jnp.eye(key_rows.shape[2], dtype=jnp.float32) - jnp.einsum(
        "hcd,hce->hde", key_rows, weights, precision=PRECISE
    )
    return (
        (state_now, jnp.einsum("hde,hef->hdf", eraser, transit, precision=PRECISE)),
        (outputs, leading, transit),
    )


def advance(linear, offset_part, incoming):
    return jnp.einsum("hde,hef->hdf", linear, incoming, precision=PRECISE) + offset_part


def into_blocks(array):
    row_count, head_count, head_dim = array.shape
    return array.reshape(row_count // BLOCK, BLOCK, head_count, head_dim).transpose(0, 2, 1, 3)


def from_blocks(array):
    block_count, head_count, block_len, head_dim = array.shape
    return array.transpose(0, 2, 1, 3).reshape(block_count * block_len, head_count, head_dim)


def local_sequence(
    tokens,
    doc_starts,
    pad_mask,
    norm1_gain,
    query_weight,
    key_weight,
    value_weight,
    conv_weight,
    beta_weight,
    out_norm_gain,
    out_weight,
    norm2_gain,
    gate_weight,
    up_weight,
    down_weight,
    cotangent,
):
    row_count, features = tokens.shape
    head_count = beta_weight.shape[1]
    head_dim = out_norm_gain.shape[0]
    block_count = row_count // BLOCK
    w_query, w_key, w_value, w_out, conv_full, gain_first = (
        lax.all_gather(query_weight, ("dp", "seq"), axis=0, tiled=True),
        lax.all_gather(key_weight, ("dp", "seq"), axis=0, tiled=True),
        lax.all_gather(value_weight, ("dp", "seq"), axis=0, tiled=True),
        lax.all_gather(out_weight, ("dp", "seq"), axis=0, tiled=True),
        lax.all_gather(conv_weight, ("dp", "seq"), axis=2, tiled=True),
        lax.all_gather(norm1_gain, ("dp", "seq"), axis=0, tiled=True),
    )
    w_gate, w_up, w_down, gain_second = (
        lax.all_gather(gate_weight, ("dp", "seq"), axis=0, tiled=True),
        lax.all_gather(up_weight, ("dp", "seq"), axis=0, tiled=True),
        lax.all_gather(down_weight, ("dp", "seq"), axis=1, tiled=True),
        lax.all_gather(norm2_gain, ("dp", "seq"), axis=0, tiled=True),
    )
    seq_place = lax.axis_index("seq")
    positions = seq_place * row_count + jnp.arange(row_count, dtype=jnp.int32)
    starts = doc_starts[0]
    offsets = jnp.repeat(starts, BLOCK)
    persist = (
        starts != seq_place * row_count + BLOCK * jnp.arange(block_count, dtype=jnp.int32)
    ).astype(jnp.float32)
    pad_rows = pad_mask[0].astype(jnp.float32)[:, None]

    def mixer_in(extended, conv_taps):
        results = []
        for member in range(3):
            columns = extended[:, member * features : (member + 1) * features]
            summed = jnp.zeros((row_count, features), jnp.float32)
            for lagged in range(CONV):
                inside = (positions - lagged >= offsets).astype(jnp.float32)[:, None]
                summed = (
                    summed
                    + conv_taps[member, lagged]
                    * inside
                    * columns[CONV - 1 - lagged : CONV - 1 - lagged + row_count]
                )
            activated = jax.nn.silu(summed).reshape(row_count, head_count, head_dim)
            if member < 2:
                activated = activated * lax.rsqrt(
                    jnp.sum(activated * activated, axis=-1, keepdims=True) + EPSILON
                )
            if member == 0:
                activated = activated * head_dim ** (-0.5)
            results.append(activated)
        return tuple(results)

    residual_in = tokens.astype(jnp.float32)
    normed, norm_first_pull = jax.vjp(rms_norm, residual_in, gain_first.astype(jnp.float32))
    normed_low = normed.astype(jnp.bfloat16)
    projected = jnp.concatenate(
        [product(normed_low, w_query), product(normed_low, w_key), product(normed_low, w_value)],
        axis=1,
    ).astype(jnp.bfloat16)
    logits = product(normed_low, beta_weight)
    sigma_vals = jax.nn.sigmoid(logits)
    strength = sigma_vals * pad_rows
    rims = from_behind(projected[row_count - CONV + 1 :], "seq", 1)
    extended_in = jnp.concatenate([rims, projected], axis=0).astype(jnp.float32)
    (queries, key_rows, values), mixer_pull = jax.vjp(
        mixer_in, extended_in, conv_full.astype(jnp.float32)
    )
    query_blocks = into_blocks(rounded(queries))
    key_blocks = into_blocks(rounded(key_rows))
    value_blocks = into_blocks(rounded(values))
    strength_blocks = strength.reshape(block_count, BLOCK, head_count).transpose(0, 2, 1)
    zero_state = jnp.zeros((head_count, head_dim, head_dim), jnp.float32)
    identity = jnp.broadcast_to(
        jnp.eye(head_dim, dtype=jnp.float32), (head_count, head_dim, head_dim)
    )
    block_inputs = (query_blocks, key_blocks, value_blocks, strength_blocks, persist)
    (final_state, final_transit), (local_out, leading, transit) = lax.scan(
        track_step, (zero_state, identity), block_inputs
    )

    def forward_turn(turn_index, incoming):
        return from_behind(advance(final_transit, final_state, incoming), "seq", 1)

    start_state = lax.fori_loop(0, lax.axis_size("seq") - 1, forward_turn, zero_state)
    carried = jnp.einsum("nhde,hef->nhdf", transit, start_state, precision=PRECISE)
    mixed = from_blocks(
        local_out + jnp.einsum("nhcd,nhdf->nhcf", leading, carried, precision=PRECISE)
    )
    out_normed, out_norm_pull = jax.vjp(rms_norm, mixed, out_norm_gain.astype(jnp.float32))
    out_low = out_normed.reshape(row_count, features).astype(jnp.bfloat16)
    residual_mid = residual_in + product(out_low, w_out)
    normed_two, norm_second_pull = jax.vjp(rms_norm, residual_mid, gain_second.astype(jnp.float32))
    normed_two_low = normed_two.astype(jnp.bfloat16)
    gate_out = product(normed_two_low, w_gate)
    up_out = product(normed_two_low, w_up)
    hidden = (jax.nn.silu(gate_out) * up_out).astype(jnp.bfloat16)
    output = (residual_mid + product(hidden, w_down)).astype(jnp.bfloat16)
    grad_out = cotangent.astype(jnp.float32)
    down_grad = product_left(hidden, cotangent)
    hidden_grad = product_right(cotangent, w_down)
    gate_sigma = jax.nn.sigmoid(gate_out)
    gate_grad_low = (
        hidden_grad * up_out * gate_sigma * (1.0 + gate_out * (1.0 - gate_sigma))
    ).astype(jnp.bfloat16)
    up_grad_low = (hidden_grad * jax.nn.silu(gate_out)).astype(jnp.bfloat16)
    gate_grad = product_left(normed_two_low, gate_grad_low)
    up_grad = product_left(normed_two_low, up_grad_low)
    normed_two_grad = product_right(gate_grad_low, w_gate) + product_right(up_grad_low, w_up)
    mid_from_norm, gain_second_grad = norm_second_pull(normed_two_grad)
    residual_mid_grad = grad_out + mid_from_norm
    mid_low = residual_mid_grad.astype(jnp.bfloat16)
    out_grad = product_left(out_low, mid_low)
    out_normed_grad = product_right(mid_low, w_out).reshape(row_count, head_count, head_dim)
    mixed_grad, out_gain_grad = out_norm_pull(out_normed_grad)
    mixed_blocks = into_blocks(mixed_grad)
    pulled = jnp.einsum("nhcd,nhcf->nhdf", leading, mixed_blocks, precision=PRECISE)
    local_back = jnp.einsum("nhed,nhef->hdf", transit, pulled, precision=PRECISE)
    transit_turned = jnp.swapaxes(final_transit, 1, 2)

    def backward_turn(turn_index, incoming):
        return from_behind(advance(transit_turned, local_back, incoming), "seq", -1)

    end_grad = lax.fori_loop(0, lax.axis_size("seq") - 1, backward_turn, zero_state)

    def delta_local(query_in, key_in, value_in, strength_in):
        ending, outputs = lax.scan(
            jax.checkpoint(delta_step),
            start_state,
            (query_in, key_in, value_in, strength_in, persist),
        )
        return (outputs, ending)

    unused_out, delta_pull = jax.vjp(
        delta_local, query_blocks, key_blocks, value_blocks, strength_blocks
    )
    query_grad_blocks, key_grad_blocks, value_grad_blocks, strength_grad_blocks = delta_pull(
        (mixed_blocks, end_grad)
    )
    extended_grad, conv_grad = mixer_pull(
        (
            from_blocks(query_grad_blocks),
            from_blocks(key_grad_blocks),
            from_blocks(value_grad_blocks),
        )
    )
    rim_grad = from_behind(extended_grad[: CONV - 1], "seq", -1)
    projected_grad = jnp.concatenate(
        [extended_grad[CONV - 1 : row_count], extended_grad[row_count:] + rim_grad], axis=0
    ).astype(jnp.bfloat16)
    strength_grad = strength_grad_blocks.transpose(0, 2, 1).reshape(row_count, head_count)
    logits_grad = (strength_grad * pad_rows * sigma_vals * (1.0 - sigma_vals)).astype(jnp.bfloat16)
    part_query = projected_grad[:, :features]
    part_key = projected_grad[:, features : 2 * features]
    part_value = projected_grad[:, 2 * features :]
    query_grad = product_left(normed_low, part_query)
    key_grad = product_left(normed_low, part_key)
    value_grad = product_left(normed_low, part_value)
    beta_grad = product_left(normed_low, logits_grad)
    normed_grad = (
        product_right(part_query, w_query)
        + product_right(part_key, w_key)
        + product_right(part_value, w_value)
        + product_right(logits_grad, beta_weight)
    )
    input_from_norm, gain_first_grad = norm_first_pull(normed_grad)
    tokens_grad = residual_mid_grad + input_from_norm
    (
        shard_q,
        shard_k,
        shard_v,
        shard_o,
        shard_conv,
        shard_gain_one,
        shard_gate,
        shard_up,
        shard_down,
        shard_gain_two,
    ) = (
        lax.psum_scatter(query_grad, ("dp", "seq"), scatter_dimension=0, tiled=True),
        lax.psum_scatter(key_grad, ("dp", "seq"), scatter_dimension=0, tiled=True),
        lax.psum_scatter(value_grad, ("dp", "seq"), scatter_dimension=0, tiled=True),
        lax.psum_scatter(out_grad, ("dp", "seq"), scatter_dimension=0, tiled=True),
        lax.psum_scatter(conv_grad, ("dp", "seq"), scatter_dimension=2, tiled=True),
        lax.psum_scatter(gain_first_grad, ("dp", "seq"), scatter_dimension=0, tiled=True),
        lax.psum_scatter(gate_grad, ("dp", "seq"), scatter_dimension=0, tiled=True),
        lax.psum_scatter(up_grad, ("dp", "seq"), scatter_dimension=0, tiled=True),
        lax.psum_scatter(down_grad, ("dp", "seq"), scatter_dimension=1, tiled=True),
        lax.psum_scatter(gain_second_grad, ("dp", "seq"), scatter_dimension=0, tiled=True),
    )
    beta_total, out_gain_total = lax.psum((beta_grad, out_gain_grad), ("dp", "seq"))
    return (
        output,
        tokens_grad,
        shard_gain_one,
        shard_q,
        shard_k,
        shard_v,
        shard_conv,
        beta_total,
        out_gain_total,
        shard_o,
        shard_gain_two,
        shard_gate,
        shard_up,
        shard_down,
    )


F32 = jnp.float32
BF = jnp.bfloat16
NN=(((1,),(0,)),((),())); NT=(((1,),(1,)),((),())); TN=(((0,),(0,)),((),()))

def mm(a,b,dims=NN):
    return lax.dot_general(a,b,dims,preferred_element_type=F32)

def halves(a):
    high=a.astype(BF)
    return high,(a-high.astype(F32)).astype(BF)

def mm_lw(a,b,dims=NN):
    high,low=halves(b)
    return mm(a,high,dims)+mm(a,low,dims)

def mm_wl(a,b,dims=NN):
    high,low=halves(a)
    return mm(high,b,dims)+mm(low,b,dims)

def mm_ww(a,b,dims=NN):
    ah,al=halves(a); bh,bl=halves(b)
    return mm(ah,bh,dims)+(mm(al,bh,dims)+mm(ah,bl,dims))

def tile_masks(tile):
    row=lax.broadcasted_iota(jnp.int32,(tile,tile),0)
    col=lax.broadcasted_iota(jnp.int32,(tile,tile),1)
    return row,col


MESH = pl.DeviceIdType.MESH
ANY = pl.BlockSpec(memory_space=pl.ANY)
VMEM = pl.BlockSpec(memory_space=pltpu.VMEM)


def flipped(index, bit):
    size = 2**bit
    return index + (1 - 2 * ((index // size) % 2)) * size


def greet(peers):
    barrier = pltpu.get_barrier_semaphore()
    for axis, peer in peers:
        pl.semaphore_signal(barrier, inc=1, device_id={axis: peer}, device_id_type=MESH)
    pl.semaphore_wait(barrier, len(peers))


def others(axis, count):
    me = lax.axis_index(axis)
    return [(axis, lax.rem(me + step, count)) for step in range(1, count)]


def send(source, target, sends, recvs, slot, axis, peer):
    copy = pltpu.make_async_remote_copy(
        src_ref=source,
        dst_ref=target,
        send_sem=sends.at[slot],
        recv_sem=recvs.at[slot],
        device_id={axis: peer},
        device_id_type=MESH,
    )
    copy.start()
    return copy


def span(size, index, axis):
    piece = pl.ds(pl.multiple_of(index * size, size), size)
    return (piece, slice(None)) if axis == 0 else (slice(None), piece)


def start_exchange(pieces, count, sends, recvs, local, first=0):
    me = lax.axis_index("seq")
    started = []
    for number, (source, source_at, target, target_at) in enumerate(pieces):
        own = pltpu.make_async_copy(
            source.at[source_at(me)], target.at[target_at(me)], local.at[first // count + number]
        )
        own.start()
        started.append(own)
        for step in range(1, count):
            peer = lax.rem(me + step, count)
            slot = first + number * count + step
            started.append(
                send(
                    source.at[source_at(peer)], target.at[target_at(me)],
                    sends, recvs, slot, "seq", peer,
                )
            )
    return started


def wait_all(copies):
    for copy in copies:
        copy.wait()


def bit_orders(count):
    bits = list(range(count.bit_length() - 1))[::-1]
    other = bits[:]
    if len(bits) >= 3:
        other[0], other[1] = bits[1], bits[0]
    return [bits, other]


class Gather:
    def __init__(self, count, source, target, axis, sends, recvs, local, slot, local_slot):
        self.count, self.source, self.target, self.axis = count, source, target, axis
        self.sends, self.recvs, self.local = sends, recvs, local
        self.slot, self.local_slot = slot, local_slot
        self.me = lax.axis_index("seq")
        self.copies = {}

    def piece(self, owner, half):
        rows, columns = self.source.shape
        part = rows // 2
        if self.axis == 0:
            return (pl.ds(pl.multiple_of(owner * rows + half * part, part), part), slice(None))
        return (
            pl.ds(half * part, part),
            pl.ds(pl.multiple_of(owner * columns, columns), columns),
        )

    def put(self, order, half, turn, known):
        owner = self.me
        for bit in known:
            owner = flipped(owner, bit)
        place = self.target.at[self.piece(owner, half)]
        part = self.source.shape[0] // 2
        source = place if known else self.source.at[pl.ds(half * part, part)]
        slot = self.slot + half * self.count + self.number(order, turn, known)
        self.copies[half, turn, known] = send(
            source, place, self.sends, self.recvs, slot, "seq", flipped(self.me, order[turn])
        )

    def number(self, order, turn, known):
        return 2**turn + sum(2 ** order.index(bit) for bit in known)

    def start(self):
        self.start_own()
        for half in range(2):
            self.start_half(half)

    def start_own(self):
        self.own = pltpu.make_async_copy(
            self.source,
            self.target.at[
                span(self.source.shape[self.axis], self.me, self.axis)
            ],
            self.local.at[self.local_slot],
        )
        self.own.start()

    def start_half(self, half):
        order = bit_orders(self.count)[half]
        for turn in range(len(order)):
            self.put(order, half, turn, ())

    def turns(self):
        return self.count.bit_length() - 1

    def forward(self, turn):
        orders = bit_orders(self.count)
        for before in range(2**turn):
            for half, order in enumerate(orders):
                known = tuple(order[i] for i in range(turn) if before // 2**i % 2)
                self.copies[half, turn, known].wait_recv()
                for later in range(turn + 1, len(order)):
                    self.put(order, half, later, known + (order[turn],))

    def finish(self):
        for copy in self.copies.values():
            copy.wait_send()
        self.own.wait()


class LineGather:
    def __init__(self, depth, target, chunks, sems):
        self.depth, self.target, self.chunks = depth, target, chunks
        self.sems = sems
        self.level = lax.axis_index("dp")
        self.rows = target.shape[0] // depth

    def copy(self, block, chunk, distance, up):
        part = self.target.shape[1] // self.chunks
        at = pl.multiple_of(block * self.rows, self.rows)
        place = self.target.at[pl.ds(at, self.rows), pl.ds(chunk * part, part)]
        way = 0 if up else 2
        return pltpu.make_async_remote_copy(
            src_ref=place,
            dst_ref=place,
            send_sem=self.sems.at[way, distance * self.chunks + chunk],
            recv_sem=self.sems.at[way + 1, distance * self.chunks + chunk],
            device_id={"dp": self.level + 1 if up else self.level - 1},
            device_id_type=MESH,
        )

    def start(self, chunks):
        level = self.level
        for chunk in chunks:

            @pl.when(level < self.depth - 1)
            def up():
                self.copy(level, chunk, 0, True).start()

            @pl.when(level > 0)
            def down():
                self.copy(level, chunk, 0, False).start()

    def forward(self, distance, chunks=None):
        level, last = self.level, self.depth - 1
        for chunk in range(self.chunks) if chunks is None else chunks:

            @pl.when(level - distance >= 0)
            def from_below():
                self.copy(level - distance, chunk, distance - 1, True).wait_recv()

                @pl.when(level < last)
                def hand_on():
                    self.copy(level - distance, chunk, distance, True).start()

            @pl.when(level + distance <= last)
            def from_above():
                self.copy(level + distance, chunk, distance - 1, False).wait_recv()

                @pl.when(level > 0)
                def hand_on():
                    self.copy(level + distance, chunk, distance, False).start()

    def finish(self):
        level, last = self.level, self.depth - 1
        for distance in range(last):
            for chunk in range(self.chunks):

                @pl.when((level - distance >= 0) & (level < last))
                def up():
                    self.copy(level - distance, chunk, distance, True).wait_send()

                @pl.when((level + distance <= last) & (level > 0))
                def down():
                    self.copy(level + distance, chunk, distance, False).wait_send()


def hypercube_peers(count):
    me = lax.axis_index("seq")
    return [("seq", flipped(me, bit)) for bit in range(count.bit_length() - 1)]


def comm_params(identity, limit=48):
    return pltpu.CompilerParams(
        collective_id=identity, has_side_effects=True, vmem_limit_bytes=limit * 2**20
    )


def start_kernel(
    count, depth, main, gain_one, gain_two, taps, pad, starts, x_ref, wq, wk, wv, wo, gate, up, down,
    small_all, mixer, native, pair, down_rest, normed_full,
    small, gain, normed, tails, pair_rest, sends, recvs, local, gather_sends, gather_recvs, far,
    mixer_sends, mixer_recvs, mixer_local, line_sems, tail_sems, early_sems,
):
    rest = gate.shape[1] // count - main
    loads = [
        pltpu.make_async_copy(weight.at[:, main * count :], tails.at[i], tail_sems.at[i])
        for i, weight in enumerate((gate, up, down))
    ]
    for load in loads:
        load.start()
    greet(others("seq", count) + others("dp", depth))
    me, level = lax.axis_index("seq"), lax.axis_index("dp")
    mine, height = wq.shape[1] // count, wq.shape[0]
    early = LineGather(depth, native, 1, early_sems)
    own = pltpu.make_async_copy(
        wo, native.at[pl.ds(pl.multiple_of(level * height, height), height)], tail_sems.at[3]
    )
    own.start()
    small[...] = jnp.zeros(small.shape, F32)
    owned, features = gain_one.shape[1], x_ref.shape[1]
    for member in range(3):
        small[member * CONV : (member + 1) * CONV, 0:owned] = taps[member].astype(F32)
    at = 3 * CONV
    for row, source in enumerate((gain_one, gain_two, pad, starts)):
        small[at + row : at + row + 1, 0 : source.shape[1]] = source[...].astype(F32)
    place = me * depth + level
    small_all[place] = small[...]
    levels = [
        send(
            small, small_all.at[place], far.at[0], far.at[1], step, "dp", lax.rem(level + step, depth)
        )
        for step in range(1, depth)
    ]
    places = [
        (
            weight,
            lambda i: span(mine, i, 1),
            mixer,
            lambda i, member=member: (
                pl.ds(pl.multiple_of((level * count + i) * height, height), height),
                slice(member * mine, (member + 1) * mine),
            ),
        )
        for member, weight in enumerate((wq, wk, wv))
    ]
    first_exchange = start_exchange(places, count, mixer_sends, mixer_recvs, mixer_local)
    own.wait()
    early.start((0,))
    wait_all(levels)
    block = small_all.at[pl.ds(me * depth, depth)]
    copies = [
        send(block, block, far.at[2], far.at[3], step, "seq", lax.rem(me + step, count))
        for step in range(1, count)
    ]
    line = LineGather(depth, mixer, 3, line_sems)
    for member in range(3):
        wait_all(first_exchange[member * count : (member + 1) * count])
        line.start((member,))
    for load in loads:
        load.wait()
    lane = lax.broadcasted_iota(jnp.int32, (1, 128), 1)
    half = height // 2
    for i in range(count):
        tile = slice(i // 2 * 128, (i // 2 + 1) * 128)
        gate_tile, up_tile, down_tile = (tails[j, :, tile].astype(F32) for j in range(3))
        if i % 2:
            gate_tile = pltpu.roll(gate_tile, rest, 1)
            top, bottom = pltpu.roll(down_tile[:half], rest, 1), down_tile[half:]
        else:
            up_tile = pltpu.roll(up_tile, rest, 1)
            top, bottom = down_tile[:half], pltpu.roll(down_tile[half:], rest, 1)
        there = slice(i * 128, (i + 1) * 128)
        pair_rest[:, there] = jnp.where(lane < rest, gate_tile, up_tile).astype(BF)
        down_rest[:, there] = jnp.where(lane < rest, top, bottom).astype(BF)
    pieces = [
        (
            source,
            lambda i, size=size: span(size, i, 1),
            pair,
            lambda i, size=size, at=at: (i, slice(None), slice(at, at + size)),
        )
        for source, size, at in ((gate, main, 0), (up, main, main), (pair_rest, 128, 2 * main))
    ]
    exchange = start_exchange(pieces, count, sends, recvs, local)
    wait_all(copies)
    per = 128 // owned
    for tile in range(features // 128):
        row = jnp.zeros((1, 128), F32)
        for part in range(per):
            owner = tile * per + part
            piece = small_all[owner % count * depth + owner // count, at : at + 1, :]
            row = row + (pltpu.roll(piece, part * owned, 1) if part else piece)
        gain[0:1, tile * 128 : (tile + 1) * 128] = row
    for first in range(0, x_ref.shape[0], 16):
        part = slice(first, first + 16)
        value = x_ref[part, :].astype(F32)
        scale = lax.rsqrt(jnp.mean(value * value, axis=1, keepdims=True) + EPSILON)
        normed[part, :] = (value * scale * gain[0:1, :]).astype(BF)
    gather = Gather(
        count, normed, normed_full, 0, gather_sends, gather_recvs, local, 0, len(pieces)
    )
    gather.start()
    early.forward(1)
    line.forward(1)
    gather.forward(0)
    early.forward(2)
    line.forward(2, (0,))
    gather.forward(1)
    line.forward(2, (1, 2))
    for turn in range(2, gather.turns()):
        gather.forward(turn)
    for distance in range(3, depth):
        line.forward(distance)
    gather.finish()
    for distance in range(3, depth):
        early.forward(distance)
    wait_all(exchange)
    line.finish()
    early.finish()


def start(count, depth, main, small, x, mixer, gate, up, down):
    rows = gate.shape[0]
    rest = gate.shape[1] // count - main
    slots = max(count, depth)
    members = 3
    shape = (3 * CONV + 4, max(128, x.shape[0]))
    whole = jax.ShapeDtypeStruct((x.shape[0] * count, x.shape[1]), BF)
    return pl.pallas_call(
        functools.partial(start_kernel, count, depth, main),
        out_shape=(
            jax.ShapeDtypeStruct((count * depth,) + shape, F32),
            jax.ShapeDtypeStruct((x.shape[1], 3 * x.shape[1] // count), BF),
            jax.ShapeDtypeStruct((depth * rows, x.shape[1]), BF),
            jax.ShapeDtypeStruct((count, rows, 2 * main + 128), BF),
            jax.ShapeDtypeStruct((rows // 2, 128 * count), BF),
            whole,
        ),
        in_specs=[VMEM] * 6 + [ANY] * 7,
        out_specs=(VMEM, ANY, ANY, ANY, VMEM, ANY),
        scratch_shapes=[
            pltpu.VMEM(shape, F32),
            pltpu.VMEM((8, x.shape[1]), F32),
            pltpu.VMEM(x.shape, BF),
            pltpu.VMEM((3, rows, rest * count), BF),
            pltpu.VMEM((rows, 128 * count), BF),
            pltpu.SemaphoreType.DMA((members * count,)),
            pltpu.SemaphoreType.DMA((members * count,)),
            pltpu.SemaphoreType.DMA((members + 1,)),
            pltpu.SemaphoreType.DMA((2 * count,)),
            pltpu.SemaphoreType.DMA((2 * count,)),
            pltpu.SemaphoreType.DMA((4, slots)),
            pltpu.SemaphoreType.DMA((4 * count,)),
            pltpu.SemaphoreType.DMA((4 * count,)),
            pltpu.SemaphoreType.DMA((4,)),
            pltpu.SemaphoreType.DMA((4, 3 * depth)),
            pltpu.SemaphoreType.DMA((4,)),
            pltpu.SemaphoreType.DMA((4, depth)),
        ],
        compiler_params=comm_params(2, 60),
    )(*small, x, *mixer, gate, up, down)


def closing_kernel(count, sizes, *refs):
    sources, targets, (sends, recvs, local) = refs[: len(sizes)], refs[len(sizes) : -3], refs[-3:]
    greet(others("seq", count))
    wait_all(start_exchange(row_pieces(sources, targets, sizes, count), count, sends, recvs, local))


def closing(sources, count, sizes, identity):
    shapes = row_shapes(sources, sizes, count)
    members = len(shapes)
    return pl.pallas_call(
        functools.partial(closing_kernel, count, sizes),
        out_shape=shapes,
        in_specs=[ANY] * len(sources),
        out_specs=(ANY,) * members,
        scratch_shapes=[
            pltpu.SemaphoreType.DMA((members * count,)),
            pltpu.SemaphoreType.DMA((members * count,)),
            pltpu.SemaphoreType.DMA((members,)),
        ],
        compiler_params=comm_params(identity),
    )(*sources)


def sums_kernel(count, depth, sizes, plane_ref, level_ref, source, total_ref, each_ref, *refs):
    targets, scratch = refs[: len(sizes)], refs[len(sizes) :]
    plane_in, joined, level_in, sends, recvs, pass_sends, pass_recvs, local = scratch
    greet(others("seq", count) + others("dp", depth))
    me, level = lax.axis_index("seq"), lax.axis_index("dp")
    cut = plane_ref.shape[1]
    plane_in[me] = plane_ref[...]
    wait_all(
        [
            send(
                plane_ref, plane_in.at[me], sends.at[0], recvs.at[0], step,
                "seq", lax.rem(me + step, count),
            )
            for step in range(1, count)
        ]
    )
    exchange = start_exchange(
        row_pieces([source], targets, [sizes], count), count, pass_sends, pass_recvs, local
    )
    value = plane_in[0]
    for i in range(1, count):
        value = value + plane_in[i]
    joined[:, 0:cut] = value
    joined[:, cut:] = level_ref[...]
    level_in[level] = joined[...]
    wait_all(
        [
            send(
                joined, level_in.at[level], sends.at[1], recvs.at[1], step,
                "dp", lax.rem(level + step, depth),
            )
            for step in range(1, depth)
        ]
    )
    value = level_in[0]
    for i in range(1, depth):
        value = value + level_in[i]
    total_ref[...] = value[:, 0:cut]
    joined[:, cut:] = value[:, cut:]
    each_ref[me] = value[:, cut:]
    wait_all(
        [
            send(
                joined.at[:, cut:], each_ref.at[me],
                sends.at[2], recvs.at[2], step, "seq", lax.rem(me + step, count),
            )
            for step in range(1, count)
        ]
    )
    wait_all(exchange)


def small_sums(plane, level, source, sizes, count, depth):
    shapes = row_shapes([source], [sizes], count)
    slots = max(count, depth)
    joined = (plane.shape[0], plane.shape[1] + level.shape[1])
    return pl.pallas_call(
        functools.partial(sums_kernel, count, depth, sizes),
        out_shape=(
            jax.ShapeDtypeStruct(plane.shape, F32),
            jax.ShapeDtypeStruct((count,) + level.shape, F32),
        )
        + shapes,
        in_specs=[VMEM, VMEM, ANY],
        out_specs=(VMEM, VMEM) + (ANY,) * len(shapes),
        scratch_shapes=[
            pltpu.VMEM((count,) + plane.shape, F32),
            pltpu.VMEM(joined, F32),
            pltpu.VMEM((depth,) + joined, F32),
            pltpu.SemaphoreType.DMA((3, slots)),
            pltpu.SemaphoreType.DMA((3, slots)),
            pltpu.SemaphoreType.DMA((len(sizes) * count,)),
            pltpu.SemaphoreType.DMA((len(sizes) * count,)),
            pltpu.SemaphoreType.DMA((len(sizes),)),
        ],
        compiler_params=comm_params(3),
    )(plane, level, source)


class Scatter:
    def __init__(self, count, part, out, landing, outgoing, total, sends, recvs):
        self.count, self.part, self.out = count, part, out
        self.landing, self.outgoing, self.total = landing, outgoing, total
        self.sends, self.recvs = sends, recvs
        self.me = lax.axis_index("seq")
        self.rows = out.shape[0] // 2
        self.bits = count.bit_length() - 1
        self.orders = [order[::-1] for order in bit_orders(count)]
        self.copies = {}

    def rows_of(self, known, half):
        owner = self.me
        for bit in known:
            owner = flipped(owner, bit)
        size = self.rows
        return pl.ds(pl.multiple_of(owner * 2 * size + half * size, size), size)

    def place(self, order, turn, known):
        later = order[turn + 1 :]
        before = sum(self.count >> (t + 1) for t in range(turn))
        return before + sum(2**i for i, bit in enumerate(later) if bit in known)

    def subsets(self, order, turn):
        later = order[turn + 1 :]
        sets = [
            tuple(later[i] for i in range(len(later)) if code // 2**i % 2)
            for code in range(2 ** len(later))
        ]
        return sorted(sets, key=lambda known: [-(bit in known) for bit in later])

    def put(self, half, turn, known, source):
        order = self.orders[half]
        place = self.place(order, turn, known)
        self.copies[half, turn, known] = send(
            source,
            self.landing.at[half, place],
            self.sends,
            self.recvs,
            half * self.count + place,
            "seq",
            flipped(self.me, order[turn]),
        )

    def start(self):
        for at in range(self.count // 2):
            for half, order in enumerate(self.orders):
                known = self.subsets(order, 0)[at]
                self.put(half, 0, known, self.part.at[self.rows_of((order[0],) + known, half)])

    def turn(self, turn):
        for at in range(2 ** (self.bits - turn - 1)):
            for half, order in enumerate(self.orders):
                known = self.subsets(order, turn)[at]
                place = self.place(order, turn, known)
                self.copies[half, turn, known].wait_recv()
                came = self.landing[half, place].astype(F32)
                if turn == 0:
                    value = self.part[self.rows_of(known, half), :].astype(F32) + came
                else:
                    value = self.total[half, self.kept(order, turn - 1, known)] + came
                if turn == self.bits - 1:
                    self.out[half * self.rows : (half + 1) * self.rows, :] = value
                elif order[turn + 1] in known:
                    rest = tuple(bit for bit in known if bit != order[turn + 1])
                    next_place = self.place(order, turn + 1, rest) - self.count // 2
                    self.outgoing[half, next_place] = value.astype(BF)
                    self.put(half, turn + 1, rest, self.outgoing.at[half, next_place])
                else:
                    self.total[half, self.kept(order, turn, known)] = value

    def kept(self, order, turn, known):
        return sum(2**i for i, bit in enumerate(order[turn + 2 :]) if bit in known)

    def finish(self):
        for copy in self.copies.values():
            copy.wait_send()


def scatter_scratch(count, rows, columns):
    half = rows // 2
    return [
        pltpu.VMEM((2, count - 1, half, columns), BF),
        pltpu.VMEM((2, count // 2 - 1, half, columns), BF),
        pltpu.VMEM((2, count // 4, half, columns), F32),
        pltpu.SemaphoreType.DMA((2 * count,)),
        pltpu.SemaphoreType.DMA((2 * count,)),
    ]


def shifted_sum(window, taps_ref, member, lanes, keep):
    length = window.shape[0] - 8
    row = lax.broadcasted_iota(jnp.int32, (length, 1), 0)
    shifts = [window[8:]]
    for lagged in range(1, CONV):
        moved = pltpu.roll(window, lagged, 0)[8:]
        shifts.append(moved * jnp.where(row >= lagged, 1.0, keep))
    summed = shifts[0] * taps_ref[member * CONV : member * CONV + 1, lanes]
    for lagged in range(1, CONV):
        at = member * CONV + lagged
        summed = summed + shifts[lagged] * taps_ref[at : at + 1, lanes]
    return summed, shifts


def front_kernel(
    count, depth, heads, main, persist_ref, x_ref, w_ref, beta_ref, taps_ref, pad_ref, gain_ref, own_ref, g_ref, down_ref, ends_ref,
    pre_ref, q_ref, k_ref, v_ref, brow_ref, sigma_ref, mixed_ref, t_ref, wide_ref, s_ref, f_ref, a_ref,
    full_ref, columns_ref, rows_ref, g_full_ref, tiles_ref,
    pre_buf, logit_buf, u_buf, c_buf, on_buf, local, gather_sends, gather_recvs, sends, recvs, row_sends, row_recvs, row_local,
    tile_sends, tile_recvs, tile_local,
):
    total, features = x_ref.shape
    mine = on_buf.shape[1]
    hd = mine // heads
    blocks = total // BLOCK
    tile = 2 * BLOCK
    greet(others("seq", count))
    height = columns_ref.shape[0] // (depth * count)
    first_exchange = start_exchange(
        [
            (
                own_ref,
                lambda i, z=z: (slice(z * height, (z + 1) * height), span(mine, i, 1)[1]),
                columns_ref,
                lambda i, z=z: span(height, z * count + i, 0),
            )
            for z in range(depth)
        ],
        count, sends, recvs, local,
    )
    beside = Gather(
        count, g_ref, g_full_ref, 0, gather_sends, gather_recvs, local, 2 * count, depth
    )
    beside.start()
    pre_buf[0:8, :] = jnp.zeros((8, 3 * mine), F32)
    chunk = 4 * BLOCK

    def project(index, carry):
        rows = pl.ds(pl.multiple_of(index * chunk, chunk), chunk)
        x = x_ref[rows, :]
        low = mm(x, w_ref[...]).astype(BF)
        pre_ref[rows, :] = low
        pre_buf[pl.ds(pl.multiple_of(index * chunk + 8, 8), chunk), :] = low.astype(F32)
        logit_buf[rows, :] = mm(x, beta_ref[...])
        return carry

    lax.fori_loop(0, total // chunk, project, 0)

    def convolve(index, carry):
        keep = persist_ref[index]
        rows = pl.ds(pl.multiple_of(index * BLOCK, BLOCK), BLOCK)
        for member, target in enumerate((q_ref, k_ref, v_ref)):
            for h in range(heads):
                lanes = slice(h * hd, (h + 1) * hd)
                there = slice(member * mine + h * hd, member * mine + (h + 1) * hd)
                window = pre_buf[pl.ds(pl.multiple_of(index * BLOCK, 8), BLOCK + 8), there]
                summed, _ = shifted_sum(window, taps_ref, member, lanes, keep)
                value = summed * jax.nn.sigmoid(summed)
                if member < 2:
                    norm = jnp.sum(value * value, axis=1, keepdims=True) + EPSILON
                    value = value * lax.rsqrt(norm)
                if member == 0:
                    value = value * hd ** (-0.5)
                target[rows, lanes] = value.astype(BF)
        return carry

    lax.fori_loop(0, blocks, convolve, 0)
    beside.forward(0)
    wait_all(first_exchange)
    tiles = start_exchange(
        [
            (target, target_at, source, source_at)
            for source, source_at, target, target_at in folded_pieces(tiles_ref, down_ref, ends_ref, count, main)
        ],
        count, tile_sends, tile_recvs, tile_local,
    )
    exchange = start_exchange(
        [(columns_ref, lambda i: span(mine, i, 0), rows_ref, lambda i: span(mine, i, 1))],
        count, row_sends, row_recvs, row_local,
    )
    row, col = tile_masks(tile)
    eyed = (
        lax.broadcasted_iota(jnp.int32, (hd, hd), 0) == lax.broadcasted_iota(jnp.int32, (hd, hd), 1)
    ).astype(F32)

    def first(step, carry):
        same = (row // BLOCK) == (col // BLOCK)
        eye = (row == col).astype(F32)
        chains = [(2 * step + i, h) for i in range(2) for h in range(heads)]
        ts, ls, ks, vs, bs = [], [], [], [], []
        for index, h in chains:
            rows = pl.ds(pl.multiple_of(index * tile, tile), tile)
            lanes = slice(h * hd, (h + 1) * hd)
            k = k_ref[rows, lanes]
            logit = jnp.sum(eye * logit_buf[rows, h : h + 1], axis=0, keepdims=True)
            sigma = jax.nn.sigmoid(logit)
            b = sigma * pad_ref[pl.ds(index, 1), :]
            sigma_ref[index, h : h + 1, :] = sigma
            brow_ref[index, h : h + 1, :] = b
            bcol = jnp.sum(eye * b, axis=1, keepdims=True)
            low = jnp.where(same & (row > col), mm(k, k, NT) * bcol, 0.0)
            ls.append(low)
            ks.append(k)
            vs.append(v_ref[rows, lanes])
            bs.append(b)
            ts.append(eye - jnp.where((row // 2) == (col // 2), low, 0.0))
        size = 2
        while size < BLOCK:
            cut = ((row // (2 * size)) == (col // (2 * size))) & ((row // size) != (col // size))
            mids = [mm_ww(jnp.where(cut, l, 0.0), t) for l, t in zip(ls, ts)]
            ts = [t - mm_ww(t, m) for t, m in zip(ts, mids)]
            size *= 2
        for at, (index, h) in enumerate(chains):
            rows = pl.ds(pl.multiple_of(index * tile, tile), tile)
            lanes = slice(h * hd, (h + 1) * hd)
            t_ref[h, rows, :] = ts[at]
            wu = mm_wl(ts[at] * bs[at], jnp.concatenate([ks[at], vs[at]], axis=1))
            wide_ref[rows, lanes] = wu[:, :hd]
            u_buf[rows, lanes] = wu[:, hd:]
            for part in range(2):
                sub = slice(part * BLOCK, (part + 1) * BLOCK)
                ab = mm_lw(ks[at][sub], wu[sub], TN)
                a_ref[h, index * 2 + part] = eyed - ab[:, :hd]
                c_buf[h, index * 2 + part] = ab[:, hd:]
        return carry

    lax.fori_loop(0, blocks // 4, first, 0)
    beside.forward(1)

    def chain(index, states):
        keep = persist_ref[index]
        new = []
        for h in range(heads):
            s = states[h] * keep
            s_ref[h, index] = s
            new.append(mm_ww(a_ref[h, index], s) + c_buf[h, index])
        return tuple(new)

    lax.fori_loop(0, blocks, chain, tuple(jnp.zeros((hd, hd), F32) for _ in range(heads)))

    def last(step, carry):
        lower_row, lower_col = tile_masks(BLOCK)
        for part in range(2):
            index = 2 * step + part
            rows = pl.ds(pl.multiple_of(index * BLOCK, BLOCK), BLOCK)
            for h in range(heads):
                lanes = slice(h * hd, (h + 1) * hd)
                q, k, s = q_ref[rows, lanes], k_ref[rows, lanes], s_ref[h, index]
                f = u_buf[rows, lanes] - mm_ww(wide_ref[rows, lanes], s)
                p = jnp.where(lower_row >= lower_col, mm(q, k, NT), 0.0)
                f_ref[rows, lanes] = f
                mixed = mm_lw(q, s) + mm_ww(p, f)
                mixed_ref[rows, lanes] = mixed
                scale = lax.rsqrt(jnp.mean(mixed * mixed, axis=1, keepdims=True) + EPSILON)
                on_buf[rows, lanes] = (mixed * scale * gain_ref[0:1, :]).astype(BF)
        return carry

    for turn in range(2, beside.turns()):
        beside.forward(turn)
    gather = Gather(count, on_buf, full_ref, 1, gather_sends, gather_recvs, local, 0, depth + 1)
    lax.fori_loop(0, blocks // 4, last, 0)
    gather.start_half(0)
    lax.fori_loop(blocks // 4, blocks // 2, last, 0)
    gather.start_half(1)
    gather.start_own()
    for turn in range(gather.turns()):
        gather.forward(turn)
    gather.finish()
    beside.finish()
    wait_all(exchange)
    wait_all(tiles)


def front(count, depth, heads, main, persist, x, w_qkv, w_beta, taps, pad, gain, own, g, down, ends):
    total, features = x.shape
    mine = features // count
    hd = mine // heads
    blocks, tiles = total // BLOCK, total // (2 * BLOCK)
    wide = jax.ShapeDtypeStruct((total, mine), F32)
    low = jax.ShapeDtypeStruct((total, mine), BF)
    strength = jax.ShapeDtypeStruct((tiles, heads, 2 * BLOCK), F32)
    states = jax.ShapeDtypeStruct((heads, blocks, hd, hd), F32)
    return pl.pallas_call(
        functools.partial(front_kernel, count, depth, heads, main),
        out_shape=(
            jax.ShapeDtypeStruct((total, 3 * mine), BF),
            low, low, low, strength, strength, wide,
            jax.ShapeDtypeStruct((heads, total, 2 * BLOCK), F32),
            wide, states, wide, states,
            jax.ShapeDtypeStruct((total, mine * count), BF),
            jax.ShapeDtypeStruct((features, mine), BF),
            jax.ShapeDtypeStruct((mine, features), BF),
            jax.ShapeDtypeStruct((total, features), BF),
            jax.ShapeDtypeStruct((count * down.shape[0] * main // 128 + count * ends.shape[0], 128), BF),
        ),
        in_specs=[
            pl.BlockSpec(memory_space=pltpu.SMEM),
            VMEM, VMEM, VMEM, VMEM, VMEM, VMEM, ANY, ANY, ANY, ANY,
        ],
        out_specs=(VMEM,) * 12 + (ANY,) * 5,
        scratch_shapes=[
            pltpu.VMEM((total + 8, 3 * mine), F32),
            pltpu.VMEM((total, w_beta.shape[1]), F32),
            pltpu.VMEM((total, mine), F32),
            pltpu.VMEM((heads, blocks, hd, hd), F32),
            pltpu.VMEM((total, mine), BF),
            pltpu.SemaphoreType.DMA((depth + 2,)),
            pltpu.SemaphoreType.DMA((4 * count,)),
            pltpu.SemaphoreType.DMA((4 * count,)),
            pltpu.SemaphoreType.DMA((depth * count,)),
            pltpu.SemaphoreType.DMA((depth * count,)),
            pltpu.SemaphoreType.DMA((count,)),
            pltpu.SemaphoreType.DMA((count,)),
            pltpu.SemaphoreType.DMA((1,)),
            pltpu.SemaphoreType.DMA(((main // 128 + 1) * count,)),
            pltpu.SemaphoreType.DMA(((main // 128 + 1) * count,)),
            pltpu.SemaphoreType.DMA((main // 128 + 1,)),
        ],
        compiler_params=comm_params(4, 52),
    )(persist, x, w_qkv, w_beta, taps, pad, gain, own, g, down, ends)


def middle_kernel(
    count, full_ref, w_ref, x_ref, gain_ref, mid_ref, normed_ref,
    staged, landed, low_buf, sends, recvs, local, gather_sends, gather_recvs,
):
    me = lax.axis_index("seq")
    rows, features = x_ref.shape
    mine = w_ref.shape[1]
    greet(others("seq", count))
    copies = []
    for step in list(range(1, count)) + [0]:
        peer = lax.rem(me + step, count)
        at = pl.ds(pl.multiple_of(peer * rows, rows), rows)
        staged[step] = mm(full_ref[at, :], w_ref[...])
        target = landed.at[span(mine, me, 1)]
        if step:
            copies.append(send(staged.at[step], target, sends, recvs, step, "seq", peer))
        else:
            own = pltpu.make_async_copy(staged.at[0], target, local.at[0])
            own.start()
            copies.append(own)
    wait_all(copies)
    for at in range(0, rows, 16):
        part = slice(at, at + 16)
        value = x_ref[part, :].astype(F32) + landed[part, :]
        mid_ref[part, :] = value
        scale = lax.rsqrt(jnp.mean(value * value, axis=1, keepdims=True) + EPSILON)
        low_buf[part, :] = (value * scale * gain_ref[0:1, :]).astype(BF)
    gather = Gather(count, low_buf, normed_ref, 0, gather_sends, gather_recvs, local, 0, 1)
    gather.start()
    for turn in range(gather.turns()):
        gather.forward(turn)
    gather.finish()


def middle(count, full, w_out, x, gain):
    rows, features = x.shape
    mine = w_out.shape[1]
    return pl.pallas_call(
        functools.partial(middle_kernel, count),
        out_shape=(
            jax.ShapeDtypeStruct((rows, features), F32),
            jax.ShapeDtypeStruct((rows * count, features), BF),
        ),
        in_specs=[VMEM] * 4,
        out_specs=(VMEM, ANY),
        scratch_shapes=[
            pltpu.VMEM((count, rows, mine), F32),
            pltpu.VMEM((rows, features), F32),
            pltpu.VMEM((rows, features), BF),
            pltpu.SemaphoreType.DMA((count,)),
            pltpu.SemaphoreType.DMA((count,)),
            pltpu.SemaphoreType.DMA((3,)),
            pltpu.SemaphoreType.DMA((2 * count,)),
            pltpu.SemaphoreType.DMA((2 * count,)),
        ],
        compiler_params=comm_params(5),
    )(full, w_out, x, gain)


def norm_backward(value_ref, grad_ref, beside_ref, gain_ref, out_ref, gain_out, low_ref=None):
    rows, features = out_ref.shape
    gain_out[...] = jnp.zeros((8, features), F32)
    for at in range(0, rows, 8):
        part = slice(at, at + 8)
        value = value_ref[part, :].astype(F32)
        scale = lax.rsqrt(jnp.mean(value * value, axis=1, keepdims=True) + EPSILON)
        unit = value * scale
        grad = grad_ref[part, :]
        gain_out[...] += grad * unit
        scaled = grad * gain_ref[0:1, :]
        mean = jnp.mean(scaled * unit, axis=1, keepdims=True)
        result = beside_ref[part, :].astype(F32) + scale * (scaled - unit * mean)
        out_ref[part, :] = result
        if low_ref is not None:
            half = (at // 16) * 16
            if at % 16 == 8:
                low_ref[half : half + 16, :] = out_ref[half : half + 16, :].astype(BF)


def reduce_kernel(
    count, part_ref, mid_ref, g_ref, gain_ref, grad_ref, gain_out, full_ref,
    summed, low_buf, landing, outgoing, kept, sends, recvs, local, gather_sends, gather_recvs,
):
    greet(hypercube_peers(count))
    scatter = Scatter(count, part_ref, summed, landing, outgoing, kept, sends, recvs)
    scatter.start()
    for turn in range(scatter.bits):
        scatter.turn(turn)
    norm_backward(mid_ref, summed, g_ref, gain_ref, grad_ref, gain_out, low_buf)
    gather = Gather(count, low_buf, full_ref, 0, gather_sends, gather_recvs, local, 0, 0)
    gather.start()
    for turn in range(gather.turns()):
        gather.forward(turn)
    gather.finish()
    scatter.finish()


def reduce_middle(count, parts, mid, g, gain):
    rows, features = mid.shape
    return pl.pallas_call(
        functools.partial(reduce_kernel, count),
        out_shape=(
            jax.ShapeDtypeStruct((rows, features), F32),
            jax.ShapeDtypeStruct((8, features), F32),
            jax.ShapeDtypeStruct((rows * count, features), BF),
        ),
        in_specs=[VMEM] * 4,
        out_specs=(VMEM, VMEM, ANY),
        scratch_shapes=[pltpu.VMEM((rows, features), F32), pltpu.VMEM((rows, features), BF)]
        + scatter_scratch(count, rows, features)
        + [
            pltpu.SemaphoreType.DMA((1,)),
            pltpu.SemaphoreType.DMA((2 * count,)),
            pltpu.SemaphoreType.DMA((2 * count,)),
        ],
        compiler_params=comm_params(6),
    )(parts, mid, g, gain)


def back_kernel(
    count, heads, persist_ref, full_ref, rows_ref, mixed_ref, gain_ref, taps_ref, pre_ref, q_ref, k_ref, v_ref,
    brow_ref, sigma_ref, pad_ref, t_ref, wide_ref, s_ref, f_ref, a_ref, done_ref,
    dpre_ref, taps_out, gain_out, main_ref, ends_ref, *scratch,
):
    total, mine = mixed_ref.shape
    hd = mine // heads
    blocks = total // BLOCK
    beta_lanes = dpre_ref.shape[1] - 3 * mine
    do_buf, y_buf, c_buf, g_buf, pre_buf, conv_buf, pass_sends, pass_recvs, local = scratch
    greet(others("seq", count))
    exchange = start_exchange(
        folded_pieces(done_ref, main_ref, ends_ref, count), count, pass_sends, pass_recvs, local
    )
    gain_out[...] = jnp.zeros((8, hd), F32)
    taps_out[...] = jnp.zeros((3 * CONV, 8, mine), F32)
    pre_buf[0:8, :] = jnp.zeros((8, 3 * mine), F32)
    conv_buf[total : total + 8, :] = jnp.zeros((8, 3 * mine), F32)
    chunk = 4 * BLOCK

    def heads_in(index, carry):
        rows = pl.ds(pl.multiple_of(index * chunk, chunk), chunk)
        pre_buf[pl.ds(pl.multiple_of(index * chunk + 8, 8), chunk), :] = pre_ref[rows, :].astype(F32)
        grad = mm(full_ref[rows, :], rows_ref[...], NT)
        for h in range(heads):
            lanes = slice(h * hd, (h + 1) * hd)
            mixed, don = mixed_ref[rows, lanes], grad[:, lanes]
            scale = lax.rsqrt(jnp.mean(mixed * mixed, axis=1, keepdims=True) + EPSILON)
            unit = mixed * scale
            gain_out[...] += jnp.sum((don * unit).reshape(chunk // 8, 8, hd), axis=0)
            scaled = don * gain_ref[0:1, :]
            mean = jnp.mean(scaled * unit, axis=1, keepdims=True)
            do_buf[rows, lanes] = scale * (scaled - unit * mean)
        return carry

    lax.fori_loop(0, total // chunk, heads_in, 0)
    row, col = tile_masks(BLOCK)

    def first(step, carry):
        for part in range(2):
            index = 2 * step + part
            rows = pl.ds(pl.multiple_of(index * BLOCK, BLOCK), BLOCK)
            for h in range(heads):
                lanes = slice(h * hd, (h + 1) * hd)
                q, k, do = q_ref[rows, lanes], k_ref[rows, lanes], do_buf[rows, lanes]
                p = jnp.where(row >= col, mm(q, k, NT), 0.0)
                y = mm_ww(p, do, TN)
                y_buf[rows, lanes] = y
                c_buf[h, index] = mm_lw(q, do, TN) - mm_ww(wide_ref[rows, lanes], y, TN)
        return carry

    lax.fori_loop(0, blocks // 2, first, 0)

    def chain(step, grads):
        index = blocks - 1 - step
        keep = persist_ref[index]
        new = []
        for h in range(heads):
            g = grads[h]
            g_buf[h, index] = g
            new.append((mm_ww(a_ref[h, index], g, TN) + c_buf[h, index]) * keep)
        return tuple(new)

    lax.fori_loop(0, blocks, chain, tuple(jnp.zeros((hd, hd), F32) for _ in range(heads)))

    def last(step, carry):
        for part in range(2):
            index = 2 * step + part
            keep = persist_ref[index]
            rows = pl.ds(pl.multiple_of(index * BLOCK, BLOCK), BLOCK)
            half = slice(part * BLOCK, (part + 1) * BLOCK)
            lane = lax.broadcasted_iota(jnp.int32, (BLOCK, beta_lanes), 1)
            dlogits = jnp.zeros((BLOCK, beta_lanes), F32)
            for h in range(heads):
                lanes = slice(h * hd, (h + 1) * hd)
                q, k, v = q_ref[rows, lanes], k_ref[rows, lanes], v_ref[rows, lanes]
                do, s, f, g = do_buf[rows, lanes], s_ref[h, index], f_ref[rows, lanes], g_buf[h, index]
                b = brow_ref[step, h : h + 1, half]
                bcol = jnp.sum(jnp.where(row == col, b, 0.0), axis=1, keepdims=True)
                t = t_ref[h, rows, half]
                df = y_buf[rows, lanes] + mm_lw(k, g)
                dr = mm_ww(t, df, TN)
                dp = jnp.where(row >= col, mm_ww(do, f, NT), 0.0)
                dl = jnp.where(row > col, -mm_ww(dr, f, NT), 0.0)
                dq = mm_ww(do, s, NT) + mm_wl(dp, k)
                dkb = mm_wl(dl, k) - mm_ww(dr, s, NT)
                dk = mm_wl(dp, q, TN) + mm_ww(f, g, NT) + mm_wl(dl * bcol, k, TN) + bcol * dkb
                dbeta = jnp.sum(dr * v.astype(F32) + dkb * k.astype(F32), axis=1, keepdims=True)
                sigma = sigma_ref[step, h : h + 1, half]
                slope = pad_ref[pl.ds(step, 1), half] * sigma * (1.0 - sigma)
                slope = jnp.sum(jnp.where(row == col, slope, 0.0), axis=1, keepdims=True)
                dlogits = jnp.where(lane == h, dbeta * slope, dlogits)
                for member, grad in enumerate((dq, dk, bcol * dr)):
                    there = slice(member * mine + h * hd, member * mine + (h + 1) * hd)
                    window = pre_buf[pl.ds(pl.multiple_of(index * BLOCK, 8), BLOCK + 8), there]
                    summed, shifts = shifted_sum(window, taps_ref, member, lanes, keep)
                    sigma = jax.nn.sigmoid(summed)
                    if member < 2:
                        value = summed * sigma
                        inverse = lax.rsqrt(jnp.sum(value * value, axis=1, keepdims=True) + EPSILON)
                        unit = value * inverse
                        along = jnp.sum(grad * unit, axis=1, keepdims=True)
                        grad = (grad - unit * along) * inverse
                    if member == 0:
                        grad = grad * hd ** (-0.5)
                    grad = grad * (sigma * (1.0 + summed * (1.0 - sigma)))
                    conv_buf[rows, there] = grad
                    for lagged in range(CONV):
                        taps_out[member * CONV + lagged, :, lanes] += jnp.sum(
                            (grad * shifts[lagged]).reshape(BLOCK // 8, 8, hd), axis=0
                        )
            dpre_ref[rows, 3 * mine :] = dlogits.astype(BF)
        return carry

    lax.fori_loop(0, blocks // 2, last, 0)

    def spread(index, carry):
        rows = pl.ds(pl.multiple_of(index * BLOCK, BLOCK), BLOCK)
        keep = persist_ref[jnp.minimum(index + 1, blocks - 1)]
        block_row = lax.broadcasted_iota(jnp.int32, (BLOCK, 1), 0)
        for member in range(3):
            there = slice(member * mine, (member + 1) * mine)
            window = conv_buf[pl.ds(pl.multiple_of(index * BLOCK, 8), BLOCK + 8), there]
            summed = window[:BLOCK] * taps_ref[member * CONV : member * CONV + 1, :]
            for lagged in range(1, CONV):
                at = member * CONV + lagged
                moved = pltpu.roll(window, BLOCK + 8 - lagged, 0)[:BLOCK]
                moved = moved * jnp.where(block_row < BLOCK - lagged, 1.0, keep)
                summed = summed + moved * taps_ref[at : at + 1, :]
            dpre_ref[rows, there] = summed.astype(BF)
        return carry

    lax.fori_loop(0, blocks, spread, 0)
    wait_all(exchange)


def back(
    count, heads, persist, full, w_rows, mixed, gain, taps, pre, q, k, v, strength, saved, done, main
):
    total, mine = mixed.shape
    hd = mine // heads
    blocks = total // BLOCK
    owned = done.shape[0] // (count * main // 128 + count // 2)
    members = main // 128 + 1
    return pl.pallas_call(
        functools.partial(back_kernel, count, heads),
        out_shape=(
            jax.ShapeDtypeStruct((total, 3 * mine + 128), BF),
            jax.ShapeDtypeStruct((3 * CONV, 8, mine), F32),
            jax.ShapeDtypeStruct((8, hd), F32),
            jax.ShapeDtypeStruct((owned, count * main), BF),
            jax.ShapeDtypeStruct((owned // 2, count * 128), BF),
        ),
        in_specs=[pl.BlockSpec(memory_space=pltpu.SMEM)] + [VMEM] * 17 + [ANY],
        out_specs=(VMEM,) * 3 + (ANY,) * 2,
        scratch_shapes=[
            pltpu.VMEM((total, mine), F32),
            pltpu.VMEM((total, mine), F32),
            pltpu.VMEM((heads, blocks, hd, hd), F32),
            pltpu.VMEM((heads, blocks, hd, hd), F32),
            pltpu.VMEM((total + 8, 3 * mine), F32),
            pltpu.VMEM((total + 8, 3 * mine), F32),
            pltpu.SemaphoreType.DMA((members * count,)),
            pltpu.SemaphoreType.DMA((members * count,)),
            pltpu.SemaphoreType.DMA((members,)),
        ],
        compiler_params=comm_params(7, 56),
    )(persist, full, w_rows, mixed, gain, taps, pre, q, k, v, *strength, *saved, done)


def end_kernel(
    count, part_ref, added_ref, x_ref, mid_ref, beside_ref, gain_ref,
    grad_ref, gain_out, out_ref, summed, added, *scratch
):
    greet(hypercube_peers(count))
    scatter = Scatter(count, part_ref, summed, *scratch[:5])
    beside = Scatter(count, added_ref, added, *scratch[5:])
    scatter.start()
    beside.start()
    for turn in range(scatter.bits):
        scatter.turn(turn)
        beside.turn(turn)
    norm_backward(x_ref, summed, beside_ref, gain_ref, grad_ref, gain_out)
    for at in range(0, out_ref.shape[0], 16):
        part = slice(at, at + 16)
        out_ref[part, :] = (mid_ref[part, :] + added[part, :]).astype(BF)
    scatter.finish()
    beside.finish()


def folded_pieces(source, main_ref, ends_ref, count, main=None):
    main = main_ref.shape[1] // count if main is None else main
    rows, half = main_ref.shape[0], ends_ref.shape[0]
    pieces = []
    for tile in range(main // 128):
        pieces.append(
            (
                source,
                lambda i, tile=tile: span(rows, tile * count + i, 0),
                main_ref,
                lambda i, tile=tile: (
                    slice(None), pl.ds(pl.multiple_of(i * main + tile * 128, 128), 128)
                ),
            )
        )
    pieces.append(
        (
            source,
            lambda i: (
                pl.ds(pl.multiple_of(main // 128 * count * rows + i * half, half), half),
                slice(None),
            ),
            ends_ref,
            lambda i: span(128, i, 1),
        )
    )
    return pieces


def row_pieces(sources, targets, sizes, count):
    pieces = []
    for source, widths in zip(sources, sizes):
        rows, at = source.shape[0] // count, 0
        for size in widths:
            pieces.append(
                (
                    source,
                    lambda i, rows=rows, at=at, size=size: (
                        pl.ds(pl.multiple_of(i * rows, rows), rows),
                        slice(at, at + size),
                    ),
                    targets[len(pieces)],
                    lambda i, size=size: span(size, i, 1),
                )
            )
            at += size
    return pieces


def row_shapes(sources, sizes, count):
    return tuple(
        jax.ShapeDtypeStruct((source.shape[0] // count, count * size), BF)
        for source, widths in zip(sources, sizes)
        for size in widths
    )


def end(count, parts, added, x, mid, beside, gain):
    rows, features = x.shape
    return pl.pallas_call(
        functools.partial(end_kernel, count),
        out_shape=(
            jax.ShapeDtypeStruct((rows, features), F32),
            jax.ShapeDtypeStruct((8, features), F32),
            jax.ShapeDtypeStruct((rows, features), BF),
        ),
        in_specs=[VMEM] * 6,
        out_specs=(VMEM,) * 3,
        scratch_shapes=[pltpu.VMEM((rows, features), F32)] * 2
        + scatter_scratch(count, rows, features)
        + scatter_scratch(count, rows, features),
        compiler_params=comm_params(8),
    )(parts, added, x, mid, beside, gain)


def hidden_grads_kernel(count, rest, g_ref, pair_ref, down_ref, low_ref, w_ref):
    main = w_ref.shape[1] - 128
    lane = lax.broadcasted_iota(jnp.int32, (1, 128), 1)

    @pl.when(pl.program_id(0) == 0)
    def assemble():
        depth = down_ref.shape[0]
        level = w_ref.shape[0] // depth
        rows = level // count
        for z in range(depth):
            at = z * level
            for tile in range(main // 128):
                w_ref[at : at + level, tile * 128 : (tile + 1) * 128] = down_ref[
                    z, tile * level : (tile + 1) * level, :
                ]
            for i in range(count):
                start = main // 128 * level + i * (rows // 2)
                pair = down_ref[z, start : start + rows // 2, :].astype(F32)
                for part in range(2):
                    piece = pair if part == 0 else pltpu.roll(pair, rest, 1)
                    first = at + i * rows + part * (rows // 2)
                    w_ref[first : first + rows // 2, main:] = jnp.where(
                        lane < rest, piece, 0.0
                    ).astype(BF)

    grad = mm(g_ref[...], w_ref[...])

    def slopes(gate, up, grad):
        sigma = jax.nn.sigmoid(gate)
        return grad * up * sigma * (1.0 + gate * (1.0 - sigma)), grad * (gate * sigma)

    dgate, dup = slopes(pair_ref[:, :main], pair_ref[:, main : 2 * main], grad[:, :main])
    low_ref[:, :main] = dgate.astype(BF)
    low_ref[:, main : 2 * main] = dup.astype(BF)
    tail = pair_ref[:, 2 * main :]
    dgate, dup = slopes(tail, pltpu.roll(tail, rest, 1), grad[:, main:])
    low_ref[:, 2 * main :] = jnp.where(lane < rest, dgate, pltpu.roll(dup, rest, 1)).astype(BF)


def hidden_gradients(count, rest, g, pair, down):
    total, features = g.shape
    main = (pair.shape[1] - 2 * rest) // 2
    step = total // 4
    return pl.pallas_call(
        functools.partial(hidden_grads_kernel, count, rest),
        grid=(total // step,),
        out_shape=(
            jax.ShapeDtypeStruct(pair.shape, BF),
            jax.ShapeDtypeStruct((features, main + 128), BF),
        ),
        in_specs=[
            pl.BlockSpec((step, features), lambda i: (i, 0)),
            pl.BlockSpec((step, pair.shape[1]), lambda i: (i, 0)),
            pl.BlockSpec(down.shape, lambda i: (0, 0, 0)),
        ],
        out_specs=(
            pl.BlockSpec((step, pair.shape[1]), lambda i: (i, 0)),
            pl.BlockSpec((features, main + 128), lambda i: (0, 0)),
        ),
        compiler_params=pltpu.CompilerParams(vmem_limit_bytes=40 * 2**20),
        cost_estimate=pl.CostEstimate(
            flops=2 * total * features * (main + 128),
            bytes_accessed=2 * total * features + 6 * total * pair.shape[1],
            transcendentals=total * pair.shape[1] // 2,
        ),
    )(g, pair, down)


def down_grads_kernel(count, rest, g_ref, hidden_ref, out_ref):
    grad = mm(g_ref[...], hidden_ref[...], TN)
    level = grad.shape[0]
    main = grad.shape[1] - 128
    rows = level // count
    lane = lax.broadcasted_iota(jnp.int32, (1, 128), 1)
    for tile in range(main // 128):
        out_ref[tile * level : (tile + 1) * level, :] = grad[:, tile * 128 : (tile + 1) * 128].astype(BF)
    for i in range(count):
        at = i * rows
        front = grad[at : at + rows // 2, main:]
        later = pltpu.roll(grad[at + rows // 2 : at + rows, main:], rest, 1)
        start = main // 128 * level + i * (rows // 2)
        out_ref[start : start + rows // 2, :] = jnp.where(lane < rest, front, later).astype(BF)


def down_gradients(count, depth, rest, g, hidden):
    total, features = g.shape
    width = hidden.shape[1]
    level = features // depth
    high = (width - 128) // 128 * level + level // 2
    return pl.pallas_call(
        functools.partial(down_grads_kernel, count, rest),
        grid=(depth,),
        out_shape=jax.ShapeDtypeStruct((depth * high, 128), BF),
        in_specs=[
            pl.BlockSpec((total, level), lambda i: (0, i)),
            pl.BlockSpec((total, width), lambda i: (0, 0)),
        ],
        out_specs=pl.BlockSpec((high, 128), lambda i: (i, 0)),
        compiler_params=pltpu.CompilerParams(vmem_limit_bytes=40 * 2**20),
        cost_estimate=pl.CostEstimate(
            flops=2 * total * features * width,
            bytes_accessed=2 * total * (features + width) + 2 * features * width,
            transcendentals=0,
        ),
    )(g, hidden)


def mixer_grads_kernel(x_ref, grad_ref, on_ref, out_ref, low_ref, beta_ref):
    wide = 3 * out_ref.shape[1]
    front = mm(x_ref[...], grad_ref[:, :wide], TN)
    low_ref[:, :wide] = front.astype(BF)
    beta_ref[...] = mm(grad_ref[:, wide:], x_ref[...], TN)[: beta_ref.shape[0]]
    low_ref[:, wide:] = mm(on_ref[...], out_ref[...], TN).astype(BF)


def mixer_gradients(x, grad, on, out):
    total, features = x.shape
    beta = grad.shape[1] - 3 * out.shape[1]
    wide = grad.shape[1] - beta + out.shape[1]
    step = features // 4
    return pl.pallas_call(
        mixer_grads_kernel,
        grid=(features // step,),
        out_shape=(
            jax.ShapeDtypeStruct((features, wide), BF),
            jax.ShapeDtypeStruct((8, features), F32),
        ),
        in_specs=[
            pl.BlockSpec((total, step), lambda i: (0, i)),
            pl.BlockSpec(grad.shape, lambda i: (0, 0)),
            pl.BlockSpec((total, step), lambda i: (0, i)),
            pl.BlockSpec(out.shape, lambda i: (0, 0)),
        ],
        out_specs=(
            pl.BlockSpec((step, wide), lambda i: (i, 0)),
            pl.BlockSpec((8, step), lambda i: (0, i)),
        ),
        compiler_params=pltpu.CompilerParams(vmem_limit_bytes=40 * 2**20),
        cost_estimate=pl.CostEstimate(
            flops=2 * total * features * (wide + beta),
            bytes_accessed=4 * total * features + 4 * features * wide,
            transcendentals=0,
        ),
    )(x, grad, on, out)


def rest_and_main(hidden_width, count):
    main = hidden_width // (128 * count) * 128
    return hidden_width // count - main, main


def local_heads(
    tokens,
    doc_starts,
    pad_mask,
    norm1_gain,
    query_weight,
    key_weight,
    value_weight,
    conv_weight,
    beta_weight,
    out_norm_gain,
    out_weight,
    norm2_gain,
    gate_weight,
    up_weight,
    down_weight,
    cotangent,
):
    row_count, features = tokens.shape
    width = lax.axis_size("seq")
    place = lax.axis_index("seq")
    head_dim = out_norm_gain.shape[0]
    heads = beta_weight.shape[1] // width
    mine = heads * head_dim
    total = row_count * width
    depth = lax.axis_size("dp")
    level = lax.axis_index("dp")
    owned = norm1_gain.shape[0]
    rest, main = rest_and_main(gate_weight.shape[1], width)
    w_beta = lax.dynamic_slice_in_dim(beta_weight, place * heads, heads, axis=1)

    small_all, w_qkv, out_native, pair_part, down_rest, normed_full = start(
        width,
        depth,
        main,
        [norm1_gain[None], norm2_gain[None], conv_weight, pad_mask, doc_starts],
        tokens,
        [query_weight, key_weight, value_weight, out_weight],
        gate_weight,
        up_weight,
        down_weight.T,
    )
    w_pair = lax.all_gather(pair_part.reshape(width * owned, -1), "dp", axis=0, tiled=True)
    small_all = small_all.reshape(width, depth, -1, small_all.shape[2])
    wide = small_all[:, :, : 3 * CONV + 2, :owned].transpose(2, 1, 0, 3)
    wide = wide.reshape(3 * CONV + 2, features)
    gain_first, gain_second = wide[3 * CONV], wide[3 * CONV + 1]
    taps = lax.dynamic_slice_in_dim(wide[: 3 * CONV], place * mine, mine, axis=1)
    marks = lax.dynamic_index_in_dim(small_all[:, :, 3 * CONV + 2 :], level, 1, keepdims=False)
    pad_rows = marks[:, 0, :row_count].reshape(-1, 2 * BLOCK)
    starts = marks[:, 1, : doc_starts.shape[1]].reshape(-1).astype(jnp.int32)
    begins = BLOCK * jnp.arange(total // BLOCK, dtype=jnp.int32)
    persist = (starts != begins).astype(F32)
    beta_wide = jnp.pad(w_beta, ((0, 0), (0, 128 - heads)))
    w_front = jnp.concatenate([w_qkv, beta_wide], axis=1)
    head_gain = out_norm_gain.astype(F32)[None]
    (
        projected, queries, key_rows, values, strength, sigma_vals, mixed,
        *saved, out_full, w_out, w_out_rows, cotangent_full, down_part,
    ) = front(
        width, depth, heads, main, persist, normed_full, w_qkv, beta_wide, taps, pad_rows, head_gain,
        out_native, cotangent, down_weight.T, down_rest,
    )
    down_tiles = lax.all_gather(down_part, "dp", axis=0)
    residual_mid, normed_two_full = middle(width, out_full, w_out, tokens, gain_second[None])
    normed_two_full, w_front = lax.optimization_barrier((normed_two_full, w_front))
    pair = product(normed_two_full, w_pair)
    tail = pair[:, 2 * main :]
    gate_out = jnp.concatenate([pair[:, :main], tail], axis=1)
    up_out = jnp.concatenate([pair[:, main : 2 * main], jnp.roll(tail, rest, axis=1)], axis=1)
    gate_sigma = jax.nn.sigmoid(gate_out)
    gate_silu = gate_out * gate_sigma
    hidden = (gate_silu * up_out).astype(BF)
    down_grads = down_gradients(width, depth, rest, cotangent_full, hidden)
    down_tiles, _ = lax.optimization_barrier((down_tiles, down_grads))
    down_sums = lax.psum_scatter(down_grads, "dp", scatter_dimension=0, tiled=True)
    pair_grad_low, w_down = hidden_gradients(width, rest, cotangent_full, pair, down_tiles)
    two_parts = product_right(pair_grad_low, w_pair).astype(BF)
    pair_grads = product_left(normed_two_full, pair_grad_low).astype(BF)
    pair_grads, two_parts = lax.optimization_barrier((pair_grads, two_parts))
    pair_sums = lax.psum_scatter(pair_grads, "dp", scatter_dimension=0, tiled=True)
    residual_mid_grad, gain_second_rows, mid_full = reduce_middle(
        width, two_parts, residual_mid, cotangent, gain_second[None]
    )
    projected_grad, conv_rows_grad, out_gain_rows, down_main, down_ends = back(
        width, heads, persist, mid_full, w_out_rows, mixed, head_gain, taps, projected,
        queries, key_rows, values, (strength, sigma_vals, pad_rows), saved, down_sums, main,
    )
    gain_second_grad = jnp.sum(gain_second_rows, axis=0)
    out_gain_grad = jnp.sum(out_gain_rows, axis=0)
    conv_grad = jnp.sum(conv_rows_grad, axis=1)
    mid_mine = lax.dynamic_slice_in_dim(mid_full, place * mine, mine, axis=1)
    mixer_grads, beta_grads = mixer_gradients(normed_full, projected_grad, out_full, mid_mine)
    beta_grad = beta_grads[:heads]
    mixer_sums = lax.psum_scatter(mixer_grads, "dp", scatter_dimension=0, tiled=True)
    normed_parts = product_right(projected_grad, w_front).astype(BF)
    hidden, normed_parts = lax.optimization_barrier((hidden, normed_parts))
    added_parts = product_right(hidden, w_down).astype(BF)
    tokens_grad, gain_first_rows, output = end(
        width, normed_parts, added_parts, tokens, residual_mid, residual_mid_grad, gain_first[None]
    )
    gain_first_grad = jnp.sum(gain_first_rows, axis=0)

    gain_row = jnp.pad(out_gain_grad[None], ((0, 0), (0, features - head_dim)))
    plane = jnp.concatenate([gain_first_grad[None], gain_second_grad[None], gain_row], axis=0)
    conv_rows = -(-3 * CONV * mine // features)
    conv_flat = jnp.pad(conv_grad.reshape(-1), (0, conv_rows * features - 3 * CONV * mine))
    levels = jnp.concatenate([beta_grad, conv_flat.reshape(conv_rows, features)], axis=0)
    sums, each, gate_main, up_main, pair_ends = small_sums(
        plane.reshape(8, -1), levels.reshape(8, -1), pair_sums, (main, main, 2 * rest), width, depth
    )
    def joined(front, back, at):
        back = back.reshape(owned, width, 2, rest)[:, :, at].reshape(owned, width * rest)
        return jnp.concatenate([front, back], axis=1).astype(F32)

    down_back = down_ends.reshape(owned // 2, width, 2, rest).transpose(2, 0, 1, 3)
    down_back = down_back.reshape(owned, width * rest)
    shard_gate, shard_up, shard_down = (
        joined(gate_main, pair_ends, 0),
        joined(up_main, pair_ends, 1),
        jnp.concatenate([down_main, down_back], axis=1).astype(F32).T,
    )
    sums = sums.reshape(3, features)
    each = each.reshape(width, heads + conv_rows, features)
    beta_total = each[:, :heads].reshape(width * heads, features).T
    conv_all = each[:, heads:].reshape(width, -1)[:, : 3 * CONV * mine]
    conv_all = conv_all.reshape(width, 3 * CONV, mine).transpose(1, 0, 2).reshape(-1, features)
    wide_sums = jnp.concatenate([sums[:2], conv_all], axis=0)
    own = level * width + place
    wide_own = lax.dynamic_slice_in_dim(wide_sums, own * owned, owned, axis=1)

    mixer_sums, gate_main = lax.optimization_barrier((mixer_sums, gate_main))
    shard_q, shard_k, shard_v, shard_o = (
        a.astype(F32) for a in closing([mixer_sums], width, [(mine,) * 4], 13)
    )

    return (
        output,
        tokens_grad,
        wide_own[0],
        shard_q,
        shard_k,
        shard_v,
        wide_own[2:].reshape(3, CONV, owned),
        beta_total,
        sums[2, :head_dim],
        shard_o,
        wide_own[1],
        shard_gate,
        shard_up,
        shard_down,
    )


def solution(mesh):
    in_specs = (
        P(("dp", "seq"), None),
        P("dp", "seq"),
        P("dp", "seq"),
        P(("dp", "seq")),
        P(("dp", "seq"), None),
        P(("dp", "seq"), None),
        P(("dp", "seq"), None),
        P(None, None, ("dp", "seq")),
        P(),
        P(),
        P(("dp", "seq"), None),
        P(("dp", "seq")),
        P(("dp", "seq"), None),
        P(("dp", "seq"), None),
        P(None, ("dp", "seq")),
        P(("dp", "seq"), None),
    )
    out_specs = (
        P(("dp", "seq"), None),
        P(("dp", "seq"), None),
        P(("dp", "seq")),
        P(("dp", "seq"), None),
        P(("dp", "seq"), None),
        P(("dp", "seq"), None),
        P(None, None, ("dp", "seq")),
        P(),
        P(),
        P(("dp", "seq"), None),
        P(("dp", "seq")),
        P(("dp", "seq"), None),
        P(("dp", "seq"), None),
        P(None, ("dp", "seq")),
    )

    def layer(*arrays):
        head_count, hidden_width = arrays[8].shape[1], arrays[12].shape[1]
        width = mesh.shape["seq"]
        rest, main = rest_and_main(hidden_width, width)
        by_heads = head_count % width == 0 and rest == 64 and main > 0
        by_heads = by_heads and width >= 4 and width & (width - 1) == 0 and head_count // width <= 8
        by_heads = by_heads and arrays[3].shape[0] // mesh.size % 32 == 0
        by_heads = by_heads and 128 % (arrays[3].shape[0] // mesh.size) == 0
        local = local_heads if by_heads else local_sequence
        return jax.shard_map(
            local, mesh=mesh, in_specs=in_specs, out_specs=out_specs, check_vma=False
        )(*arrays)

    return layer
```
